128 devices in a mesh: blk: 64 (over z, x_lo, y, core), head: 2 (over x_hi).
Axes of the slice: x: 4 (x_hi: 2, x_lo: 2; x = x_hi * 2 + x_lo), y: 4, z: 4, core: 2. Of those that a mesh axis runs over, the one named last changes fastest.
Arguments:
- tokens: bfloat16 [16384, 512], P('blk'), may hold values from -6 to 6
- cotangents: bfloat16 [2, 16384, 512], P(None, 'blk'), may hold values from -24 to 24
- segment_ids: int32 [16384], P('blk'), may hold values from 0 to 256, as said below
- in_weights: bfloat16 [3, 512, 512], P(None, None, 'head'), may hold values from -0.25 to 0.25
- in_biases: float32 [2, 512], P(None, 'head'), may hold values from -3 to 3
- out_weight: bfloat16 [512, 512], P('head'), may hold values from -6 to 6
- up_weight: bfloat16 [512, 2048], P(None, 'head'), may hold values from -0.25 to 0.25
- up_biases: float32 [2048], P('head'), may hold values from -3 to 3
- down_weight: bfloat16 [2048, 512], P('head'), may hold values from -0.125 to 0.125
- gains: float32 [2, 512], replicated, may hold values from 0.1 to 1.9
- shifts: float32 [4, 512], replicated, may hold values from -3 to 3
Outputs:
- mixed: bfloat16 [16384, 512], P('blk')
- grad_tokens: float32 [2, 16384, 512], P(None, 'blk')
- grad_in_weights: float32 [2, 3, 512, 512], P(None, None, None, 'head')
- grad_in_biases: float32 [2, 2, 512], P(None, None, 'head')
- grad_out_weight: float32 [2, 512, 512], P(None, 'head')
- grad_up_weight: float32 [2, 512, 2048], P(None, None, 'head')
- grad_up_biases: float32 [2, 2048], P(None, 'head')
- grad_down_weight: float32 [2, 2048, 512], P(None, 'head')
- grad_gains: float32 [2, 2, 512], replicated
- grad_shifts: float32 [2, 4, 512], replicated
The draws below stay inside these ranges and needn't reach their ends.
Inputs may be any that keep to these rules, and one draw needn't show every extreme that they name: `segment_ids`: id 0 is one image: in every block of 256 rows of one device its tokens come first, 64 times a number from 1 to 3 of them; in every draw some device holds 192 image tokens and another holds 64. Every other token has the id 1 + its position // 64, so each thumbnail is 64 tokens on one device.
All inputs are finite; a program needn't handle non-finite values.
Results may differ from the reference program's by a relative error of at most 0.025.
Values may be sent and summed in bfloat16 or wider, within the bound.
No kernel may reach another device: no remote copies, remote signals or barrier semaphores. Data moves between devices by JAX's collectives and lax.ppermute only.
A program may use at most 320 MiB of HBM per device.

```python
import math
import jax
import jax.numpy as jnp
from jax import lax

D = 512
HEADS = 8
HEAD_DIM = 64
FF = 2048
TOK_DEV = 256
THUMB = 64
TOKENS = 16384


def image_rows(key):
    key = jax.random.fold_in(key, 11)
    first_key, most_key, least_key = jax.random.split(key, 3)
    blocks = TOKENS // TOK_DEV
    slots = TOK_DEV // THUMB
    image_slots = jax.random.randint(first_key, (blocks,), 1, slots)
    fullest = jax.random.randint(most_key, (), 0, blocks)
    emptiest = (fullest + jax.random.randint(least_key, (), 1, blocks)) % blocks
    block_index = jnp.arange(blocks, dtype=jnp.int32)
    image_slots = jnp.where(block_index == fullest, slots - 1, image_slots)
    image_slots = jnp.where(block_index == emptiest, 1, image_slots)
    position = jnp.arange(TOKENS, dtype=jnp.int32)
    limit = jnp.repeat(image_slots, TOK_DEV, total_repeat_length=TOKENS) * THUMB
    within = position % TOK_DEV
    return (within < limit, position)


def draw_segment_ids(key, part):
    marked, position = image_rows(key)
    return jnp.where(marked, 0, 1 + position // THUMB).astype(jnp.int32)


def draw_cotangents(key, part):
    marked, position = image_rows(key)
    key = jax.random.fold_in(key, 29)
    noise = jnp.clip(jax.random.normal(key, (2, TOKENS, D), jnp.float32), -6.0, 6.0)
    factor = jnp.where(marked, 4.0, 0.5).astype(jnp.float32)
    return (noise * factor[None, :, None]).astype(jnp.bfloat16)


def levels(key, extent, shards, least, largest):
    factor_of = 1.0
    for dim, shards_of in shards:
        steps = jax.random.uniform(jax.random.fold_in(jax.random.fold_in(key, 6), dim), (shards_of,), jnp.float32, least / len(shards), largest / len(shards))
        factor_of = factor_of * jnp.repeat(jnp.exp(steps), extent[dim] // shards_of).reshape((-1,) + (1,) * (len(extent) - 1 - dim))
    return factor_of


def scatter_about(key, shape, width, bound, cuts=(), held_as=jnp.bfloat16):
    entries = jax.random.normal(key, shape, jnp.float32) * width
    if len(cuts) > 0:
        entries = levels(key, shape, cuts, -0.22, 0.18) * entries
    return jnp.clip(entries, min=-bound, max=bound).astype(held_as)


def setup_inputs(seed: int = 0) -> dict:
    seeds = jax.random.split(jax.random.key(seed), 12)
    tokens = scatter_about(seeds[0], (TOKENS, D), 1.0, 6.0, ((0, 64),))
    cotangents = draw_cotangents(jax.random.fold_in(seeds[11], 71), 0)
    segment_ids = draw_segment_ids(jax.random.fold_in(seeds[11], 71), 0)
    in_weights = scatter_about(seeds[3], (3, D, D), D ** -0.5, 0.25, ((2, 2),))
    in_biases = scatter_about(seeds[4], (2, D), 0.5, 3.0, ((1, 2),), jnp.float32)
    out_weight = scatter_about(seeds[5], (D, D), 1 ** -0.5, 6.0, ((0, 2),))
    up_weight = scatter_about(seeds[6], (D, FF), D ** -0.5, 0.25, ((1, 2),))
    up_biases = scatter_about(seeds[7], (FF,), 0.5, 3.0, ((0, 2),), jnp.float32)
    down_weight = scatter_about(seeds[8], (FF, D), FF ** -0.5, 0.125, ((0, 2),))
    gains = jnp.clip(1.0 + 0.18 * jax.random.normal(seeds[9], (2, D), jnp.float32), 0.1, 1.9)
    shifts = scatter_about(seeds[10], (4, D), 0.5, 3.0, (), jnp.float32)
    return {"tokens": tokens, "cotangents": cotangents, "segment_ids": segment_ids, "in_weights": in_weights, "in_biases": in_biases, "out_weight": out_weight, "up_weight": up_weight, "up_biases": up_biases, "down_weight": down_weight, "gains": gains, "shifts": shifts}


@jax.custom_vjp
def low(v):
    return lax.optimization_barrier(v.astype(jnp.bfloat16)).astype(jnp.float32)

@jax.custom_vjp
def low_back(v):
    return v

def low_keep(v):
    return (low(v), None)

def low_pass(kept, grad):
    return (grad,)

def back_keep(v):
    return (v, None)

def back_low(kept, grad):
    return (low(grad),)
low.defvjp(low_keep, low_pass)
low_back.defvjp(back_keep, back_low)
NEG = -1e+30
EPS = 1e-06
SCALE = 0.125

def product(left, right):
    return jnp.dot(left, right, precision=lax.Precision.HIGHEST)

def normalize(field, gain, shift):
    center = field - lax.optimization_barrier(jnp.mean(field, axis=-1, keepdims=True))
    spread = lax.optimization_barrier(jnp.mean(center * center, axis=-1, keepdims=True))
    return center * lax.rsqrt(spread + EPS) * gain + shift

def attend_block(query_block, label_block, key_heads, value_heads, labels):
    scores = low_back(jnp.einsum('qhd,khd->hqk', query_block, key_heads, precision=lax.Precision.HIGHEST) * SCALE)
    visible = (label_block[:, None] == labels[None, :])[None]
    masked = jnp.where(visible, scores, NEG)
    expo = jnp.exp(masked - lax.optimization_barrier(jnp.max(masked, axis=-1, keepdims=True)))
    total = lax.optimization_barrier(jnp.sum(expo, axis=-1))
    heads_out = jnp.einsum('hqk,khd->hqd', low(expo), value_heads, precision=lax.Precision.HIGHEST) / total[..., None]
    return jnp.transpose(heads_out, (1, 0, 2))

def forward(inputs, labels, in_weights, in_biases, out_weight, up_weight, up_biases, down_weight, gains, shifts):
    count = inputs.shape[0]
    hidden_one = low(normalize(inputs, gains[0], shifts[0]))
    query = low(low_back(product(hidden_one, in_weights[0]) + in_biases[0]))
    keys = low(low_back(product(hidden_one, in_weights[1])))
    values = low(low_back(product(hidden_one, in_weights[2]) + in_biases[1]))
    block = math.gcd(count, 512)
    query_blocks = query.reshape(count // block, block, HEADS, HEAD_DIM)
    label_blocks = labels.reshape(count // block, block)
    key_heads = keys.reshape(count, HEADS, HEAD_DIM)
    value_heads = values.reshape(count, HEADS, HEAD_DIM)

    def one_block(pair):
        return attend_block(pair[0], pair[1], key_heads, value_heads, labels)
    attended = lax.map(jax.checkpoint(one_block), (query_blocks, label_blocks)).reshape(count, D)
    attended = low(low_back(attended))
    middle = inputs + low_back(product(attended, out_weight) + shifts[1])
    hidden_two = low(normalize(middle, gains[1], shifts[2]))
    pre_gate = low_back(product(hidden_two, up_weight) + up_biases)
    activation = low(jax.nn.gelu(pre_gate, approximate=True))
    return middle + product(activation, down_weight) + shifts[3]

def reference(tokens, cotangents, segment_ids, in_weights, in_biases, out_weight, up_weight, up_biases, down_weight, gains, shifts):

    def layer(inputs, first_weights, first_biases, proj_weight, wide_weight, wide_biases, narrow_weight, norm_gains, norm_shifts):
        return forward(inputs, segment_ids, first_weights, first_biases, proj_weight, wide_weight, wide_biases, narrow_weight, norm_gains, norm_shifts)
    result, pullback = jax.vjp(layer, tokens.astype(jnp.float32), in_weights.astype(jnp.float32), in_biases, out_weight.astype(jnp.float32), up_weight.astype(jnp.float32), up_biases, down_weight.astype(jnp.float32), gains, shifts)
    first = pullback(cotangents[0].astype(jnp.float32))
    second = pullback(cotangents[1].astype(jnp.float32))
    stacked = [jnp.stack([first[entry], second[entry]], axis=0) for entry in range(9)]
    return (result.astype(jnp.bfloat16), stacked[0], stacked[1], stacked[2], stacked[3], stacked[4], stacked[5], stacked[6], stacked[7], stacked[8])
```

```python
import functools

import jax
import jax.numpy as jnp
from jax import lax
from jax.experimental import pallas as pl
from jax.experimental.pallas import tpu as pltpu
from jax.sharding import Mesh
from jax.sharding import PartitionSpec as P

HD = 64
LANES = 128
TILE = 64
BLOCK = 256
EPS = 1e-06
SCALE = 0.125
FAR = -1e30
BF = jnp.bfloat16
F32 = jnp.float32
VMEM_LIMIT = 56 * 1024 * 1024

NT = (((1,), (1,)), ((), ()))
TN = (((0,), (0,)), ((), ()))


def shift_by(array, axis, step):
    size = lax.axis_size(axis)
    return lax.ppermute(array, axis, [(i, (i + step) % size) for i in range(size)])


def dot(a, b):
    return jnp.dot(a, b, preferred_element_type=F32)


def dot_nt(a, b):
    return lax.dot_general(a, b, NT, preferred_element_type=F32)


def dot_tn(a, b):
    return lax.dot_general(a, b, TN, preferred_element_type=F32)


def normalize(field, gain, shift):
    center = field - jnp.mean(field, axis=-1, keepdims=True)
    spread = jnp.mean(center * center, axis=-1, keepdims=True)
    return center * lax.rsqrt(spread + EPS) * gain + shift


def pieces(value):
    high = value.astype(BF)
    rest = value - high.astype(F32)
    middle = rest.astype(BF)
    low = (rest - middle.astype(F32)).astype(BF)
    return high, middle, low


def iota(shape, dim):
    return lax.broadcasted_iota(jnp.int32, shape, dim)


def whole(count):
    return [pl.BlockSpec(memory_space=pltpu.VMEM)] * count


def count_of(ref, rows):
    return jnp.max(ref[rows : rows + 16, :LANES].astype(F32)).astype(jnp.int32)


def compact(counts, read, target, rows):
    start = jnp.int32(0)
    for g, n in enumerate(counts):
        target[pl.ds(pl.multiple_of(start, TILE), rows), :] = read(g)
        start = start + n * TILE
    return start


def attend_kernel(rows, groups, heads, *refs):
    near = refs[:groups]
    far, weights, biases, gains, shifts = refs[groups : groups + 5]
    out, hq, hk, qx, kx, vx, counts_ref = refs[groups + 5 : groups + 12]
    scores, place = refs[groups + 12], refs[groups + 13]
    width = heads * LANES
    model = far.shape[2]
    q_counts = [count_of(r, rows) for r in near]
    k_counts = [count_of(far.at[g], rows) for g in range(groups)]
    for g in range(groups):
        counts_ref[g] = q_counts[g]
        counts_ref[groups + g] = k_counts[g]

    def normal(block):
        return normalize(block.astype(F32), gains[0:1, :], shifts[0:1, :]).astype(BF)

    q_total = compact(q_counts, lambda g: normal(near[g][:rows, :]), hq, rows)
    k_total = compact(k_counts, lambda g: normal(far[g, :rows, :]), hk, rows)
    hq[pl.ds(pl.multiple_of(q_total, TILE), BLOCK), :] = jnp.zeros((BLOCK, model), BF)
    hk[pl.ds(pl.multiple_of(k_total, TILE), BLOCK), :] = jnp.zeros((BLOCK, model), BF)
    q_blocks = (q_total + BLOCK - 1) // BLOCK
    k_blocks = (k_total + BLOCK - 1) // BLOCK

    @pl.loop(0, q_blocks)
    def _(b):
        here = pl.ds(pl.multiple_of(b * BLOCK, BLOCK), BLOCK)
        qx[here, :] = (dot(hq[here, :], weights[:, :width]) + biases[:, :width]).astype(BF)

    @pl.loop(0, k_blocks)
    def _(b):
        here = pl.ds(pl.multiple_of(b * BLOCK, BLOCK), BLOCK)
        both = dot(hk[here, :], weights[:, width:]) + biases[:, width:]
        unseen = (iota((BLOCK, width), 0) + b * BLOCK >= k_total) & (
            iota((BLOCK, width), 1) % LANES == HD
        )
        kx[here, :] = jnp.where(unseen, FAR, both[:, :width]).astype(BF)
        vx[here, :] = both[:, width:].astype(BF)

    @pl.loop(0, q_blocks)
    def _(b):
        here = pl.ds(pl.multiple_of(b * BLOCK, BLOCK), BLOCK)

        def score(j, tops):
            there = pl.ds(pl.multiple_of(j * BLOCK, BLOCK), BLOCK)
            new = []
            for h in range(heads):
                lanes = slice(h * LANES, (h + 1) * LANES)
                s = dot_nt(qx[here, lanes], kx[there, lanes])
                scores[h, j] = s
                part = jnp.maximum(s[:, :LANES], s[:, LANES:])
                new.append(jnp.maximum(tops[h], part))
            return tuple(new)

        tops = lax.fori_loop(
            0, k_blocks, score, tuple(jnp.full((BLOCK, LANES), FAR, F32) for _ in range(heads))
        )
        tops = [jnp.max(t, axis=-1, keepdims=True) for t in tops]

        def weigh(j, sums):
            there = pl.ds(pl.multiple_of(j * BLOCK, BLOCK), BLOCK)
            new = []
            for h in range(heads):
                lanes = slice(h * LANES, (h + 1) * LANES)
                expo = jnp.exp(scores[h, j] - tops[h]).astype(BF)
                new.append(sums[h] + dot(expo, vx[there, lanes]))
            return tuple(new)

        sums = lax.fori_loop(
            0, k_blocks, weigh, tuple(jnp.zeros((BLOCK, LANES), F32) for _ in range(heads))
        )
        lane = iota((BLOCK, LANES), 1)
        stats = jnp.zeros((BLOCK, LANES), F32)
        for h in range(heads):
            total = sums[h][:, HD : HD + 1]
            place[here, h * HD : (h + 1) * HD] = (sums[h][:, :HD] / total).astype(BF)
            for i, piece in enumerate(pieces(tops[h] + jnp.log(total))):
                stats = jnp.where(lane == 3 * h + i, piece.astype(F32), stats)
        place[here, heads * HD :] = stats.astype(BF)

    start = jnp.int32(0)
    for g in range(groups):
        out[g] = place[pl.ds(pl.multiple_of(start, TILE), rows), :]
        start = start + q_counts[g] * TILE


def attend(near, far, weights, biases, gains, shifts, rows, heads):
    groups = len(near)
    model = far.shape[2]
    room = rows * groups + BLOCK
    width = heads * LANES
    parts = heads * HD + LANES
    return pl.pallas_call(
        functools.partial(attend_kernel, rows, groups, heads),
        out_shape=(
            jax.ShapeDtypeStruct((groups, rows, parts), BF),
            jax.ShapeDtypeStruct((room, model), BF),
            jax.ShapeDtypeStruct((room, model), BF),
            jax.ShapeDtypeStruct((room, width), BF),
            jax.ShapeDtypeStruct((room, width), BF),
            jax.ShapeDtypeStruct((room, width), BF),
            jax.ShapeDtypeStruct((2 * groups,), jnp.int32),
        ),
        in_specs=whole(groups + 5),
        out_specs=(*whole(6), pl.BlockSpec(memory_space=pltpu.SMEM)),
        scratch_shapes=[
            pltpu.VMEM((heads, room // BLOCK, BLOCK, BLOCK), F32),
            pltpu.VMEM((room, parts), BF),
        ],
        compiler_params=pltpu.CompilerParams(vmem_limit_bytes=VMEM_LIMIT),
        name="attend",
    )(*near, far, weights, biases, gains, shifts)


def expander(heads):
    row, col = (iota((LANES, heads * HD), d) for d in (0, 1))
    return (row // 3 == col // HD).astype(BF)


def selector(heads, offset):
    row, col = (iota((heads * HD, LANES), d) for d in (0, 1))
    return ((row % HD == 0) & (col == 3 * (row // HD) + offset)).astype(BF)


def same_tile(rows):
    return iota((rows, rows), 0) // TILE == iota((rows, rows), 1) // TILE


def own_kernel(heads, counts, tokens, weights, biases, gains, shifts, parts, low, full, lse, hidden, x):
    width = heads * LANES
    cols = heads * HD
    count = tokens.shape[0]
    rows = parts.shape[1]
    hidden[...] = normalize(tokens[...].astype(F32), gains[0:1, :], shifts[0:1, :]).astype(BF)
    x[...] = (dot(hidden[...], weights[...]) + biases[...]).astype(BF)
    spread = expander(heads)
    marks = [dot(parts[g, :, cols:], spread) for g in range(parts.shape[0])]
    top = functools.reduce(jnp.maximum, marks)
    expos = [jnp.exp(m - top) for m in marks]
    total = sum(expos)
    mixed = sum(e * parts[g, :, :cols].astype(F32) for g, e in enumerate(expos)) / total
    minus = -(top + jnp.log(total))
    packed = sum(
        dot(piece, selector(heads, i)) for i, piece in enumerate(pieces(minus))
    )
    lse[...] = packed.astype(BF)
    visible = same_tile(count - TILE)
    for h in range(heads):
        q = x[TILE:, h * LANES : (h + 1) * LANES]
        k = x[TILE:, width + h * LANES : width + (h + 1) * LANES]
        v = x[TILE:, 2 * width + h * LANES : 2 * width + (h + 1) * LANES]
        s = jnp.where(visible, dot_nt(q, k), FAR)
        e = jnp.exp(s - jnp.max(s, axis=-1, keepdims=True))
        o = dot(e.astype(BF), v)[:, :HD] / jnp.sum(e, axis=-1, keepdims=True)
        full[TILE:, h * HD : (h + 1) * HD] = o
    image = iota((rows, cols), 0) < counts[0] * TILE
    full[:TILE, :] = mixed[:TILE]
    full[TILE:rows, :] = jnp.where(image[TILE:], mixed[TILE:], full[TILE:rows, :])
    low[...] = full[...].astype(BF)


def own_rows(count, tokens, weights, biases, gains, shifts, parts, heads):
    size, model = tokens.shape
    rows = parts.shape[1]
    cols = heads * HD
    return pl.pallas_call(
        functools.partial(own_kernel, heads),
        out_shape=(
            jax.ShapeDtypeStruct((size, cols), BF),
            jax.ShapeDtypeStruct((size, cols), F32),
            jax.ShapeDtypeStruct((rows, LANES), BF),
            jax.ShapeDtypeStruct((size, model), BF),
            jax.ShapeDtypeStruct((size, 3 * heads * LANES), BF),
        ),
        in_specs=[pl.BlockSpec(memory_space=pltpu.SMEM)] + whole(6),
        out_specs=tuple(whole(5)),
        compiler_params=pltpu.CompilerParams(vmem_limit_bytes=VMEM_LIMIT),
        name="own_rows",
    )(count, tokens, weights, biases, gains, shifts, parts)


def thumb_kernel(heads, counts, x, grad, full, packed, out):
    width = heads * LANES
    cols = heads * HD
    size = x.shape[0]
    passes = grad.shape[0]
    rows = packed.shape[0]
    visible = same_tile(size - TILE)
    outside = iota((size - TILE, HD), 0) + TILE >= counts[0] * TILE
    lane = iota((rows, LANES), 1)
    stats = jnp.zeros((rows, LANES), F32)
    for p in range(passes):
        out[p, :TILE, :] = jnp.zeros((TILE, 3 * cols), BF)
        packed[:, p * cols : (p + 1) * cols] = grad[p, :rows, :]
    for h in range(heads):
        q = x[TILE:, h * LANES : (h + 1) * LANES]
        k = x[TILE:, width + h * LANES : width + (h + 1) * LANES]
        v = x[TILE:, 2 * width + h * LANES : 2 * width + h * LANES + HD]
        s = jnp.where(visible, dot_nt(q, k), FAR)
        e = jnp.exp(s - jnp.max(s, axis=-1, keepdims=True))
        w = e / jnp.sum(e, axis=-1, keepdims=True)
        w_low = w.astype(BF)
        for p in range(passes):
            g = grad[p, :, h * HD : (h + 1) * HD]
            delta = jnp.sum(g.astype(F32) * full[:, h * HD : (h + 1) * HD], axis=-1, keepdims=True)
            for i, piece in enumerate(pieces(-delta[:rows])):
                at = 3 * heads * (p + 1) + 3 * h + i
                stats = jnp.where(lane == at, piece.astype(F32), stats)
            gt = g[TILE:]
            ds = (w * (dot_nt(gt, v) - delta[TILE:])).astype(BF)
            dq = dot(ds, k[:, :HD]) * SCALE
            dk = dot_tn(ds, q)[:, :HD]
            dv = dot_tn(w_low, gt)
            for c, piece in enumerate((dq, dk, dv)):
                piece = jnp.where(outside, piece, 0.0).astype(BF)
                out[p, TILE:, c * cols + h * HD : c * cols + (h + 1) * HD] = piece
    packed[:, passes * cols :] = stats.astype(BF)


def thumb_back(count, x, grad, full, rows, heads):
    passes, size, cols = grad.shape
    return pl.pallas_call(
        functools.partial(thumb_kernel, heads),
        out_shape=(
            jax.ShapeDtypeStruct((rows, passes * cols + LANES), BF),
            jax.ShapeDtypeStruct((passes, size, 3 * cols), BF),
        ),
        in_specs=[pl.BlockSpec(memory_space=pltpu.SMEM)] + whole(3),
        out_specs=tuple(whole(2)),
        compiler_params=pltpu.CompilerParams(vmem_limit_bytes=VMEM_LIMIT),
        name="thumb_back",
    )(count, x, grad, full)


def spread_grads(heads, passes):
    cols = heads * HD
    row, col = (iota((passes * cols + LANES, heads * passes * LANES), d) for d in (0, 1))
    head, rest = col // (passes * LANES), col % (passes * LANES)
    turn, at = rest // LANES, rest % LANES
    plain = (at < HD) & (row == turn * cols + head * HD + at)
    extra = (
        (at >= HD)
        & (at < HD + 3)
        & (row == passes * cols + 3 * heads * (turn + 1) + 3 * head + at - HD)
    )
    return (plain | extra).astype(BF)


def spread_marks(heads):
    row, col = (iota((LANES, heads * LANES), d) for d in (0, 1))
    head, at = col // LANES, col % LANES
    return ((at >= HD + 1) & (at < HD + 4) & (row == 3 * head + at - HD - 1)).astype(BF)


def reverse_kernel(rows, groups, heads, passes, *refs):
    counts = refs[0]
    grads = refs[1 : 1 + groups]
    hq, hk, qx_in, kx, vx, key_t = refs[1 + groups : 7 + groups]
    out_q, out_kv, out_in, out_bias = refs[7 + groups : 11 + groups]
    packed, qx, gx, kt, dq_t, dv, dk, low_q, low_kv = refs[11 + groups :]
    cols = heads * HD
    wide = passes * LANES
    q_counts = [counts[g] for g in range(groups)]
    k_counts = [counts[groups + g] for g in range(groups)]
    q_total = compact(q_counts, lambda g: grads[g][...], packed, rows)
    k_total = sum(k_counts) * TILE
    tail_lane = iota((BLOCK, packed.shape[1]), 1) - passes * cols
    empty = (tail_lane >= 0) & (tail_lane < 3 * heads) & (tail_lane % 3 == 0)
    packed[pl.ds(pl.multiple_of(q_total, TILE), BLOCK), :] = jnp.where(empty, FAR, 0.0).astype(BF)
    q_blocks = (q_total + BLOCK - 1) // BLOCK
    k_blocks = (k_total + BLOCK - 1) // BLOCK
    to_grads, to_marks = spread_grads(heads, passes), spread_marks(heads)

    @pl.loop(0, q_blocks)
    def _(b):
        here = pl.ds(pl.multiple_of(b * BLOCK, BLOCK), BLOCK)
        marks = dot(packed[here, passes * cols :], to_marks)
        qx[here, :] = (qx_in[here, :].astype(F32) + marks).astype(BF)
        gx[here, :] = dot(packed[here, :], to_grads).astype(BF)
        dq_t[b] = jnp.zeros(dq_t.shape[1:], F32)

    out_in[...] = jnp.zeros(out_in.shape, F32)
    out_bias[...] = jnp.zeros(out_bias.shape, F32)

    @pl.loop(0, k_blocks)
    def _(j):
        there = pl.ds(pl.multiple_of(j * BLOCK, BLOCK), BLOCK)
        kt[...] = dot_nt(key_t[...], hk[there, :]).astype(BF)
        dv[...] = jnp.zeros(dv.shape, F32)
        dk[...] = jnp.zeros(dk.shape, F32)

        @pl.loop(0, q_blocks)
        def _(b):
            here = pl.ds(pl.multiple_of(b * BLOCK, BLOCK), BLOCK)
            for h in range(heads):
                lanes = slice(h * LANES, (h + 1) * LANES)
                q = qx[here, lanes]
                g = gx[here, h * wide : (h + 1) * wide]
                w = jnp.exp(dot_nt(kx[there, lanes], q))
                dv[h] += dot(w.astype(BF), g)
                for p in range(passes):
                    ds = dot_nt(vx[there, lanes], g[:, p * LANES : (p + 1) * LANES])
                    ds = (w * ds).astype(BF)
                    dk[p, h] += dot(ds, q)
                    span = slice(h * HD, (h + 1) * HD)
                    dq_t[b, p, span, :] += dot(kt[span, :], ds)

        for p in range(passes):
            for h in range(heads):
                at = 2 * cols * p + h * HD
                low_kv[there, at : at + HD] = dk[p, h][:, :HD].astype(BF)
                piece = dv[h][:, p * LANES : p * LANES + HD].astype(BF)
                low_kv[there, at + cols : at + cols + HD] = piece
        block = low_kv[there, :]
        out_in[:, passes * cols :] += dot_tn(hk[there, :], block)
        out_bias[0:1, passes * cols :] += jnp.sum(block.astype(F32), axis=0, keepdims=True)

    @pl.loop(0, q_blocks)
    def _(b):
        here = pl.ds(pl.multiple_of(b * BLOCK, BLOCK), BLOCK)
        for p in range(passes):
            low_q[here, p * cols : (p + 1) * cols] = (jnp.transpose(dq_t[b, p]) * SCALE).astype(BF)
        block = low_q[here, :]
        out_in[:, : passes * cols] += dot_tn(hq[here, :], block)
        out_bias[0:1, : passes * cols] += jnp.sum(block.astype(F32), axis=0, keepdims=True)

    starts = jnp.int32(0)
    for g in range(groups):
        out_kv[g] = low_kv[pl.ds(pl.multiple_of(starts, TILE), rows), :]
        starts = starts + k_counts[g] * TILE
    starts = jnp.int32(0)
    for g in range(groups):
        slot = counts[2 * groups + g]
        out_q[slot] = low_q[pl.ds(pl.multiple_of(starts, TILE), rows), :]
        starts = starts + q_counts[g] * TILE


def reverse(counts, grads, hq, hk, qx, kx, vx, key_t, rows, heads, passes):
    groups = len(grads)
    model = hq.shape[1]
    room = rows * groups + BLOCK
    cols = heads * HD
    return pl.pallas_call(
        functools.partial(reverse_kernel, rows, groups, heads, passes),
        out_shape=(
            jax.ShapeDtypeStruct((groups, rows, passes * cols), BF),
            jax.ShapeDtypeStruct((groups, rows, passes * 2 * cols), BF),
            jax.ShapeDtypeStruct((model, passes * 3 * cols), F32),
            jax.ShapeDtypeStruct((8, passes * 3 * cols), F32),
        ),
        in_specs=[pl.BlockSpec(memory_space=pltpu.SMEM)] + whole(groups + 6),
        out_specs=tuple(whole(4)),
        scratch_shapes=[
            pltpu.VMEM((room, passes * cols + LANES), BF),
            pltpu.VMEM((room, heads * LANES), BF),
            pltpu.VMEM((room, heads * passes * LANES), BF),
            pltpu.VMEM((cols, BLOCK), BF),
            pltpu.VMEM((room // BLOCK, passes, cols, BLOCK), F32),
            pltpu.VMEM((heads, BLOCK, passes * LANES), F32),
            pltpu.VMEM((passes, heads, BLOCK, LANES), F32),
            pltpu.VMEM((room, passes * cols), BF),
            pltpu.VMEM((room, passes * 2 * cols), BF),
        ],
        compiler_params=pltpu.CompilerParams(vmem_limit_bytes=VMEM_LIMIT),
        name="reverse",
    )(counts, *grads, hq, hk, qx, kx, vx, key_t)


def gather_near(array):
    mine = [array] + [shift_by(array, "y", d) for d in range(1, lax.axis_size("y"))]
    return mine + [shift_by(a, "c", 1) for a in mine]


def to_each(array, axes):
    size = lax.axis_size(axes)
    return lax.all_to_all(jnp.broadcast_to(array[None], (size, *array.shape)), axes, 0, 0, tiled=True)


def summed_over(array, axis):
    size = lax.axis_size(axis)
    parts = array.reshape(size, array.shape[0] // size, array.shape[1])
    parts = lax.all_to_all(parts, axis, 0, 0, tiled=True)
    return jnp.sum(parts.astype(F32), axis=0).astype(BF)


def with_partner(array, axis):
    low = array.astype(BF)
    return low.astype(F32) + shift_by(low, axis, 1).astype(F32)


def total(array):
    for axis in ("c", "y", "z"):
        array = summed_over(array, axis)
    array = with_partner(array, "xl").astype(BF)
    for axis in ("z", "y", "c"):
        array = to_each(array, axis).reshape(-1, array.shape[1])
    return array


def padded(weight, heads):
    lead = weight.shape[0]
    return jnp.pad(weight.reshape(lead, heads, HD), ((0, 0), (0, 0), (0, LANES - HD))).reshape(
        lead, heads * LANES
    )


def local(
    tokens,
    cotangents,
    segment_ids,
    in_weights,
    in_biases,
    out_weight,
    up_weight,
    up_biases,
    down_weight,
    gains,
    shifts,
):
    size, model = tokens.shape
    passes = cotangents.shape[0]
    cols = in_weights.shape[2]
    heads = cols // HD
    rows = size - TILE
    hidden_units = up_weight.shape[1]

    number = jnp.sum((segment_ids == 0).astype(jnp.int32)) // TILE
    own_count = number.reshape(1)
    told = jnp.concatenate(
        [tokens[:rows], jnp.full((16, model), number.astype(BF), BF)], axis=0
    )
    near = gather_near(told)
    far = to_each(told, ("z", "xl"))

    weights = jnp.concatenate(
        [
            padded(in_weights[0] * jnp.asarray(SCALE, BF), heads),
            padded(in_weights[1], heads),
            padded(in_weights[2], heads),
        ],
        axis=1,
    )
    lane = jnp.arange(heads * LANES) % LANES
    biases = jnp.concatenate(
        [
            padded(in_biases[0:1] * SCALE, heads) + (lane == HD),
            ((lane > HD) & (lane < HD + 4)).astype(F32)[None],
            padded(in_biases[1:2], heads) + ((lane >= HD) & (lane < HD + 3)),
        ],
        axis=1,
    )
    key_t = jnp.transpose(in_weights[1])
    parts, hq, hk, qx, kx, vx, counts = attend(
        near, far, weights, biases, gains, shifts, rows, heads
    )
    y, c = lax.axis_index("y"), lax.axis_index("c")
    y_size = lax.axis_size("y")
    steps = jnp.arange(len(near), dtype=jnp.int32)
    slots = ((y - steps % y_size) % y_size) * 2 + jnp.where(steps < y_size, c, 1 - c)
    counts = jnp.concatenate([counts, slots.astype(jnp.int32)])
    parts = jnp.take(parts, jnp.argsort(slots), axis=0)
    parts = lax.all_to_all(parts, ("y", "c"), 0, 0, tiled=True)
    low, full, lse, hidden_one, x = own_rows(
        own_count, tokens, weights, biases, gains, shifts, parts, heads
    )

    inputs = tokens.astype(F32)
    branch = with_partner(dot(low, out_weight), "h")
    middle = inputs + (branch + shifts[1])
    hidden_two = normalize(middle, gains[1], shifts[2]).astype(BF)
    pre_gate = dot(hidden_two, up_weight) + up_biases
    smooth = functools.partial(jax.nn.gelu, approximate=True)
    activation, gate_back = jax.vjp(smooth, pre_gate)
    activation = activation.astype(BF)
    output = with_partner(dot(activation, down_weight), "h")
    mixed = (middle + (output + shifts[3])).astype(BF)
    _, second_back = jax.vjp(normalize, middle, gains[1], shifts[2])
    _, first_back = jax.vjp(normalize, inputs, gains[0], shifts[0])

    outer = cotangents.astype(F32)
    shift_down = jnp.sum(outer, axis=1)
    grad_down = jnp.einsum("tf,ptd->pfd", activation, cotangents, preferred_element_type=F32)
    grad_act = jnp.einsum("ptd,fd->ptf", cotangents, down_weight, preferred_element_type=F32)
    grad_pre = jax.vmap(lambda g: gate_back(g)[0])(grad_act).astype(BF)
    grad_up = jnp.einsum("td,ptf->pdf", hidden_two, grad_pre, preferred_element_type=F32)
    grad_up_bias = jnp.sum(grad_pre.astype(F32), axis=1)
    grad_two = with_partner(
        jnp.einsum("ptf,df->ptd", grad_pre, up_weight, preferred_element_type=F32), "h"
    )
    norm_part, gain_two, shift_two = jax.vmap(second_back)(grad_two)
    grad_mid = outer + norm_part
    grad_mid_low = grad_mid.astype(BF)
    shift_out = jnp.sum(grad_mid_low.astype(F32), axis=1)
    grad_proj = jnp.einsum("tj,ptd->pjd", low, grad_mid_low, preferred_element_type=F32)
    grad_att = jnp.einsum(
        "ptd,jd->ptj", grad_mid_low, out_weight, preferred_element_type=F32
    ).astype(BF)

    packed, thumbs = thumb_back(own_count, x, grad_att, full, rows, heads)
    packed = packed + jnp.pad(lse, ((0, 0), (passes * cols, 0)))
    part_q, part_kv, part_in, part_bias = reverse(
        counts, gather_near(packed), hq, hk, qx, kx, vx, key_t, rows, heads, passes
    )
    early = total(
        jnp.concatenate(
            [
                grad_down.reshape(-1, model),
                grad_up.reshape(-1, model),
                grad_proj.reshape(-1, model),
            ],
            axis=0,
        ).astype(BF)
    )
    thumb_in = jnp.einsum("td,ptj->dpj", hidden_one, thumbs, preferred_element_type=F32)
    thumb_in = thumb_in.reshape(model, passes, 3, cols)
    part_bias = part_bias[0]

    def arranged(flat):
        q = flat[..., : passes * cols].reshape(*flat.shape[:-1], passes, 1, cols)
        kv = flat[..., passes * cols :].reshape(*flat.shape[:-1], passes, 2, cols)
        return jnp.concatenate([q, kv], axis=-2)

    part_in = jnp.transpose(arranged(part_in) + thumb_in, (1, 2, 0, 3))
    bias = arranged(part_bias) + jnp.sum(thumbs.astype(F32), axis=1).reshape(passes, 3, cols)
    late = total(part_in.reshape(-1, model).astype(BF))

    image = (jnp.arange(rows) < number * TILE)[None, :, None]
    sum_q = jnp.sum(
        lax.all_to_all(part_q, ("y", "c"), 0, 0, tiled=True).astype(F32), axis=0
    )
    sum_kv = jnp.sum(
        lax.all_to_all(part_kv, ("z", "xl"), 0, 0, tiled=True).astype(F32), axis=0
    )
    sum_q = sum_q.reshape(rows, passes, cols)
    sum_kv = sum_kv.reshape(rows, passes, 2 * cols)
    sums = jnp.transpose(jnp.concatenate([sum_q, sum_kv], axis=-1), (1, 0, 2))
    sums = jnp.where(image, sums.astype(BF), thumbs[:, :rows])
    grad_qkv = jnp.concatenate([sums, thumbs[:, rows:]], axis=1)
    grad_one = with_partner(
        jnp.einsum(
            "ptcj,cdj->ptd",
            grad_qkv.reshape(passes, size, 3, cols),
            in_weights,
            preferred_element_type=F32,
        ),
        "h",
    )
    first_part, gain_one, shift_one = jax.vmap(first_back)(grad_one)
    grad_tokens = grad_mid + first_part

    gain_rows = jnp.stack([gain_one, gain_two], axis=1)
    shift_rows = jnp.stack([shift_one, shift_out, shift_two, shift_down], axis=1)
    small = jnp.concatenate(
        [
            jnp.stack([bias[:, 0], bias[:, 2]], axis=1).reshape(-1, model),
            grad_up_bias.reshape(-1, model),
            gain_rows.reshape(-1, model),
            shift_rows.reshape(-1, model),
        ],
        axis=0,
    )
    for axis in ("c", "y", "z", "xl"):
        small = jnp.sum(to_each(small, axis), axis=0)

    early, late = early.astype(F32), late.astype(F32)
    down_rows = passes * hidden_units
    out_rows = passes * cols
    at = [down_rows, 2 * down_rows]
    bias_rows = passes * 2 * cols // model
    up_rows = passes * hidden_units // model
    cut = [bias_rows, bias_rows + up_rows, bias_rows + up_rows + 2 * passes]
    return (
        mixed,
        grad_tokens,
        late.reshape(passes, 3, model, cols),
        small[: cut[0]].reshape(passes, 2, cols),
        early[at[1] :].reshape(passes, cols, model),
        early[at[0] : at[1]].reshape(passes, model, hidden_units),
        small[cut[0] : cut[1]].reshape(passes, hidden_units),
        early[: at[0]].reshape(passes, hidden_units, model),
        small[cut[1] : cut[2]].reshape(passes, 2, model),
        small[cut[2] :].reshape(passes, 4, model),
    )


def solution(mesh):
    fine = Mesh(mesh.devices.reshape(4, 2, 4, 2, 2), ("z", "xl", "y", "c", "h"))
    blk = ("z", "xl", "y", "c")
    return jax.shard_map(
        local,
        mesh=fine,
        in_specs=(
            P(blk, None),
            P(None, blk, None),
            P(blk),
            P(None, None, "h"),
            P(None, "h"),
            P("h", None),
            P(None, "h"),
            P("h"),
            P("h", None),
            P(),
            P(),
        ),
        out_specs=(
            P(blk, None),
            P(None, blk, None),
            P(None, None, None, "h"),
            P(None, None, "h"),
            P(None, "h", None),
            P(None, None, "h"),
            P(None, "h"),
            P(None, "h", None),
            P(),
            P(),
        ),
        check_vma=False,
    )
```

```python
import functools

import jax
import jax.numpy as jnp
from jax import lax
from jax.experimental import pallas as pl
from jax.experimental.pallas import tpu as pltpu
from jax.sharding import Mesh
from jax.sharding import PartitionSpec as P

HD = 64
LANES = 128
TILE = 64
BLOCK = 256
EPS = 1e-06
SCALE = 0.125
FAR = -1e30
BF = jnp.bfloat16
F32 = jnp.float32
MIB = 1024 * 1024
REVERSE_ROOM = 40

NT = (((1,), (1,)), ((), ()))
TN = (((0,), (0,)), ((), ()))


def shift_by(array, axis, step):
    size = lax.axis_size(axis)
    return lax.ppermute(array, axis, [(i, (i + step) % size) for i in range(size)])


def dot(a, b):
    return jnp.dot(a, b, preferred_element_type=F32)


def dot_nt(a, b):
    return lax.dot_general(a, b, NT, preferred_element_type=F32)


def dot_tn(a, b):
    return lax.dot_general(a, b, TN, preferred_element_type=F32)


def standard(field):
    center = field - jnp.mean(field, axis=-1, keepdims=True)
    factor = lax.rsqrt(jnp.mean(center * center, axis=-1, keepdims=True) + EPS)
    return center * factor, factor


def norm_back(grad, gain, xhat, factor):
    h = grad * gain
    mean = jnp.mean(h, axis=-1, keepdims=True)
    return factor * (h - mean - xhat * jnp.mean(h * xhat, axis=-1, keepdims=True))


def pieces(value):
    high = value.astype(BF)
    rest = value - high.astype(F32)
    middle = rest.astype(BF)
    low = (rest - middle.astype(F32)).astype(BF)
    return high, middle, low


def iota(shape, dim):
    return lax.broadcasted_iota(jnp.int32, shape, dim)


VMEM = pl.BlockSpec(memory_space=pltpu.VMEM)
SMEM = pl.BlockSpec(memory_space=pltpu.SMEM)


def local_call(body, name, out, ins, outs, args, scratch=(), cost=None, room=16):
    return pl.pallas_call(
        body,
        out_shape=out,
        in_specs=ins,
        out_specs=outs,
        scratch_shapes=scratch,
        cost_estimate=cost,
        compiler_params=pltpu.CompilerParams(vmem_limit_bytes=room * MIB),
        name=name,
    )(*args)


def shaped(*shape, dtype=BF):
    return jax.ShapeDtypeStruct(shape, dtype)


def cost(micros):
    return pl.CostEstimate(flops=int(micros * 1e9), bytes_accessed=0, transcendentals=0)


def front_kernel(tokens, ids, told, copies, number):
    rows = told.shape[0] - 16
    marks = jnp.where(ids[...] == 0, 1.0, 0.0)
    tiles = jnp.sum(marks).astype(jnp.int32) // TILE
    number[0] = tiles
    told[:rows, :] = tokens[:rows, :]
    told[rows:, :] = jnp.full((16, told.shape[1]), tiles.astype(F32), F32).astype(BF)
    for g in range(copies.shape[0]):
        copies[g] = told[...]


def front(tokens, ids, copies):
    size, model = tokens.shape
    told = size - TILE + 16
    return local_call(
        front_kernel,
        "front",
        (shaped(told, model), shaped(copies, told, model), shaped(1, dtype=jnp.int32)),
        [VMEM, VMEM],
        (VMEM, VMEM, SMEM),
        (tokens, ids.reshape(-1, LANES)),
    )


def bundle_kernel(place, up, down, bias, out_weight, out):
    core = place[0]
    half = out.shape[1]
    at = pl.ds(pl.multiple_of(core * half, half), half)
    out[:half, :] = up[:, at]
    out[half : 2 * half, :] = down[at, :]
    mine = jnp.where(core == 0, bias[:, :half], bias[:, half:])
    row = iota((16, half), 0)
    rows = jnp.zeros((16, half), F32)
    for i, piece in enumerate(pieces(mine)):
        rows = jnp.where(row == i, piece.astype(F32), rows)
    out[2 * half : 2 * half + 16, :] = rows.astype(BF)
    out[2 * half + 16 :, :] = out_weight[...]


def bundled(core, up, down, bias, out_weight):
    model = up.shape[0]
    return local_call(
        bundle_kernel,
        "bundle",
        shaped(2 * model + 16 + out_weight.shape[0], model),
        [SMEM] + [VMEM] * 4,
        VMEM,
        (core, up, down, bias, out_weight),
    )


def count_of(ref, rows):
    return jnp.max(ref[rows : rows + 16, :LANES].astype(F32)).astype(jnp.int32)


def rows_at(start, rows, step=TILE):
    return pl.ds(pl.multiple_of(start, step), rows)


def attend_kernel(rows, groups, heads, *refs):
    near = refs[:groups]
    far, weights, biases, gains, shifts = refs[groups : groups + 5]
    out, give = refs[groups + 5 : groups + 5 + groups // 2], refs[groups + 5 + groups // 2]
    xq, xk, qx, kx, vx, counts, place = refs[groups + 6 + groups // 2 :]
    model = far.shape[2]
    q_counts = [count_of(r, rows) for r in near]
    k_counts = [count_of(far.at[g], rows) for g in range(groups)]
    for g in range(groups):
        counts[g] = q_counts[g]
        counts[groups + g] = k_counts[g]

    def compact(numbers, read, target):
        start = jnp.int32(0)
        for g, n in enumerate(numbers):
            target[rows_at(start, rows), :] = read(g)
            start = start + n * TILE
        target[rows_at(start, BLOCK), :] = jnp.zeros((BLOCK, model), BF)
        return start

    q_total = compact(q_counts, lambda g: near[g][:rows, :], xq)
    k_total = compact(k_counts, lambda g: far[g, :rows, :], xk)
    q_blocks = (q_total + BLOCK - 1) // BLOCK
    k_blocks = (k_total + BLOCK - 1) // BLOCK
    width = heads * LANES

    def hidden(ref, here):
        clean = standard(ref[here, :].astype(F32))[0].astype(BF)
        ref[here, :] = clean
        return (clean.astype(F32) * gains[0:1, :] + shifts[0:1, :]).astype(BF)

    @pl.loop(0, q_blocks)
    def _(b):
        here = rows_at(b * BLOCK, BLOCK, BLOCK)
        q = (dot(hidden(xq, here), weights[:, :width]) + biases[:, :width]).astype(BF)
        for h in range(heads):
            qx[h, here, :] = q[:, h * LANES : (h + 1) * LANES]

    @pl.loop(0, k_blocks)
    def _(b):
        here = rows_at(b * BLOCK, BLOCK, BLOCK)
        both = dot(hidden(xk, here), weights[:, width:]) + biases[:, width:]
        unseen = (iota((BLOCK, width), 0) + b * BLOCK >= k_total) & (
            iota((BLOCK, width), 1) % LANES == HD
        )
        k = jnp.where(unseen, FAR, both[:, :width]).astype(BF)
        v = both[:, width:].astype(BF)
        for h in range(heads):
            kx[h, here, :] = k[:, h * LANES : (h + 1) * LANES]
            vx[h, here, :] = v[:, h * LANES : (h + 1) * LANES]

    def attend_all(span):
        @pl.loop(0, q_blocks)
        def _(b):
            here = rows_at(b * BLOCK, BLOCK, BLOCK)
            lane = iota((BLOCK, LANES), 1)
            for h in range(heads):
                s = dot_nt(qx[h, here, :], kx[h, :span, :])
                top = jnp.max(s, axis=-1, keepdims=True)
                o = dot(jnp.exp(s - top).astype(BF), vx[h, :span, :])
                total = o[:, HD : HD + 1]
                o = o / total
                for i, piece in enumerate(pieces(top + jnp.log(total))):
                    o = jnp.where(lane == HD + i, piece.astype(F32), o)
                place[h, here, :] = o.astype(BF)

    for blocks in range(groups * TILE // BLOCK, groups * rows // BLOCK + 1):
        pl.when(k_blocks == blocks)(functools.partial(attend_all, blocks * BLOCK))

    gather = [
        (iota((LANES, LANES), 0) - HD + 3 * h == iota((LANES, LANES), 1))
        & (iota((LANES, LANES), 0) >= HD)
        & (iota((LANES, LANES), 0) < HD + 3)
        for h in range(heads)
    ]
    gather = [jnp.where(m, 1.0, 0.0).astype(BF) for m in gather]
    start = jnp.int32(0)
    for g in range(groups):
        mine = [place[h, rows_at(start, rows), :] for h in range(heads)]
        stats = sum(dot(m, s) for m, s in zip(mine, gather)).astype(BF)
        value = jnp.concatenate([m[:, :HD] for m in mine] + [stats], axis=1)
        if g < groups // 2:
            out[g][...] = value
        else:
            give[g - groups // 2] = value
        start = start + q_counts[g] * TILE


def attend(near, far, weights, biases, gains, shifts, rows, heads):
    groups = len(near)
    model = far.shape[2]
    room = rows * groups + BLOCK
    parts = heads * HD + LANES
    return local_call(
        functools.partial(attend_kernel, rows, groups, heads),
        "attend",
        (
            *[shaped(rows, parts)] * (groups // 2),
            shaped(groups // 2, rows, parts),
            shaped(room, model),
            shaped(room, model),
            shaped(heads, room, LANES),
            shaped(heads, room, LANES),
            shaped(heads, room, LANES),
            shaped(2 * groups, dtype=jnp.int32),
        ),
        [VMEM] * (groups + 5),
        (*[VMEM] * (groups // 2 + 6), SMEM),
        (*near, far, weights, biases, gains, shifts),
        [pltpu.VMEM((heads, room, LANES), BF)],
        cost(15),
        32,
    )


def same_tile(rows):
    return iota((rows, rows), 0) // TILE == iota((rows, rows), 1) // TILE


def thumb_kernel(heads, tokens, weights, biases, gains, shifts, out, xhat, x):
    width = heads * LANES
    size = tokens.shape[0]
    clean = standard(tokens[...].astype(F32))[0].astype(BF)
    xhat[...] = clean
    hidden = (clean.astype(F32) * gains[0:1, :] + shifts[0:1, :]).astype(BF)
    x[...] = (dot(hidden, weights[...]) + biases[...]).astype(BF)
    visible = same_tile(size - TILE)
    out[:TILE, :] = jnp.zeros((TILE, heads * HD), F32)
    for h in range(heads):
        q = x[TILE:, h * LANES : (h + 1) * LANES]
        k = x[TILE:, width + h * LANES : width + (h + 1) * LANES]
        v = x[TILE:, 2 * width + h * LANES : 2 * width + (h + 1) * LANES]
        s = jnp.where(visible, dot_nt(q, k), FAR)
        e = jnp.exp(s - jnp.max(s, axis=-1, keepdims=True))
        o = dot(e.astype(BF), v)[:, :HD] / jnp.sum(e, axis=-1, keepdims=True)
        out[TILE:, h * HD : (h + 1) * HD] = o


def thumbs(tokens, weights, biases, gains, shifts, heads):
    size, model = tokens.shape
    return local_call(
        functools.partial(thumb_kernel, heads),
        "thumbs",
        (
            shaped(size, heads * HD, dtype=F32),
            shaped(size, model),
            shaped(size, 3 * heads * LANES),
        ),
        [VMEM] * 5,
        (VMEM,) * 3,
        (tokens, weights, biases, gains, shifts),
        cost=cost(5),
    )


def zero_one(mask):
    return jnp.where(mask, 1.0, 0.0).astype(BF)


def merged(parts, heads):
    cols = heads * HD
    row, col = (iota((LANES, cols), d) for d in (0, 1))
    spread = zero_one(row // 3 == col // HD)
    marks = [dot(p[:, cols:], spread) for p in parts]
    top = functools.reduce(jnp.maximum, marks)
    expos = [jnp.exp(m - top) for m in marks]
    total = sum(expos)
    mixed = sum(e * p[:, :cols].astype(F32) for p, e in zip(parts, expos)) / total
    row, col = (iota((cols, LANES), d) for d in (0, 1))
    packed = [
        dot(piece, zero_one((row % HD == 0) & (col == 3 * (row // HD) + i)))
        for i, piece in enumerate(pieces(top + jnp.log(total)))
    ]
    return mixed, sum(packed)


def pair_kernel(heads, *refs):
    count = (len(refs) - 1) // 2
    for j, (mine, out) in enumerate(zip(refs[:count], refs[count + 1 :])):
        mixed, marks = merged([mine[...], refs[count][j]], heads)
        out[...] = jnp.concatenate([mixed.astype(BF), marks.astype(BF)], axis=1)


def pair_merge(parts, other, heads):
    return local_call(
        functools.partial(pair_kernel, heads),
        "pair_merge",
        tuple(shaped(*p.shape) for p in parts),
        [VMEM] * (len(parts) + 1),
        (VMEM,) * len(parts),
        (*parts, other),
        cost=cost(3),
    )


def merge_kernel(heads, counts, thumb, *refs):
    parts, (low, full, lse) = refs[:-3], refs[-3:]
    cols = heads * HD
    rows = lse.shape[0]
    mixed, marks = merged([p[...] for p in parts], heads)
    lse[...] = (-marks).astype(BF)
    image = iota((rows, cols), 0) < counts[0] * TILE
    full[:rows, :] = jnp.where(image, mixed, thumb[:rows, :])
    full[rows:, :] = thumb[rows:, :]
    low[...] = full[...].astype(BF)


def merge(count, parts, thumb, heads):
    size, cols = thumb.shape
    return local_call(
        functools.partial(merge_kernel, heads),
        "merge",
        (shaped(size, cols), shaped(size, cols, dtype=F32), shaped(parts[0].shape[0], LANES)),
        [SMEM] + [VMEM] * (1 + len(parts)),
        (VMEM,) * 3,
        (count, thumb, *parts),
        cost=cost(3),
    )


def fold_kernel(*refs):
    count = (len(refs) - 1) // 2
    for j, (mine, out) in enumerate(zip(refs[:count], refs[count + 1 :])):
        out[...] = (mine[...].astype(F32) + refs[count][j].astype(F32)).astype(BF)


def fold(parts, other):
    return local_call(
        fold_kernel,
        "fold",
        tuple(shaped(*p.shape) for p in parts),
        [VMEM] * (len(parts) + 1),
        (VMEM,) * len(parts),
        (*parts, other),
        cost=cost(2),
    )


ROOT = 0.7978845608028654
CUBE = 0.044715


def ff_kernel(
    heads, tokens, outer, low, low_far, full, lse, out_weight, up, up_bias, down, far_one, far_two,
    gains, shifts, mixed, grad_mid, grad_low, packed, hidden_out, act_out, pre_out, small,
):
    size, model = tokens.shape
    passes = outer.shape[0]
    cols = heads * HD
    chunk = far_one.shape[1]
    units = up.shape[1]
    rows = packed.shape[0]
    branch = dot(low[...], out_weight[...]) + dot(
        low_far[...], far_one[2 * chunk + 16 :, :]
    )
    middle = tokens[...].astype(F32) + (branch + shifts[1:2, :])
    xhat, factor = standard(middle)
    hidden = (xhat * gains[1:2, :] + shifts[2:3, :]).astype(BF)
    hidden_out[...] = hidden

    def one_chunk(up_part, bias, down_part, keep):
        v = dot(hidden, up_part) + bias
        t = jnp.tanh(ROOT * (v + CUBE * (v * v * v)))
        act = (0.5 * v * (1.0 + t)).astype(BF)
        slope = 0.5 * (1.0 + t) + 0.5 * v * (1.0 - t * t) * (ROOT * (1.0 + 3.0 * CUBE * (v * v)))
        two = []
        for p in range(passes):
            pre = (dot_nt(outer[p], down_part) * slope).astype(BF)
            if keep is not None:
                pre_out[p, :, keep] = pre
            two.append(dot_nt(pre, up_part))
        if keep is not None:
            act_out[:, keep] = act
        return dot(act, down_part), two

    def far_chunk(ref):
        told = ref[2 * chunk : 2 * chunk + 16, :].astype(F32)
        bias = told[0:1] + told[1:2] + told[2:3]
        return one_chunk(ref[:chunk, :], bias, ref[chunk : 2 * chunk, :], None)

    done = []
    for i in range(units // chunk):
        at = slice(i * chunk, (i + 1) * chunk)
        done.append(one_chunk(up[:, at], up_bias[:, at], down[at, :], at))
    done += [far_chunk(far_one), far_chunk(far_two)]

    def tree(parts):
        half = len(parts) // 2
        return sum(parts[:half]) + sum(parts[half:])

    output = tree([d[0] for d in done])
    mixed[...] = (middle + (output + shifts[3:4, :])).astype(BF)
    small[...] = jnp.zeros(small.shape, F32)
    lane = iota((rows, LANES), 1)
    stats = jnp.zeros((rows, LANES), F32)
    for p in range(passes):
        two = tree([d[1][p] for d in done])
        c = outer[p].astype(F32)
        mid = c + norm_back(two, gains[1:2, :], xhat, factor)
        mid_low = mid.astype(BF)
        grad_mid[p] = mid
        grad_low[p] = mid_low
        att = dot_nt(mid_low, out_weight[...]).astype(BF)
        packed[:, p * cols : (p + 1) * cols] = att[:rows, :]
        pre_out_p = pre_out[p].astype(F32)
        bias = jnp.sum(pre_out_p, axis=0, keepdims=True)
        small[p, 0:1, :] = jnp.sum(two * xhat, axis=0, keepdims=True)
        small[p, 1:2, :] = jnp.sum(two, axis=0, keepdims=True)
        small[p, 2:3, :] = jnp.sum(mid_low.astype(F32), axis=0, keepdims=True)
        small[p, 3:4, :] = jnp.sum(c, axis=0, keepdims=True)
        for i in range(units // model):
            small[p, 4 + i : 5 + i, :] = bias[:, i * model : (i + 1) * model]
        product = att[:rows, :].astype(F32) * full[:rows, :]
        for h in range(heads):
            delta = jnp.sum(product[:, h * HD : (h + 1) * HD], axis=-1, keepdims=True)
            for i, piece in enumerate(pieces(-delta)):
                stats = jnp.where(lane == 3 * heads * (p + 1) + 3 * h + i, piece.astype(F32), stats)
    packed[:, passes * cols :] = (stats + lse[...].astype(F32)).astype(BF)


def feed_forward(
    tokens, outer, low, low_far, full, lse, out_weight, up, up_bias, down, far_one, far_two,
    gains, shifts, rows, heads,
):
    size, model = tokens.shape
    passes = outer.shape[0]
    units = up.shape[1]
    return local_call(
        functools.partial(ff_kernel, heads),
        "feed_forward",
        (
            shaped(size, model),
            shaped(passes, size, model, dtype=F32),
            shaped(passes, size, model),
            shaped(rows, passes * heads * HD + LANES),
            shaped(size, model),
            shaped(size, units),
            shaped(passes, size, units),
            shaped(passes, 8, model, dtype=F32),
        ),
        [VMEM] * 14,
        (VMEM,) * 8,
        (
            tokens, outer, low, low_far, full, lse, out_weight, up, up_bias, down, far_one, far_two,
            gains, shifts,
        ),
        cost=cost(12),
        room=32,
    )


def thumb_back_kernel(heads, counts, x, mid_low, out_weight, out):
    width = heads * LANES
    size = x.shape[0]
    passes = mid_low.shape[0]
    visible = same_tile(size - TILE)
    outside = iota((size - TILE, HD), 0) + TILE >= counts[0] * TILE
    grads = [dot_nt(mid_low[p], out_weight[...]).astype(BF) for p in range(passes)]
    out[:, :, :TILE, :] = jnp.zeros((*out.shape[:2], TILE, out.shape[3]), BF)
    for h in range(heads):
        q = x[TILE:, h * LANES : (h + 1) * LANES]
        k = x[TILE:, width + h * LANES : width + (h + 1) * LANES]
        v = x[TILE:, 2 * width + h * LANES : 2 * width + h * LANES + HD]
        s = jnp.where(visible, dot_nt(q, k), FAR)
        e = jnp.exp(s - jnp.max(s, axis=-1, keepdims=True))
        w = e / jnp.sum(e, axis=-1, keepdims=True)
        w_low = w.astype(BF)
        for p in range(passes):
            g = grads[p][TILE:, h * HD : (h + 1) * HD]
            gw = dot_nt(g, v)
            ds = (w * (gw - jnp.sum(w * gw, axis=-1, keepdims=True))).astype(BF)
            dq = dot(ds, k[:, :HD]) * SCALE
            dk = dot_tn(ds, q)[:, :HD]
            dv = dot_tn(w_low, g)
            for c, piece in enumerate((dq, dk, dv)):
                at = c * LANES + (h % 2) * HD
                out[h // 2, p, TILE:, at : at + HD] = jnp.where(outside, piece, 0.0).astype(BF)


def thumbs_back(count, x, mid_low, out_weight, heads):
    passes, size, _ = mid_low.shape
    return local_call(
        functools.partial(thumb_back_kernel, heads),
        "thumbs_back",
        shaped(heads // 2, passes, size, 3 * LANES),
        [SMEM] + [VMEM] * 3,
        VMEM,
        (count, x, mid_low, out_weight),
        cost=cost(6),
    )


def early_at(units, model, low):
    ends = [model, 2 * model, 2 * model + units, 2 * model + units + low]
    return [slice(b - w, b) for b, w in zip(ends, (model, model, units, low))]


def early_cuts(parts, units, model, low):
    high, wide, turns = units // parts // 2, model // parts, model // low
    narrow = low * turns // parts
    for i in range(parts):
        yield (
            (slice(2 * i * high, (2 * i + 1) * high), slice(0, model)),
            (slice((2 * i + 1) * high, (2 * i + 2) * high), slice(0, model)),
            (slice(i * wide, (i + 1) * wide), slice(0, units)),
            (
                slice(i // turns * narrow, (i // turns + 1) * narrow),
                slice(i % turns * low, (i % turns + 1) * low),
            ),
        )


def weight_kernel(place, act, outer, hidden, pre, low, mid_low, keep, give):
    units, model, cols = act.shape[1], hidden.shape[1], low.shape[1]
    core = place[0]
    for turn, out in ((core, keep), (1 - core, give)):
        down = dot_tn(act[...], outer[turn]).astype(BF)
        up = dot_tn(hidden[...], pre[turn]).astype(BF)
        proj = dot_tn(low[...], mid_low[turn]).astype(BF)
        for i, cut in enumerate(early_cuts(keep.shape[0], units, model, cols)):
            for value, (rows, lanes), at in zip(
                (down, down, up, proj), cut, early_at(units, model, cols)
            ):
                out[i, :, at] = value[rows, lanes]


def weight_grads(core, act, outer, hidden, pre, low, mid_low, parts):
    units, model = act.shape[1], outer.shape[2]
    out = shaped(parts, model // parts, 2 * model + units + low.shape[1])
    return local_call(
        weight_kernel,
        "weight_grads",
        (out, out),
        [SMEM] + [VMEM] * 6,
        (VMEM,) * 2,
        (core, act, outer, hidden, pre, low, mid_low),
        cost=cost(8),
        room=24,
    )


def reverse_kernel(rows, groups, heads, passes, pair, first, *refs):
    last = not first
    counts, place = refs[:2]
    grads = refs[2 : 2 + groups]
    xq, xk, qx_in, kx, vx, own, thumb, weights, columns = refs[2 + groups : 11 + groups]
    at = 11 + groups
    more, at = refs[at], at + 1
    if first:
        small, (low_q, out_kv), at = more, refs[at : at + 2], at + 2
    else:
        before, out_q, give_q = more, refs[at : at + groups // 2], refs[at + groups // 2]
        at += groups // 2 + 1
        out_kv, at = refs[at : at + groups], at + groups
    keep, give = refs[at : at + 2]
    packed, qx, gx, kt, dq_t, dv, dk, low_kv, total, sums, starts = refs[at + 2 : at + 13]
    if last:
        low_q = refs[at + 13]
    cols = heads * HD
    q_counts = [counts[g] for g in range(groups)]
    k_counts = [counts[groups + g] for g in range(groups)]
    start = jnp.int32(0)
    for g in range(groups):
        packed[rows_at(start, rows), :] = grads[g][...]
        start = start + q_counts[g] * TILE
    q_total, k_total = start, sum(k_counts) * TILE
    tail_lane = iota((BLOCK, packed.shape[1]), 1) - passes * cols
    empty = (tail_lane >= 0) & (tail_lane < 3 * heads) & (tail_lane % 3 == 0)
    packed[rows_at(q_total, BLOCK), :] = jnp.where(empty, FAR, 0.0).astype(BF)
    q_blocks = (q_total + BLOCK - 1) // BLOCK
    k_blocks = (k_total + BLOCK - 1) // BLOCK

    to_grads, to_marks = [], []
    for i in range(2):
        h = 2 * pair + i
        row, col = (iota((packed.shape[1], passes * LANES), d) for d in (0, 1))
        turn, lane = col // LANES, col % LANES
        plain = (lane < HD) & (row == turn * cols + h * HD + lane)
        extra = (lane >= HD) & (lane < HD + 3) & (
            row == passes * cols + 3 * heads * (turn + 1) + 3 * h + lane - HD
        )
        to_grads.append(zero_one(plain | extra))
        row, lane = (iota((LANES, LANES), d) for d in (0, 1))
        to_marks.append(
            zero_one((lane > HD) & (lane < HD + 4) & (row == 3 * h + lane - HD - 1))
        )

    @pl.loop(0, q_blocks)
    def _(b):
        here = rows_at(b * BLOCK, BLOCK, BLOCK)
        for i in range(2):
            marks = dot(packed[here, passes * cols :], to_marks[i])
            qx[i, here, :] = (qx_in[i, here, :].astype(F32) + marks).astype(BF)
            gx[i, here, :] = dot(packed[here, :], to_grads[i]).astype(BF)

    @pl.loop(0, k_blocks)
    def _(b):
        here = rows_at(b * BLOCK, BLOCK, BLOCK)
        for i in range(2):
            kt[i, b] = jnp.transpose(kx[i, here, :].astype(F32))[:HD, :].astype(BF)

    def reverse_all(blocks):
        span = blocks * BLOCK
        dv[:, :span, :] = jnp.zeros((2, span, passes * LANES), F32)
        dk[:, :, :span, :] = jnp.zeros((passes, 2, span, LANES), F32)

        @pl.loop(0, q_blocks)
        def _(b):
            here = rows_at(b * BLOCK, BLOCK, BLOCK)
            for i in range(2):
                q, g = qx[i, here, :], gx[i, here, :]
                k_t = jnp.concatenate([kt[i, j] for j in range(blocks)], axis=1)
                w = jnp.exp(dot_nt(kx[i, :span, :], q))
                dv[i, :span, :] += dot(w.astype(BF), g)
                for p in range(passes):
                    ds = dot_nt(vx[i, :span, :], g[:, p * LANES : (p + 1) * LANES])
                    ds = (w * ds).astype(BF)
                    dk[p, i, :span, :] += dot(ds, q)
                    dq_t[p, i * HD : (i + 1) * HD, :] = dot(k_t, ds)
            for p in range(passes):
                piece = jnp.transpose(dq_t[p]) * SCALE
                low_q[here, p * LANES : (p + 1) * LANES] = piece.astype(BF)

        for p in range(passes):
            for i in range(2):
                for c, piece in enumerate(
                    (dk[p, i, :span, :HD], dv[i, :span, p * LANES : p * LANES + HD])
                ):
                    lane = (2 * p + c) * LANES + i * HD
                    low_kv[:span, lane : lane + HD] = piece.astype(BF)
        flat = low_kv[:span, :]
        total[:, passes * LANES :] = dot_tn(xk[:span, :], flat)
        sums[:, passes * LANES :] = dot(jnp.ones((8, span), BF), flat)


    for blocks in range(groups * TILE // BLOCK, groups * rows // BLOCK + 1):
        pl.when(k_blocks == blocks)(functools.partial(reverse_all, blocks))

    start = jnp.int32(0)
    for g in range(groups):
        starts[g] = start
        start = start + k_counts[g] * TILE
    for g in range(groups):
        slot = place[1 + g] if last else g
        value = low_kv[rows_at(starts[slot], rows), :]
        if last:
            out_kv[g][...] = value
        else:
            out_kv[g] = value
    if last:
        start = jnp.int32(0)
        for g in range(groups):
            here = rows_at(start, rows)
            value = jnp.concatenate([before[here, :], low_q[here, :]], axis=1)
            if g < groups // 2:
                out_q[g][...] = value
            else:
                give_q[g - groups // 2] = value
            start = start + q_counts[g] * TILE

    total[:, : passes * LANES] = jnp.zeros((total.shape[0], passes * LANES), F32)
    sums[:, : passes * LANES] = jnp.zeros((8, passes * LANES), F32)

    @pl.loop(0, q_blocks)
    def _(b):
        here = rows_at(b * BLOCK, BLOCK, BLOCK)
        total[:, : passes * LANES] += dot_tn(xq[here, :], low_q[here, :])
        sums[:, : passes * LANES] += dot(jnp.ones((8, BLOCK), BF), low_q[here, :])

    model = total.shape[0]
    gain, shift = columns[:, 0:1], columns[:, 1:2]
    ones = jnp.ones((8, own.shape[0]), BF)
    core = place[0]
    for p in range(passes):
        mine = thumb[p]
        part = dot_tn(own[...], mine)
        part_sum = dot(ones, mine)[0:1, :]
        q_at = slice(p * LANES, (p + 1) * LANES)
        kv_at = slice((passes + 2 * p) * LANES, (passes + 2 * p + 2) * LANES)
        part += jnp.concatenate([total[:, q_at], total[:, kv_at]], axis=1)
        part_sum += jnp.concatenate([sums[0:1, q_at], sums[0:1, kv_at]], axis=1)
        w = weights[...].astype(F32)
        gain_one = jnp.sum(w * part, axis=1, keepdims=True)
        shift_one = jnp.sum(w * part_sum, axis=1, keepdims=True)
        lane = iota((model, LANES), 1)
        tall = jnp.where(lane == 0, gain_one, jnp.where(lane == 1, shift_one, 0.0))
        flat = jnp.concatenate(
            [part_sum[:, :LANES], part_sum[:, LANES : 2 * LANES], part_sum[:, 2 * LANES :]]
            + [jnp.zeros((LANES - 3, LANES), F32)],
            axis=0,
        )
        flat = jnp.transpose(flat)
        flat = jnp.concatenate([jnp.zeros((LANES, 2), F32), flat[:, : LANES - 2]], axis=1)
        tall = jnp.concatenate([tall[:LANES] + flat, tall[LANES:]], axis=0)
        if first:
            turned = jnp.concatenate(
                [
                    jnp.zeros((8, model), F32),
                    small[p],
                    jnp.zeros((LANES - 16, model), F32),
                ],
                axis=0,
            )
            tall = tall + jnp.transpose(turned)
        grad = part * gain + shift * part_sum
        whole = jnp.concatenate([grad, tall], axis=1).astype(BF)

        @pl.when(core == p)
        def _():
            keep[...] = whole

        @pl.when(core != p)
        def _():
            give[...] = whole


def reverse(counts, place, grads, xq, xk, qx, kx, vx, own, thumb, weights, columns, more, rows, heads, pair):
    groups = len(grads)
    passes, size, _ = thumb.shape[1:]
    model = xq.shape[1]
    room = rows * groups + BLOCK
    cols = heads * HD
    first = pair == 0
    two = lambda shape: pl.BlockSpec((2, *shape[1:]), lambda i: (pair, 0, 0))
    one = lambda shape: pl.BlockSpec((None, *shape[1:]), lambda i: (pair,) + (0,) * (len(shape) - 1))
    mine = shaped(model, 4 * LANES)
    piece = shaped(rows, passes * 2 * LANES)
    if first:
        out = (shaped(room, passes * LANES), shaped(groups, rows, passes * 2 * LANES), mine, mine)
    else:
        half = groups // 2
        out = (*[piece] * half, shaped(half, *piece.shape), *[piece] * groups, mine, mine)
    scratch = [
        pltpu.VMEM((room, passes * cols + LANES), BF),
        pltpu.VMEM((2, room, LANES), BF),
        pltpu.VMEM((2, room, passes * LANES), BF),
        pltpu.VMEM((2, room // BLOCK, HD, BLOCK), BF),
        pltpu.VMEM((passes, LANES, BLOCK), F32),
        pltpu.VMEM((2, room, passes * LANES), F32),
        pltpu.VMEM((passes, 2, room, LANES), F32),
        pltpu.VMEM((room, passes * 2 * LANES), BF),
        pltpu.VMEM((model, passes * 3 * LANES), F32),
        pltpu.VMEM((8, passes * 3 * LANES), F32),
        pltpu.SMEM((groups,), jnp.int32),
    ]
    if not first:
        scratch.append(pltpu.VMEM((room, passes * LANES), BF))
    return pl.pallas_call(
        functools.partial(reverse_kernel, rows, groups, heads, passes, pair, first),
        grid=(1,),
        out_shape=out,
        in_specs=[SMEM, SMEM]
        + [VMEM] * (groups + 2)
        + [two(qx.shape)] * 3
        + [VMEM, one(thumb.shape), one(weights.shape), VMEM, VMEM],
        out_specs=(VMEM,) * len(out),
        scratch_shapes=scratch,
        cost_estimate=cost(20),
        compiler_params=pltpu.CompilerParams(vmem_limit_bytes=REVERSE_ROOM * MIB),
        name="reverse" + str(pair),
    )(counts, place, *grads, xq, xk, qx, kx, vx, own, thumb, weights, columns, more)


def chosen(counts, far, thumb, rows):
    image = iota(far.shape, 0) < counts[0] * TILE
    return jnp.concatenate(
        [jnp.where(image, far.astype(BF), thumb[:rows]), thumb[rows:]], axis=0
    )


def grad_kv_kernel(counts, from_kv, thumb, weights, out):
    groups, rows, _ = from_kv.shape
    total = sum(from_kv[g].astype(F32) for g in range(groups))
    for p in range(thumb.shape[0]):
        far = total[:, 2 * p * LANES : 2 * (p + 1) * LANES]
        flat = chosen(counts, far, thumb[p, :, LANES:], rows)
        out[p] = dot_nt(flat, weights[:, LANES:])


def grad_kv(count, from_kv, thumb, weights):
    passes, size, _ = thumb.shape[1:]
    one = lambda shape: pl.BlockSpec((None, *shape[1:]), lambda i: (0,) * len(shape))
    return pl.pallas_call(
        grad_kv_kernel,
        grid=(1,),
        out_shape=shaped(passes, size, weights.shape[1], dtype=F32),
        in_specs=[SMEM, VMEM, one(thumb.shape), one(weights.shape)],
        out_specs=VMEM,
        cost_estimate=cost(4),
        compiler_params=pltpu.CompilerParams(vmem_limit_bytes=16 * MIB),
        name="grad_kv",
    )(count, from_kv, thumb, weights)


def grad_one_kernel(near, counts, *refs):
    from_q, from_kv, (thumb, weights, before, out) = refs[:near], refs[near:-4], refs[-4:]
    rows = from_q[0].shape[0]
    passes = thumb.shape[1]
    sum_q = sum(r[...].astype(F32) for r in from_q)
    sum_kv = sum(r[...].astype(F32) for r in from_kv)
    for p in range(passes):
        part = before[p]
        for pair in range(2):
            far = sum_q[:, (passes * pair + p) * LANES : (passes * pair + p + 1) * LANES]
            flat = chosen(counts, far, thumb[pair, p, :, :LANES], rows)
            part = part + dot_nt(flat, weights[pair, :, :LANES])
        far = sum_kv[:, 2 * p * LANES : 2 * (p + 1) * LANES]
        flat = chosen(counts, far, thumb[1, p, :, LANES:], rows)
        part = part + dot_nt(flat, weights[1, :, LANES:])
        out[p] = part.astype(BF)


def grad_one(count, from_q, from_kv, thumb, weights, before):
    near = len(from_q)
    return local_call(
        functools.partial(grad_one_kernel, near),
        "grad_one",
        shaped(*before.shape),
        [SMEM] + [VMEM] * (near + len(from_kv) + 3),
        VMEM,
        (count, *from_q, *from_kv, thumb, weights, before),
        cost=cost(5),
    )


def close_kernel(tokens, mid, mine, other, gains, out):
    xhat, factor = standard(tokens[...].astype(F32))
    for p in range(mid.shape[0]):
        grad = mine[p].astype(F32) + other[p].astype(F32)
        out[p] = mid[p] + norm_back(grad, gains[0:1, :], xhat, factor)


def close(tokens, mid, mine, other, gains):
    return local_call(
        close_kernel,
        "close",
        shaped(*mid.shape, dtype=F32),
        [VMEM] * 5,
        VMEM,
        (tokens, mid, mine, other, gains),
        cost=cost(4),
    )


def early_kernel(place, own, far, down, up, proj):
    core = place[0]
    (units, model), low = down.shape[1:], proj.shape[1]
    for turn, ref in ((core, own), (1 - core, far)):
        for i, cut in enumerate(early_cuts(own.shape[0], units, model, low)):
            for out, (rows, lanes), at in zip(
                (down, down, up, proj), cut, early_at(units, model, low)
            ):
                out[turn, rows, lanes] = ref[i, :, at].astype(F32)


def early_out(core, own, far, units, low):
    model = own.shape[0] * own.shape[1]
    return local_call(
        early_kernel,
        "early_out",
        (
            shaped(2, units, model, dtype=F32),
            shaped(2, model, units, dtype=F32),
            shaped(2, low, model, dtype=F32),
        ),
        [SMEM] + [VMEM] * 2,
        (VMEM,) * 3,
        (core, own, far),
        cost=cost(8),
        room=24,
    )


def late_kernel(place, own, far, grad_in, in_bias, up_bias, gains, shifts):
    core = place[0]
    for turn, ref in ((core, own), (1 - core, far)):
        turned = []
        for pair in range(2):
            at = 4 * LANES * pair
            for c in range(3):
                grad_in[turn, c, :, pair * LANES : (pair + 1) * LANES] = ref[
                    :, at + c * LANES : at + (c + 1) * LANES
                ].astype(F32)
            turned.append(jnp.transpose(ref[:, at + 3 * LANES : at + 4 * LANES].astype(F32)))
        a, b = turned
        in_bias[turn] = jnp.concatenate(
            [
                jnp.concatenate([a[2:3, :LANES], b[2:3, :LANES]], axis=1),
                jnp.concatenate([a[4:5, :LANES], b[4:5, :LANES]], axis=1),
            ],
            axis=0,
        )
        up_bias[turn] = jnp.concatenate([a[12:13], a[13:14]], axis=1)
        gains[turn] = jnp.concatenate([a[0:1] + b[0:1], a[8:9]], axis=0)
        shifts[turn] = jnp.concatenate([a[1:2] + b[1:2], a[10:11], a[9:10], a[11:12]], axis=0)


def late_out(core, own, far, units):
    model = own.shape[0]
    return local_call(
        late_kernel,
        "late_out",
        (
            shaped(2, 3, model, 2 * LANES, dtype=F32),
            shaped(2, 2, 2 * LANES, dtype=F32),
            shaped(2, 1, units, dtype=F32),
            shaped(2, 2, model, dtype=F32),
            shaped(2, 4, model, dtype=F32),
        ),
        [SMEM] + [VMEM] * 2,
        (VMEM,) * 5,
        (core, own, far),
        cost=cost(4),
    )


def gather_near(array):
    mine = [array] + [shift_by(array, "y", d) for d in range(1, lax.axis_size("y"))]
    return mine + [shift_by(a, "c", 1) for a in mine]


def return_near(parts):
    return [parts[0]] + [shift_by(p, "y", -j) for j, p in enumerate(parts) if j > 0]


def offsets(size):
    return [(step, flip) for step in range(size) for flip in range(2)]


def return_far(pieces_):
    size = lax.axis_size("z")
    out = []
    for piece, (step, flip) in zip(pieces_, offsets(size)):
        if step == flip == 0:
            out.append(piece)
            continue
        perm = [
            (i * 2 + k, ((i + step) % size) * 2 + (k ^ flip)) for i in range(size) for k in range(2)
        ]
        out.append(lax.ppermute(piece, ("z", "xl"), perm))
    return out


PLANE = ("z", "xl", "y")


def core_sum(keep, give):
    return (keep.astype(F32) + shift_by(give, "c", 1).astype(F32)).astype(BF)


def plane_sum(mine):
    parts = lax.all_to_all(mine, PLANE, 0, 0, tiled=True)
    return jnp.sum(parts.astype(F32), axis=0)


def tied(arrays, others):
    return lax.optimization_barrier((arrays, others))


def padded(weight, heads):
    lead = weight.shape[0]
    return jnp.pad(weight.reshape(lead, heads, HD), ((0, 0), (0, 0), (0, LANES - HD))).reshape(
        lead, heads * LANES
    )


def local(
    tokens,
    cotangents,
    segment_ids,
    in_weights,
    in_biases,
    out_weight,
    up_weight,
    up_biases,
    down_weight,
    gains,
    shifts,
):
    size, model = tokens.shape
    cols = in_weights.shape[2]
    heads = cols // HD
    rows = size - TILE
    units = up_weight.shape[1]
    c = lax.axis_index("c")

    told, copies, count = front(tokens, segment_ids, lax.axis_size(("z", "xl")))
    far = lax.all_to_all(copies, ("z", "xl"), 0, 0, tiled=True)
    near = gather_near(told)
    core = c.astype(jnp.int32).reshape(1)
    z, xl, z_size = lax.axis_index("z"), lax.axis_index("xl"), lax.axis_size("z")
    routes = [((z + step) % z_size) * 2 + (xl ^ flip) for step, flip in offsets(z_size)]
    place = jnp.concatenate([core, jnp.stack(routes).astype(jnp.int32)])
    plane = lax.axis_size(PLANE)

    bundle = bundled(core, up_weight, down_weight, up_biases[None], out_weight)
    n_x = lax.axis_size(("xl", "h"))
    far_one = lax.ppermute(bundle, ("xl", "h"), [(i, n_x - 1 - i) for i in range(n_x)])
    far_two = shift_by(far_one[: 2 * model + 16], "c", 1)

    weights = jnp.concatenate(
        [
            padded(in_weights[0] * jnp.asarray(SCALE, BF), heads),
            padded(in_weights[1], heads),
            padded(in_weights[2], heads),
        ],
        axis=1,
    )
    lane = jnp.arange(heads * LANES) % LANES
    biases = jnp.concatenate(
        [
            padded(in_biases[0:1] * SCALE, heads) + (lane == HD),
            ((lane > HD) & (lane < HD + 4)).astype(F32)[None],
            padded(in_biases[1:2], heads) + ((lane >= HD) & (lane < HD + 3)),
        ],
        axis=1,
    )
    pairs = jnp.stack(
        [
            jnp.concatenate([in_weights[i, :, at : at + LANES] for i in range(3)], axis=1)
            for at in range(0, cols, LANES)
        ]
    )
    columns = jnp.pad(jnp.stack([gains[0], shifts[0]], axis=1), ((0, 0), (0, LANES - 2)))

    *parts, give, xq, xk, qx, kx, vx, counts = attend(
        near, far, weights, biases, gains, shifts, rows, heads
    )
    thumb_out, xhat, x = thumbs(tokens, weights, biases, gains, shifts, heads)
    parts = pair_merge(parts, shift_by(give, "c", 1), heads)
    low, full, lse = merge(count, return_near(parts), thumb_out, heads)
    low_far = shift_by(low, "h", 1)
    mixed, grad_mid, mid_low, packed, hidden, act, pre, small = feed_forward(
        tokens, cotangents, low, low_far, full, lse, out_weight, up_weight, up_biases[None],
        down_weight, far_one, far_two, gains, shifts, rows, heads,
    )
    grads = gather_near(packed)
    keep, give = weight_grads(core, act, cotangents, hidden, pre, low, mid_low, plane)
    mid_low, (keep, give) = tied(mid_low, (keep, give))
    thumb = thumbs_back(count, x, mid_low, out_weight, heads)
    early = core_sum(keep, give)

    grads, (early, thumb) = tied(grads, (early, thumb))
    low_q, out_kv, keep, give = reverse(
        counts, place, grads, xq, xk, qx, kx, vx, xhat, thumb, pairs, columns, small, rows, heads, 0
    )
    early = plane_sum(early).astype(BF)
    low_q, (early, out_kv, keep, give) = tied(low_q, (early, out_kv, keep, give))
    from_kv_one = lax.all_to_all(out_kv, ("z", "xl"), 0, 0, tiled=True)
    give = shift_by(give, "c", 1)
    for axis in ("y", "xl", "z"):
        early = lax.all_gather(early[None] if axis == "y" else early, axis, axis=0, tiled=True)
    out = reverse(
        counts, place, grads, xq, xk, qx, kx, vx, xhat, thumb, pairs, columns, low_q, rows, heads, 1
    )
    out, (from_kv_one, give) = tied(out, (from_kv_one, give))
    half = len(near) // 2
    out_q, give_q, out_kv = out[:half], out[half], out[half + 1 : half + 1 + len(near)]
    keep_two, give_two = out[-2:]
    late = [(keep.astype(F32) + give.astype(F32)).astype(BF), core_sum(keep_two, give_two)]
    mine = jnp.concatenate(late, axis=1)
    part = plane_sum(mine.reshape(plane, -1, mine.shape[1])).astype(BF)
    from_q = return_near(fold(out_q, shift_by(give_q, "c", 1)))
    from_kv = return_far(out_kv)
    before = grad_kv(count, from_kv_one, thumb, pairs)
    part, (from_q, from_kv, before) = tied(part, (from_q, from_kv, before))
    mine = grad_one(count, from_q, from_kv, thumb, pairs, before)
    grad_tokens = close(tokens, grad_mid, mine, shift_by(mine, "h", 1), gains)

    lanes = jnp.arange(part.shape[1]) % (4 * LANES) - 3 * LANES
    lone = jnp.concatenate([part[:, 3 * LANES : 4 * LANES], part[:, 7 * LANES :]], axis=1)
    lone = jnp.pad(shift_by(lone, "h", 1).reshape(-1, 2, LANES), ((0, 0), (0, 0), (3 * LANES, 0)))
    lone = jnp.where((lanes >= 0) & (lanes < 2), lone.reshape(part.shape), 0).astype(F32)
    part = (part.astype(F32) + lone).astype(BF)
    part = jnp.broadcast_to(part[None], (plane, *part.shape))
    own = lax.all_to_all(part, PLANE, 0, 0, tiled=True).reshape(model, -1)
    grad_down, grad_up, grad_out = early_out(core, early, shift_by(early, "c", 1), units, cols)
    grad_in, in_bias, up_bias, grad_gains, grad_shifts = late_out(
        core, own, shift_by(own, "c", 1), units
    )
    return (
        mixed,
        grad_tokens,
        grad_in,
        in_bias,
        grad_out,
        grad_up,
        up_bias.reshape(2, units),
        grad_down,
        grad_gains,
        grad_shifts,
    )


def solution(mesh):
    fine = Mesh(mesh.devices.reshape(4, 2, 4, 2, 2), ("z", "xl", "y", "c", "h"))
    blk = ("z", "xl", "y", "c")
    return jax.shard_map(
        local,
        mesh=fine,
        in_specs=(
            P(blk, None),
            P(None, blk, None),
            P(blk),
            P(None, None, "h"),
            P(None, "h"),
            P("h", None),
            P(None, "h"),
            P("h"),
            P("h", None),
            P(),
            P(),
        ),
        out_specs=(
            P(blk, None),
            P(None, blk, None),
            P(None, None, None, "h"),
            P(None, None, "h"),
            P(None, "h", None),
            P(None, None, "h"),
            P(None, "h"),
            P(None, "h", None),
            P(),
            P(),
        ),
        check_vma=False,
    )
```

```python
import functools

import jax
import jax.numpy as jnp
from jax import lax
from jax.experimental import pallas as pl
from jax.experimental.pallas import tpu as pltpu
from jax.sharding import Mesh
from jax.sharding import PartitionSpec as P

HD = 64
LANES = 128
TILE = 64
BLOCK = 256
EPS = 1e-06
SCALE = 0.125
FAR = -1e30
BF = jnp.bfloat16
F32 = jnp.float32
MIB = 1024 * 1024
REVERSE_ROOM = 56

NT = (((1,), (1,)), ((), ()))
TN = (((0,), (0,)), ((), ()))


def shift_by(array, axis, step):
    size = lax.axis_size(axis)
    return lax.ppermute(array, axis, [(i, (i + step) % size) for i in range(size)])


def dot(a, b):
    return jnp.dot(a, b, preferred_element_type=F32)


def dot_nt(a, b):
    return lax.dot_general(a, b, NT, preferred_element_type=F32)


def dot_tn(a, b):
    return lax.dot_general(a, b, TN, preferred_element_type=F32)


def standard(field):
    center = field - jnp.mean(field, axis=-1, keepdims=True)
    factor = lax.rsqrt(jnp.mean(center * center, axis=-1, keepdims=True) + EPS)
    return center * factor, factor


def norm_back(grad, gain, xhat, factor):
    h = grad * gain
    mean = jnp.mean(h, axis=-1, keepdims=True)
    return factor * (h - mean - xhat * jnp.mean(h * xhat, axis=-1, keepdims=True))


def pieces(value):
    high = value.astype(BF)
    rest = value - high.astype(F32)
    middle = rest.astype(BF)
    low = (rest - middle.astype(F32)).astype(BF)
    return high, middle, low


def iota(shape, dim):
    return lax.broadcasted_iota(jnp.int32, shape, dim)


VMEM = pl.BlockSpec(memory_space=pltpu.VMEM)
ANY = pl.BlockSpec(memory_space=pl.ANY)
SMEM = pl.BlockSpec(memory_space=pltpu.SMEM)


def local_call(body, name, out, ins, outs, args, scratch=(), cost=None, room=16):
    return pl.pallas_call(
        body,
        out_shape=out,
        in_specs=ins,
        out_specs=outs,
        scratch_shapes=scratch,
        cost_estimate=cost,
        compiler_params=pltpu.CompilerParams(vmem_limit_bytes=room * MIB),
        name=name,
    )(*args)


def shaped(*shape, dtype=BF):
    return jax.ShapeDtypeStruct(shape, dtype)


def cost(micros):
    return pl.CostEstimate(flops=int(micros * 1e9), bytes_accessed=0, transcendentals=0)


def front_kernel(tokens, ids, told, number):
    rows = told.shape[0] - 16
    marks = jnp.where(ids[...] == 0, 1.0, 0.0)
    tiles = jnp.sum(marks).astype(jnp.int32) // TILE
    number[0] = tiles
    told[:rows, :] = tokens[:rows, :]
    told[rows:, :] = jnp.full((16, told.shape[1]), tiles.astype(F32), F32).astype(BF)


def front(tokens, ids):
    size, model = tokens.shape
    return local_call(
        front_kernel,
        "front",
        (shaped(size - TILE + 16, model), shaped(1, dtype=jnp.int32)),
        [VMEM, VMEM],
        (VMEM, SMEM),
        (tokens, ids.reshape(-1, LANES)),
    )


def bundle_kernel(place, up, down, bias, out):
    core = place[0]
    half = out.shape[1]
    at = pl.ds(pl.multiple_of(core * half, half), half)
    out[:half, :] = up[:, at]
    out[half : 2 * half, :] = down[at, :]
    mine = jnp.where(core == 0, bias[:, :half], bias[:, half:])
    row = iota((16, half), 0)
    rows = jnp.zeros((16, half), F32)
    for i, piece in enumerate(pieces(mine)):
        rows = jnp.where(row == i, piece.astype(F32), rows)
    out[2 * half :, :] = rows.astype(BF)


def bundled(core, up, down, bias):
    model = up.shape[0]
    return local_call(
        bundle_kernel,
        "bundle",
        shaped(2 * model + 16, model),
        [SMEM] + [VMEM] * 3,
        VMEM,
        (core, up, down, bias),
    )


def count_of(ref, rows):
    return jnp.max(ref[rows : rows + 16, :LANES].astype(F32)).astype(jnp.int32)


def rows_at(start, rows, step=TILE):
    return pl.ds(pl.multiple_of(start, step), rows)


def attend_kernel(rows, groups, heads, *refs):
    near, far = refs[:groups], refs[groups : 2 * groups]
    weights, biases, gains, shifts = refs[2 * groups : 2 * groups + 4]
    at = 2 * groups + 4 + groups // 2
    out, give = refs[2 * groups + 4 : at], refs[at]
    kept, counts, place = refs[at + 1 : at + 6], refs[at + 6], refs[at + 7]
    (xq, xk, qx, kx, vx), sems = refs[at + 8 : at + 13], refs[at + 13]
    model = xq.shape[1]
    q_counts = [count_of(r, rows) for r in near]
    k_counts = [count_of(r, rows) for r in far]
    for g in range(groups):
        counts[g] = q_counts[g]
        counts[groups + g] = k_counts[g]

    def compact(numbers, read, target):
        start = jnp.int32(0)
        for g, n in enumerate(numbers):
            target[rows_at(start, rows), :] = read(g)
            start = start + n * TILE
        target[rows_at(start, BLOCK), :] = jnp.zeros((BLOCK, model), BF)
        return start

    q_total = compact(q_counts, lambda g: near[g][:rows, :], xq)
    k_total = compact(k_counts, lambda g: far[g][:rows, :], xk)
    q_blocks = (q_total + BLOCK - 1) // BLOCK
    k_blocks = (k_total + BLOCK - 1) // BLOCK
    width = heads * LANES

    def hidden(ref, here):
        clean = standard(ref[here, :].astype(F32))[0].astype(BF)
        ref[here, :] = clean
        return (clean.astype(F32) * gains[0:1, :] + shifts[0:1, :]).astype(BF)

    @pl.loop(0, q_blocks)
    def _(b):
        here = rows_at(b * BLOCK, BLOCK, BLOCK)
        q = (dot(hidden(xq, here), weights[:, :width]) + biases[:, :width]).astype(BF)
        for h in range(heads):
            qx[h, here, :] = q[:, h * LANES : (h + 1) * LANES]

    @pl.loop(0, k_blocks)
    def _(b):
        here = rows_at(b * BLOCK, BLOCK, BLOCK)
        both = dot(hidden(xk, here), weights[:, width:]) + biases[:, width:]
        unseen = (iota((BLOCK, width), 0) + b * BLOCK >= k_total) & (
            iota((BLOCK, width), 1) % LANES == HD
        )
        k = jnp.where(unseen, FAR, both[:, :width]).astype(BF)
        v = both[:, width:].astype(BF)
        for h in range(heads):
            kx[h, here, :] = k[:, h * LANES : (h + 1) * LANES]
            vx[h, here, :] = v[:, h * LANES : (h + 1) * LANES]

    copies = [
        pltpu.make_async_copy(held, to, sems.at[i])
        for i, (held, to) in enumerate(zip((xq, xk, qx, kx, vx), kept))
    ]
    for copy in copies:
        copy.start()

    def attend_all(span):
        @pl.loop(0, q_blocks)
        def _(b):
            here = rows_at(b * BLOCK, BLOCK, BLOCK)
            lane = iota((BLOCK, LANES), 1)
            for h in range(heads):
                s = dot_nt(qx[h, here, :], kx[h, :span, :])
                top = jnp.max(s, axis=-1, keepdims=True)
                o = dot(jnp.exp(s - top).astype(BF), vx[h, :span, :])
                total = o[:, HD : HD + 1]
                o = o / total
                for i, piece in enumerate(pieces(top + jnp.log(total))):
                    o = jnp.where(lane == HD + i, piece.astype(F32), o)
                place[h, here, :] = o.astype(BF)

    for blocks in range(groups * TILE // BLOCK, groups * rows // BLOCK + 1):
        pl.when(k_blocks == blocks)(functools.partial(attend_all, blocks * BLOCK))

    gather = [
        (iota((LANES, LANES), 0) - HD + 3 * h == iota((LANES, LANES), 1))
        & (iota((LANES, LANES), 0) >= HD)
        & (iota((LANES, LANES), 0) < HD + 3)
        for h in range(heads)
    ]
    gather = [jnp.where(m, 1.0, 0.0).astype(BF) for m in gather]
    start = jnp.int32(0)
    for g in range(groups):
        mine = [place[h, rows_at(start, rows), :] for h in range(heads)]
        stats = sum(dot(m, s) for m, s in zip(mine, gather)).astype(BF)
        value = jnp.concatenate([m[:, :HD] for m in mine] + [stats], axis=1)
        if g < groups // 2:
            out[g][...] = value
        else:
            give[g - groups // 2] = value
        start = start + q_counts[g] * TILE
    for copy in copies:
        copy.wait()


def attend(near, far, weights, biases, gains, shifts, rows, heads):
    groups = len(near)
    model = near[0].shape[1]
    room = rows * groups + BLOCK
    parts = heads * HD + LANES
    kept = [(room, model)] * 2 + [(heads, room, LANES)] * 3
    return local_call(
        functools.partial(attend_kernel, rows, groups, heads),
        "attend",
        (
            *[shaped(rows, parts)] * (groups // 2),
            shaped(groups // 2, rows, parts),
            *[shaped(*k) for k in kept],
            shaped(2 * groups, dtype=jnp.int32),
        ),
        [VMEM] * (2 * groups + 4),
        (*[VMEM] * (groups // 2 + 1), *[ANY] * 5, SMEM),
        (*near, *far, weights, biases, gains, shifts),
        [
            pltpu.VMEM((heads, room, LANES), BF),
            *[pltpu.VMEM(k, BF) for k in kept],
            pltpu.SemaphoreType.DMA((5,)),
        ],
        cost(15),
        32,
    )


def same_tile(rows):
    return iota((rows, rows), 0) // TILE == iota((rows, rows), 1) // TILE


def thumb_kernel(heads, tokens, weights, biases, gains, shifts, out, xhat, x):
    width = heads * LANES
    size = tokens.shape[0]
    clean = standard(tokens[...].astype(F32))[0].astype(BF)
    xhat[...] = clean
    hidden = (clean.astype(F32) * gains[0:1, :] + shifts[0:1, :]).astype(BF)
    x[...] = (dot(hidden, weights[...]) + biases[...]).astype(BF)
    visible = same_tile(size - TILE)
    out[:TILE, :] = jnp.zeros((TILE, heads * HD), F32)
    for h in range(heads):
        q = x[TILE:, h * LANES : (h + 1) * LANES]
        k = x[TILE:, width + h * LANES : width + (h + 1) * LANES]
        v = x[TILE:, 2 * width + h * LANES : 2 * width + (h + 1) * LANES]
        s = jnp.where(visible, dot_nt(q, k), FAR)
        e = jnp.exp(s - jnp.max(s, axis=-1, keepdims=True))
        o = dot(e.astype(BF), v)[:, :HD] / jnp.sum(e, axis=-1, keepdims=True)
        out[TILE:, h * HD : (h + 1) * HD] = o


def thumbs(tokens, weights, biases, gains, shifts, heads):
    size, model = tokens.shape
    return local_call(
        functools.partial(thumb_kernel, heads),
        "thumbs",
        (
            shaped(size, heads * HD, dtype=F32),
            shaped(size, model),
            shaped(size, 3 * heads * LANES),
        ),
        [VMEM] * 5,
        (VMEM,) * 3,
        (tokens, weights, biases, gains, shifts),
        cost=cost(5),
    )


def zero_one(mask):
    return jnp.where(mask, 1.0, 0.0).astype(BF)


def merged(parts, heads):
    cols = heads * HD
    row, col = (iota((LANES, cols), d) for d in (0, 1))
    spread = zero_one(row // 3 == col // HD)
    marks = [dot(p[:, cols:], spread) for p in parts]
    top = functools.reduce(jnp.maximum, marks)
    expos = [jnp.exp(m - top) for m in marks]
    total = sum(expos)
    mixed = sum(e * p[:, :cols].astype(F32) for p, e in zip(parts, expos)) / total
    row, col = (iota((cols, LANES), d) for d in (0, 1))
    packed = [
        dot(piece, zero_one((row % HD == 0) & (col == 3 * (row // HD) + i)))
        for i, piece in enumerate(pieces(top + jnp.log(total)))
    ]
    return mixed, sum(packed)


def pair_kernel(heads, *refs):
    count = (len(refs) - 1) // 2
    for j, (mine, out) in enumerate(zip(refs[:count], refs[count + 1 :])):
        mixed, marks = merged([mine[...], refs[count][j]], heads)
        out[...] = jnp.concatenate([mixed.astype(BF), marks.astype(BF)], axis=1)


def pair_merge(parts, other, heads):
    return local_call(
        functools.partial(pair_kernel, heads),
        "pair_merge",
        tuple(shaped(*p.shape) for p in parts),
        [VMEM] * (len(parts) + 1),
        (VMEM,) * len(parts),
        (*parts, other),
        cost=cost(3),
    )


def merge_kernel(heads, counts, thumb, *refs):
    parts, (low, full, lse) = refs[:-3], refs[-3:]
    cols = heads * HD
    rows = lse.shape[0]
    mixed, marks = merged([p[...] for p in parts], heads)
    lse[...] = (-marks).astype(BF)
    image = iota((rows, cols), 0) < counts[0] * TILE
    full[:rows, :] = jnp.where(image, mixed, thumb[:rows, :])
    full[rows:, :] = thumb[rows:, :]
    low[...] = full[...].astype(BF)


def merge(count, parts, thumb, heads):
    size, cols = thumb.shape
    return local_call(
        functools.partial(merge_kernel, heads),
        "merge",
        (shaped(size, cols), shaped(size, cols, dtype=F32), shaped(parts[0].shape[0], LANES)),
        [SMEM] + [VMEM] * (1 + len(parts)),
        (VMEM,) * 3,
        (count, thumb, *parts),
        cost=cost(3),
    )


def fold_kernel(*refs):
    count = (len(refs) - 1) // 2
    for j, (mine, out) in enumerate(zip(refs[:count], refs[count + 1 :])):
        out[...] = (mine[...].astype(F32) + refs[count][j].astype(F32)).astype(BF)


def fold(parts, other):
    return local_call(
        fold_kernel,
        "fold",
        tuple(shaped(*p.shape) for p in parts),
        [VMEM] * (len(parts) + 1),
        (VMEM,) * len(parts),
        (*parts, other),
        cost=cost(2),
    )


ROOT = 0.7978845608028654
CUBE = 0.044715


def ff_kernel(
    heads, tokens, outer, low, low_far, full, lse, out_weight, out_far, up, up_bias, down, far_one,
    far_two, gains, shifts, mixed, grad_mid, grad_low, packed, hidden_out, act_out, pre_out, small,
):
    size, model = tokens.shape
    passes = outer.shape[0]
    cols = heads * HD
    chunk = far_one.shape[1]
    units = up.shape[1]
    rows = packed.shape[0]
    branch = dot(low[...], out_weight[...]) + dot(low_far[...], out_far[...])
    middle = tokens[...].astype(F32) + (branch + shifts[1:2, :])
    xhat, factor = standard(middle)
    hidden = (xhat * gains[1:2, :] + shifts[2:3, :]).astype(BF)
    hidden_out[...] = hidden

    def one_chunk(up_part, bias, down_part, keep):
        v = dot(hidden, up_part) + bias
        t = jnp.tanh(ROOT * (v + CUBE * (v * v * v)))
        act = (0.5 * v * (1.0 + t)).astype(BF)
        slope = 0.5 * (1.0 + t) + 0.5 * v * (1.0 - t * t) * (ROOT * (1.0 + 3.0 * CUBE * (v * v)))
        two = []
        for p in range(passes):
            pre = (dot_nt(outer[p], down_part) * slope).astype(BF)
            if keep is not None:
                pre_out[p, :, keep] = pre
            two.append(dot_nt(pre, up_part))
        if keep is not None:
            act_out[:, keep] = act
        return dot(act, down_part), two

    def far_chunk(ref):
        told = ref[2 * chunk : 2 * chunk + 16, :].astype(F32)
        bias = told[0:1] + told[1:2] + told[2:3]
        return one_chunk(ref[:chunk, :], bias, ref[chunk : 2 * chunk, :], None)

    done = []
    for i in range(units // chunk):
        at = slice(i * chunk, (i + 1) * chunk)
        done.append(one_chunk(up[:, at], up_bias[:, at], down[at, :], at))
    done += [far_chunk(far_one), far_chunk(far_two)]

    def tree(parts):
        half = len(parts) // 2
        return sum(parts[:half]) + sum(parts[half:])

    output = tree([d[0] for d in done])
    mixed[...] = (middle + (output + shifts[3:4, :])).astype(BF)
    small[...] = jnp.zeros(small.shape, F32)
    lane = iota((rows, LANES), 1)
    stats = jnp.zeros((rows, LANES), F32)
    for p in range(passes):
        two = tree([d[1][p] for d in done])
        c = outer[p].astype(F32)
        mid = c + norm_back(two, gains[1:2, :], xhat, factor)
        mid_low = mid.astype(BF)
        grad_mid[p] = mid
        grad_low[p] = mid_low
        att = dot_nt(mid_low, out_weight[...]).astype(BF)
        packed[:, p * cols : (p + 1) * cols] = att[:rows, :]
        pre_out_p = pre_out[p].astype(F32)
        bias = jnp.sum(pre_out_p, axis=0, keepdims=True)
        small[p, 0:1, :] = jnp.sum(two * xhat, axis=0, keepdims=True)
        small[p, 1:2, :] = jnp.sum(two, axis=0, keepdims=True)
        small[p, 2:3, :] = jnp.sum(mid_low.astype(F32), axis=0, keepdims=True)
        small[p, 3:4, :] = jnp.sum(c, axis=0, keepdims=True)
        for i in range(units // model):
            small[p, 4 + i : 5 + i, :] = bias[:, i * model : (i + 1) * model]
        product = att[:rows, :].astype(F32) * full[:rows, :]
        for h in range(heads):
            delta = jnp.sum(product[:, h * HD : (h + 1) * HD], axis=-1, keepdims=True)
            for i, piece in enumerate(pieces(-delta)):
                stats = jnp.where(lane == 3 * heads * (p + 1) + 3 * h + i, piece.astype(F32), stats)
    packed[:, passes * cols :] = (stats + lse[...].astype(F32)).astype(BF)


def feed_forward(
    tokens, outer, low, low_far, full, lse, out_weight, out_far, up, up_bias, down, far_one, far_two,
    gains, shifts, rows, heads,
):
    size, model = tokens.shape
    passes = outer.shape[0]
    units = up.shape[1]
    return local_call(
        functools.partial(ff_kernel, heads),
        "feed_forward",
        (
            shaped(size, model),
            shaped(passes, size, model, dtype=F32),
            shaped(passes, size, model),
            shaped(rows, passes * heads * HD + LANES),
            shaped(size, model),
            shaped(size, units),
            shaped(passes, size, units),
            shaped(passes, 8, model, dtype=F32),
        ),
        [VMEM] * 15,
        (VMEM,) * 8,
        (
            tokens, outer, low, low_far, full, lse, out_weight, out_far, up, up_bias, down, far_one,
            far_two, gains, shifts,
        ),
        cost=cost(12),
        room=32,
    )


def thumb_back_kernel(heads, counts, x, mid_low, out_weight, out):
    width = heads * LANES
    size = x.shape[0]
    passes = mid_low.shape[0]
    visible = same_tile(size - TILE)
    outside = iota((size - TILE, HD), 0) + TILE >= counts[0] * TILE
    grads = [dot_nt(mid_low[p], out_weight[...]).astype(BF) for p in range(passes)]
    out[:, :, :TILE, :] = jnp.zeros((*out.shape[:2], TILE, out.shape[3]), BF)
    for h in range(heads):
        q = x[TILE:, h * LANES : (h + 1) * LANES]
        k = x[TILE:, width + h * LANES : width + (h + 1) * LANES]
        v = x[TILE:, 2 * width + h * LANES : 2 * width + h * LANES + HD]
        s = jnp.where(visible, dot_nt(q, k), FAR)
        e = jnp.exp(s - jnp.max(s, axis=-1, keepdims=True))
        w = e / jnp.sum(e, axis=-1, keepdims=True)
        w_low = w.astype(BF)
        for p in range(passes):
            g = grads[p][TILE:, h * HD : (h + 1) * HD]
            gw = dot_nt(g, v)
            ds = (w * (gw - jnp.sum(w * gw, axis=-1, keepdims=True))).astype(BF)
            dq = dot(ds, k[:, :HD]) * SCALE
            dk = dot_tn(ds, q)[:, :HD]
            dv = dot_tn(w_low, g)
            for c, piece in enumerate((dq, dk, dv)):
                at = c * LANES + (h % 2) * HD
                out[h // 2, p, TILE:, at : at + HD] = jnp.where(outside, piece, 0.0).astype(BF)


def thumbs_back(count, x, mid_low, out_weight, heads):
    passes, size, _ = mid_low.shape
    return local_call(
        functools.partial(thumb_back_kernel, heads),
        "thumbs_back",
        shaped(heads // 2, passes, size, 3 * LANES),
        [SMEM] + [VMEM] * 3,
        VMEM,
        (count, x, mid_low, out_weight),
        cost=cost(6),
    )


def early_at(units, model, low):
    ends = [model, 2 * model, 2 * model + units, 2 * model + units + low]
    return [slice(b - w, b) for b, w in zip(ends, (model, model, units, low))]


def early_cuts(parts, units, model, low):
    high, wide, turns = units // parts // 2, model // parts, model // low
    narrow = low * turns // parts
    for i in range(parts):
        yield (
            (slice(2 * i * high, (2 * i + 1) * high), slice(0, model)),
            (slice((2 * i + 1) * high, (2 * i + 2) * high), slice(0, model)),
            (slice(i * wide, (i + 1) * wide), slice(0, units)),
            (
                slice(i // turns * narrow, (i // turns + 1) * narrow),
                slice(i % turns * low, (i % turns + 1) * low),
            ),
        )


def weight_kernel(place, act, outer, hidden, pre, low, mid_low, keep, give):
    units, model, cols = act.shape[1], hidden.shape[1], low.shape[1]
    core = place[0]
    for turn, out in ((core, keep), (1 - core, give)):
        down = dot_tn(act[...], outer[turn]).astype(BF)
        up = dot_tn(hidden[...], pre[turn]).astype(BF)
        proj = dot_tn(low[...], mid_low[turn]).astype(BF)
        for i, cut in enumerate(early_cuts(keep.shape[0], units, model, cols)):
            for value, (rows, lanes), at in zip(
                (down, down, up, proj), cut, early_at(units, model, cols)
            ):
                out[i, :, at] = value[rows, lanes]


def weight_grads(core, act, outer, hidden, pre, low, mid_low, parts):
    units, model = act.shape[1], outer.shape[2]
    out = shaped(parts, model // parts, 2 * model + units + low.shape[1])
    return local_call(
        weight_kernel,
        "weight_grads",
        (out, out),
        [SMEM] + [VMEM] * 6,
        (VMEM,) * 2,
        (core, act, outer, hidden, pre, low, mid_low),
        cost=cost(8),
        room=24,
    )


def reverse_kernel(rows, groups, heads, passes, pair, first, *refs):
    last = not first
    counts, place = refs[:2]
    grads, kept = refs[2 : 2 + groups], refs[2 + groups : 7 + groups]
    own, thumb, weights, columns = refs[7 + groups : 11 + groups]
    at = 11 + groups
    if first:
        small, (low_q, low_kv), at = refs[at], refs[at + 1 : at + 3], at + 3
    else:
        before, at = refs[at : at + 2], at + 2
        out_q, give_q, at = refs[at : at + groups // 2], refs[at + groups // 2], at + groups // 2 + 1
        out_kv, at = refs[at : at + groups], at + groups
    keep, give = refs[at : at + 2]
    stage, xq, xk, qx, kx, vx, packed, gx, kt, dq_t, dv, dk, total, sums, starts, sems = refs[
        at + 2 : at + 18
    ]
    pairs = pl.ds(2 * pair, 2)
    sources = [*grads, *[k.at[pairs] for k in kept[2:]], *kept[:2]]
    targets = [*[stage.at[g] for g in range(groups)], qx, kx, vx, xq, xk]
    if last:
        low_q, low_kv, q_before, kv_before = refs[at + 18 :]
        sources += before
        targets += [q_before, kv_before]
    copies = [
        pltpu.make_async_copy(f, t, sems.at[i]) for i, (f, t) in enumerate(zip(sources, targets))
    ]
    for copy in copies:
        copy.start()
    cols = heads * HD
    q_counts = [counts[g] for g in range(groups)]
    k_counts = [counts[groups + g] for g in range(groups)]
    start = jnp.int32(0)
    for g in range(groups):
        copies[g].wait()
        packed[rows_at(start, rows), :] = stage[g]
        start = start + q_counts[g] * TILE
    q_total, k_total = start, sum(k_counts) * TILE
    tail_lane = iota((BLOCK, packed.shape[1]), 1) - passes * cols
    empty = (tail_lane >= 0) & (tail_lane < 3 * heads) & (tail_lane % 3 == 0)
    packed[rows_at(q_total, BLOCK), :] = jnp.where(empty, FAR, 0.0).astype(BF)
    q_blocks = (q_total + BLOCK - 1) // BLOCK
    k_blocks = (k_total + BLOCK - 1) // BLOCK

    to_grads, to_marks = [], []
    for i in range(2):
        h = 2 * pair + i
        row, col = (iota((packed.shape[1], passes * LANES), d) for d in (0, 1))
        turn, lane = col // LANES, col % LANES
        plain = (lane < HD) & (row == turn * cols + h * HD + lane)
        extra = (lane >= HD) & (lane < HD + 3) & (
            row == passes * cols + 3 * heads * (turn + 1) + 3 * h + lane - HD
        )
        to_grads.append(zero_one(plain | extra))
        row, lane = (iota((LANES, LANES), d) for d in (0, 1))
        to_marks.append(
            zero_one((lane > HD) & (lane < HD + 4) & (row == 3 * h + lane - HD - 1))
        )

    for copy in copies[groups : groups + 3]:
        copy.wait()

    @pl.loop(0, q_blocks)
    def _(b):
        here = rows_at(b * BLOCK, BLOCK, BLOCK)
        for i in range(2):
            marks = dot(packed[here, passes * cols :], to_marks[i])
            qx[i, here, :] = (qx[i, here, :].astype(F32) + marks).astype(BF)
            gx[i, here, :] = dot(packed[here, :], to_grads[i]).astype(BF)

    @pl.loop(0, k_blocks)
    def _(b):
        here = rows_at(b * BLOCK, BLOCK, BLOCK)
        for i in range(2):
            kt[i, b] = jnp.transpose(kx[i, here, :].astype(F32))[:HD, :].astype(BF)

    def reverse_all(blocks):
        span = blocks * BLOCK
        dv[:, :span, :] = jnp.zeros((2, span, passes * LANES), F32)
        dk[:, :, :span, :] = jnp.zeros((passes, 2, span, LANES), F32)

        @pl.loop(0, q_blocks)
        def _(b):
            here = rows_at(b * BLOCK, BLOCK, BLOCK)
            for i in range(2):
                q, g = qx[i, here, :], gx[i, here, :]
                k_t = jnp.concatenate([kt[i, j] for j in range(blocks)], axis=1)
                w = jnp.exp(dot_nt(kx[i, :span, :], q))
                dv[i, :span, :] += dot(w.astype(BF), g)
                for p in range(passes):
                    ds = dot_nt(vx[i, :span, :], g[:, p * LANES : (p + 1) * LANES])
                    ds = (w * ds).astype(BF)
                    dk[p, i, :span, :] += dot(ds, q)
                    dq_t[p, i * HD : (i + 1) * HD, :] = dot(k_t, ds)
            for p in range(passes):
                piece = jnp.transpose(dq_t[p]) * SCALE
                low_q[here, p * LANES : (p + 1) * LANES] = piece.astype(BF)

        for p in range(passes):
            for i in range(2):
                for c, piece in enumerate(
                    (dk[p, i, :span, :HD], dv[i, :span, p * LANES : p * LANES + HD])
                ):
                    lane = (2 * p + c) * LANES + i * HD
                    low_kv[:span, lane : lane + HD] = piece.astype(BF)

    for blocks in range(groups * TILE // BLOCK, groups * rows // BLOCK + 1):
        pl.when(k_blocks == blocks)(functools.partial(reverse_all, blocks))

    copies[groups + 3].wait()
    copies[groups + 4].wait()

    def key_sums(blocks):
        flat = low_kv[: blocks * BLOCK, :]
        total[:, passes * LANES :] = dot_tn(xk[: blocks * BLOCK, :], flat)
        sums[:, passes * LANES :] = dot(jnp.ones((8, blocks * BLOCK), BF), flat)

    for blocks in range(groups * TILE // BLOCK, groups * rows // BLOCK + 1):
        pl.when(k_blocks == blocks)(functools.partial(key_sums, blocks))

    start = jnp.int32(0)
    for g in range(groups):
        starts[g] = start
        start = start + k_counts[g] * TILE
    if last:
        for copy in copies[groups + 5 :]:
            copy.wait()
        for g in range(groups):
            here = rows_at(starts[g], rows)
            out_kv[g][...] = jnp.concatenate([kv_before[here, :], low_kv[here, :]], axis=1)
        start = jnp.int32(0)
        for g in range(groups):
            here = rows_at(start, rows)
            value = jnp.concatenate([q_before[here, :], low_q[here, :]], axis=1)
            if g < groups // 2:
                out_q[g][...] = value
            else:
                give_q[g - groups // 2] = value
            start = start + q_counts[g] * TILE

    total[:, : passes * LANES] = jnp.zeros((total.shape[0], passes * LANES), F32)
    sums[:, : passes * LANES] = jnp.zeros((8, passes * LANES), F32)

    @pl.loop(0, q_blocks)
    def _(b):
        here = rows_at(b * BLOCK, BLOCK, BLOCK)
        total[:, : passes * LANES] += dot_tn(xq[here, :], low_q[here, :])
        sums[:, : passes * LANES] += dot(jnp.ones((8, BLOCK), BF), low_q[here, :])

    model = total.shape[0]
    gain, shift = columns[:, 0:1], columns[:, 1:2]
    ones = jnp.ones((8, own.shape[0]), BF)
    core = place[0]
    for p in range(passes):
        mine = thumb[pair, p]
        part = dot_tn(own[...], mine)
        part_sum = dot(ones, mine)[0:1, :]
        q_at = slice(p * LANES, (p + 1) * LANES)
        kv_at = slice((passes + 2 * p) * LANES, (passes + 2 * p + 2) * LANES)
        part += jnp.concatenate([total[:, q_at], total[:, kv_at]], axis=1)
        part_sum += jnp.concatenate([sums[0:1, q_at], sums[0:1, kv_at]], axis=1)
        w = weights[pair].astype(F32)
        gain_one = jnp.sum(w * part, axis=1, keepdims=True)
        shift_one = jnp.sum(w * part_sum, axis=1, keepdims=True)
        lane = iota((model, LANES), 1)
        tall = jnp.where(lane == 0, gain_one, jnp.where(lane == 1, shift_one, 0.0))
        flat = jnp.concatenate(
            [part_sum[:, :LANES], part_sum[:, LANES : 2 * LANES], part_sum[:, 2 * LANES :]]
            + [jnp.zeros((LANES - 3, LANES), F32)],
            axis=0,
        )
        flat = jnp.transpose(flat)
        flat = jnp.concatenate([jnp.zeros((LANES, 2), F32), flat[:, : LANES - 2]], axis=1)
        tall = jnp.concatenate([tall[:LANES] + flat, tall[LANES:]], axis=0)
        if first:
            turned = jnp.concatenate(
                [
                    jnp.zeros((8, model), F32),
                    small[p],
                    jnp.zeros((LANES - 16, model), F32),
                ],
                axis=0,
            )
            tall = tall + jnp.transpose(turned)
        grad = part * gain + shift * part_sum
        whole = jnp.concatenate([grad, tall], axis=1).astype(BF)

        @pl.when(core == p)
        def _():
            keep[...] = whole

        @pl.when(core != p)
        def _():
            give[...] = whole


def reverse(counts, place, grads, kept, own, thumb, weights, columns, more, rows, heads, pair):
    groups = len(grads)
    passes = thumb.shape[1]
    model = own.shape[1]
    room = rows * groups + BLOCK
    cols = heads * HD
    wide = passes * LANES
    first = pair == 0
    mine = shaped(model, 4 * LANES)
    if first:
        out = (shaped(room, wide), shaped(room, 2 * wide), mine, mine)
    else:
        half = groups // 2
        q, kv = shaped(rows, 2 * wide), shaped(rows, 4 * wide)
        out = (*[q] * half, shaped(half, rows, 2 * wide), *[kv] * groups, mine, mine)
    scratch = [
        pltpu.VMEM((groups, rows, passes * cols + LANES), BF),
        pltpu.VMEM((room, model), BF),
        pltpu.VMEM((room, model), BF),
        pltpu.VMEM((2, room, LANES), BF),
        pltpu.VMEM((2, room, LANES), BF),
        pltpu.VMEM((2, room, LANES), BF),
        pltpu.VMEM((room, passes * cols + LANES), BF),
        pltpu.VMEM((2, room, wide), BF),
        pltpu.VMEM((2, room // BLOCK, HD, BLOCK), BF),
        pltpu.VMEM((passes, LANES, BLOCK), F32),
        pltpu.VMEM((2, room, wide), F32),
        pltpu.VMEM((passes, 2, room, LANES), F32),
        pltpu.VMEM((model, 3 * wide), F32),
        pltpu.VMEM((8, 3 * wide), F32),
        pltpu.SMEM((groups,), jnp.int32),
        pltpu.SemaphoreType.DMA((groups + 7,)),
    ]
    if not first:
        scratch += [pltpu.VMEM((room, w), BF) for w in (wide, 2 * wide) * 2]
    return local_call(
        functools.partial(reverse_kernel, rows, groups, heads, passes, pair, first),
        "reverse" + str(pair),
        out,
        [SMEM, SMEM] + [ANY] * (groups + 5) + [VMEM] * 4 + ([VMEM] if first else [ANY] * 2),
        (VMEM,) * len(out),
        (counts, place, *grads, *kept, own, thumb, weights, columns, *more),
        scratch,
        cost(25),
        REVERSE_ROOM,
    )


def chosen(counts, far, thumb, rows):
    image = iota(far.shape, 0) < counts[0] * TILE
    return jnp.concatenate(
        [jnp.where(image, far.astype(BF), thumb[:rows]), thumb[rows:]], axis=0
    )


def grad_one_kernel(near, counts, *refs):
    from_q, from_kv, (thumb, weights, out) = refs[:near], refs[near:-3], refs[-3:]
    rows = from_q[0].shape[0]
    passes = thumb.shape[1]
    sum_q = sum(r[...].astype(F32) for r in from_q)
    sum_kv = sum(r[...].astype(F32) for r in from_kv)
    for p in range(passes):
        part = 0.0
        for pair in range(2):
            far = sum_q[:, (passes * pair + p) * LANES : (passes * pair + p + 1) * LANES]
            flat = chosen(counts, far, thumb[pair, p, :, :LANES], rows)
            part = part + dot_nt(flat, weights[pair, :, :LANES])
            at = 2 * (passes * pair + p) * LANES
            flat = chosen(counts, sum_kv[:, at : at + 2 * LANES], thumb[pair, p, :, LANES:], rows)
            part = part + dot_nt(flat, weights[pair, :, LANES:])
        out[p] = part.astype(BF)


def grad_one(count, from_q, from_kv, thumb, weights):
    near = len(from_q)
    return local_call(
        functools.partial(grad_one_kernel, near),
        "grad_one",
        shaped(*thumb.shape[1:3], weights.shape[1]),
        [SMEM] + [VMEM] * (near + len(from_kv) + 2),
        VMEM,
        (count, *from_q, *from_kv, thumb, weights),
        cost=cost(5),
        room=24,
    )


def close_kernel(tokens, mid, mine, other, gains, out):
    xhat, factor = standard(tokens[...].astype(F32))
    for p in range(mid.shape[0]):
        grad = mine[p].astype(F32) + other[p].astype(F32)
        out[p] = mid[p] + norm_back(grad, gains[0:1, :], xhat, factor)


def close(tokens, mid, mine, other, gains):
    return local_call(
        close_kernel,
        "close",
        shaped(*mid.shape, dtype=F32),
        [VMEM] * 5,
        VMEM,
        (tokens, mid, mine, other, gains),
        cost=cost(4),
    )


def early_kernel(place, own, far, down, up, proj):
    core = place[0]
    (units, model), low = down.shape[1:], proj.shape[1]
    for turn, ref in ((core, own), (1 - core, far)):
        for i, cut in enumerate(early_cuts(own.shape[0], units, model, low)):
            for out, (rows, lanes), at in zip(
                (down, down, up, proj), cut, early_at(units, model, low)
            ):
                out[turn, rows, lanes] = ref[i, :, at].astype(F32)


def early_out(core, own, far, units, low):
    model = own.shape[0] * own.shape[1]
    return local_call(
        early_kernel,
        "early_out",
        (
            shaped(2, units, model, dtype=F32),
            shaped(2, model, units, dtype=F32),
            shaped(2, low, model, dtype=F32),
        ),
        [SMEM] + [VMEM] * 2,
        (VMEM,) * 3,
        (core, own, far),
        cost=cost(8),
        room=24,
    )


def late_kernel(place, own, far, grad_in, in_bias, up_bias, gains, shifts):
    core = place[0]
    for turn, ref in ((core, own), (1 - core, far)):
        turned = []
        for pair in range(2):
            at = 4 * LANES * pair
            for c in range(3):
                grad_in[turn, c, :, pair * LANES : (pair + 1) * LANES] = ref[
                    :, at + c * LANES : at + (c + 1) * LANES
                ].astype(F32)
            turned.append(jnp.transpose(ref[:, at + 3 * LANES : at + 4 * LANES].astype(F32)))
        a, b = turned
        in_bias[turn] = jnp.concatenate(
            [
                jnp.concatenate([a[2:3, :LANES], b[2:3, :LANES]], axis=1),
                jnp.concatenate([a[4:5, :LANES], b[4:5, :LANES]], axis=1),
            ],
            axis=0,
        )
        up_bias[turn] = jnp.concatenate([a[12:13], a[13:14]], axis=1)
        gains[turn] = jnp.concatenate([a[0:1] + b[0:1], a[8:9]], axis=0)
        shifts[turn] = jnp.concatenate([a[1:2] + b[1:2], a[10:11], a[9:10], a[11:12]], axis=0)


def late_out(core, own, far, units):
    model = own.shape[0]
    return local_call(
        late_kernel,
        "late_out",
        (
            shaped(2, 3, model, 2 * LANES, dtype=F32),
            shaped(2, 2, 2 * LANES, dtype=F32),
            shaped(2, 1, units, dtype=F32),
            shaped(2, 2, model, dtype=F32),
            shaped(2, 4, model, dtype=F32),
        ),
        [SMEM] + [VMEM] * 2,
        (VMEM,) * 5,
        (core, own, far),
        cost=cost(4),
    )


def gather_near(array):
    mine = [array] + [shift_by(array, "y", d) for d in range(1, lax.axis_size("y"))]
    return mine + [shift_by(a, "c", 1) for a in mine]


def return_near(parts):
    return [parts[0]] + [shift_by(p, "y", -j) for j, p in enumerate(parts) if j > 0]


def gather_far(array):
    mine = [array, shift_by(array, "xl", 1)]
    return mine + [shift_by(a, "z", d) for d in range(1, lax.axis_size("z")) for a in mine]


def return_far(parts):
    size = lax.axis_size("z")
    out = []
    for j, part in enumerate(parts):
        step, flip = j // 2, j % 2
        perm = [
            (i * 2 + k, ((i - step) % size) * 2 + (k ^ flip)) for i in range(size) for k in range(2)
        ]
        out.append(lax.ppermute(part, ("z", "xl"), perm) if j else part)
    return out


PLANE = ("z", "xl", "y")


def core_sum(keep, give):
    return (keep.astype(F32) + shift_by(give, "c", 1).astype(F32)).astype(BF)


def plane_sum(mine):
    parts = lax.all_to_all(mine, PLANE, 0, 0, tiled=True)
    return jnp.sum(parts.astype(F32), axis=0)


def tied(arrays, others):
    return lax.optimization_barrier((arrays, others))


def padded(weight, heads):
    lead = weight.shape[0]
    return jnp.pad(weight.reshape(lead, heads, HD), ((0, 0), (0, 0), (0, LANES - HD))).reshape(
        lead, heads * LANES
    )


def local(
    tokens,
    cotangents,
    segment_ids,
    in_weights,
    in_biases,
    out_weight,
    up_weight,
    up_biases,
    down_weight,
    gains,
    shifts,
):
    size, model = tokens.shape
    cols = in_weights.shape[2]
    heads = cols // HD
    rows = size - TILE
    units = up_weight.shape[1]
    c = lax.axis_index("c")

    told, count = front(tokens, segment_ids)
    far = gather_far(told)
    near = gather_near(told)
    core = c.astype(jnp.int32).reshape(1)
    plane = lax.axis_size(PLANE)

    bundle = bundled(core, up_weight, down_weight, up_biases[None])
    n_x = lax.axis_size(("xl", "h"))
    crossed = [(i, n_x - 1 - i) for i in range(n_x)]
    out_far = lax.ppermute(out_weight, ("xl", "h"), crossed)
    far_one = lax.ppermute(bundle, ("xl", "h"), crossed)
    far_two = shift_by(far_one, "c", 1)

    weights = jnp.concatenate(
        [
            padded(in_weights[0] * jnp.asarray(SCALE, BF), heads),
            padded(in_weights[1], heads),
            padded(in_weights[2], heads),
        ],
        axis=1,
    )
    lane = jnp.arange(heads * LANES) % LANES
    biases = jnp.concatenate(
        [
            padded(in_biases[0:1] * SCALE, heads) + (lane == HD),
            ((lane > HD) & (lane < HD + 4)).astype(F32)[None],
            padded(in_biases[1:2], heads) + ((lane >= HD) & (lane < HD + 3)),
        ],
        axis=1,
    )
    pairs = jnp.stack(
        [
            jnp.concatenate([in_weights[i, :, at : at + LANES] for i in range(3)], axis=1)
            for at in range(0, cols, LANES)
        ]
    )
    columns = jnp.pad(jnp.stack([gains[0], shifts[0]], axis=1), ((0, 0), (0, LANES - 2)))

    *parts, give, xq, xk, qx, kx, vx, counts = attend(
        near, far, weights, biases, gains, shifts, rows, heads
    )
    thumb_out, xhat, x = thumbs(tokens, weights, biases, gains, shifts, heads)
    parts = pair_merge(parts, shift_by(give, "c", 1), heads)
    low, full, lse = merge(count, return_near(parts), thumb_out, heads)
    low_far = shift_by(low, "h", 1)
    mixed, grad_mid, mid_low, packed, hidden, act, pre, small = feed_forward(
        tokens, cotangents, low, low_far, full, lse, out_weight, out_far, up_weight, up_biases[None],
        down_weight, far_one, far_two, gains, shifts, rows, heads,
    )
    grads = gather_near(packed)
    keep, give = weight_grads(core, act, cotangents, hidden, pre, low, mid_low, plane)
    mid_low, (keep, give) = tied(mid_low, (keep, give))
    thumb = thumbs_back(count, x, mid_low, out_weight, heads)
    early = core_sum(keep, give)

    grads, (early, thumb) = tied(grads, (early, thumb))
    kept = (xq, xk, qx, kx, vx)
    *before, keep, give = reverse(
        counts, core, grads, kept, xhat, thumb, pairs, columns, [small], rows, heads, 0
    )
    early = plane_sum(early).astype(BF)
    early = jnp.broadcast_to(early[None], (plane, *early.shape))
    before, (early, keep, give) = tied(before, (early, keep, give))
    early = lax.all_to_all(early, PLANE, 0, 0, tiled=True)
    give = shift_by(give, "c", 1)
    out = reverse(
        counts, core, grads, kept, xhat, thumb, pairs, columns, before, rows, heads, 1
    )
    out, (early, give) = tied(out, (early, give))
    half = len(near) // 2
    out_q, give_q, out_kv = out[:half], out[half], out[half + 1 : half + 1 + len(far)]
    keep_two, give_two = out[-2:]
    late = [(keep.astype(F32) + give.astype(F32)).astype(BF), core_sum(keep_two, give_two)]
    mine = jnp.concatenate(late, axis=1)
    part = plane_sum(mine.reshape(plane, -1, mine.shape[1])).astype(BF)
    from_q = return_near(fold(out_q, shift_by(give_q, "c", 1)))
    from_kv = return_far(out_kv)
    part, (from_q, from_kv) = tied(part, (from_q, from_kv))
    mine = grad_one(count, from_q, from_kv, thumb, pairs)
    grad_tokens = close(tokens, grad_mid, mine, shift_by(mine, "h", 1), gains)

    lanes = jnp.arange(part.shape[1]) % (4 * LANES) - 3 * LANES
    lone = jnp.concatenate([part[:, 3 * LANES : 4 * LANES], part[:, 7 * LANES :]], axis=1)
    lone = jnp.pad(shift_by(lone, "h", 1).reshape(-1, 2, LANES), ((0, 0), (0, 0), (3 * LANES, 0)))
    lone = jnp.where((lanes >= 0) & (lanes < 2), lone.reshape(part.shape), 0).astype(F32)
    part = (part.astype(F32) + lone).astype(BF)
    part = jnp.broadcast_to(part[None], (plane, *part.shape))
    own = lax.all_to_all(part, PLANE, 0, 0, tiled=True).reshape(model, -1)
    grad_down, grad_up, grad_out = early_out(core, early, shift_by(early, "c", 1), units, cols)
    grad_in, in_bias, up_bias, grad_gains, grad_shifts = late_out(
        core, own, shift_by(own, "c", 1), units
    )
    return (
        mixed,
        grad_tokens,
        grad_in,
        in_bias,
        grad_out,
        grad_up,
        up_bias.reshape(2, units),
        grad_down,
        grad_gains,
        grad_shifts,
    )


def solution(mesh):
    fine = Mesh(mesh.devices.reshape(4, 2, 4, 2, 2), ("z", "xl", "y", "c", "h"))
    blk = ("z", "xl", "y", "c")
    return jax.shard_map(
        local,
        mesh=fine,
        in_specs=(
            P(blk, None),
            P(None, blk, None),
            P(blk),
            P(None, None, "h"),
            P(None, "h"),
            P("h", None),
            P(None, "h"),
            P("h"),
            P("h", None),
            P(),
            P(),
        ),
        out_specs=(
            P(blk, None),
            P(None, blk, None),
            P(None, None, None, "h"),
            P(None, None, "h"),
            P(None, "h", None),
            P(None, None, "h"),
            P(None, "h"),
            P(None, "h", None),
            P(),
            P(),
        ),
        check_vma=False,
    )
```

```python
import functools

import jax
import jax.numpy as jnp
from jax import lax
from jax.experimental import pallas as pl
from jax.experimental.pallas import tpu as pltpu
from jax.sharding import Mesh
from jax.sharding import PartitionSpec as P

HD = 64
LANES = 128
TILE = 64
BLOCK = 256
EPS = 1e-06
SCALE = 0.125
FAR = -1e30
BF = jnp.bfloat16
F32 = jnp.float32
MIB = 1024 * 1024
ROOM = 56

NT = (((1,), (1,)), ((), ()))
TN = (((0,), (0,)), ((), ()))


def shift_by(array, axis, step):
    size = lax.axis_size(axis)
    return lax.ppermute(array, axis, [(i, (i + step) % size) for i in range(size)])


def dot(a, b):
    return jnp.dot(a, b, preferred_element_type=F32)


def dot_nt(a, b):
    return lax.dot_general(a, b, NT, preferred_element_type=F32)


def dot_tn(a, b):
    return lax.dot_general(a, b, TN, preferred_element_type=F32)


def standard(field):
    center = field - jnp.mean(field, axis=-1, keepdims=True)
    factor = lax.rsqrt(jnp.mean(center * center, axis=-1, keepdims=True) + EPS)
    return center * factor, factor


def norm_back(grad, gain, xhat, factor):
    h = grad * gain
    mean = jnp.mean(h, axis=-1, keepdims=True)
    return factor * (h - mean - xhat * jnp.mean(h * xhat, axis=-1, keepdims=True))


def pieces(value):
    high = value.astype(BF)
    rest = value - high.astype(F32)
    middle = rest.astype(BF)
    low = (rest - middle.astype(F32)).astype(BF)
    return high, middle, low


def iota(shape, dim):
    return lax.broadcasted_iota(jnp.int32, shape, dim)


VMEM = pl.BlockSpec(memory_space=pltpu.VMEM)
ANY = pl.BlockSpec(memory_space=pl.ANY)
SMEM = pl.BlockSpec(memory_space=pltpu.SMEM)


def local_call(body, name, out, ins, outs, args, scratch=(), cost=None, room=16):
    return pl.pallas_call(
        body,
        out_shape=out,
        in_specs=ins,
        out_specs=outs,
        scratch_shapes=scratch,
        cost_estimate=cost,
        compiler_params=pltpu.CompilerParams(vmem_limit_bytes=room * MIB),
        name=name,
    )(*args)


def shaped(*shape, dtype=BF):
    return jax.ShapeDtypeStruct(shape, dtype)


def cost(micros):
    return pl.CostEstimate(flops=int(micros * 1e9), bytes_accessed=0, transcendentals=0)


def front_kernel(tokens, ids, told, copies, number):
    rows = told.shape[0] - 16
    marks = jnp.where(ids[...] == 0, 1.0, 0.0)
    tiles = jnp.sum(marks).astype(jnp.int32) // TILE
    number[0] = tiles
    told[:rows, :] = tokens[:rows, :]
    told[rows:, :] = jnp.full((16, told.shape[1]), tiles.astype(F32), F32).astype(BF)
    for g in range(copies.shape[0]):
        copies[g] = told[...]


def front(tokens, ids, copies):
    size, model = tokens.shape
    told = size - TILE + 16
    return local_call(
        front_kernel,
        "front",
        (shaped(told, model), shaped(copies, told, model), shaped(1, dtype=jnp.int32)),
        [VMEM, VMEM],
        (VMEM, VMEM, SMEM),
        (tokens, ids.reshape(-1, LANES)),
    )


def bundle_kernel(place, up, down, bias, out):
    core = place[0]
    half = out.shape[1]
    at = pl.ds(pl.multiple_of(core * half, half), half)
    out[:half, :] = up[:, at]
    out[half : 2 * half, :] = down[at, :]
    mine = jnp.where(core == 0, bias[:, :half], bias[:, half:])
    row = iota((16, half), 0)
    rows = jnp.zeros((16, half), F32)
    for i, piece in enumerate(pieces(mine)):
        rows = jnp.where(row == i, piece.astype(F32), rows)
    out[2 * half :, :] = rows.astype(BF)


def bundled(core, up, down, bias):
    model = up.shape[0]
    return local_call(
        bundle_kernel,
        "bundle",
        shaped(2 * model + 16, model),
        [SMEM] + [VMEM] * 3,
        VMEM,
        (core, up, down, bias),
    )


def count_of(ref, rows):
    return jnp.max(ref[rows : rows + 16, :LANES].astype(F32)).astype(jnp.int32)


def rows_at(start, rows, step=TILE):
    return pl.ds(pl.multiple_of(start, step), rows)


def attend_kernel(rows, groups, heads, *refs):
    near, far = refs[:groups], refs[groups]
    weights, biases, gains, shifts = refs[groups + 1 : groups + 5]
    at = groups + 5 + groups // 2
    out, give = refs[groups + 5 : at], refs[at]
    kept, counts, place = refs[at + 1 : at + 6], refs[at + 6], refs[at + 7]
    (xq, xk, qx, kx, vx), sems = refs[at + 8 : at + 13], refs[at + 13]
    model = xq.shape[1]
    q_counts = [count_of(r, rows) for r in near]
    k_counts = [count_of(far.at[g], rows) for g in range(groups)]
    for g in range(groups):
        counts[g] = q_counts[g]
        counts[groups + g] = k_counts[g]

    def compact(numbers, read, target):
        start = jnp.int32(0)
        for g, n in enumerate(numbers):
            target[rows_at(start, rows), :] = read(g)
            start = start + n * TILE
        target[rows_at(start, BLOCK), :] = jnp.zeros((BLOCK, model), BF)
        return start

    q_total = compact(q_counts, lambda g: near[g][:rows, :], xq)
    k_total = compact(k_counts, lambda g: far[g, :rows, :], xk)
    q_blocks = (q_total + BLOCK - 1) // BLOCK
    k_blocks = (k_total + BLOCK - 1) // BLOCK
    width = heads * LANES

    def hidden(ref, here):
        clean = standard(ref[here, :].astype(F32))[0].astype(BF)
        ref[here, :] = clean
        return (clean.astype(F32) * gains[0:1, :] + shifts[0:1, :]).astype(BF)

    @pl.loop(0, q_blocks)
    def _(b):
        here = rows_at(b * BLOCK, BLOCK, BLOCK)
        q = (dot(hidden(xq, here), weights[:, :width]) + biases[:, :width]).astype(BF)
        for h in range(heads):
            qx[h, here, :] = q[:, h * LANES : (h + 1) * LANES]

    @pl.loop(0, k_blocks)
    def _(b):
        here = rows_at(b * BLOCK, BLOCK, BLOCK)
        both = dot(hidden(xk, here), weights[:, width:]) + biases[:, width:]
        unseen = (iota((BLOCK, width), 0) + b * BLOCK >= k_total) & (
            iota((BLOCK, width), 1) % LANES == HD
        )
        k = jnp.where(unseen, FAR, both[:, :width]).astype(BF)
        v = both[:, width:].astype(BF)
        for h in range(heads):
            kx[h, here, :] = k[:, h * LANES : (h + 1) * LANES]
            vx[h, here, :] = v[:, h * LANES : (h + 1) * LANES]

    copies = [
        pltpu.make_async_copy(held, to, sems.at[i])
        for i, (held, to) in enumerate(zip((xq, xk, qx, kx, vx), kept))
    ]
    for copy in copies:
        copy.start()

    def attend_all(span):
        @pl.loop(0, q_blocks)
        def _(b):
            here = rows_at(b * BLOCK, BLOCK, BLOCK)
            lane = iota((BLOCK, LANES), 1)
            for h in range(heads):
                s = dot_nt(qx[h, here, :], kx[h, :span, :])
                top = jnp.max(s, axis=-1, keepdims=True)
                o = dot(jnp.exp(s - top).astype(BF), vx[h, :span, :])
                total = o[:, HD : HD + 1]
                o = o / total
                for i, piece in enumerate(pieces(top + jnp.log(total))):
                    o = jnp.where(lane == HD + i, piece.astype(F32), o)
                place[h, here, :] = o.astype(BF)

    for blocks in range(groups * TILE // BLOCK, groups * rows // BLOCK + 1):
        pl.when(k_blocks == blocks)(functools.partial(attend_all, blocks * BLOCK))

    gather = [
        (iota((LANES, LANES), 0) - HD + 3 * h == iota((LANES, LANES), 1))
        & (iota((LANES, LANES), 0) >= HD)
        & (iota((LANES, LANES), 0) < HD + 3)
        for h in range(heads)
    ]
    gather = [jnp.where(m, 1.0, 0.0).astype(BF) for m in gather]
    start = jnp.int32(0)
    for g in range(groups):
        mine = [place[h, rows_at(start, rows), :] for h in range(heads)]
        stats = sum(dot(m, s) for m, s in zip(mine, gather)).astype(BF)
        value = jnp.concatenate([m[:, :HD] for m in mine] + [stats], axis=1)
        if g < groups // 2:
            out[g][...] = value
        else:
            give[g - groups // 2] = value
        start = start + q_counts[g] * TILE
    for copy in copies:
        copy.wait()


def attend(near, far, weights, biases, gains, shifts, rows, heads):
    groups = len(near)
    model = near[0].shape[1]
    room = rows * groups + BLOCK
    parts = heads * HD + LANES
    kept = [(room, model)] * 2 + [(heads, room, LANES)] * 3
    return local_call(
        functools.partial(attend_kernel, rows, groups, heads),
        "attend",
        (
            *[shaped(rows, parts)] * (groups // 2),
            shaped(groups // 2, rows, parts),
            *[shaped(*k) for k in kept],
            shaped(2 * groups, dtype=jnp.int32),
        ),
        [VMEM] * (groups + 5),
        (*[VMEM] * (groups // 2 + 1), *[ANY] * 5, SMEM),
        (*near, far, weights, biases, gains, shifts),
        [
            pltpu.VMEM((heads, room, LANES), BF),
            *[pltpu.VMEM(k, BF) for k in kept],
            pltpu.SemaphoreType.DMA((5,)),
        ],
        cost(15),
        ROOM,
    )


def same_tile(rows):
    return iota((rows, rows), 0) // TILE == iota((rows, rows), 1) // TILE


def thumb_kernel(heads, tokens, weights, biases, gains, shifts, out, xhat, x):
    width = heads * LANES
    size = tokens.shape[0]
    clean = standard(tokens[...].astype(F32))[0].astype(BF)
    xhat[...] = clean
    hidden = (clean.astype(F32) * gains[0:1, :] + shifts[0:1, :]).astype(BF)
    x[...] = (dot(hidden, weights[...]) + biases[...]).astype(BF)
    visible = same_tile(size - TILE)
    out[:TILE, :] = jnp.zeros((TILE, heads * HD), F32)
    for h in range(heads):
        q = x[TILE:, h * LANES : (h + 1) * LANES]
        k = x[TILE:, width + h * LANES : width + (h + 1) * LANES]
        v = x[TILE:, 2 * width + h * LANES : 2 * width + (h + 1) * LANES]
        s = jnp.where(visible, dot_nt(q, k), FAR)
        e = jnp.exp(s - jnp.max(s, axis=-1, keepdims=True))
        o = dot(e.astype(BF), v)[:, :HD] / jnp.sum(e, axis=-1, keepdims=True)
        out[TILE:, h * HD : (h + 1) * HD] = o


def thumbs(tokens, weights, biases, gains, shifts, heads):
    size, model = tokens.shape
    return local_call(
        functools.partial(thumb_kernel, heads),
        "thumbs",
        (
            shaped(size, heads * HD, dtype=F32),
            shaped(size, model),
            shaped(size, 3 * heads * LANES),
        ),
        [VMEM] * 5,
        (VMEM,) * 3,
        (tokens, weights, biases, gains, shifts),
        cost=cost(5),
    )


def zero_one(mask):
    return jnp.where(mask, 1.0, 0.0).astype(BF)


def merged(parts, heads):
    cols = heads * HD
    row, col = (iota((LANES, cols), d) for d in (0, 1))
    spread = zero_one(row // 3 == col // HD)
    marks = [dot(p[:, cols:], spread) for p in parts]
    top = functools.reduce(jnp.maximum, marks)
    expos = [jnp.exp(m - top) for m in marks]
    total = sum(expos)
    mixed = sum(e * p[:, :cols].astype(F32) for p, e in zip(parts, expos)) / total
    row, col = (iota((cols, LANES), d) for d in (0, 1))
    packed = [
        dot(piece, zero_one((row % HD == 0) & (col == 3 * (row // HD) + i)))
        for i, piece in enumerate(pieces(top + jnp.log(total)))
    ]
    return mixed, sum(packed)


def pair_kernel(heads, *refs):
    count = (len(refs) - 1) // 2
    for j, (mine, out) in enumerate(zip(refs[:count], refs[count + 1 :])):
        mixed, marks = merged([mine[...], refs[count][j]], heads)
        out[...] = jnp.concatenate([mixed.astype(BF), marks.astype(BF)], axis=1)


def pair_merge(parts, other, heads):
    return local_call(
        functools.partial(pair_kernel, heads),
        "pair_merge",
        tuple(shaped(*p.shape) for p in parts),
        [VMEM] * (len(parts) + 1),
        (VMEM,) * len(parts),
        (*parts, other),
        cost=cost(3),
    )


def merge_kernel(heads, counts, thumb, *refs):
    parts, (low, full, lse) = refs[:-3], refs[-3:]
    cols = heads * HD
    rows = lse.shape[0]
    mixed, marks = merged([p[...] for p in parts], heads)
    lse[...] = (-marks).astype(BF)
    image = iota((rows, cols), 0) < counts[0] * TILE
    full[:rows, :] = jnp.where(image, mixed, thumb[:rows, :])
    full[rows:, :] = thumb[rows:, :]
    low[...] = full[...].astype(BF)


def merge(count, parts, thumb, heads):
    size, cols = thumb.shape
    return local_call(
        functools.partial(merge_kernel, heads),
        "merge",
        (shaped(size, cols), shaped(size, cols, dtype=F32), shaped(parts[0].shape[0], LANES)),
        [SMEM] + [VMEM] * (1 + len(parts)),
        (VMEM,) * 3,
        (count, thumb, *parts),
        cost=cost(3),
    )


def fold_kernel(*refs):
    count = (len(refs) - 1) // 2
    for j, (mine, out) in enumerate(zip(refs[:count], refs[count + 1 :])):
        out[...] = (mine[...].astype(F32) + refs[count][j].astype(F32)).astype(BF)


def fold(parts, other):
    return local_call(
        fold_kernel,
        "fold",
        tuple(shaped(*p.shape) for p in parts),
        [VMEM] * (len(parts) + 1),
        (VMEM,) * len(parts),
        (*parts, other),
        cost=cost(2),
        room=ROOM,
    )


ROOT = 0.7978845608028654
CUBE = 0.044715


def ff_kernel(
    heads, tokens, outer, low, low_far, full, lse, out_weight, out_far, up, up_bias, down, far_one,
    far_two, gains, shifts, mixed, grad_mid, grad_low, packed, hidden_out, act_out, pre_out, small,
):
    size, model = tokens.shape
    passes = outer.shape[0]
    cols = heads * HD
    chunk = far_one.shape[1]
    units = up.shape[1]
    rows = packed.shape[0]
    branch = dot(low[...], out_weight[...]) + dot(low_far[...], out_far[...])
    middle = tokens[...].astype(F32) + (branch + shifts[1:2, :])
    xhat, factor = standard(middle)
    hidden = (xhat * gains[1:2, :] + shifts[2:3, :]).astype(BF)
    hidden_out[...] = hidden

    def one_chunk(up_part, bias, down_part, keep):
        v = dot(hidden, up_part) + bias
        t = jnp.tanh(ROOT * (v + CUBE * (v * v * v)))
        act = (0.5 * v * (1.0 + t)).astype(BF)
        slope = 0.5 * (1.0 + t) + 0.5 * v * (1.0 - t * t) * (ROOT * (1.0 + 3.0 * CUBE * (v * v)))
        two = []
        for p in range(passes):
            pre = (dot_nt(outer[p], down_part) * slope).astype(BF)
            if keep is not None:
                pre_out[p, :, keep] = pre
            two.append(dot_nt(pre, up_part))
        if keep is not None:
            act_out[:, keep] = act
        return dot(act, down_part), two

    def far_chunk(ref):
        told = ref[2 * chunk : 2 * chunk + 16, :].astype(F32)
        bias = told[0:1] + told[1:2] + told[2:3]
        return one_chunk(ref[:chunk, :], bias, ref[chunk : 2 * chunk, :], None)

    done = []
    for i in range(units // chunk):
        at = slice(i * chunk, (i + 1) * chunk)
        done.append(one_chunk(up[:, at], up_bias[:, at], down[at, :], at))
    done += [far_chunk(far_one), far_chunk(far_two)]

    def tree(parts):
        half = len(parts) // 2
        return sum(parts[:half]) + sum(parts[half:])

    output = tree([d[0] for d in done])
    mixed[...] = (middle + (output + shifts[3:4, :])).astype(BF)
    small[...] = jnp.zeros(small.shape, F32)
    lane = iota((rows, LANES), 1)
    stats = jnp.zeros((rows, LANES), F32)
    for p in range(passes):
        two = tree([d[1][p] for d in done])
        c = outer[p].astype(F32)
        mid = c + norm_back(two, gains[1:2, :], xhat, factor)
        mid_low = mid.astype(BF)
        grad_mid[p] = mid
        grad_low[p] = mid_low
        att = dot_nt(mid_low, out_weight[...]).astype(BF)
        packed[:, p * cols : (p + 1) * cols] = att[:rows, :]
        pre_out_p = pre_out[p].astype(F32)
        bias = jnp.sum(pre_out_p, axis=0, keepdims=True)
        small[p, 0:1, :] = jnp.sum(two * xhat, axis=0, keepdims=True)
        small[p, 1:2, :] = jnp.sum(two, axis=0, keepdims=True)
        small[p, 2:3, :] = jnp.sum(mid_low.astype(F32), axis=0, keepdims=True)
        small[p, 3:4, :] = jnp.sum(c, axis=0, keepdims=True)
        for i in range(units // model):
            small[p, 4 + i : 5 + i, :] = bias[:, i * model : (i + 1) * model]
        product = att[:rows, :].astype(F32) * full[:rows, :]
        for h in range(heads):
            delta = jnp.sum(product[:, h * HD : (h + 1) * HD], axis=-1, keepdims=True)
            for i, piece in enumerate(pieces(-delta)):
                stats = jnp.where(lane == 3 * heads * (p + 1) + 3 * h + i, piece.astype(F32), stats)
    packed[:, passes * cols :] = (stats + lse[...].astype(F32)).astype(BF)


def feed_forward(
    tokens, outer, low, low_far, full, lse, out_weight, out_far, up, up_bias, down, far_one, far_two,
    gains, shifts, rows, heads,
):
    size, model = tokens.shape
    passes = outer.shape[0]
    units = up.shape[1]
    return local_call(
        functools.partial(ff_kernel, heads),
        "feed_forward",
        (
            shaped(size, model),
            shaped(passes, size, model, dtype=F32),
            shaped(passes, size, model),
            shaped(rows, passes * heads * HD + LANES),
            shaped(size, model),
            shaped(size, units),
            shaped(passes, size, units),
            shaped(passes, 8, model, dtype=F32),
        ),
        [VMEM] * 15,
        (VMEM,) * 8,
        (
            tokens, outer, low, low_far, full, lse, out_weight, out_far, up, up_bias, down, far_one,
            far_two, gains, shifts,
        ),
        cost=cost(12),
        room=32,
    )


def thumb_back_kernel(heads, counts, x, mid_low, out_weight, out):
    width = heads * LANES
    size = x.shape[0]
    passes = mid_low.shape[0]
    visible = same_tile(size - TILE)
    outside = iota((size - TILE, HD), 0) + TILE >= counts[0] * TILE
    grads = [dot_nt(mid_low[p], out_weight[...]).astype(BF) for p in range(passes)]
    out[:, :, :TILE, :] = jnp.zeros((*out.shape[:2], TILE, out.shape[3]), BF)
    for h in range(heads):
        q = x[TILE:, h * LANES : (h + 1) * LANES]
        k = x[TILE:, width + h * LANES : width + (h + 1) * LANES]
        v = x[TILE:, 2 * width + h * LANES : 2 * width + h * LANES + HD]
        s = jnp.where(visible, dot_nt(q, k), FAR)
        e = jnp.exp(s - jnp.max(s, axis=-1, keepdims=True))
        w = e / jnp.sum(e, axis=-1, keepdims=True)
        w_low = w.astype(BF)
        for p in range(passes):
            g = grads[p][TILE:, h * HD : (h + 1) * HD]
            gw = dot_nt(g, v)
            ds = (w * (gw - jnp.sum(w * gw, axis=-1, keepdims=True))).astype(BF)
            dq = dot(ds, k[:, :HD]) * SCALE
            dk = dot_tn(ds, q)[:, :HD]
            dv = dot_tn(w_low, g)
            for c, piece in enumerate((dq, dk, dv)):
                at = c * LANES + (h % 2) * HD
                out[h // 2, p, TILE:, at : at + HD] = jnp.where(outside, piece, 0.0).astype(BF)


def thumbs_back(count, x, mid_low, out_weight, heads):
    passes, size, _ = mid_low.shape
    return local_call(
        functools.partial(thumb_back_kernel, heads),
        "thumbs_back",
        shaped(heads // 2, passes, size, 3 * LANES),
        [SMEM] + [VMEM] * 3,
        VMEM,
        (count, x, mid_low, out_weight),
        cost=cost(6),
    )


def early_at(units, model, low):
    ends = [model, 2 * model, 2 * model + units, 2 * model + units + low]
    return [slice(b - w, b) for b, w in zip(ends, (model, model, units, low))]


def early_cuts(parts, units, model, low):
    high, wide, turns = units // parts // 2, model // parts, model // low
    narrow = low * turns // parts
    for i in range(parts):
        yield (
            (slice(2 * i * high, (2 * i + 1) * high), slice(0, model)),
            (slice((2 * i + 1) * high, (2 * i + 2) * high), slice(0, model)),
            (slice(i * wide, (i + 1) * wide), slice(0, units)),
            (
                slice(i // turns * narrow, (i // turns + 1) * narrow),
                slice(i % turns * low, (i % turns + 1) * low),
            ),
        )


def weight_kernel(place, act, outer, hidden, pre, low, mid_low, keep, give):
    units, model, cols = act.shape[1], hidden.shape[1], low.shape[1]
    core = place[0]
    for turn, out in ((core, keep), (1 - core, give)):
        down = dot_tn(act[...], outer[turn]).astype(BF)
        up = dot_tn(hidden[...], pre[turn]).astype(BF)
        proj = dot_tn(low[...], mid_low[turn]).astype(BF)
        for i, cut in enumerate(early_cuts(keep.shape[0], units, model, cols)):
            for value, (rows, lanes), at in zip(
                (down, down, up, proj), cut, early_at(units, model, cols)
            ):
                out[i, :, at] = value[rows, lanes]


def weight_grads(core, act, outer, hidden, pre, low, mid_low, parts):
    units, model = act.shape[1], outer.shape[2]
    out = shaped(parts, model // parts, 2 * model + units + low.shape[1])
    return local_call(
        weight_kernel,
        "weight_grads",
        (out, out),
        [SMEM] + [VMEM] * 6,
        (VMEM,) * 2,
        (core, act, outer, hidden, pre, low, mid_low),
        cost=cost(8),
        room=24,
    )


def reverse_kernel(rows, groups, heads, passes, counts, place, *refs):
    grads, kept = refs[:groups], refs[groups : groups + 5]
    own, thumb, weights, columns, small = refs[groups + 5 : groups + 10]
    at = groups + 10
    out_q, give_q, at = refs[at : at + groups // 2], refs[at + groups // 2], at + groups // 2 + 1
    out_kv, at = refs[at : at + groups], at + groups
    keep, give = refs[at : at + 2]
    (
        stage, xq, xk, qx, kx, vx, packed, gx, kt, dq_t, dv, dk, low_q, low_kv, total, sums,
        starts, sems,
    ) = refs[at + 2 :]
    couples = heads // 2
    sources = [*grads, *kept[2:], *kept[:2]]
    targets = [*[stage.at[g] for g in range(groups)], qx, kx, vx, xq, xk]
    copies = [
        pltpu.make_async_copy(f, t, sems.at[i]) for i, (f, t) in enumerate(zip(sources, targets))
    ]
    for copy in copies:
        copy.start()
    cols = heads * HD
    wide = passes * LANES
    q_counts = [counts[g] for g in range(groups)]
    k_counts = [counts[groups + g] for g in range(groups)]
    start = jnp.int32(0)
    for g in range(groups):
        copies[g].wait()
        packed[rows_at(start, rows), :] = stage[g]
        start = start + q_counts[g] * TILE
    q_total, k_total = start, sum(k_counts) * TILE
    tail_lane = iota((BLOCK, packed.shape[1]), 1) - passes * cols
    empty = (tail_lane >= 0) & (tail_lane < 3 * heads) & (tail_lane % 3 == 0)
    packed[rows_at(q_total, BLOCK), :] = jnp.where(empty, FAR, 0.0).astype(BF)
    q_blocks = (q_total + BLOCK - 1) // BLOCK
    k_blocks = (k_total + BLOCK - 1) // BLOCK
    spans = range(groups * TILE // BLOCK, groups * rows // BLOCK + 1)

    row, col = (iota((LANES, heads * LANES), d) for d in (0, 1))
    head, lane = col // LANES, col % LANES
    to_marks = zero_one((lane > HD) & (lane < HD + 4) & (row == 3 * head + lane - HD - 1))
    row, col = (iota((LANES, heads * wide), d) for d in (0, 1))
    head, turn, lane = col // wide, col % wide // LANES, col % LANES
    to_deltas = zero_one(
        (lane >= HD) & (lane < HD + 3) & (row == 3 * heads * (turn + 1) + 3 * head + lane - HD)
    )
    for copy in copies[groups : groups + 3]:
        copy.wait()

    @pl.loop(0, q_blocks)
    def _(b):
        here = rows_at(b * BLOCK, BLOCK, BLOCK)
        stats = packed[here, passes * cols :]
        marks = dot(stats, to_marks)
        deltas = dot(stats, to_deltas).astype(BF)
        for h in range(heads):
            more = marks[:, h * LANES : (h + 1) * LANES]
            qx[h, here, :] = (qx[h, here, :].astype(F32) + more).astype(BF)
            for p in range(passes):
                at = p * cols + h * HD
                mine = (h * passes + p) * LANES
                gx[h, here, p * LANES : (p + 1) * LANES] = jnp.concatenate(
                    [packed[here, at : at + HD], deltas[:, mine + HD : mine + LANES]], axis=1
                )

    @pl.loop(0, k_blocks)
    def _(b):
        here = rows_at(b * BLOCK, BLOCK, BLOCK)
        for h in range(heads):
            kt[h, b] = jnp.transpose(kx[h, here, :].astype(F32))[:HD, :].astype(BF)

    def reverse_all(blocks):
        span = blocks * BLOCK

        @pl.loop(0, couples)
        def _(pair):
            dv[:, :span, :] = jnp.zeros((2, span, wide), F32)
            dk[:, :, :span, :] = jnp.zeros((passes, 2, span, LANES), F32)

            @pl.loop(0, q_blocks)
            def _(b):
                here = rows_at(b * BLOCK, BLOCK, BLOCK)
                for i in range(2):
                    h = 2 * pair + i
                    q, g = qx[h, here, :], gx[h, here, :]
                    k_t = jnp.concatenate([kt[h, j] for j in range(blocks)], axis=1)
                    w = jnp.exp(dot_nt(kx[h, :span, :], q))
                    dv[i, :span, :] += dot(w.astype(BF), g)
                    for p in range(passes):
                        ds = dot_nt(vx[h, :span, :], g[:, p * LANES : (p + 1) * LANES])
                        ds = (w * ds).astype(BF)
                        dk[p, i, :span, :] += dot(ds, q)
                        dq_t[p, i * HD : (i + 1) * HD, :] = dot(k_t, ds)
                for p in range(passes):
                    piece = jnp.transpose(dq_t[p]) * SCALE
                    low_q[pair, here, p * LANES : (p + 1) * LANES] = piece.astype(BF)

            for p in range(passes):
                for c, both in enumerate(
                    (
                        [dk[p, i, :span, :HD] for i in range(2)],
                        [dv[i, :span, p * LANES : p * LANES + HD] for i in range(2)],
                    )
                ):
                    lane = (2 * p + c) * LANES
                    low_kv[pair, :span, lane : lane + LANES] = jnp.concatenate(both, axis=1).astype(BF)

    for blocks in spans:
        pl.when(k_blocks == blocks)(functools.partial(reverse_all, blocks))

    start = jnp.int32(0)
    for g in range(groups):
        starts[g] = start
        start = start + k_counts[g] * TILE
    for g in range(groups):
        here = rows_at(starts[place[1 + g]], rows)
        out_kv[g][...] = jnp.concatenate([low_kv[i, here, :] for i in range(couples)], axis=1)
    start = jnp.int32(0)
    for g in range(groups):
        here = rows_at(start, rows)
        value = jnp.concatenate([low_q[i, here, :] for i in range(couples)], axis=1)
        if g < groups // 2:
            out_q[g][...] = value
        else:
            give_q[g - groups // 2] = value
        start = start + q_counts[g] * TILE

    copies[groups + 3].wait()
    copies[groups + 4].wait()

    def key_sums(blocks):
        span = blocks * BLOCK
        for i in range(couples):
            flat = low_kv[i, :span, :]
            total[i, :, wide:] = dot_tn(xk[:span, :], flat)
            sums[i, :, wide:] = dot(jnp.ones((8, span), BF), flat)

    for blocks in spans:
        pl.when(k_blocks == blocks)(functools.partial(key_sums, blocks))

    total[:, :, :wide] = jnp.zeros((couples, total.shape[1], wide), F32)
    sums[:, :, :wide] = jnp.zeros((couples, 8, wide), F32)

    @pl.loop(0, q_blocks)
    def _(b):
        here = rows_at(b * BLOCK, BLOCK, BLOCK)
        for i in range(couples):
            total[i, :, :wide] += dot_tn(xq[here, :], low_q[i, here, :])
            sums[i, :, :wide] += dot(jnp.ones((8, BLOCK), BF), low_q[i, here, :])

    model = total.shape[1]
    gain, shift = columns[:, 0:1], columns[:, 1:2]
    ones = jnp.ones((8, own.shape[0]), BF)
    core = place[0]
    for p in range(passes):
        whole = []
        for i in range(couples):
            mine = thumb[i, p]
            part = dot_tn(own[...], mine)
            part_sum = dot(ones, mine)[0:1, :]
            q_at = slice(p * LANES, (p + 1) * LANES)
            kv_at = slice((passes + 2 * p) * LANES, (passes + 2 * p + 2) * LANES)
            part += jnp.concatenate([total[i, :, q_at], total[i, :, kv_at]], axis=1)
            part_sum += jnp.concatenate([sums[i, 0:1, q_at], sums[i, 0:1, kv_at]], axis=1)
            w = weights[i].astype(F32)
            gain_one = jnp.sum(w * part, axis=1, keepdims=True)
            shift_one = jnp.sum(w * part_sum, axis=1, keepdims=True)
            lane = iota((model, LANES), 1)
            tall = jnp.where(lane == 0, gain_one, jnp.where(lane == 1, shift_one, 0.0))
            flat = jnp.concatenate(
                [jnp.zeros((2, LANES), F32)]
                + [part_sum[:, c * LANES : (c + 1) * LANES] for c in range(3)]
                + [jnp.zeros((LANES - 5, LANES), F32)],
                axis=0,
            )
            tall = jnp.concatenate([tall[:LANES] + jnp.transpose(flat), tall[LANES:]], axis=0)
            if i == 0:
                turned = jnp.concatenate(
                    [
                        jnp.zeros((8, model), F32),
                        small[p],
                        jnp.zeros((LANES - 16, model), F32),
                    ],
                    axis=0,
                )
                tall = tall + jnp.transpose(turned)
            whole += [part * gain + shift * part_sum, tall]
        whole = jnp.concatenate(whole, axis=1).astype(BF)

        @pl.when(core == p)
        def _():
            keep[...] = whole

        @pl.when(core != p)
        def _():
            give[...] = whole


def reverse(counts, place, grads, kept, own, thumb, weights, columns, small, rows, heads):
    groups = len(grads)
    couples, passes = thumb.shape[:2]
    model = own.shape[1]
    room = rows * groups + BLOCK
    cols = heads * HD
    wide = passes * LANES
    half = groups // 2
    mine = shaped(model, couples * 4 * LANES)
    q, kv = shaped(rows, couples * wide), shaped(rows, couples * 2 * wide)
    out = (*[q] * half, shaped(half, rows, couples * wide), *[kv] * groups, mine, mine)
    return local_call(
        functools.partial(reverse_kernel, rows, groups, heads, passes),
        "reverse",
        out,
        [SMEM, SMEM] + [ANY] * (groups + 5) + [VMEM] * 5,
        (VMEM,) * len(out),
        (counts, place, *grads, *kept, own, thumb, weights, columns, small),
        [
            pltpu.VMEM((groups, rows, passes * cols + LANES), BF),
            pltpu.VMEM((room, model), BF),
            pltpu.VMEM((room, model), BF),
            pltpu.VMEM((heads, room, LANES), BF),
            pltpu.VMEM((heads, room, LANES), BF),
            pltpu.VMEM((heads, room, LANES), BF),
            pltpu.VMEM((room, passes * cols + LANES), BF),
            pltpu.VMEM((heads, room, wide), BF),
            pltpu.VMEM((heads, room // BLOCK, HD, BLOCK), BF),
            pltpu.VMEM((passes, LANES, BLOCK), F32),
            pltpu.VMEM((2, room, wide), F32),
            pltpu.VMEM((passes, 2, room, LANES), F32),
            pltpu.VMEM((couples, room, wide), BF),
            pltpu.VMEM((couples, room, 2 * wide), BF),
            pltpu.VMEM((couples, model, 3 * wide), F32),
            pltpu.VMEM((couples, 8, 3 * wide), F32),
            pltpu.SMEM((groups,), jnp.int32),
            pltpu.SemaphoreType.DMA((groups + 5,)),
        ],
        cost(45),
        ROOM,
    )


def chosen(counts, far, thumb, rows):
    image = iota(far.shape, 0) < counts[0] * TILE
    return jnp.concatenate(
        [jnp.where(image, far.astype(BF), thumb[:rows]), thumb[rows:]], axis=0
    )


def grad_one_kernel(near, counts, *refs):
    from_q, from_kv, (thumb, weights, out) = refs[:near], refs[near:-3], refs[-3:]
    rows = from_q[0].shape[0]
    passes = thumb.shape[1]
    sum_q = sum(r[...].astype(F32) for r in from_q)
    sum_kv = sum(r[...].astype(F32) for r in from_kv)
    for p in range(passes):
        part = 0.0
        for pair in range(2):
            far = sum_q[:, (passes * pair + p) * LANES : (passes * pair + p + 1) * LANES]
            flat = chosen(counts, far, thumb[pair, p, :, :LANES], rows)
            part = part + dot_nt(flat, weights[pair, :, :LANES])
            at = 2 * (passes * pair + p) * LANES
            flat = chosen(counts, sum_kv[:, at : at + 2 * LANES], thumb[pair, p, :, LANES:], rows)
            part = part + dot_nt(flat, weights[pair, :, LANES:])
        out[p] = part.astype(BF)


def grad_one(count, from_q, from_kv, thumb, weights):
    near = len(from_q)
    return local_call(
        functools.partial(grad_one_kernel, near),
        "grad_one",
        shaped(*thumb.shape[1:3], weights.shape[1]),
        [SMEM] + [VMEM] * (near + len(from_kv) + 2),
        VMEM,
        (count, *from_q, *from_kv, thumb, weights),
        cost=cost(5),
        room=ROOM,
    )


def close_kernel(tokens, mid, mine, other, gains, out):
    xhat, factor = standard(tokens[...].astype(F32))
    for p in range(mid.shape[0]):
        grad = mine[p].astype(F32) + other[p].astype(F32)
        out[p] = mid[p] + norm_back(grad, gains[0:1, :], xhat, factor)


def close(tokens, mid, mine, other, gains):
    return local_call(
        close_kernel,
        "close",
        shaped(*mid.shape, dtype=F32),
        [VMEM] * 5,
        VMEM,
        (tokens, mid, mine, other, gains),
        cost=cost(4),
        room=ROOM,
    )


def early_kernel(place, own, far, down, up, proj):
    core, turn = place[0], place[1]
    (units, model), low = down.shape[1:], proj.shape[1]
    lines, steps, rows = own.shape[:3]
    lane_down, lane_next, lane_up, lane_proj = early_at(units, model, low)
    for out, ref in ((core, own), (1 - core, far)):
        for y in range(lines):
            for j in range(steps):
                i = y * steps + (turn + steps - j) % steps
                at = pl.multiple_of(2 * rows * i, 2 * rows)
                down[out, pl.ds(at, rows), :] = ref[y, j, :, lane_down].astype(F32)
                down[out, pl.ds(at + rows, rows), :] = ref[y, j, :, lane_next].astype(F32)
                up[out, rows_at(rows * i, rows, rows), :] = ref[y, j, :, lane_up].astype(F32)
                turns = model // low
                here = rows_at(i // turns * rows, rows, rows)
                value = ref[y, j, :, lane_proj].astype(F32)
                for t in range(turns):

                    @pl.when(i % turns == t)
                    def _(value=value, here=here, t=t):
                        proj[out, here, t * low : (t + 1) * low] = value


def early_out(place, own, far, units, low):
    model = own.shape[0] * own.shape[1] * own.shape[2]
    return local_call(
        early_kernel,
        "early_out",
        (
            shaped(2, units, model, dtype=F32),
            shaped(2, model, units, dtype=F32),
            shaped(2, low, model, dtype=F32),
        ),
        [SMEM] + [VMEM] * 2,
        (VMEM,) * 3,
        (place, own, far),
        cost=cost(8),
        room=ROOM,
    )


def late_kernel(place, own, far, grad_in, in_bias, up_bias, gains, shifts):
    core = place[0]
    for turn, ref in ((core, own), (1 - core, far)):
        turned = []
        for pair in range(2):
            at = 4 * LANES * pair
            for c in range(3):
                grad_in[turn, c, :, pair * LANES : (pair + 1) * LANES] = ref[
                    :, at + c * LANES : at + (c + 1) * LANES
                ].astype(F32)
            turned.append(jnp.transpose(ref[:, at + 3 * LANES : at + 4 * LANES].astype(F32)))
        a, b = turned
        in_bias[turn] = jnp.concatenate(
            [
                jnp.concatenate([a[2:3, :LANES], b[2:3, :LANES]], axis=1),
                jnp.concatenate([a[4:5, :LANES], b[4:5, :LANES]], axis=1),
            ],
            axis=0,
        )
        up_bias[turn] = jnp.concatenate([a[12:13], a[13:14]], axis=1)
        gains[turn] = jnp.concatenate([a[0:1] + b[0:1], a[8:9]], axis=0)
        shifts[turn] = jnp.concatenate([a[1:2] + b[1:2], a[10:11], a[9:10], a[11:12]], axis=0)


def late_out(core, own, far, units):
    model = own.shape[0]
    return local_call(
        late_kernel,
        "late_out",
        (
            shaped(2, 3, model, 2 * LANES, dtype=F32),
            shaped(2, 2, 2 * LANES, dtype=F32),
            shaped(2, 1, units, dtype=F32),
            shaped(2, 2, model, dtype=F32),
            shaped(2, 4, model, dtype=F32),
        ),
        [SMEM] + [VMEM] * 2,
        (VMEM,) * 5,
        (core, own, far),
        cost=cost(4),
        room=ROOM,
    )


def gather_near(array):
    mine = [array] + [shift_by(array, "y", d) for d in range(1, lax.axis_size("y"))]
    return mine + [shift_by(a, "c", 1) for a in mine]


def return_near(parts):
    return [parts[0]] + [shift_by(p, "y", -j) for j, p in enumerate(parts) if j > 0]


def offsets(size):
    return [(step, flip) for step in range(size) for flip in range(2)]


def return_far(parts):
    size = lax.axis_size("z")
    out = []
    for part, (step, flip) in zip(parts, offsets(size)):
        perm = [
            (i * 2 + k, ((i + step) % size) * 2 + (k ^ flip)) for i in range(size) for k in range(2)
        ]
        out.append(lax.ppermute(part, ("z", "xl"), perm) if step + flip else part)
    return out


PLANE = ("z", "y")


def core_sum(keep, give):
    return (keep.astype(F32) + shift_by(give, "c", 1).astype(F32)).astype(BF)


def plane_sum(mine):
    parts = lax.all_to_all(mine, PLANE, 0, 0, tiled=True)
    return jnp.sum(parts.astype(F32), axis=0)


def across(low):
    done = low.astype(F32) + shift_by(low, "xl", 1).astype(F32)
    size = 4 * LANES
    ones = jnp.concatenate([low[:, i + 3 * LANES : i + size] for i in range(0, low.shape[1], size)], axis=1)
    n = lax.axis_size(("xl", "h"))
    more = shift_by(ones, "h", 1).astype(F32) + lax.ppermute(
        ones, ("xl", "h"), [(i, n - 1 - i) for i in range(n)]
    ).astype(F32)
    more = jnp.where(jnp.arange(more.shape[1]) % LANES < 2, more, 0.0)
    nothing = jnp.zeros((low.shape[0], 3 * LANES), F32)
    laid = [[nothing, more[:, i : i + LANES]] for i in range(0, more.shape[1], LANES)]
    return (done + jnp.concatenate(sum(laid, []), axis=1)).astype(BF)


def tied(arrays, others):
    return lax.optimization_barrier((arrays, others))


def padded(weight, heads):
    lead = weight.shape[0]
    return jnp.pad(weight.reshape(lead, heads, HD), ((0, 0), (0, 0), (0, LANES - HD))).reshape(
        lead, heads * LANES
    )


def local(
    tokens,
    cotangents,
    segment_ids,
    in_weights,
    in_biases,
    out_weight,
    up_weight,
    up_biases,
    down_weight,
    gains,
    shifts,
):
    size, model = tokens.shape
    cols = in_weights.shape[2]
    heads = cols // HD
    rows = size - TILE
    units = up_weight.shape[1]
    c = lax.axis_index("c")

    told, copies, count = front(tokens, segment_ids, lax.axis_size(("z", "xl")))
    far = lax.all_to_all(copies, ("z", "xl"), 0, 0, tiled=True)
    near = gather_near(told)
    core = c.astype(jnp.int32).reshape(1)
    z, xl, z_size = lax.axis_index("z"), lax.axis_index("xl"), lax.axis_size("z")
    routes = [((z + step) % z_size) * 2 + (xl ^ flip) for step, flip in offsets(z_size)]
    place = jnp.concatenate([core, jnp.stack(routes).astype(jnp.int32)])
    turns = jnp.concatenate([core, z.astype(jnp.int32).reshape(1)])
    plane = lax.axis_size(PLANE)

    bundle = bundled(core, up_weight, down_weight, up_biases[None])
    n_x = lax.axis_size(("xl", "h"))
    crossed = [(i, n_x - 1 - i) for i in range(n_x)]
    out_far = lax.ppermute(out_weight, ("xl", "h"), crossed)
    far_one = lax.ppermute(bundle, ("xl", "h"), crossed)
    far_two = shift_by(far_one, "c", 1)

    weights = jnp.concatenate(
        [
            padded(in_weights[0] * jnp.asarray(SCALE, BF), heads),
            padded(in_weights[1], heads),
            padded(in_weights[2], heads),
        ],
        axis=1,
    )
    lane = jnp.arange(heads * LANES) % LANES
    biases = jnp.concatenate(
        [
            padded(in_biases[0:1] * SCALE, heads) + (lane == HD),
            ((lane > HD) & (lane < HD + 4)).astype(F32)[None],
            padded(in_biases[1:2], heads) + ((lane >= HD) & (lane < HD + 3)),
        ],
        axis=1,
    )
    pairs = jnp.stack(
        [
            jnp.concatenate([in_weights[i, :, at : at + LANES] for i in range(3)], axis=1)
            for at in range(0, cols, LANES)
        ]
    )
    columns = jnp.pad(jnp.stack([gains[0], shifts[0]], axis=1), ((0, 0), (0, LANES - 2)))

    weights, (pairs, columns, place, turns) = tied(weights, (pairs, columns, place, turns))
    *parts, give, xq, xk, qx, kx, vx, counts = attend(
        near, far, weights, biases, gains, shifts, rows, heads
    )
    thumb_out, xhat, x = thumbs(tokens, weights, biases, gains, shifts, heads)
    parts = pair_merge(parts, shift_by(give, "c", 1), heads)
    low, full, lse = merge(count, return_near(parts), thumb_out, heads)
    low_far = shift_by(low, "h", 1)
    mixed, grad_mid, mid_low, packed, hidden, act, pre, small = feed_forward(
        tokens, cotangents, low, low_far, full, lse, out_weight, out_far, up_weight, up_biases[None],
        down_weight, far_one, far_two, gains, shifts, rows, heads,
    )
    grads = gather_near(packed)
    keep, give = weight_grads(core, act, cotangents, hidden, pre, low, mid_low, plane)
    mid_low, (keep, give) = tied(mid_low, (keep, give))
    thumb = thumbs_back(count, x, mid_low, out_weight, heads)
    early = core_sum(keep, give)

    grads, (early, thumb) = tied(grads, (early, thumb))
    early = early.reshape(-1, early.shape[2])
    for axis in ("y", "z"):
        early = lax.psum_scatter(early, axis, scatter_dimension=0, tiled=True)
    out = reverse(
        counts, place, grads, (xq, xk, qx, kx, vx), xhat, thumb, pairs, columns, small, rows, heads
    )
    half = len(near) // 2
    out_q, give_q, out_kv, (keep, give) = out[:half], out[half], out[half + 1 : -2], out[-2:]
    mine = core_sum(keep, give)
    part = plane_sum(mine.reshape(plane, -1, mine.shape[1])).astype(BF)
    from_q = return_near(fold(out_q, shift_by(give_q, "c", 1)))
    from_kv = return_far(out_kv)
    part, from_kv[1:5] = tied(part, from_kv[1:5])
    mine = grad_one(count, from_q, from_kv, thumb, pairs)
    grad_tokens = close(tokens, grad_mid, mine, shift_by(mine, "h", 1), gains)

    early = early.astype(F32) + shift_by(early, "xl", 1).astype(F32)
    early = early.astype(BF)
    early = jnp.stack([early] + [shift_by(early, "z", d) for d in range(1, z_size)])
    early = lax.all_gather(early, "y", axis=0)
    part = jnp.broadcast_to(across(part)[None], (plane, *part.shape))
    own = lax.all_to_all(part, PLANE, 0, 0, tiled=True).reshape(model, -1)
    grad_down, grad_up, grad_out = early_out(turns, early, shift_by(early, "c", 1), units, cols)
    grad_in, in_bias, up_bias, grad_gains, grad_shifts = late_out(
        core, own, shift_by(own, "c", 1), units
    )
    return (
        mixed,
        grad_tokens,
        grad_in,
        in_bias,
        grad_out,
        grad_up,
        up_bias.reshape(2, units),
        grad_down,
        grad_gains,
        grad_shifts,
    )


def solution(mesh):
    fine = Mesh(mesh.devices.reshape(4, 2, 4, 2, 2), ("z", "xl", "y", "c", "h"))
    blk = ("z", "xl", "y", "c")
    return jax.shard_map(
        local,
        mesh=fine,
        in_specs=(
            P(blk, None),
            P(None, blk, None),
            P(blk),
            P(None, None, "h"),
            P(None, "h"),
            P("h", None),
            P(None, "h"),
            P("h"),
            P("h", None),
            P(),
            P(),
        ),
        out_specs=(
            P(blk, None),
            P(None, blk, None),
            P(None, None, None, "h"),
            P(None, None, "h"),
            P(None, "h", None),
            P(None, None, "h"),
            P(None, "h"),
            P(None, "h", None),
            P(),
            P(),
        ),
        check_vma=False,
    )
```

```python
import functools

import jax
import jax.numpy as jnp
from jax import lax
from jax.experimental import pallas as pl
from jax.experimental.pallas import tpu as pltpu
from jax.sharding import Mesh
from jax.sharding import PartitionSpec as P

HD = 64
LANES = 128
TILE = 64
BLOCK = 256
EPS = 1e-06
SCALE = 0.125
FAR = -1e30
BF = jnp.bfloat16
F32 = jnp.float32
MIB = 1024 * 1024
ROOM = 56

NT = (((1,), (1,)), ((), ()))
TN = (((0,), (0,)), ((), ()))


def shift_by(array, axis, step):
    size = lax.axis_size(axis)
    return lax.ppermute(array, axis, [(i, (i + step) % size) for i in range(size)])


def dot(a, b):
    return jnp.dot(a, b, preferred_element_type=F32)


def dot_nt(a, b):
    return lax.dot_general(a, b, NT, preferred_element_type=F32)


def dot_tn(a, b):
    return lax.dot_general(a, b, TN, preferred_element_type=F32)


def standard(field):
    center = field - jnp.mean(field, axis=-1, keepdims=True)
    factor = lax.rsqrt(jnp.mean(center * center, axis=-1, keepdims=True) + EPS)
    return center * factor, factor


def norm_back(grad, gain, xhat, factor):
    h = grad * gain
    mean = jnp.mean(h, axis=-1, keepdims=True)
    return factor * (h - mean - xhat * jnp.mean(h * xhat, axis=-1, keepdims=True))


def pieces(value):
    high = value.astype(BF)
    rest = value - high.astype(F32)
    middle = rest.astype(BF)
    low = (rest - middle.astype(F32)).astype(BF)
    return high, middle, low


def zero_one(mask):
    return jnp.where(mask, 1.0, 0.0).astype(BF)


def iota(shape, dim):
    return lax.broadcasted_iota(jnp.int32, shape, dim)


VMEM = pl.BlockSpec(memory_space=pltpu.VMEM)
ANY = pl.BlockSpec(memory_space=pl.ANY)
SMEM = pl.BlockSpec(memory_space=pltpu.SMEM)


def local_call(body, name, out, ins, outs, args, scratch=(), cost=None, room=16):
    return pl.pallas_call(
        body,
        out_shape=out,
        in_specs=ins,
        out_specs=outs,
        scratch_shapes=scratch,
        cost_estimate=cost,
        compiler_params=pltpu.CompilerParams(vmem_limit_bytes=room * MIB),
        name=name,
    )(*args)


def shaped(*shape, dtype=BF):
    return jax.ShapeDtypeStruct(shape, dtype)


def cost(micros):
    return pl.CostEstimate(flops=int(micros * 1e9), bytes_accessed=0, transcendentals=0)


def front_kernel(tokens, ids, told, copies, number):
    rows = told.shape[0] - 16
    marks = jnp.where(ids[...] == 0, 1.0, 0.0)
    tiles = jnp.sum(marks).astype(jnp.int32) // TILE
    number[0] = tiles
    told[:rows, :] = tokens[:rows, :]
    told[rows:, :] = jnp.full((16, told.shape[1]), tiles.astype(F32), F32).astype(BF)
    for g in range(copies.shape[0]):
        copies[g] = told[...]


def front(tokens, ids, copies):
    size, model = tokens.shape
    told = size - TILE + 16
    return local_call(
        front_kernel,
        "front",
        (shaped(told, model), shaped(copies, told, model), shaped(1, dtype=jnp.int32)),
        [VMEM, VMEM],
        (VMEM, VMEM, SMEM),
        (tokens, ids.reshape(-1, LANES)),
    )


def prepare_kernel(
    heads, place, in_weights, in_biases, gains, shifts, up, down, bias,
    weights, biases, pairs, columns, out,
):
    core = place[0]
    half = out.shape[1]
    at = pl.ds(pl.multiple_of(core * half, half), half)
    out[:half, :] = up[:, at]
    out[half : 2 * half, :] = down[at, :]
    mine = jnp.where(core == 0, bias[:, :half], bias[:, half:])
    row = iota((16, half), 0)
    rows = jnp.zeros((16, half), F32)
    for i, piece in enumerate(pieces(mine)):
        rows = jnp.where(row == i, piece.astype(F32), rows)
    out[2 * half :, :] = rows.astype(BF)

    model, cols = in_weights.shape[1:]
    width = heads * LANES
    row, col = (iota((cols, width), d) for d in (0, 1))
    spread = zero_one((row // HD == col // LANES) & (row % HD == col % LANES))
    lane = iota((1, width), 1) % LANES
    gap = jnp.zeros((1, HD), F32)

    def apart(line):
        return jnp.concatenate(
            sum([[line[:, h * HD : (h + 1) * HD], gap] for h in range(heads)], []), axis=1
        )

    extra = [
        apart(in_biases[0:1, :] * SCALE) + jnp.where(lane == HD, 1.0, 0.0),
        jnp.where((lane > HD) & (lane < HD + 4), 1.0, 0.0),
        apart(in_biases[1:2, :]) + jnp.where((lane >= HD) & (lane < HD + 3), 1.0, 0.0),
    ]
    for i in range(3):
        factor = SCALE if i == 0 else 1.0
        weights[:, i * width : (i + 1) * width] = (dot(in_weights[i], spread) * factor).astype(BF)
        biases[:, i * width : (i + 1) * width] = extra[i]
        for pair in range(heads // 2):
            pairs[pair, :, i * LANES : (i + 1) * LANES] = in_weights[
                i, :, pair * LANES : (pair + 1) * LANES
            ]
    tall = jnp.concatenate(
        [gains[0:1, :], shifts[0:1, :], jnp.zeros((LANES - 2, model), F32)], axis=0
    )
    columns[...] = jnp.transpose(tall)


def prepare(core, in_weights, in_biases, gains, shifts, up, down, bias, heads):
    model = up.shape[0]
    width = 3 * heads * LANES
    return local_call(
        functools.partial(prepare_kernel, heads),
        "prepare",
        (
            shaped(model, width),
            shaped(1, width, dtype=F32),
            shaped(heads // 2, model, 3 * LANES),
            shaped(model, LANES, dtype=F32),
            shaped(2 * model + 16, model),
        ),
        [SMEM] + [VMEM] * 7,
        (VMEM,) * 5,
        (core, in_weights, in_biases, gains, shifts, up, down, bias),
        cost=cost(4),
        room=24,
    )


def count_of(ref, rows):
    return jnp.max(ref[rows : rows + 16, :LANES].astype(F32)).astype(jnp.int32)


def rows_at(start, rows, step=TILE):
    return pl.ds(pl.multiple_of(start, step), rows)


def attend_kernel(rows, groups, heads, *refs):
    near, far = refs[:groups], refs[groups]
    weights, biases, gains, shifts = refs[groups + 1 : groups + 5]
    at = groups + 5 + groups // 2
    out, give = refs[groups + 5 : at], refs[at]
    kept, counts, place = refs[at + 1 : at + 6], refs[at + 6], refs[at + 7]
    (xq, xk, qx, kx, vx), sems = refs[at + 8 : at + 13], refs[at + 13]
    model = xq.shape[1]
    q_counts = [count_of(r, rows) for r in near]
    k_counts = [count_of(far.at[g], rows) for g in range(groups)]
    for g in range(groups):
        counts[g] = q_counts[g]
        counts[groups + g] = k_counts[g]

    def compact(numbers, read, target):
        start = jnp.int32(0)
        for g, n in enumerate(numbers):
            target[rows_at(start, rows), :] = read(g)
            start = start + n * TILE
        target[rows_at(start, BLOCK), :] = jnp.zeros((BLOCK, model), BF)
        return start

    q_total = compact(q_counts, lambda g: near[g][:rows, :], xq)
    k_total = compact(k_counts, lambda g: far[g, :rows, :], xk)
    q_blocks = (q_total + BLOCK - 1) // BLOCK
    k_blocks = (k_total + BLOCK - 1) // BLOCK
    width = heads * LANES

    def hidden(ref, here):
        clean = standard(ref[here, :].astype(F32))[0].astype(BF)
        ref[here, :] = clean
        return (clean.astype(F32) * gains[0:1, :] + shifts[0:1, :]).astype(BF)

    @pl.loop(0, q_blocks)
    def _(b):
        here = rows_at(b * BLOCK, BLOCK, BLOCK)
        q = (dot(hidden(xq, here), weights[:, :width]) + biases[:, :width]).astype(BF)
        for h in range(heads):
            qx[h, here, :] = q[:, h * LANES : (h + 1) * LANES]

    @pl.loop(0, k_blocks)
    def _(b):
        here = rows_at(b * BLOCK, BLOCK, BLOCK)
        both = dot(hidden(xk, here), weights[:, width:]) + biases[:, width:]
        unseen = (iota((BLOCK, width), 0) + b * BLOCK >= k_total) & (
            iota((BLOCK, width), 1) % LANES == HD
        )
        k = jnp.where(unseen, FAR, both[:, :width]).astype(BF)
        v = both[:, width:].astype(BF)
        for h in range(heads):
            kx[h, here, :] = k[:, h * LANES : (h + 1) * LANES]
            vx[h, here, :] = v[:, h * LANES : (h + 1) * LANES]

    copies = [
        pltpu.make_async_copy(held, to, sems.at[i])
        for i, (held, to) in enumerate(zip((xq, xk, qx, kx, vx), kept))
    ]
    for copy in copies:
        copy.start()

    def attend_all(span):
        @pl.loop(0, q_blocks)
        def _(b):
            here = rows_at(b * BLOCK, BLOCK, BLOCK)
            lane = iota((BLOCK, LANES), 1)
            for h in range(heads):
                s = dot_nt(qx[h, here, :], kx[h, :span, :])
                top = jnp.max(s, axis=-1, keepdims=True)
                o = dot(jnp.exp(s - top).astype(BF), vx[h, :span, :])
                total = o[:, HD : HD + 1]
                o = o / total
                for i, piece in enumerate(pieces(top + jnp.log(total))):
                    o = jnp.where(lane == HD + i, piece.astype(F32), o)
                place[h, here, :] = o.astype(BF)

    for blocks in range(groups * TILE // BLOCK, groups * rows // BLOCK + 1):
        pl.when(k_blocks == blocks)(functools.partial(attend_all, blocks * BLOCK))

    gather = [
        (iota((LANES, LANES), 0) - HD + 3 * h == iota((LANES, LANES), 1))
        & (iota((LANES, LANES), 0) >= HD)
        & (iota((LANES, LANES), 0) < HD + 3)
        for h in range(heads)
    ]
    gather = [jnp.where(m, 1.0, 0.0).astype(BF) for m in gather]
    start = jnp.int32(0)
    for g in range(groups):
        mine = [place[h, rows_at(start, rows), :] for h in range(heads)]
        stats = sum(dot(m, s) for m, s in zip(mine, gather)).astype(BF)
        value = jnp.concatenate([m[:, :HD] for m in mine] + [stats], axis=1)
        if g < groups // 2:
            out[g][...] = value
        else:
            give[g - groups // 2] = value
        start = start + q_counts[g] * TILE
    for copy in copies:
        copy.wait()


def attend(near, far, weights, biases, gains, shifts, rows, heads):
    groups = len(near)
    model = near[0].shape[1]
    room = rows * groups + BLOCK
    parts = heads * HD + LANES
    kept = [(room, model)] * 2 + [(heads, room, LANES)] * 3
    return local_call(
        functools.partial(attend_kernel, rows, groups, heads),
        "attend",
        (
            *[shaped(rows, parts)] * (groups // 2),
            shaped(groups // 2, rows, parts),
            *[shaped(*k) for k in kept],
            shaped(2 * groups, dtype=jnp.int32),
        ),
        [VMEM] * (groups + 5),
        (*[VMEM] * (groups // 2 + 1), *[ANY] * 5, SMEM),
        (*near, far, weights, biases, gains, shifts),
        [
            pltpu.VMEM((heads, room, LANES), BF),
            *[pltpu.VMEM(k, BF) for k in kept],
            pltpu.SemaphoreType.DMA((5,)),
        ],
        cost(15),
        ROOM,
    )


def same_tile(rows):
    return iota((rows, rows), 0) // TILE == iota((rows, rows), 1) // TILE


def thumb_kernel(heads, tokens, weights, biases, gains, shifts, out, xhat, x):
    width = heads * LANES
    size = tokens.shape[0]
    clean = standard(tokens[...].astype(F32))[0].astype(BF)
    xhat[...] = clean
    hidden = (clean.astype(F32) * gains[0:1, :] + shifts[0:1, :]).astype(BF)
    x[...] = (dot(hidden, weights[...]) + biases[...]).astype(BF)
    visible = same_tile(size - TILE)
    out[:TILE, :] = jnp.zeros((TILE, heads * HD), F32)
    for h in range(heads):
        q = x[TILE:, h * LANES : (h + 1) * LANES]
        k = x[TILE:, width + h * LANES : width + (h + 1) * LANES]
        v = x[TILE:, 2 * width + h * LANES : 2 * width + (h + 1) * LANES]
        s = jnp.where(visible, dot_nt(q, k), FAR)
        e = jnp.exp(s - jnp.max(s, axis=-1, keepdims=True))
        o = dot(e.astype(BF), v)[:, :HD] / jnp.sum(e, axis=-1, keepdims=True)
        out[TILE:, h * HD : (h + 1) * HD] = o


def thumbs(tokens, weights, biases, gains, shifts, heads):
    size, model = tokens.shape
    return local_call(
        functools.partial(thumb_kernel, heads),
        "thumbs",
        (
            shaped(size, heads * HD, dtype=F32),
            shaped(size, model),
            shaped(size, 3 * heads * LANES),
        ),
        [VMEM] * 5,
        (VMEM,) * 3,
        (tokens, weights, biases, gains, shifts),
        cost=cost(5),
    )


def merged(parts, heads):
    cols = heads * HD
    row, col = (iota((LANES, cols), d) for d in (0, 1))
    spread = zero_one(row // 3 == col // HD)
    marks = [dot(p[:, cols:], spread) for p in parts]
    top = functools.reduce(jnp.maximum, marks)
    expos = [jnp.exp(m - top) for m in marks]
    total = sum(expos)
    mixed = sum(e * p[:, :cols].astype(F32) for p, e in zip(parts, expos)) / total
    row, col = (iota((cols, LANES), d) for d in (0, 1))
    packed = [
        dot(piece, zero_one((row % HD == 0) & (col == 3 * (row // HD) + i)))
        for i, piece in enumerate(pieces(top + jnp.log(total)))
    ]
    return mixed, sum(packed)


def pair_kernel(heads, *refs):
    count = (len(refs) - 1) // 2
    for j, (mine, out) in enumerate(zip(refs[:count], refs[count + 1 :])):
        mixed, marks = merged([mine[...], refs[count][j]], heads)
        out[...] = jnp.concatenate([mixed.astype(BF), marks.astype(BF)], axis=1)


def pair_merge(parts, other, heads):
    return local_call(
        functools.partial(pair_kernel, heads),
        "pair_merge",
        tuple(shaped(*p.shape) for p in parts),
        [VMEM] * (len(parts) + 1),
        (VMEM,) * len(parts),
        (*parts, other),
        cost=cost(3),
        room=ROOM,
    )


def merge_kernel(heads, counts, thumb, *refs):
    parts, (low, full, lse) = refs[:-3], refs[-3:]
    cols = heads * HD
    rows = lse.shape[0]
    mixed, marks = merged([p[...] for p in parts], heads)
    lse[...] = (-marks).astype(BF)
    image = iota((rows, cols), 0) < counts[0] * TILE
    full[:rows, :] = jnp.where(image, mixed, thumb[:rows, :])
    full[rows:, :] = thumb[rows:, :]
    low[...] = full[...].astype(BF)


def merge(count, parts, thumb, heads):
    size, cols = thumb.shape
    return local_call(
        functools.partial(merge_kernel, heads),
        "merge",
        (shaped(size, cols), shaped(size, cols, dtype=F32), shaped(parts[0].shape[0], LANES)),
        [SMEM] + [VMEM] * (1 + len(parts)),
        (VMEM,) * 3,
        (count, thumb, *parts),
        cost=cost(3),
    )


def fold_kernel(*refs):
    count = (len(refs) - 1) // 2
    for j, (mine, out) in enumerate(zip(refs[:count], refs[count + 1 :])):
        out[...] = (mine[...].astype(F32) + refs[count][j].astype(F32)).astype(BF)


def fold_far_kernel(*refs):
    for f, out in enumerate(refs[-2:]):
        out[...] = sum(r[f].astype(F32) for r in refs[:-2]).astype(BF)


def fold_far(parts):
    out = shaped(*parts[0].shape[1:])
    return local_call(
        fold_far_kernel,
        "fold_far",
        (out, out),
        [VMEM] * len(parts),
        (VMEM,) * 2,
        parts,
        cost=cost(3),
        room=ROOM,
    )


def fold(parts, other):
    return local_call(
        fold_kernel,
        "fold",
        tuple(shaped(*p.shape) for p in parts),
        [VMEM] * (len(parts) + 1),
        (VMEM,) * len(parts),
        (*parts, other),
        cost=cost(2),
        room=ROOM,
    )


ROOT = 0.7978845608028654
CUBE = 0.044715


def ff_kernel(
    heads, tokens, outer, low, low_far, full, lse, out_weight, out_far, up, up_bias, down, far_one,
    far_two, gains, shifts, mixed, grad_mid, grad_low, packed, hidden_out, act_out, pre_out, small,
):
    size, model = tokens.shape
    passes = outer.shape[0]
    cols = heads * HD
    chunk = far_one.shape[1]
    units = up.shape[1]
    rows = packed.shape[0]
    branch = dot(low[...], out_weight[...]) + dot(low_far[...], out_far[...])
    middle = tokens[...].astype(F32) + (branch + shifts[1:2, :])
    xhat, factor = standard(middle)
    hidden = (xhat * gains[1:2, :] + shifts[2:3, :]).astype(BF)
    hidden_out[...] = hidden

    def one_chunk(up_part, bias, down_part, keep):
        v = dot(hidden, up_part) + bias
        t = jnp.tanh(ROOT * (v + CUBE * (v * v * v)))
        act = (0.5 * v * (1.0 + t)).astype(BF)
        slope = 0.5 * (1.0 + t) + 0.5 * v * (1.0 - t * t) * (ROOT * (1.0 + 3.0 * CUBE * (v * v)))
        two = []
        for p in range(passes):
            pre = (dot_nt(outer[p], down_part) * slope).astype(BF)
            if keep is not None:
                pre_out[p, :, keep] = pre
            two.append(dot_nt(pre, up_part))
        if keep is not None:
            act_out[:, keep] = act
        return dot(act, down_part), two

    def far_chunk(ref):
        told = ref[2 * chunk : 2 * chunk + 16, :].astype(F32)
        bias = told[0:1] + told[1:2] + told[2:3]
        return one_chunk(ref[:chunk, :], bias, ref[chunk : 2 * chunk, :], None)

    done = []
    for i in range(units // chunk):
        at = slice(i * chunk, (i + 1) * chunk)
        done.append(one_chunk(up[:, at], up_bias[:, at], down[at, :], at))
    done += [far_chunk(far_one), far_chunk(far_two)]

    def tree(parts):
        half = len(parts) // 2
        return sum(parts[:half]) + sum(parts[half:])

    output = tree([d[0] for d in done])
    mixed[...] = (middle + (output + shifts[3:4, :])).astype(BF)
    small[...] = jnp.zeros(small.shape, F32)
    lane = iota((rows, LANES), 1)
    stats = jnp.zeros((rows, LANES), F32)
    for p in range(passes):
        two = tree([d[1][p] for d in done])
        c = outer[p].astype(F32)
        mid = c + norm_back(two, gains[1:2, :], xhat, factor)
        mid_low = mid.astype(BF)
        grad_mid[p] = mid
        grad_low[p] = mid_low
        att = dot_nt(mid_low, out_weight[...]).astype(BF)
        packed[:, p * cols : (p + 1) * cols] = att[:rows, :]
        pre_out_p = pre_out[p].astype(F32)
        bias = jnp.sum(pre_out_p, axis=0, keepdims=True)
        small[p, 0:1, :] = jnp.sum(two * xhat, axis=0, keepdims=True)
        small[p, 1:2, :] = jnp.sum(two, axis=0, keepdims=True)
        small[p, 2:3, :] = jnp.sum(mid_low.astype(F32), axis=0, keepdims=True)
        small[p, 3:4, :] = jnp.sum(c, axis=0, keepdims=True)
        for i in range(units // model):
            small[p, 4 + i : 5 + i, :] = bias[:, i * model : (i + 1) * model]
        product = att[:rows, :].astype(F32) * full[:rows, :]
        for h in range(heads):
            delta = jnp.sum(product[:, h * HD : (h + 1) * HD], axis=-1, keepdims=True)
            for i, piece in enumerate(pieces(-delta)):
                stats = jnp.where(lane == 3 * heads * (p + 1) + 3 * h + i, piece.astype(F32), stats)
    packed[:, passes * cols :] = (stats + lse[...].astype(F32)).astype(BF)


def feed_forward(
    tokens, outer, low, low_far, full, lse, out_weight, out_far, up, up_bias, down, far_one, far_two,
    gains, shifts, rows, heads,
):
    size, model = tokens.shape
    passes = outer.shape[0]
    units = up.shape[1]
    return local_call(
        functools.partial(ff_kernel, heads),
        "feed_forward",
        (
            shaped(size, model),
            shaped(passes, size, model, dtype=F32),
            shaped(passes, size, model),
            shaped(rows, passes * heads * HD + LANES),
            shaped(size, model),
            shaped(size, units),
            shaped(passes, size, units),
            shaped(passes, 8, model, dtype=F32),
        ),
        [VMEM] * 15,
        (VMEM,) * 8,
        (
            tokens, outer, low, low_far, full, lse, out_weight, out_far, up, up_bias, down, far_one,
            far_two, gains, shifts,
        ),
        cost=cost(12),
        room=32,
    )


def thumb_back_kernel(heads, counts, x, mid_low, out_weight, out):
    width = heads * LANES
    size = x.shape[0]
    passes = mid_low.shape[0]
    visible = same_tile(size - TILE)
    outside = iota((size - TILE, HD), 0) + TILE >= counts[0] * TILE
    grads = [dot_nt(mid_low[p], out_weight[...]).astype(BF) for p in range(passes)]
    out[:, :, :TILE, :] = jnp.zeros((*out.shape[:2], TILE, out.shape[3]), BF)
    for h in range(heads):
        q = x[TILE:, h * LANES : (h + 1) * LANES]
        k = x[TILE:, width + h * LANES : width + (h + 1) * LANES]
        v = x[TILE:, 2 * width + h * LANES : 2 * width + h * LANES + HD]
        s = jnp.where(visible, dot_nt(q, k), FAR)
        e = jnp.exp(s - jnp.max(s, axis=-1, keepdims=True))
        w = e / jnp.sum(e, axis=-1, keepdims=True)
        w_low = w.astype(BF)
        for p in range(passes):
            g = grads[p][TILE:, h * HD : (h + 1) * HD]
            gw = dot_nt(g, v)
            ds = (w * (gw - jnp.sum(w * gw, axis=-1, keepdims=True))).astype(BF)
            dq = dot(ds, k[:, :HD]) * SCALE
            dk = dot_tn(ds, q)[:, :HD]
            dv = dot_tn(w_low, g)
            for c, piece in enumerate((dq, dk, dv)):
                at = c * LANES + (h % 2) * HD
                out[h // 2, p, TILE:, at : at + HD] = jnp.where(outside, piece, 0.0).astype(BF)


def thumbs_back(count, x, mid_low, out_weight, heads):
    passes, size, _ = mid_low.shape
    return local_call(
        functools.partial(thumb_back_kernel, heads),
        "thumbs_back",
        shaped(heads // 2, passes, size, 3 * LANES),
        [SMEM] + [VMEM] * 3,
        VMEM,
        (count, x, mid_low, out_weight),
        cost=cost(6),
    )


def early_at(units, model, low):
    ends = [model, 2 * model, 2 * model + units, 2 * model + units + low]
    return [slice(b - w, b) for b, w in zip(ends, (model, model, units, low))]


def early_cuts(parts, units, model, low):
    high, wide, turns = units // parts // 2, model // parts, model // low
    narrow = low * turns // parts
    for i in range(parts):
        yield (
            (slice(2 * i * high, (2 * i + 1) * high), slice(0, model)),
            (slice((2 * i + 1) * high, (2 * i + 2) * high), slice(0, model)),
            (slice(i * wide, (i + 1) * wide), slice(0, units)),
            (
                slice(i // turns * narrow, (i // turns + 1) * narrow),
                slice(i % turns * low, (i % turns + 1) * low),
            ),
        )


def weight_kernel(place, act, outer, hidden, pre, low, mid_low, keep, give):
    units, model, cols = act.shape[1], hidden.shape[1], low.shape[1]
    core = place[0]
    for turn, out in ((core, keep), (1 - core, give)):
        down = dot_tn(act[...], outer[turn]).astype(BF)
        up = dot_tn(hidden[...], pre[turn]).astype(BF)
        proj = dot_tn(low[...], mid_low[turn]).astype(BF)
        for i, cut in enumerate(early_cuts(keep.shape[0], units, model, cols)):
            for value, (rows, lanes), at in zip(
                (down, down, up, proj), cut, early_at(units, model, cols)
            ):
                out[i, :, at] = value[rows, lanes]


def weight_grads(core, act, outer, hidden, pre, low, mid_low, parts):
    units, model = act.shape[1], outer.shape[2]
    out = shaped(parts, model // parts, 2 * model + units + low.shape[1])
    return local_call(
        weight_kernel,
        "weight_grads",
        (out, out),
        [SMEM] + [VMEM] * 6,
        (VMEM,) * 2,
        (core, act, outer, hidden, pre, low, mid_low),
        cost=cost(8),
        room=24,
    )


def reverse_kernel(rows, groups, heads, passes, counts, place, *refs):
    grads, kept = refs[:groups], refs[groups : groups + 5]
    own, thumb, weights, columns, small = refs[groups + 5 : groups + 10]
    at = groups + 10
    out_q, give_q, at = refs[at : at + groups // 2], refs[at + groups // 2], at + groups // 2 + 1
    out_kv, at = refs[at : at + groups // 2], at + groups // 2
    keep, give = refs[at : at + 2]
    (
        stage, xq, xk, qx, kx, vx, packed, gx, kt, dq_t, dv, dk, low_q, low_kv, total, sums,
        starts, sems,
    ) = refs[at + 2 :]
    couples = heads // 2
    sources = [*grads, *kept[2:], *kept[:2]]
    targets = [*[stage.at[g] for g in range(groups)], qx, kx, vx, xq, xk]
    copies = [
        pltpu.make_async_copy(f, t, sems.at[i]) for i, (f, t) in enumerate(zip(sources, targets))
    ]
    for copy in copies:
        copy.start()
    cols = heads * HD
    wide = passes * LANES
    q_counts = [counts[g] for g in range(groups)]
    k_counts = [counts[groups + g] for g in range(groups)]
    start = jnp.int32(0)
    for g in range(groups):
        copies[g].wait()
        packed[rows_at(start, rows), :] = stage[g]
        start = start + q_counts[g] * TILE
    q_total, k_total = start, sum(k_counts) * TILE
    tail_lane = iota((BLOCK, packed.shape[1]), 1) - passes * cols
    empty = (tail_lane >= 0) & (tail_lane < 3 * heads) & (tail_lane % 3 == 0)
    packed[rows_at(q_total, BLOCK), :] = jnp.where(empty, FAR, 0.0).astype(BF)
    q_blocks = (q_total + BLOCK - 1) // BLOCK
    k_blocks = (k_total + BLOCK - 1) // BLOCK
    spans = range(groups * TILE // BLOCK, groups * rows // BLOCK + 1)

    row, col = (iota((LANES, heads * LANES), d) for d in (0, 1))
    head, lane = col // LANES, col % LANES
    to_marks = zero_one((lane > HD) & (lane < HD + 4) & (row == 3 * head + lane - HD - 1))
    row, col = (iota((LANES, heads * wide), d) for d in (0, 1))
    head, turn, lane = col // wide, col % wide // LANES, col % LANES
    to_deltas = zero_one(
        (lane >= HD) & (lane < HD + 3) & (row == 3 * heads * (turn + 1) + 3 * head + lane - HD)
    )
    for copy in copies[groups : groups + 3]:
        copy.wait()

    @pl.loop(0, q_blocks)
    def _(b):
        here = rows_at(b * BLOCK, BLOCK, BLOCK)
        stats = packed[here, passes * cols :]
        marks = dot(stats, to_marks)
        deltas = dot(stats, to_deltas).astype(BF)
        for h in range(heads):
            more = marks[:, h * LANES : (h + 1) * LANES]
            qx[h, here, :] = (qx[h, here, :].astype(F32) + more).astype(BF)
            for p in range(passes):
                at = p * cols + h * HD
                mine = (h * passes + p) * LANES
                gx[h, here, p * LANES : (p + 1) * LANES] = jnp.concatenate(
                    [packed[here, at : at + HD], deltas[:, mine + HD : mine + LANES]], axis=1
                )

    @pl.loop(0, k_blocks)
    def _(b):
        here = rows_at(b * BLOCK, BLOCK, BLOCK)
        for h in range(heads):
            kt[h, b] = jnp.transpose(kx[h, here, :].astype(F32))[:HD, :].astype(BF)

    def reverse_all(blocks):
        span = blocks * BLOCK

        @pl.loop(0, couples)
        def _(pair):
            dv[:, :span, :] = jnp.zeros((2, span, wide), F32)
            dk[:, :, :span, :] = jnp.zeros((passes, 2, span, LANES), F32)

            @pl.loop(0, q_blocks)
            def _(b):
                here = rows_at(b * BLOCK, BLOCK, BLOCK)
                for i in range(2):
                    h = 2 * pair + i
                    q, g = qx[h, here, :], gx[h, here, :]
                    k_t = jnp.concatenate([kt[h, j] for j in range(blocks)], axis=1)
                    w = jnp.exp(dot_nt(kx[h, :span, :], q))
                    dv[i, :span, :] += dot(w.astype(BF), g)
                    for p in range(passes):
                        ds = dot_nt(vx[h, :span, :], g[:, p * LANES : (p + 1) * LANES])
                        ds = (w * ds).astype(BF)
                        dk[p, i, :span, :] += dot(ds, q)
                        dq_t[p, i * HD : (i + 1) * HD, :] = dot(k_t, ds)
                for p in range(passes):
                    piece = jnp.transpose(dq_t[p]) * SCALE
                    low_q[pair, here, p * LANES : (p + 1) * LANES] = piece.astype(BF)

            for p in range(passes):
                for c, both in enumerate(
                    (
                        [dk[p, i, :span, :HD] for i in range(2)],
                        [dv[i, :span, p * LANES : p * LANES + HD] for i in range(2)],
                    )
                ):
                    lane = (2 * p + c) * LANES
                    low_kv[pair, :span, lane : lane + LANES] = jnp.concatenate(both, axis=1).astype(BF)

    for blocks in spans:
        pl.when(k_blocks == blocks)(functools.partial(reverse_all, blocks))

    start = jnp.int32(0)
    for g in range(groups):
        starts[g] = start
        start = start + k_counts[g] * TILE
    for g in range(groups):
        here = rows_at(starts[place[1 + g]], rows)
        out_kv[g // 2][g % 2] = jnp.concatenate([low_kv[i, here, :] for i in range(couples)], axis=1)
    start = jnp.int32(0)
    for g in range(groups):
        here = rows_at(start, rows)
        value = jnp.concatenate([low_q[i, here, :] for i in range(couples)], axis=1)
        if g < groups // 2:
            out_q[g][...] = value
        else:
            give_q[g - groups // 2] = value
        start = start + q_counts[g] * TILE

    copies[groups + 3].wait()
    copies[groups + 4].wait()

    def key_sums(blocks):
        span = blocks * BLOCK
        for i in range(couples):
            flat = low_kv[i, :span, :]
            total[i, :, wide:] = dot_tn(xk[:span, :], flat)
            sums[i, :, wide:] = dot(jnp.ones((8, span), BF), flat)

    for blocks in spans:
        pl.when(k_blocks == blocks)(functools.partial(key_sums, blocks))

    total[:, :, :wide] = jnp.zeros((couples, total.shape[1], wide), F32)
    sums[:, :, :wide] = jnp.zeros((couples, 8, wide), F32)

    @pl.loop(0, q_blocks)
    def _(b):
        here = rows_at(b * BLOCK, BLOCK, BLOCK)
        for i in range(couples):
            total[i, :, :wide] += dot_tn(xq[here, :], low_q[i, here, :])
            sums[i, :, :wide] += dot(jnp.ones((8, BLOCK), BF), low_q[i, here, :])

    model = total.shape[1]
    gain, shift = columns[:, 0:1], columns[:, 1:2]
    ones = jnp.ones((8, own.shape[0]), BF)
    core = place[0]
    for p in range(passes):
        whole = []
        for i in range(couples):
            mine = thumb[i, p]
            part = dot_tn(own[...], mine)
            part_sum = dot(ones, mine)[0:1, :]
            q_at = slice(p * LANES, (p + 1) * LANES)
            kv_at = slice((passes + 2 * p) * LANES, (passes + 2 * p + 2) * LANES)
            part += jnp.concatenate([total[i, :, q_at], total[i, :, kv_at]], axis=1)
            part_sum += jnp.concatenate([sums[i, 0:1, q_at], sums[i, 0:1, kv_at]], axis=1)
            w = weights[i].astype(F32)
            gain_one = jnp.sum(w * part, axis=1, keepdims=True)
            shift_one = jnp.sum(w * part_sum, axis=1, keepdims=True)
            lane = iota((model, LANES), 1)
            tall = jnp.where(lane == 0, gain_one, jnp.where(lane == 1, shift_one, 0.0))
            flat = jnp.concatenate(
                [jnp.zeros((2, LANES), F32)]
                + [part_sum[:, c * LANES : (c + 1) * LANES] for c in range(3)]
                + [jnp.zeros((LANES - 5, LANES), F32)],
                axis=0,
            )
            tall = jnp.concatenate([tall[:LANES] + jnp.transpose(flat), tall[LANES:]], axis=0)
            if i == 0:
                turned = jnp.concatenate(
                    [
                        jnp.zeros((8, model), F32),
                        small[p],
                        jnp.zeros((LANES - 16, model), F32),
                    ],
                    axis=0,
                )
                tall = tall + jnp.transpose(turned)
            whole += [part * gain + shift * part_sum, tall]
        whole = jnp.concatenate(whole, axis=1).astype(BF)

        @pl.when(core == p)
        def _():
            keep[...] = whole

        @pl.when(core != p)
        def _():
            give[...] = whole


def reverse(counts, place, grads, kept, own, thumb, weights, columns, small, rows, heads):
    groups = len(grads)
    couples, passes = thumb.shape[:2]
    model = own.shape[1]
    room = rows * groups + BLOCK
    cols = heads * HD
    wide = passes * LANES
    half = groups // 2
    mine = shaped(model, couples * 4 * LANES)
    q, kv = shaped(rows, couples * wide), shaped(2, rows, couples * 2 * wide)
    out = (*[q] * half, shaped(half, rows, couples * wide), *[kv] * half, mine, mine)
    return local_call(
        functools.partial(reverse_kernel, rows, groups, heads, passes),
        "reverse",
        out,
        [SMEM, SMEM] + [ANY] * (groups + 5) + [VMEM] * 5,
        (VMEM,) * len(out),
        (counts, place, *grads, *kept, own, thumb, weights, columns, small),
        [
            pltpu.VMEM((groups, rows, passes * cols + LANES), BF),
            pltpu.VMEM((room, model), BF),
            pltpu.VMEM((room, model), BF),
            pltpu.VMEM((heads, room, LANES), BF),
            pltpu.VMEM((heads, room, LANES), BF),
            pltpu.VMEM((heads, room, LANES), BF),
            pltpu.VMEM((room, passes * cols + LANES), BF),
            pltpu.VMEM((heads, room, wide), BF),
            pltpu.VMEM((heads, room // BLOCK, HD, BLOCK), BF),
            pltpu.VMEM((passes, LANES, BLOCK), F32),
            pltpu.VMEM((2, room, wide), F32),
            pltpu.VMEM((passes, 2, room, LANES), F32),
            pltpu.VMEM((couples, room, wide), BF),
            pltpu.VMEM((couples, room, 2 * wide), BF),
            pltpu.VMEM((couples, model, 3 * wide), F32),
            pltpu.VMEM((couples, 8, 3 * wide), F32),
            pltpu.SMEM((groups,), jnp.int32),
            pltpu.SemaphoreType.DMA((groups + 5,)),
        ],
        cost(45),
        ROOM,
    )


def chosen(counts, far, thumb, rows):
    image = iota(far.shape, 0) < counts[0] * TILE
    return jnp.concatenate(
        [jnp.where(image, far.astype(BF), thumb[:rows]), thumb[rows:]], axis=0
    )


def grad_one_kernel(near, counts, *refs):
    from_q, from_kv, (thumb, weights, out) = refs[:near], refs[near:-3], refs[-3:]
    rows = from_q[0].shape[0]
    passes = thumb.shape[1]
    sum_q = sum(r[...].astype(F32) for r in from_q)
    sum_kv = sum(r[...].astype(F32) for r in from_kv)
    for p in range(passes):
        part = 0.0
        for pair in range(2):
            far = sum_q[:, (passes * pair + p) * LANES : (passes * pair + p + 1) * LANES]
            flat = chosen(counts, far, thumb[pair, p, :, :LANES], rows)
            part = part + dot_nt(flat, weights[pair, :, :LANES])
            at = 2 * (passes * pair + p) * LANES
            flat = chosen(counts, sum_kv[:, at : at + 2 * LANES], thumb[pair, p, :, LANES:], rows)
            part = part + dot_nt(flat, weights[pair, :, LANES:])
        out[p] = part.astype(BF)


def grad_one(count, from_q, from_kv, thumb, weights):
    near = len(from_q)
    return local_call(
        functools.partial(grad_one_kernel, near),
        "grad_one",
        shaped(*thumb.shape[1:3], weights.shape[1]),
        [SMEM] + [VMEM] * (near + len(from_kv) + 2),
        VMEM,
        (count, *from_q, *from_kv, thumb, weights),
        cost=cost(5),
        room=ROOM,
    )


def close_kernel(tokens, mid, mine, other, gains, out):
    xhat, factor = standard(tokens[...].astype(F32))
    for p in range(mid.shape[0]):
        grad = mine[p].astype(F32) + other[p].astype(F32)
        out[p] = mid[p] + norm_back(grad, gains[0:1, :], xhat, factor)


def close(tokens, mid, mine, other, gains):
    return local_call(
        close_kernel,
        "close",
        shaped(*mid.shape, dtype=F32),
        [VMEM] * 5,
        VMEM,
        (tokens, mid, mine, other, gains),
        cost=cost(4),
        room=ROOM,
    )


def early_kernel(place, own, far, down, up, proj):
    core, turn = place[0], place[1]
    (units, model), low = down.shape[1:], proj.shape[1]
    lines, steps, rows = own.shape[:3]
    lane_down, lane_next, lane_up, lane_proj = early_at(units, model, low)
    for out, ref in ((core, own), (1 - core, far)):
        for y in range(lines):
            for j in range(steps):
                i = (turn + steps - j) % steps * lines + y
                at = pl.multiple_of(2 * rows * i, 2 * rows)
                down[out, pl.ds(at, rows), :] = ref[y, j, :, lane_down].astype(F32)
                down[out, pl.ds(at + rows, rows), :] = ref[y, j, :, lane_next].astype(F32)
                up[out, rows_at(rows * i, rows, rows), :] = ref[y, j, :, lane_up].astype(F32)
                turns = model // low
                here = rows_at(i // turns * rows, rows, rows)
                value = ref[y, j, :, lane_proj].astype(F32)
                for t in range(turns):

                    @pl.when(i % turns == t)
                    def _(value=value, here=here, t=t):
                        proj[out, here, t * low : (t + 1) * low] = value


def early_out(place, own, far, units, low):
    model = own.shape[0] * own.shape[1] * own.shape[2]
    return local_call(
        early_kernel,
        "early_out",
        (
            shaped(2, units, model, dtype=F32),
            shaped(2, model, units, dtype=F32),
            shaped(2, low, model, dtype=F32),
        ),
        [SMEM] + [VMEM] * 2,
        (VMEM,) * 3,
        (place, own, far),
        cost=cost(8),
        room=ROOM,
    )


def late_kernel(place, own, far, grad_in, in_bias, up_bias, gains, shifts):
    core = place[0]
    for turn, ref in ((core, own), (1 - core, far)):
        turned = []
        for pair in range(2):
            at = 4 * LANES * pair
            for c in range(3):
                grad_in[turn, c, :, pair * LANES : (pair + 1) * LANES] = ref[
                    :, at + c * LANES : at + (c + 1) * LANES
                ].astype(F32)
            turned.append(jnp.transpose(ref[:, at + 3 * LANES : at + 4 * LANES].astype(F32)))
        a, b = turned
        in_bias[turn] = jnp.concatenate(
            [
                jnp.concatenate([a[2:3, :LANES], b[2:3, :LANES]], axis=1),
                jnp.concatenate([a[4:5, :LANES], b[4:5, :LANES]], axis=1),
            ],
            axis=0,
        )
        up_bias[turn] = jnp.concatenate([a[12:13], a[13:14]], axis=1)
        gains[turn] = jnp.concatenate([a[0:1] + b[0:1], a[8:9]], axis=0)
        shifts[turn] = jnp.concatenate([a[1:2] + b[1:2], a[10:11], a[9:10], a[11:12]], axis=0)


def late_out(core, own, far, units):
    model = own.shape[0]
    return local_call(
        late_kernel,
        "late_out",
        (
            shaped(2, 3, model, 2 * LANES, dtype=F32),
            shaped(2, 2, 2 * LANES, dtype=F32),
            shaped(2, 1, units, dtype=F32),
            shaped(2, 2, model, dtype=F32),
            shaped(2, 4, model, dtype=F32),
        ),
        [SMEM] + [VMEM] * 2,
        (VMEM,) * 5,
        (core, own, far),
        cost=cost(4),
        room=ROOM,
    )


def gather_near(array):
    mine = [array] + [shift_by(array, "y", d) for d in range(1, lax.axis_size("y"))]
    return mine + [shift_by(a, "c", 1) for a in mine]


def return_near(parts):
    return [parts[0]] + [shift_by(p, "y", -j) for j, p in enumerate(parts) if j > 0]


def offsets(size):
    return [(step, flip) for step in range(size) for flip in range(2)]


def return_far(parts):
    parts = [parts[0]] + [shift_by(p, "z", step) for step, p in enumerate(parts) if step > 0]
    mine, other = fold_far(parts)
    return parts, [mine, shift_by(other, "xl", 1)]


PLANE = ("z", "y")


def core_sum(keep, give):
    return (keep.astype(F32) + shift_by(give, "c", 1).astype(F32)).astype(BF)


def plane_sum(mine):
    parts = lax.all_to_all(mine, PLANE, 0, 0, tiled=True)
    return jnp.sum(parts.astype(F32), axis=0)


def across(low):
    done = low.astype(F32) + shift_by(low, "xl", 1).astype(F32)
    size = 4 * LANES
    ones = jnp.concatenate([low[:, i + 3 * LANES : i + size] for i in range(0, low.shape[1], size)], axis=1)
    n = lax.axis_size(("xl", "h"))
    more = shift_by(ones, "h", 1).astype(F32) + lax.ppermute(
        ones, ("xl", "h"), [(i, n - 1 - i) for i in range(n)]
    ).astype(F32)
    more = jnp.where(jnp.arange(more.shape[1]) % LANES < 2, more, 0.0)
    nothing = jnp.zeros((low.shape[0], 3 * LANES), F32)
    laid = [[nothing, more[:, i : i + LANES]] for i in range(0, more.shape[1], LANES)]
    return (done + jnp.concatenate(sum(laid, []), axis=1)).astype(BF)


def tied(arrays, others):
    return lax.optimization_barrier((arrays, others))


def local(
    tokens,
    cotangents,
    segment_ids,
    in_weights,
    in_biases,
    out_weight,
    up_weight,
    up_biases,
    down_weight,
    gains,
    shifts,
):
    size, model = tokens.shape
    cols = in_weights.shape[2]
    heads = cols // HD
    rows = size - TILE
    units = up_weight.shape[1]
    c = lax.axis_index("c")

    told, copies, count = front(tokens, segment_ids, lax.axis_size(("z", "xl")))
    far = lax.all_to_all(copies, ("z", "xl"), 0, 0, tiled=True)
    near = gather_near(told)
    core = c.astype(jnp.int32).reshape(1)
    z, xl, z_size = lax.axis_index("z"), lax.axis_index("xl"), lax.axis_size("z")
    routes = [((z + step) % z_size) * 2 + (xl ^ flip) for step, flip in offsets(z_size)]
    place = jnp.concatenate([core, jnp.stack(routes).astype(jnp.int32)])
    turns = jnp.concatenate([core, z.astype(jnp.int32).reshape(1)])
    plane = lax.axis_size(PLANE)

    weights, biases, pairs, columns, bundle = prepare(
        core, in_weights, in_biases, gains, shifts, up_weight, down_weight, up_biases[None], heads
    )
    n_x = lax.axis_size(("xl", "h"))
    crossed = [(i, n_x - 1 - i) for i in range(n_x)]
    out_far = lax.ppermute(out_weight, ("xl", "h"), crossed)
    far_one = lax.ppermute(bundle, ("xl", "h"), crossed)
    far_two = shift_by(far_one, "c", 1)

    weights, (place, turns) = tied(weights, (place, turns))
    *parts, give, xq, xk, qx, kx, vx, counts = attend(
        near, far, weights, biases, gains, shifts, rows, heads
    )
    thumb_out, xhat, x = thumbs(tokens, weights, biases, gains, shifts, heads)
    parts = pair_merge(parts, shift_by(give, "c", 1), heads)
    low, full, lse = merge(count, return_near(parts), thumb_out, heads)
    low_far = shift_by(low, "h", 1)
    mixed, grad_mid, mid_low, packed, hidden, act, pre, small = feed_forward(
        tokens, cotangents, low, low_far, full, lse, out_weight, out_far, up_weight, up_biases[None],
        down_weight, far_one, far_two, gains, shifts, rows, heads,
    )
    grads = gather_near(packed)
    keep, give = weight_grads(core, act, cotangents, hidden, pre, low, mid_low, plane)
    mid_low, (keep, give) = tied(mid_low, (keep, give))
    thumb = thumbs_back(count, x, mid_low, out_weight, heads)
    early = core_sum(keep, give)

    grads, (early, thumb) = tied(grads, (early, thumb))
    early = lax.all_to_all(early, PLANE, 0, 0, tiled=True)
    out = reverse(
        counts, place, grads, (xq, xk, qx, kx, vx), xhat, thumb, pairs, columns, small, rows, heads
    )
    half = len(near) // 2
    out_q, give_q, out_kv, (keep, give) = out[:half], out[half], out[half + 1 : -2], out[-2:]
    mine, early = tied(core_sum(keep, give), early)
    part = plane_sum(mine.reshape(plane, -1, mine.shape[1])).astype(BF)
    from_q = return_near(fold(out_q, shift_by(give_q, "c", 1)))
    arrived, from_kv = return_far(out_kv)
    part, arrived = tied(part, arrived)
    mine = grad_one(count, from_q, from_kv, thumb, pairs)
    grad_tokens = close(tokens, grad_mid, mine, shift_by(mine, "h", 1), gains)

    early = jnp.sum(early.astype(F32), axis=0).astype(BF)
    early = (early.astype(F32) + shift_by(early, "xl", 1).astype(F32)).astype(BF)
    early = jnp.stack([early] + [shift_by(early, "z", d) for d in range(1, z_size)])
    early = lax.all_gather(early, "y", axis=0)
    part = jnp.broadcast_to(across(part)[None], (plane, *part.shape))
    own = lax.all_to_all(part, PLANE, 0, 0, tiled=True).reshape(model, -1)
    grad_down, grad_up, grad_out = early_out(turns, early, shift_by(early, "c", 1), units, cols)
    grad_in, in_bias, up_bias, grad_gains, grad_shifts = late_out(
        core, own, shift_by(own, "c", 1), units
    )
    return (
        mixed,
        grad_tokens,
        grad_in,
        in_bias,
        grad_out,
        grad_up,
        up_bias.reshape(2, units),
        grad_down,
        grad_gains,
        grad_shifts,
    )


def solution(mesh):
    fine = Mesh(mesh.devices.reshape(4, 2, 4, 2, 2), ("z", "xl", "y", "c", "h"))
    blk = ("z", "xl", "y", "c")
    return jax.shard_map(
        local,
        mesh=fine,
        in_specs=(
            P(blk, None),
            P(None, blk, None),
            P(blk),
            P(None, None, "h"),
            P(None, "h"),
            P("h", None),
            P(None, "h"),
            P("h"),
            P("h", None),
            P(),
            P(),
        ),
        out_specs=(
            P(blk, None),
            P(None, blk, None),
            P(None, None, None, "h"),
            P(None, None, "h"),
            P(None, "h", None),
            P(None, None, "h"),
            P(None, "h"),
            P(None, "h", None),
            P(),
            P(),
        ),
        check_vma=False,
    )
```

```python
import functools

import jax
import jax.numpy as jnp
from jax import lax
from jax.experimental import pallas as pl
from jax.experimental.pallas import tpu as pltpu
from jax.sharding import Mesh
from jax.sharding import PartitionSpec as P

HD = 64
LANES = 128
TILE = 64
BLOCK = 256
EPS = 1e-06
SCALE = 0.125
FAR = -1e30
BF = jnp.bfloat16
F32 = jnp.float32
MIB = 1024 * 1024
ROOM = 56

NT = (((1,), (1,)), ((), ()))
TN = (((0,), (0,)), ((), ()))


def shift_by(array, axis, step):
    size = lax.axis_size(axis)
    return lax.ppermute(array, axis, [(i, (i + step) % size) for i in range(size)])


def dot(a, b):
    return jnp.dot(a, b, preferred_element_type=F32)


def dot_nt(a, b):
    return lax.dot_general(a, b, NT, preferred_element_type=F32)


def dot_tn(a, b):
    return lax.dot_general(a, b, TN, preferred_element_type=F32)


def standard(field):
    center = field - jnp.mean(field, axis=-1, keepdims=True)
    factor = lax.rsqrt(jnp.mean(center * center, axis=-1, keepdims=True) + EPS)
    return center * factor, factor


def norm_back(grad, gain, xhat, factor):
    h = grad * gain
    mean = jnp.mean(h, axis=-1, keepdims=True)
    return factor * (h - mean - xhat * jnp.mean(h * xhat, axis=-1, keepdims=True))


def pieces(value):
    high = value.astype(BF)
    rest = value - high.astype(F32)
    middle = rest.astype(BF)
    low = (rest - middle.astype(F32)).astype(BF)
    return high, middle, low


def zero_one(mask):
    return jnp.where(mask, 1.0, 0.0).astype(BF)


def iota(shape, dim):
    return lax.broadcasted_iota(jnp.int32, shape, dim)


VMEM = pl.BlockSpec(memory_space=pltpu.VMEM)
ANY = pl.BlockSpec(memory_space=pl.ANY)
SMEM = pl.BlockSpec(memory_space=pltpu.SMEM)


def local_call(body, name, out, ins, outs, args, scratch=(), cost=None, room=16):
    return pl.pallas_call(
        body,
        out_shape=out,
        in_specs=ins,
        out_specs=outs,
        scratch_shapes=scratch,
        cost_estimate=cost,
        compiler_params=pltpu.CompilerParams(vmem_limit_bytes=room * MIB),
        name=name,
    )(*args)


def shaped(*shape, dtype=BF):
    return jax.ShapeDtypeStruct(shape, dtype)


def cost(micros):
    return pl.CostEstimate(flops=int(micros * 1e9), bytes_accessed=0, transcendentals=0)


def front_kernel(tokens, ids, told, copies, number):
    rows = told.shape[0] - 16
    marks = jnp.where(ids[...] == 0, 1.0, 0.0)
    tiles = jnp.sum(marks).astype(jnp.int32) // TILE
    number[0] = tiles
    told[:rows, :] = tokens[:rows, :]
    told[rows:, :] = jnp.full((16, told.shape[1]), tiles.astype(F32), F32).astype(BF)
    for g in range(copies.shape[0]):
        copies[g] = told[...]


def front(tokens, ids, copies):
    size, model = tokens.shape
    told = size - TILE + 16
    return local_call(
        front_kernel,
        "front",
        (shaped(told, model), shaped(copies, told, model), shaped(1, dtype=jnp.int32)),
        [VMEM, VMEM],
        (VMEM, VMEM, SMEM),
        (tokens, ids.reshape(-1, LANES)),
        room=ROOM,
    )


def prepare_kernel(
    heads, place, in_weights, in_biases, gains, shifts, up, down, bias,
    weights, biases, pairs, columns, out,
):
    core = place[0]
    half = out.shape[1]
    at = pl.ds(pl.multiple_of(core * half, half), half)
    out[:half, :] = up[:, at]
    out[half : 2 * half, :] = down[at, :]
    mine = jnp.where(core == 0, bias[:, :half], bias[:, half:])
    row = iota((16, half), 0)
    rows = jnp.zeros((16, half), F32)
    for i, piece in enumerate(pieces(mine)):
        rows = jnp.where(row == i, piece.astype(F32), rows)
    out[2 * half :, :] = rows.astype(BF)

    model, cols = in_weights.shape[1:]
    width = heads * LANES
    row, col = (iota((cols, width), d) for d in (0, 1))
    spread = zero_one((row // HD == col // LANES) & (row % HD == col % LANES))
    lane = iota((1, width), 1) % LANES
    gap = jnp.zeros((1, HD), F32)

    def apart(line):
        return jnp.concatenate(
            sum([[line[:, h * HD : (h + 1) * HD], gap] for h in range(heads)], []), axis=1
        )

    extra = [
        apart(in_biases[0:1, :] * SCALE) + jnp.where(lane == HD, 1.0, 0.0),
        jnp.where((lane > HD) & (lane < HD + 4), 1.0, 0.0),
        apart(in_biases[1:2, :]) + jnp.where((lane >= HD) & (lane < HD + 3), 1.0, 0.0),
    ]
    for i in range(3):
        factor = SCALE if i == 0 else 1.0
        weights[:, i * width : (i + 1) * width] = (dot(in_weights[i], spread) * factor).astype(BF)
        biases[:, i * width : (i + 1) * width] = extra[i]
        for pair in range(heads // 2):
            pairs[pair, :, i * LANES : (i + 1) * LANES] = in_weights[
                i, :, pair * LANES : (pair + 1) * LANES
            ]
    tall = jnp.concatenate(
        [gains[0:1, :], shifts[0:1, :], jnp.zeros((LANES - 2, model), F32)], axis=0
    )
    columns[...] = jnp.transpose(tall)


def prepare(core, in_weights, in_biases, gains, shifts, up, down, bias, heads):
    model = up.shape[0]
    width = 3 * heads * LANES
    return local_call(
        functools.partial(prepare_kernel, heads),
        "prepare",
        (
            shaped(model, width),
            shaped(1, width, dtype=F32),
            shaped(heads // 2, model, 3 * LANES),
            shaped(model, LANES, dtype=F32),
            shaped(2 * model + 16, model),
        ),
        [SMEM] + [VMEM] * 7,
        (VMEM,) * 5,
        (core, in_weights, in_biases, gains, shifts, up, down, bias),
        cost=cost(4),
        room=ROOM,
    )


def count_of(ref, rows):
    return jnp.max(ref[rows : rows + 16, :LANES].astype(F32)).astype(jnp.int32)


def rows_at(start, rows, step=TILE):
    return pl.ds(pl.multiple_of(start, step), rows)


def attend_kernel(rows, groups, heads, *refs):
    near, far = refs[:groups], refs[groups]
    weights, biases, gains, shifts = refs[groups + 1 : groups + 5]
    at = groups + 5 + groups // 2
    out, give = refs[groups + 5 : at], refs[at]
    kept, counts, place = refs[at + 1 : at + 6], refs[at + 6], refs[at + 7]
    (xq, xk, qx, kx, vx), sems = refs[at + 8 : at + 13], refs[at + 13]
    model = xq.shape[1]
    q_counts = [count_of(r, rows) for r in near]
    k_counts = [count_of(far.at[g], rows) for g in range(groups)]
    for g in range(groups):
        counts[g] = q_counts[g]
        counts[groups + g] = k_counts[g]

    def compact(numbers, read, target):
        start = jnp.int32(0)
        for g, n in enumerate(numbers):
            target[rows_at(start, rows), :] = read(g)
            start = start + n * TILE
        target[rows_at(start, BLOCK), :] = jnp.zeros((BLOCK, model), BF)
        return start

    q_total = compact(q_counts, lambda g: near[g][:rows, :], xq)
    k_total = compact(k_counts, lambda g: far[g, :rows, :], xk)
    q_blocks = (q_total + BLOCK - 1) // BLOCK
    k_blocks = (k_total + BLOCK - 1) // BLOCK
    width = heads * LANES

    def hidden(ref, here):
        clean = standard(ref[here, :].astype(F32))[0].astype(BF)
        ref[here, :] = clean
        return (clean.astype(F32) * gains[0:1, :] + shifts[0:1, :]).astype(BF)

    @pl.loop(0, q_blocks)
    def _(b):
        here = rows_at(b * BLOCK, BLOCK, BLOCK)
        q = (dot(hidden(xq, here), weights[:, :width]) + biases[:, :width]).astype(BF)
        for h in range(heads):
            qx[h, here, :] = q[:, h * LANES : (h + 1) * LANES]

    @pl.loop(0, k_blocks)
    def _(b):
        here = rows_at(b * BLOCK, BLOCK, BLOCK)
        both = dot(hidden(xk, here), weights[:, width:]) + biases[:, width:]
        unseen = (iota((BLOCK, width), 0) + b * BLOCK >= k_total) & (
            iota((BLOCK, width), 1) % LANES == HD
        )
        k = jnp.where(unseen, FAR, both[:, :width]).astype(BF)
        v = both[:, width:].astype(BF)
        for h in range(heads):
            kx[h, here, :] = k[:, h * LANES : (h + 1) * LANES]
            vx[h, here, :] = v[:, h * LANES : (h + 1) * LANES]

    copies = [
        pltpu.make_async_copy(held, to, sems.at[i])
        for i, (held, to) in enumerate(zip((xq, xk, qx, kx, vx), kept))
    ]
    for copy in copies:
        copy.start()

    def attend_all(span):
        @pl.loop(0, q_blocks)
        def _(b):
            here = rows_at(b * BLOCK, BLOCK, BLOCK)
            lane = iota((BLOCK, LANES), 1)
            for h in range(heads):
                s = dot_nt(qx[h, here, :], kx[h, :span, :])
                top = jnp.max(s, axis=-1, keepdims=True)
                o = dot(jnp.exp(s - top).astype(BF), vx[h, :span, :])
                total = o[:, HD : HD + 1]
                o = o / total
                for i, piece in enumerate(pieces(top + jnp.log(total))):
                    o = jnp.where(lane == HD + i, piece.astype(F32), o)
                place[h, here, :] = o.astype(BF)

    for blocks in range(groups * TILE // BLOCK, groups * rows // BLOCK + 1):
        pl.when(k_blocks == blocks)(functools.partial(attend_all, blocks * BLOCK))

    gather = [
        (iota((LANES, LANES), 0) - HD + 3 * h == iota((LANES, LANES), 1))
        & (iota((LANES, LANES), 0) >= HD)
        & (iota((LANES, LANES), 0) < HD + 3)
        for h in range(heads)
    ]
    gather = [jnp.where(m, 1.0, 0.0).astype(BF) for m in gather]
    start = jnp.int32(0)
    for g in range(groups):
        mine = [place[h, rows_at(start, rows), :] for h in range(heads)]
        stats = sum(dot(m, s) for m, s in zip(mine, gather)).astype(BF)
        value = jnp.concatenate([m[:, :HD] for m in mine] + [stats], axis=1)
        if g < groups // 2:
            out[g][...] = value
        else:
            give[g - groups // 2] = value
        start = start + q_counts[g] * TILE
    for copy in copies:
        copy.wait()


def attend(near, far, weights, biases, gains, shifts, rows, heads):
    groups = len(near)
    model = near[0].shape[1]
    room = rows * groups + BLOCK
    parts = heads * HD + LANES
    kept = [(room, model)] * 2 + [(heads, room, LANES)] * 3
    return local_call(
        functools.partial(attend_kernel, rows, groups, heads),
        "attend",
        (
            *[shaped(rows, parts)] * (groups // 2),
            shaped(groups // 2, rows, parts),
            *[shaped(*k) for k in kept],
            shaped(2 * groups, dtype=jnp.int32),
        ),
        [VMEM] * (groups + 5),
        (*[VMEM] * (groups // 2 + 1), *[ANY] * 5, SMEM),
        (*near, far, weights, biases, gains, shifts),
        [
            pltpu.VMEM((heads, room, LANES), BF),
            *[pltpu.VMEM(k, BF) for k in kept],
            pltpu.SemaphoreType.DMA((5,)),
        ],
        cost(15),
        ROOM,
    )


def same_tile(rows):
    return iota((rows, rows), 0) // TILE == iota((rows, rows), 1) // TILE


def thumb_kernel(heads, tokens, weights, biases, gains, shifts, out, xhat, x):
    width = heads * LANES
    size = tokens.shape[0]
    clean = standard(tokens[...].astype(F32))[0].astype(BF)
    xhat[...] = clean
    hidden = (clean.astype(F32) * gains[0:1, :] + shifts[0:1, :]).astype(BF)
    x[...] = (dot(hidden, weights[...]) + biases[...]).astype(BF)
    visible = same_tile(size - TILE)
    out[:TILE, :] = jnp.zeros((TILE, heads * HD), F32)
    for h in range(heads):
        q = x[TILE:, h * LANES : (h + 1) * LANES]
        k = x[TILE:, width + h * LANES : width + (h + 1) * LANES]
        v = x[TILE:, 2 * width + h * LANES : 2 * width + (h + 1) * LANES]
        s = jnp.where(visible, dot_nt(q, k), FAR)
        e = jnp.exp(s - jnp.max(s, axis=-1, keepdims=True))
        o = dot(e.astype(BF), v)[:, :HD] / jnp.sum(e, axis=-1, keepdims=True)
        out[TILE:, h * HD : (h + 1) * HD] = o


def thumbs(tokens, weights, biases, gains, shifts, heads):
    size, model = tokens.shape
    return local_call(
        functools.partial(thumb_kernel, heads),
        "thumbs",
        (
            shaped(size, heads * HD, dtype=F32),
            shaped(size, model),
            shaped(size, 3 * heads * LANES),
        ),
        [VMEM] * 5,
        (VMEM,) * 3,
        (tokens, weights, biases, gains, shifts),
        cost=cost(5),
    )


def merged(parts, heads):
    cols = heads * HD
    row, col = (iota((LANES, cols), d) for d in (0, 1))
    spread = zero_one(row // 3 == col // HD)
    marks = [dot(p[:, cols:], spread) for p in parts]
    top = functools.reduce(jnp.maximum, marks)
    expos = [jnp.exp(m - top) for m in marks]
    total = sum(expos)
    mixed = sum(e * p[:, :cols].astype(F32) for p, e in zip(parts, expos)) / total
    row, col = (iota((cols, LANES), d) for d in (0, 1))
    packed = [
        dot(piece, zero_one((row % HD == 0) & (col == 3 * (row // HD) + i)))
        for i, piece in enumerate(pieces(top + jnp.log(total)))
    ]
    return mixed, sum(packed)


def pair_kernel(heads, *refs):
    count = (len(refs) - 1) // 2
    for j, (mine, out) in enumerate(zip(refs[:count], refs[count + 1 :])):
        mixed, marks = merged([mine[...], refs[count][j]], heads)
        out[...] = jnp.concatenate([mixed.astype(BF), marks.astype(BF)], axis=1)


def pair_merge(parts, other, heads):
    return local_call(
        functools.partial(pair_kernel, heads),
        "pair_merge",
        tuple(shaped(*p.shape) for p in parts),
        [VMEM] * (len(parts) + 1),
        (VMEM,) * len(parts),
        (*parts, other),
        cost=cost(3),
        room=ROOM,
    )


def merge_kernel(heads, counts, thumb, *refs):
    parts, (low, full, lse) = refs[:-3], refs[-3:]
    cols = heads * HD
    rows = lse.shape[0]
    mixed, marks = merged([p[...] for p in parts], heads)
    lse[...] = (-marks).astype(BF)
    image = iota((rows, cols), 0) < counts[0] * TILE
    full[:rows, :] = jnp.where(image, mixed, thumb[:rows, :])
    full[rows:, :] = thumb[rows:, :]
    low[...] = full[...].astype(BF)


def merge(count, parts, thumb, heads):
    size, cols = thumb.shape
    return local_call(
        functools.partial(merge_kernel, heads),
        "merge",
        (shaped(size, cols), shaped(size, cols, dtype=F32), shaped(parts[0].shape[0], LANES)),
        [SMEM] + [VMEM] * (1 + len(parts)),
        (VMEM,) * 3,
        (count, thumb, *parts),
        cost=cost(3),
    )


def fold_kernel(*refs):
    count = (len(refs) - 1) // 2
    for j, (mine, out) in enumerate(zip(refs[:count], refs[count + 1 :])):
        out[...] = (mine[...].astype(F32) + refs[count][j].astype(F32)).astype(BF)


def fold(parts, other):
    return local_call(
        fold_kernel,
        "fold",
        tuple(shaped(*p.shape) for p in parts),
        [VMEM] * (len(parts) + 1),
        (VMEM,) * len(parts),
        (*parts, other),
        cost=cost(2),
        room=ROOM,
    )


ROOT = 0.7978845608028654
CUBE = 0.044715


def ff_kernel(
    heads, tokens, outer, low, low_far, full, lse, out_weight, out_far, up, up_bias, down, far_one,
    far_two, gains, shifts, mixed, grad_mid, grad_low, packed, hidden_out, act_out, pre_out, small,
):
    size, model = tokens.shape
    passes = outer.shape[0]
    cols = heads * HD
    chunk = far_one.shape[1]
    units = up.shape[1]
    rows = packed.shape[0]
    branch = dot(low[...], out_weight[...]) + dot(low_far[...], out_far[...])
    middle = tokens[...].astype(F32) + (branch + shifts[1:2, :])
    xhat, factor = standard(middle)
    hidden = (xhat * gains[1:2, :] + shifts[2:3, :]).astype(BF)
    hidden_out[...] = hidden

    def one_chunk(up_part, bias, down_part, keep):
        v = dot(hidden, up_part) + bias
        t = jnp.tanh(ROOT * (v + CUBE * (v * v * v)))
        act = (0.5 * v * (1.0 + t)).astype(BF)
        slope = 0.5 * (1.0 + t) + 0.5 * v * (1.0 - t * t) * (ROOT * (1.0 + 3.0 * CUBE * (v * v)))
        two = []
        for p in range(passes):
            pre = (dot_nt(outer[p], down_part) * slope).astype(BF)
            if keep is not None:
                pre_out[p, :, keep] = pre
            two.append(dot_nt(pre, up_part))
        if keep is not None:
            act_out[:, keep] = act
        return dot(act, down_part), two

    def far_chunk(ref):
        told = ref[2 * chunk : 2 * chunk + 16, :].astype(F32)
        bias = told[0:1] + told[1:2] + told[2:3]
        return one_chunk(ref[:chunk, :], bias, ref[chunk : 2 * chunk, :], None)

    done = []
    for i in range(units // chunk):
        at = slice(i * chunk, (i + 1) * chunk)
        done.append(one_chunk(up[:, at], up_bias[:, at], down[at, :], at))
    done += [far_chunk(far_one), far_chunk(far_two)]

    def tree(parts):
        half = len(parts) // 2
        return sum(parts[:half]) + sum(parts[half:])

    output = tree([d[0] for d in done])
    mixed[...] = (middle + (output + shifts[3:4, :])).astype(BF)
    small[...] = jnp.zeros(small.shape, F32)
    lane = iota((rows, LANES), 1)
    stats = jnp.zeros((rows, LANES), F32)
    for p in range(passes):
        two = tree([d[1][p] for d in done])
        c = outer[p].astype(F32)
        mid = c + norm_back(two, gains[1:2, :], xhat, factor)
        mid_low = mid.astype(BF)
        grad_mid[p] = mid
        grad_low[p] = mid_low
        att = dot_nt(mid_low, out_weight[...]).astype(BF)
        packed[:, p * cols : (p + 1) * cols] = att[:rows, :]
        pre_out_p = pre_out[p].astype(F32)
        bias = jnp.sum(pre_out_p, axis=0, keepdims=True)
        small[p, 0:1, :] = jnp.sum(two * xhat, axis=0, keepdims=True)
        small[p, 1:2, :] = jnp.sum(two, axis=0, keepdims=True)
        small[p, 2:3, :] = jnp.sum(mid_low.astype(F32), axis=0, keepdims=True)
        small[p, 3:4, :] = jnp.sum(c, axis=0, keepdims=True)
        for i in range(units // model):
            small[p, 4 + i : 5 + i, :] = bias[:, i * model : (i + 1) * model]
        product = att[:rows, :].astype(F32) * full[:rows, :]
        for h in range(heads):
            delta = jnp.sum(product[:, h * HD : (h + 1) * HD], axis=-1, keepdims=True)
            for i, piece in enumerate(pieces(-delta)):
                stats = jnp.where(lane == 3 * heads * (p + 1) + 3 * h + i, piece.astype(F32), stats)
    packed[:, passes * cols :] = (stats + lse[...].astype(F32)).astype(BF)


def feed_forward(
    tokens, outer, low, low_far, full, lse, out_weight, out_far, up, up_bias, down, far_one, far_two,
    gains, shifts, rows, heads,
):
    size, model = tokens.shape
    passes = outer.shape[0]
    units = up.shape[1]
    return local_call(
        functools.partial(ff_kernel, heads),
        "feed_forward",
        (
            shaped(size, model),
            shaped(passes, size, model, dtype=F32),
            shaped(passes, size, model),
            shaped(rows, passes * heads * HD + LANES),
            shaped(size, model),
            shaped(size, units),
            shaped(passes, size, units),
            shaped(passes, 8, model, dtype=F32),
        ),
        [VMEM] * 15,
        (VMEM,) * 8,
        (
            tokens, outer, low, low_far, full, lse, out_weight, out_far, up, up_bias, down, far_one,
            far_two, gains, shifts,
        ),
        cost=cost(12),
        room=32,
    )


def thumb_back_kernel(heads, counts, x, mid_low, out_weight, out):
    width = heads * LANES
    size = x.shape[0]
    passes = mid_low.shape[0]
    visible = same_tile(size - TILE)
    outside = iota((size - TILE, HD), 0) + TILE >= counts[0] * TILE
    grads = [dot_nt(mid_low[p], out_weight[...]).astype(BF) for p in range(passes)]
    out[:, :, :TILE, :] = jnp.zeros((*out.shape[:2], TILE, out.shape[3]), BF)
    for h in range(heads):
        q = x[TILE:, h * LANES : (h + 1) * LANES]
        k = x[TILE:, width + h * LANES : width + (h + 1) * LANES]
        v = x[TILE:, 2 * width + h * LANES : 2 * width + h * LANES + HD]
        s = jnp.where(visible, dot_nt(q, k), FAR)
        e = jnp.exp(s - jnp.max(s, axis=-1, keepdims=True))
        w = e / jnp.sum(e, axis=-1, keepdims=True)
        w_low = w.astype(BF)
        for p in range(passes):
            g = grads[p][TILE:, h * HD : (h + 1) * HD]
            gw = dot_nt(g, v)
            ds = (w * (gw - jnp.sum(w * gw, axis=-1, keepdims=True))).astype(BF)
            dq = dot(ds, k[:, :HD]) * SCALE
            dk = dot_tn(ds, q)[:, :HD]
            dv = dot_tn(w_low, g)
            for c, piece in enumerate((dq, dk, dv)):
                at = c * LANES + (h % 2) * HD
                out[h // 2, p, TILE:, at : at + HD] = jnp.where(outside, piece, 0.0).astype(BF)


def thumbs_back(count, x, mid_low, out_weight, heads):
    passes, size, _ = mid_low.shape
    return local_call(
        functools.partial(thumb_back_kernel, heads),
        "thumbs_back",
        shaped(heads // 2, passes, size, 3 * LANES),
        [SMEM] + [VMEM] * 3,
        VMEM,
        (count, x, mid_low, out_weight),
        cost=cost(6),
    )


def early_at(units, model, low):
    ends = [model, 2 * model, 2 * model + units, 2 * model + units + low]
    return [slice(b - w, b) for b, w in zip(ends, (model, model, units, low))]


def early_cuts(parts, units, model, low):
    high, wide, turns = units // parts // 2, model // parts, model // low
    narrow = low * turns // parts
    for i in range(parts):
        yield (
            (slice(2 * i * high, (2 * i + 1) * high), slice(0, model)),
            (slice((2 * i + 1) * high, (2 * i + 2) * high), slice(0, model)),
            (slice(i * wide, (i + 1) * wide), slice(0, units)),
            (
                slice(i // turns * narrow, (i // turns + 1) * narrow),
                slice(i % turns * low, (i % turns + 1) * low),
            ),
        )


def weight_kernel(place, act, outer, hidden, pre, low, mid_low, keep, give):
    units, model, cols = act.shape[1], hidden.shape[1], low.shape[1]
    core = place[0]
    for turn, out in ((core, keep), (1 - core, give)):
        down = dot_tn(act[...], outer[turn]).astype(BF)
        up = dot_tn(hidden[...], pre[turn]).astype(BF)
        proj = dot_tn(low[...], mid_low[turn]).astype(BF)
        for i, cut in enumerate(early_cuts(keep.shape[0], units, model, cols)):
            for value, (rows, lanes), at in zip(
                (down, down, up, proj), cut, early_at(units, model, cols)
            ):
                out[i, :, at] = value[rows, lanes]


def weight_grads(core, act, outer, hidden, pre, low, mid_low, parts):
    units, model = act.shape[1], outer.shape[2]
    out = shaped(parts, model // parts, 2 * model + units + low.shape[1])
    return local_call(
        weight_kernel,
        "weight_grads",
        (out, out),
        [SMEM] + [VMEM] * 6,
        (VMEM,) * 2,
        (core, act, outer, hidden, pre, low, mid_low),
        cost=cost(8),
        room=24,
    )


def reverse_kernel(rows, groups, heads, passes, counts, place, *refs):
    grads, kept = refs[:groups], refs[groups : groups + 5]
    own, thumb, weights, columns, small = refs[groups + 5 : groups + 10]
    at = groups + 10
    out_q, give_q, at = refs[at : at + groups // 2], refs[at + groups // 2], at + groups // 2 + 1
    out_kv, at = refs[at : at + groups // 2], at + groups // 2
    late, at = refs[at], at + 1
    (
        stage, xq, xk, qx, kx, vx, packed, gx, kt, dq_t, dv, dk, low_q, low_kv, total, sums,
        starts, sems,
    ) = refs[at:]
    couples = heads // 2
    sources = [*grads, *kept[2:], *kept[:2]]
    targets = [*[stage.at[g] for g in range(groups)], qx, kx, vx, xq, xk]
    copies = [
        pltpu.make_async_copy(f, t, sems.at[i]) for i, (f, t) in enumerate(zip(sources, targets))
    ]
    for copy in copies:
        copy.start()
    cols = heads * HD
    wide = passes * LANES
    q_counts = [counts[g] for g in range(groups)]
    k_counts = [counts[groups + g] for g in range(groups)]
    start = jnp.int32(0)
    for g in range(groups):
        copies[g].wait()
        packed[rows_at(start, rows), :] = stage[g]
        start = start + q_counts[g] * TILE
    q_total, k_total = start, sum(k_counts) * TILE
    tail_lane = iota((BLOCK, packed.shape[1]), 1) - passes * cols
    empty = (tail_lane >= 0) & (tail_lane < 3 * heads) & (tail_lane % 3 == 0)
    packed[rows_at(q_total, BLOCK), :] = jnp.where(empty, FAR, 0.0).astype(BF)
    q_blocks = (q_total + BLOCK - 1) // BLOCK
    k_blocks = (k_total + BLOCK - 1) // BLOCK
    spans = range(groups * TILE // BLOCK, groups * rows // BLOCK + 1)

    row, col = (iota((LANES, heads * LANES), d) for d in (0, 1))
    head, lane = col // LANES, col % LANES
    to_marks = zero_one((lane > HD) & (lane < HD + 4) & (row == 3 * head + lane - HD - 1))
    row, col = (iota((LANES, heads * wide), d) for d in (0, 1))
    head, turn, lane = col // wide, col % wide // LANES, col % LANES
    to_deltas = zero_one(
        (lane >= HD) & (lane < HD + 3) & (row == 3 * heads * (turn + 1) + 3 * head + lane - HD)
    )
    for copy in copies[groups : groups + 3]:
        copy.wait()

    @pl.loop(0, q_blocks)
    def _(b):
        here = rows_at(b * BLOCK, BLOCK, BLOCK)
        stats = packed[here, passes * cols :]
        marks = dot(stats, to_marks)
        deltas = dot(stats, to_deltas).astype(BF)
        for h in range(heads):
            more = marks[:, h * LANES : (h + 1) * LANES]
            qx[h, here, :] = (qx[h, here, :].astype(F32) + more).astype(BF)
            for p in range(passes):
                at = p * cols + h * HD
                mine = (h * passes + p) * LANES
                gx[h, here, p * LANES : (p + 1) * LANES] = jnp.concatenate(
                    [packed[here, at : at + HD], deltas[:, mine + HD : mine + LANES]], axis=1
                )

    @pl.loop(0, k_blocks)
    def _(b):
        here = rows_at(b * BLOCK, BLOCK, BLOCK)
        for h in range(heads):
            kt[h, b] = jnp.transpose(kx[h, here, :].astype(F32))[:HD, :].astype(BF)

    def reverse_all(blocks):
        span = blocks * BLOCK

        @pl.loop(0, couples)
        def _(pair):
            dv[:, :span, :] = jnp.zeros((2, span, wide), F32)
            dk[:, :, :span, :] = jnp.zeros((passes, 2, span, LANES), F32)

            @pl.loop(0, q_blocks)
            def _(b):
                here = rows_at(b * BLOCK, BLOCK, BLOCK)
                for i in range(2):
                    h = 2 * pair + i
                    q, g = qx[h, here, :], gx[h, here, :]
                    k_t = jnp.concatenate([kt[h, j] for j in range(blocks)], axis=1)
                    w = jnp.exp(dot_nt(kx[h, :span, :], q))
                    dv[i, :span, :] += dot(w.astype(BF), g)
                    for p in range(passes):
                        ds = dot_nt(vx[h, :span, :], g[:, p * LANES : (p + 1) * LANES])
                        ds = (w * ds).astype(BF)
                        dk[p, i, :span, :] += dot(ds, q)
                        dq_t[p, i * HD : (i + 1) * HD, :] = dot(k_t, ds)
                for p in range(passes):
                    piece = jnp.transpose(dq_t[p]) * SCALE
                    low_q[pair, here, p * LANES : (p + 1) * LANES] = piece.astype(BF)

            for p in range(passes):
                for c, both in enumerate(
                    (
                        [dk[p, i, :span, :HD] for i in range(2)],
                        [dv[i, :span, p * LANES : p * LANES + HD] for i in range(2)],
                    )
                ):
                    lane = (2 * p + c) * LANES
                    low_kv[pair, :span, lane : lane + LANES] = jnp.concatenate(both, axis=1).astype(BF)

    for blocks in spans:
        pl.when(k_blocks == blocks)(functools.partial(reverse_all, blocks))

    start = jnp.int32(0)
    for g in range(groups):
        starts[g] = start
        start = start + k_counts[g] * TILE
    for g in range(groups):
        here = rows_at(starts[place[1 + g]], rows)
        out_kv[g // 2][g % 2] = jnp.concatenate([low_kv[i, here, :] for i in range(couples)], axis=1)
    start = jnp.int32(0)
    for g in range(groups):
        here = rows_at(start, rows)
        value = jnp.concatenate([low_q[i, here, :] for i in range(couples)], axis=1)
        if g < groups // 2:
            out_q[g][...] = value
        else:
            give_q[g - groups // 2] = value
        start = start + q_counts[g] * TILE

    copies[groups + 3].wait()
    copies[groups + 4].wait()

    def key_sums(blocks):
        span = blocks * BLOCK
        for i in range(couples):
            flat = low_kv[i, :span, :]
            total[i, :, wide:] = dot_tn(xk[:span, :], flat)
            sums[i, :, wide:] = dot(jnp.ones((8, span), BF), flat)

    for blocks in spans:
        pl.when(k_blocks == blocks)(functools.partial(key_sums, blocks))

    total[:, :, :wide] = jnp.zeros((couples, total.shape[1], wide), F32)
    sums[:, :, :wide] = jnp.zeros((couples, 8, wide), F32)

    @pl.loop(0, q_blocks)
    def _(b):
        here = rows_at(b * BLOCK, BLOCK, BLOCK)
        for i in range(couples):
            total[i, :, :wide] += dot_tn(xq[here, :], low_q[i, here, :])
            sums[i, :, :wide] += dot(jnp.ones((8, BLOCK), BF), low_q[i, here, :])

    model = total.shape[1]
    gain, shift = columns[:, 0:1], columns[:, 1:2]
    ones = jnp.ones((8, own.shape[0]), BF)
    for p in range(passes):
        whole = []
        for i in range(couples):
            mine = thumb[i, p]
            part = dot_tn(own[...], mine)
            part_sum = dot(ones, mine)[0:1, :]
            q_at = slice(p * LANES, (p + 1) * LANES)
            kv_at = slice((passes + 2 * p) * LANES, (passes + 2 * p + 2) * LANES)
            part += jnp.concatenate([total[i, :, q_at], total[i, :, kv_at]], axis=1)
            part_sum += jnp.concatenate([sums[i, 0:1, q_at], sums[i, 0:1, kv_at]], axis=1)
            w = weights[i].astype(F32)
            gain_one = jnp.sum(w * part, axis=1, keepdims=True)
            shift_one = jnp.sum(w * part_sum, axis=1, keepdims=True)
            lane = iota((model, LANES), 1)
            tall = jnp.where(lane == 0, gain_one, jnp.where(lane == 1, shift_one, 0.0))
            flat = jnp.concatenate(
                [jnp.zeros((2, LANES), F32)]
                + [part_sum[:, c * LANES : (c + 1) * LANES] for c in range(3)]
                + [jnp.zeros((LANES - 5, LANES), F32)],
                axis=0,
            )
            tall = jnp.concatenate([tall[:LANES] + jnp.transpose(flat), tall[LANES:]], axis=0)
            if i == 0:
                turned = jnp.concatenate(
                    [
                        jnp.zeros((8, model), F32),
                        small[p],
                        jnp.zeros((LANES - 16, model), F32),
                    ],
                    axis=0,
                )
                tall = tall + jnp.transpose(turned)
            whole += [part * gain + shift * part_sum, tall]
        whole = jnp.concatenate(whole, axis=1).astype(BF)
        high = late.shape[2]
        for i in range(late.shape[0]):
            late[i, p] = whole[i * high : (i + 1) * high]


def reverse(counts, place, grads, kept, own, thumb, weights, columns, small, rows, heads, plane):
    groups = len(grads)
    couples, passes = thumb.shape[:2]
    model = own.shape[1]
    room = rows * groups + BLOCK
    cols = heads * HD
    wide = passes * LANES
    half = groups // 2
    late = shaped(plane, passes, model // plane, couples * 4 * LANES)
    q, kv = shaped(rows, couples * wide), shaped(2, rows, couples * 2 * wide)
    out = (*[q] * half, shaped(half, rows, couples * wide), *[kv] * half, late)
    return local_call(
        functools.partial(reverse_kernel, rows, groups, heads, passes),
        "reverse",
        out,
        [SMEM, SMEM] + [ANY] * (groups + 5) + [VMEM] * 5,
        (VMEM,) * len(out),
        (counts, place, *grads, *kept, own, thumb, weights, columns, small),
        [
            pltpu.VMEM((groups, rows, passes * cols + LANES), BF),
            pltpu.VMEM((room, model), BF),
            pltpu.VMEM((room, model), BF),
            pltpu.VMEM((heads, room, LANES), BF),
            pltpu.VMEM((heads, room, LANES), BF),
            pltpu.VMEM((heads, room, LANES), BF),
            pltpu.VMEM((room, passes * cols + LANES), BF),
            pltpu.VMEM((heads, room, wide), BF),
            pltpu.VMEM((heads, room // BLOCK, HD, BLOCK), BF),
            pltpu.VMEM((passes, LANES, BLOCK), F32),
            pltpu.VMEM((2, room, wide), F32),
            pltpu.VMEM((passes, 2, room, LANES), F32),
            pltpu.VMEM((couples, room, wide), BF),
            pltpu.VMEM((couples, room, 2 * wide), BF),
            pltpu.VMEM((couples, model, 3 * wide), F32),
            pltpu.VMEM((couples, 8, 3 * wide), F32),
            pltpu.SMEM((groups,), jnp.int32),
            pltpu.SemaphoreType.DMA((groups + 5,)),
        ],
        cost(45),
        ROOM,
    )


def grad_one_kernel(near, counts, *refs):
    from_q, from_kv, (thumb, weights, mine, other) = refs[:near], refs[near:-4], refs[-4:]
    couples, passes, size, _ = thumb.shape
    rows = from_q[0].shape[0]
    sum_q = sum(r[...].astype(F32) for r in from_q)
    sum_kv = [sum(r[f].astype(F32) for r in from_kv) for f in range(2)]
    image = iota((rows, 3 * LANES), 0) < counts[0] * TILE
    for p in range(passes):
        parts = []
        for i in range(couples):
            at = (passes * i + p) * LANES
            there = slice(2 * at, 2 * at + 2 * LANES)
            far = jnp.concatenate([sum_q[:, at : at + LANES], sum_kv[0][:, there]], axis=1)
            flat = jnp.concatenate(
                [jnp.where(image, far.astype(BF), thumb[i, p, :rows]), thumb[i, p, rows:]], axis=0
            )
            parts.append(
                (
                    dot_nt(flat, weights[i]),
                    dot_nt(sum_kv[1][:, there].astype(BF), weights[i, :, LANES:]),
                )
            )
        mine[p] = sum(a for a, _ in parts).astype(BF)
        other[p] = sum(b for _, b in parts).astype(BF)


def grad_one(count, from_q, from_kv, thumb, weights):
    near = len(from_q)
    passes, size, _ = thumb.shape[1:]
    model = weights.shape[1]
    return local_call(
        functools.partial(grad_one_kernel, near),
        "grad_one",
        (shaped(passes, size, model), shaped(passes, from_q[0].shape[0], model)),
        [SMEM] + [VMEM] * (near + len(from_kv) + 2),
        (VMEM,) * 2,
        (count, *from_q, *from_kv, thumb, weights),
        cost=cost(5),
        room=ROOM,
    )


def close_kernel(counts, tokens, mid, mine, head, side, cross, gains, out):
    xhat, factor = standard(tokens[...].astype(F32))
    rows = side.shape[1]
    image = iota(side.shape[1:], 0) < counts[0] * TILE
    for p in range(mid.shape[0]):
        grad = mine[p].astype(F32) + head[p].astype(F32)
        more = jnp.where(image, side[p].astype(F32) + cross[p].astype(F32), 0.0)
        grad = jnp.concatenate([grad[:rows] + more, grad[rows:]], axis=0)
        out[p] = mid[p] + norm_back(grad, gains[0:1, :], xhat, factor)


def close(count, tokens, mid, mine, head, side, cross, gains):
    return local_call(
        close_kernel,
        "close",
        shaped(*mid.shape, dtype=F32),
        [SMEM] + [VMEM] * 7,
        VMEM,
        (count, tokens, mid, mine, head, side, cross, gains),
        cost=cost(4),
        room=ROOM,
    )


def early_kernel(lines, place, *refs):
    own, far, (down, up, proj) = refs[:lines], refs[lines : 2 * lines], refs[2 * lines :]
    core, z, y = place[0], place[9], place[10]
    (units, model), low = down.shape[1:], proj.shape[1]
    steps, rows = own[0].shape[:2]
    lane_down, lane_next, lane_up, lane_proj = early_at(units, model, low)
    turns = model // low
    for out, parts in ((core, own), (1 - core, far)):
        for d, ref in enumerate(parts):
            for j in range(steps):
                i = (z + steps - j) % steps * lines + (y + lines - d) % lines
                at = pl.multiple_of(2 * rows * i, 2 * rows)
                down[out, pl.ds(at, rows), :] = ref[j, :, lane_down].astype(F32)
                down[out, pl.ds(at + rows, rows), :] = ref[j, :, lane_next].astype(F32)
                up[out, rows_at(rows * i, rows, rows), :] = ref[j, :, lane_up].astype(F32)
                here = rows_at(i // turns * rows, rows, rows)
                value = ref[j, :, lane_proj].astype(F32)
                for t in range(turns):

                    @pl.when(i % turns == t)
                    def _(value=value, here=here, t=t):
                        proj[out, here, t * low : (t + 1) * low] = value


def early_out(place, own, far, units, low):
    model = len(own) * own[0].shape[0] * own[0].shape[1]
    return local_call(
        functools.partial(early_kernel, len(own)),
        "early_out",
        (
            shaped(2, units, model, dtype=F32),
            shaped(2, model, units, dtype=F32),
            shaped(2, low, model, dtype=F32),
        ),
        [SMEM] + [VMEM] * (2 * len(own)),
        (VMEM,) * 3,
        (place, *own, *far),
        cost=cost(8),
        room=ROOM,
    )


def late_kernel(place, own, far, grad_in, in_bias, up_bias, gains, shifts):
    core = place[0]
    for turn, ref in ((core, own), (1 - core, far)):
        turned = []
        for pair in range(2):
            at = 4 * LANES * pair
            for c in range(3):
                grad_in[turn, c, :, pair * LANES : (pair + 1) * LANES] = ref[
                    :, at + c * LANES : at + (c + 1) * LANES
                ].astype(F32)
            turned.append(jnp.transpose(ref[:, at + 3 * LANES : at + 4 * LANES].astype(F32)))
        a, b = turned
        in_bias[turn] = jnp.concatenate(
            [
                jnp.concatenate([a[2:3, :LANES], b[2:3, :LANES]], axis=1),
                jnp.concatenate([a[4:5, :LANES], b[4:5, :LANES]], axis=1),
            ],
            axis=0,
        )
        up_bias[turn] = jnp.concatenate([a[12:13], a[13:14]], axis=1)
        gains[turn] = jnp.concatenate([a[0:1] + b[0:1], a[8:9]], axis=0)
        shifts[turn] = jnp.concatenate([a[1:2] + b[1:2], a[10:11], a[9:10], a[11:12]], axis=0)


def late_out(core, own, far, units):
    model = own.shape[0]
    return local_call(
        late_kernel,
        "late_out",
        (
            shaped(2, 3, model, 2 * LANES, dtype=F32),
            shaped(2, 2, 2 * LANES, dtype=F32),
            shaped(2, 1, units, dtype=F32),
            shaped(2, 2, model, dtype=F32),
            shaped(2, 4, model, dtype=F32),
        ),
        [SMEM] + [VMEM] * 2,
        (VMEM,) * 5,
        (core, own, far),
        cost=cost(4),
        room=ROOM,
    )


def gather_near(array):
    mine = [array] + [shift_by(array, "y", d) for d in range(1, lax.axis_size("y"))]
    return mine + [shift_by(a, "c", 1) for a in mine]


def return_near(parts):
    return [parts[0]] + [shift_by(p, "y", -j) for j, p in enumerate(parts) if j > 0]


def offsets(size):
    return [(step, flip) for step in range(size) for flip in range(2)]


def return_far(parts):
    return [parts[0]] + [shift_by(p, "z", step) for step, p in enumerate(parts) if step > 0]


PLANE = ("z", "y")


def core_sum(keep, give):
    return (keep.astype(F32) + shift_by(give, "c", 1).astype(F32)).astype(BF)


def crossed(array):
    n = lax.axis_size(("xl", "h"))
    return lax.ppermute(array, ("xl", "h"), [(i, n - 1 - i) for i in range(n)])


def across(low):
    done = low.astype(F32) + shift_by(low, "xl", 1).astype(F32)
    size = 4 * LANES
    ones = jnp.concatenate([low[:, i + 3 * LANES : i + size] for i in range(0, low.shape[1], size)], axis=1)
    more = shift_by(ones, "h", 1).astype(F32) + crossed(ones).astype(F32)
    more = jnp.where(jnp.arange(more.shape[1]) % LANES < 2, more, 0.0)
    nothing = jnp.zeros((low.shape[0], 3 * LANES), F32)
    laid = [[nothing, more[:, i : i + LANES]] for i in range(0, more.shape[1], LANES)]
    return (done + jnp.concatenate(sum(laid, []), axis=1)).astype(BF)


def tied(arrays, others):
    return lax.optimization_barrier((arrays, others))


def local(
    tokens,
    cotangents,
    segment_ids,
    in_weights,
    in_biases,
    out_weight,
    up_weight,
    up_biases,
    down_weight,
    gains,
    shifts,
):
    size, model = tokens.shape
    cols = in_weights.shape[2]
    heads = cols // HD
    rows = size - TILE
    units = up_weight.shape[1]
    c = lax.axis_index("c")

    told, copies, count = front(tokens, segment_ids, lax.axis_size(("z", "xl")))
    far = lax.all_to_all(copies, ("z", "xl"), 0, 0, tiled=True)
    near = gather_near(told)
    core = c.astype(jnp.int32).reshape(1)
    z, xl, z_size = lax.axis_index("z"), lax.axis_index("xl"), lax.axis_size("z")
    routes = [((z + step) % z_size) * 2 + (xl ^ flip) for step, flip in offsets(z_size)]
    place = jnp.stack([c, *routes, z, lax.axis_index("y")]).astype(jnp.int32)
    plane = lax.axis_size(PLANE)

    weights, biases, pairs, columns, bundle = prepare(
        core, in_weights, in_biases, gains, shifts, up_weight, down_weight, up_biases[None], heads
    )
    out_far = crossed(out_weight)
    far_one = crossed(bundle)
    far_two = shift_by(far_one, "c", 1)

    *parts, give, xq, xk, qx, kx, vx, counts = attend(
        near, far, weights, biases, gains, shifts, rows, heads
    )
    thumb_out, xhat, x = thumbs(tokens, weights, biases, gains, shifts, heads)
    parts = pair_merge(parts, shift_by(give, "c", 1), heads)
    low, full, lse = merge(count, return_near(parts), thumb_out, heads)
    low_far = shift_by(low, "h", 1)
    mixed, grad_mid, mid_low, packed, hidden, act, pre, small = feed_forward(
        tokens, cotangents, low, low_far, full, lse, out_weight, out_far, up_weight, up_biases[None],
        down_weight, far_one, far_two, gains, shifts, rows, heads,
    )
    grads = gather_near(packed)
    keep, give = weight_grads(core, act, cotangents, hidden, pre, low, mid_low, plane)
    mid_low, (keep, give) = tied(mid_low, (keep, give))
    thumb = thumbs_back(count, x, mid_low, out_weight, heads)
    early = core_sum(keep, give)

    grads, (early, thumb) = tied(grads, (early, thumb))
    early = lax.all_to_all(early, PLANE, 0, 0, tiled=True)
    *out, late = reverse(
        counts, place, grads, (xq, xk, qx, kx, vx), xhat, thumb, pairs, columns, small, rows, heads,
        plane,
    )
    early = jnp.sum(early.astype(F32), axis=0).astype(BF)
    late, early = tied(late, early)
    late = lax.all_to_all(late, PLANE, 0, 0, tiled=True)
    half = len(near) // 2
    out_q, give_q, out_kv = out[:half], out[half], out[half + 1 :]
    from_kv = return_far(out_kv)
    from_q = return_near(fold(out_q, shift_by(give_q, "c", 1)))
    early_side = shift_by(early, "xl", 1)

    late, early_side = tied(late, early_side)
    late = jnp.sum(late.astype(F32), axis=0).astype(BF)
    give = lax.dynamic_index_in_dim(late, 1 - c, 0, keepdims=False)
    keep = lax.dynamic_index_in_dim(late, c, 0, keepdims=False)
    late = core_sum(keep, give)
    late, from_kv[1] = tied(late, from_kv[1])
    late = across(late)
    late, from_kv = tied(late, from_kv)
    late = jnp.broadcast_to(late[None], (plane, *late.shape))
    late = lax.all_to_all(late, PLANE, 0, 0, tiled=True).reshape(model, -1)

    mine, other = grad_one(count, from_q, from_kv, thumb, pairs)
    grad_tokens = close(
        count, tokens, grad_mid, mine, shift_by(mine, "h", 1), shift_by(other, "xl", 1),
        crossed(other), gains,
    )
    early = (early.astype(F32) + early_side.astype(F32)).astype(BF)
    early = jnp.stack([early] + [shift_by(early, "z", d) for d in range(1, z_size)])
    early = [early] + [shift_by(early, "y", d) for d in range(1, lax.axis_size("y"))]
    early_far = [shift_by(e, "c", 1) for e in early]
    grad_down, grad_up, grad_out = early_out(place, early, early_far, units, cols)
    grad_in, in_bias, up_bias, grad_gains, grad_shifts = late_out(
        core, late, shift_by(late, "c", 1), units
    )
    return (
        mixed,
        grad_tokens,
        grad_in,
        in_bias,
        grad_out,
        grad_up,
        up_bias.reshape(2, units),
        grad_down,
        grad_gains,
        grad_shifts,
    )


def solution(mesh):
    fine = Mesh(mesh.devices.reshape(4, 2, 4, 2, 2), ("z", "xl", "y", "c", "h"))
    blk = ("z", "xl", "y", "c")
    return jax.shard_map(
        local,
        mesh=fine,
        in_specs=(
            P(blk, None),
            P(None, blk, None),
            P(blk),
            P(None, None, "h"),
            P(None, "h"),
            P("h", None),
            P(None, "h"),
            P("h"),
            P("h", None),
            P(),
            P(),
        ),
        out_specs=(
            P(blk, None),
            P(None, blk, None),
            P(None, None, None, "h"),
            P(None, None, "h"),
            P(None, "h", None),
            P(None, None, "h"),
            P(None, "h"),
            P(None, "h", None),
            P(),
            P(),
        ),
        check_vma=False,
    )
```

```python
import functools

import jax
import jax.numpy as jnp
from jax import lax
from jax.experimental import pallas as pl
from jax.experimental.pallas import tpu as pltpu
from jax.sharding import Mesh
from jax.sharding import PartitionSpec as P

HD = 64
LANES = 128
TILE = 64
BLOCK = 256
EPS = 1e-06
SCALE = 0.125
FAR = -1e30
BF = jnp.bfloat16
F32 = jnp.float32
MIB = 1024 * 1024
ROOM = 56

NT = (((1,), (1,)), ((), ()))
TN = (((0,), (0,)), ((), ()))


def shift_by(array, axis, step):
    size = lax.axis_size(axis)
    return lax.ppermute(array, axis, [(i, (i + step) % size) for i in range(size)])


def dot(a, b):
    return jnp.dot(a, b, preferred_element_type=F32)


def dot_nt(a, b):
    return lax.dot_general(a, b, NT, preferred_element_type=F32)


def dot_tn(a, b):
    return lax.dot_general(a, b, TN, preferred_element_type=F32)


def standard(field):
    center = field - jnp.mean(field, axis=-1, keepdims=True)
    factor = lax.rsqrt(jnp.mean(center * center, axis=-1, keepdims=True) + EPS)
    return center * factor, factor


def norm_back(grad, gain, xhat, factor):
    h = grad * gain
    mean = jnp.mean(h, axis=-1, keepdims=True)
    return factor * (h - mean - xhat * jnp.mean(h * xhat, axis=-1, keepdims=True))


def pieces(value):
    high = value.astype(BF)
    rest = value - high.astype(F32)
    middle = rest.astype(BF)
    low = (rest - middle.astype(F32)).astype(BF)
    return high, middle, low


def zero_one(mask):
    return jnp.where(mask, 1.0, 0.0).astype(BF)


def iota(shape, dim):
    return lax.broadcasted_iota(jnp.int32, shape, dim)


VMEM = pl.BlockSpec(memory_space=pltpu.VMEM)
ANY = pl.BlockSpec(memory_space=pl.ANY)
SMEM = pl.BlockSpec(memory_space=pltpu.SMEM)


def local_call(body, name, out, ins, outs, args, scratch=(), cost=None, room=16):
    return pl.pallas_call(
        body,
        out_shape=out,
        in_specs=ins,
        out_specs=outs,
        scratch_shapes=scratch,
        cost_estimate=cost,
        compiler_params=pltpu.CompilerParams(vmem_limit_bytes=room * MIB),
        name=name,
    )(*args)


def shaped(*shape, dtype=BF):
    return jax.ShapeDtypeStruct(shape, dtype)


def cost(micros):
    return pl.CostEstimate(flops=int(micros * 1e9), bytes_accessed=0, transcendentals=0)


def front_kernel(tokens, ids, told, copies, number):
    rows = told.shape[0] - 16
    marks = jnp.where(ids[...] == 0, 1.0, 0.0)
    tiles = jnp.sum(marks).astype(jnp.int32) // TILE
    number[0] = tiles
    told[:rows, :] = tokens[:rows, :]
    told[rows:, :] = jnp.full((16, told.shape[1]), tiles.astype(F32), F32).astype(BF)
    for g in range(copies.shape[0]):
        copies[g] = told[...]


def front(tokens, ids, copies):
    size, model = tokens.shape
    told = size - TILE + 16
    return local_call(
        front_kernel,
        "front",
        (shaped(told, model), shaped(copies, told, model), shaped(1, dtype=jnp.int32)),
        [VMEM, VMEM],
        (VMEM, VMEM, SMEM),
        (tokens, ids.reshape(-1, LANES)),
        room=ROOM,
    )


def prepare_kernel(
    heads, place, in_weights, in_biases, gains, shifts, up, down, bias,
    weights, biases, pairs, columns, out,
):
    core = place[0]
    half = out.shape[1]
    at = pl.ds(pl.multiple_of(core * half, half), half)
    out[:half, :] = up[:, at]
    out[half : 2 * half, :] = down[at, :]
    mine = jnp.where(core == 0, bias[:, :half], bias[:, half:])
    row = iota((16, half), 0)
    rows = jnp.zeros((16, half), F32)
    for i, piece in enumerate(pieces(mine)):
        rows = jnp.where(row == i, piece.astype(F32), rows)
    out[2 * half :, :] = rows.astype(BF)

    model, cols = in_weights.shape[1:]
    width = heads * LANES
    row, col = (iota((cols, width), d) for d in (0, 1))
    spread = zero_one((row // HD == col // LANES) & (row % HD == col % LANES))
    lane = iota((1, width), 1) % LANES
    gap = jnp.zeros((1, HD), F32)

    def apart(line):
        return jnp.concatenate(
            sum([[line[:, h * HD : (h + 1) * HD], gap] for h in range(heads)], []), axis=1
        )

    extra = [
        apart(in_biases[0:1, :] * SCALE) + jnp.where(lane == HD, 1.0, 0.0),
        jnp.where((lane > HD) & (lane < HD + 4), 1.0, 0.0),
        apart(in_biases[1:2, :]) + jnp.where((lane >= HD) & (lane < HD + 3), 1.0, 0.0),
    ]
    for i in range(3):
        factor = SCALE if i == 0 else 1.0
        weights[:, i * width : (i + 1) * width] = (dot(in_weights[i], spread) * factor).astype(BF)
        biases[:, i * width : (i + 1) * width] = extra[i]
        for pair in range(heads // 2):
            pairs[pair, :, i * LANES : (i + 1) * LANES] = in_weights[
                i, :, pair * LANES : (pair + 1) * LANES
            ]
    tall = jnp.concatenate(
        [gains[0:1, :], shifts[0:1, :], jnp.zeros((LANES - 2, model), F32)], axis=0
    )
    columns[...] = jnp.transpose(tall)


def prepare(core, in_weights, in_biases, gains, shifts, up, down, bias, heads):
    model = up.shape[0]
    width = 3 * heads * LANES
    return local_call(
        functools.partial(prepare_kernel, heads),
        "prepare",
        (
            shaped(model, width),
            shaped(1, width, dtype=F32),
            shaped(heads // 2, model, 3 * LANES),
            shaped(model, LANES, dtype=F32),
            shaped(2 * model + 16, model),
        ),
        [SMEM] + [VMEM] * 7,
        (VMEM,) * 5,
        (core, in_weights, in_biases, gains, shifts, up, down, bias),
        cost=cost(4),
        room=ROOM,
    )


def count_of(ref, rows):
    return jnp.max(ref[rows : rows + 16, :LANES].astype(F32)).astype(jnp.int32)


def rows_at(start, rows, step=TILE):
    return pl.ds(pl.multiple_of(start, step), rows)


def attend_kernel(rows, groups, heads, *refs):
    near, far = refs[:groups], refs[groups]
    weights, biases, gains, shifts = refs[groups + 1 : groups + 5]
    at = groups + 5 + groups // 2
    out, give = refs[groups + 5 : at], refs[at]
    kept, counts, place = refs[at + 1 : at + 6], refs[at + 6], refs[at + 7]
    (xq, xk, qx, kx, vx), sems = refs[at + 8 : at + 13], refs[at + 13]
    model = xq.shape[1]
    q_counts = [count_of(r, rows) for r in near]
    k_counts = [count_of(far.at[g], rows) for g in range(groups)]
    for g in range(groups):
        counts[g] = q_counts[g]
        counts[groups + g] = k_counts[g]

    def compact(numbers, read, target):
        start = jnp.int32(0)
        for g, n in enumerate(numbers):
            target[rows_at(start, rows), :] = read(g)
            start = start + n * TILE
        target[rows_at(start, BLOCK), :] = jnp.zeros((BLOCK, model), BF)
        return start

    q_total = compact(q_counts, lambda g: near[g][:rows, :], xq)
    k_total = compact(k_counts, lambda g: far[g, :rows, :], xk)
    q_blocks = (q_total + BLOCK - 1) // BLOCK
    k_blocks = (k_total + BLOCK - 1) // BLOCK
    width = heads * LANES

    def hidden(ref, here):
        clean = standard(ref[here, :].astype(F32))[0].astype(BF)
        ref[here, :] = clean
        return (clean.astype(F32) * gains[0:1, :] + shifts[0:1, :]).astype(BF)

    @pl.loop(0, q_blocks)
    def _(b):
        here = rows_at(b * BLOCK, BLOCK, BLOCK)
        q = (dot(hidden(xq, here), weights[:, :width]) + biases[:, :width]).astype(BF)
        for h in range(heads):
            qx[h, here, :] = q[:, h * LANES : (h + 1) * LANES]

    @pl.loop(0, k_blocks)
    def _(b):
        here = rows_at(b * BLOCK, BLOCK, BLOCK)
        both = dot(hidden(xk, here), weights[:, width:]) + biases[:, width:]
        unseen = (iota((BLOCK, width), 0) + b * BLOCK >= k_total) & (
            iota((BLOCK, width), 1) % LANES == HD
        )
        k = jnp.where(unseen, FAR, both[:, :width]).astype(BF)
        v = both[:, width:].astype(BF)
        for h in range(heads):
            kx[h, here, :] = k[:, h * LANES : (h + 1) * LANES]
            vx[h, here, :] = v[:, h * LANES : (h + 1) * LANES]

    copies = [
        pltpu.make_async_copy(held, to, sems.at[i])
        for i, (held, to) in enumerate(zip((xq, xk, qx, kx, vx), kept))
    ]
    for copy in copies:
        copy.start()

    def attend_all(span):
        @pl.loop(0, q_blocks)
        def _(b):
            here = rows_at(b * BLOCK, BLOCK, BLOCK)
            lane = iota((BLOCK, LANES), 1)
            for h in range(heads):
                s = dot_nt(qx[h, here, :], kx[h, :span, :])
                top = jnp.max(s, axis=-1, keepdims=True)
                o = dot(jnp.exp(s - top).astype(BF), vx[h, :span, :])
                total = o[:, HD : HD + 1]
                o = o / total
                for i, piece in enumerate(pieces(top + jnp.log(total))):
                    o = jnp.where(lane == HD + i, piece.astype(F32), o)
                place[h, here, :] = o.astype(BF)

    for blocks in range(groups * TILE // BLOCK, groups * rows // BLOCK + 1):
        pl.when(k_blocks == blocks)(functools.partial(attend_all, blocks * BLOCK))

    gather = [
        (iota((LANES, LANES), 0) - HD + 3 * h == iota((LANES, LANES), 1))
        & (iota((LANES, LANES), 0) >= HD)
        & (iota((LANES, LANES), 0) < HD + 3)
        for h in range(heads)
    ]
    gather = [jnp.where(m, 1.0, 0.0).astype(BF) for m in gather]
    start = jnp.int32(0)
    for g in range(groups):
        mine = [place[h, rows_at(start, rows), :] for h in range(heads)]
        stats = sum(dot(m, s) for m, s in zip(mine, gather)).astype(BF)
        value = jnp.concatenate([m[:, :HD] for m in mine] + [stats], axis=1)
        if g < groups // 2:
            out[g][...] = value
        else:
            give[g - groups // 2] = value
        start = start + q_counts[g] * TILE
    for copy in copies:
        copy.wait()


def attend(near, far, weights, biases, gains, shifts, rows, heads):
    groups = len(near)
    model = near[0].shape[1]
    room = rows * groups + BLOCK
    parts = heads * HD + LANES
    kept = [(room, model)] * 2 + [(heads, room, LANES)] * 3
    return local_call(
        functools.partial(attend_kernel, rows, groups, heads),
        "attend",
        (
            *[shaped(rows, parts)] * (groups // 2),
            shaped(groups // 2, rows, parts),
            *[shaped(*k) for k in kept],
            shaped(2 * groups, dtype=jnp.int32),
        ),
        [VMEM] * (groups + 5),
        (*[VMEM] * (groups // 2 + 1), *[ANY] * 5, SMEM),
        (*near, far, weights, biases, gains, shifts),
        [
            pltpu.VMEM((heads, room, LANES), BF),
            *[pltpu.VMEM(k, BF) for k in kept],
            pltpu.SemaphoreType.DMA((5,)),
        ],
        cost(15),
        ROOM,
    )


def same_tile(rows):
    return iota((rows, rows), 0) // TILE == iota((rows, rows), 1) // TILE


def thumb_kernel(heads, tokens, weights, biases, gains, shifts, out, xhat, x):
    width = heads * LANES
    size = tokens.shape[0]
    clean = standard(tokens[...].astype(F32))[0].astype(BF)
    xhat[...] = clean
    hidden = (clean.astype(F32) * gains[0:1, :] + shifts[0:1, :]).astype(BF)
    x[...] = (dot(hidden, weights[...]) + biases[...]).astype(BF)
    visible = same_tile(size - TILE)
    out[:TILE, :] = jnp.zeros((TILE, heads * HD), F32)
    for h in range(heads):
        q = x[TILE:, h * LANES : (h + 1) * LANES]
        k = x[TILE:, width + h * LANES : width + (h + 1) * LANES]
        v = x[TILE:, 2 * width + h * LANES : 2 * width + (h + 1) * LANES]
        s = jnp.where(visible, dot_nt(q, k), FAR)
        e = jnp.exp(s - jnp.max(s, axis=-1, keepdims=True))
        o = dot(e.astype(BF), v)[:, :HD] / jnp.sum(e, axis=-1, keepdims=True)
        out[TILE:, h * HD : (h + 1) * HD] = o


def thumbs(tokens, weights, biases, gains, shifts, heads):
    size, model = tokens.shape
    return local_call(
        functools.partial(thumb_kernel, heads),
        "thumbs",
        (
            shaped(size, heads * HD, dtype=F32),
            shaped(size, model),
            shaped(size, 3 * heads * LANES),
        ),
        [VMEM] * 5,
        (VMEM,) * 3,
        (tokens, weights, biases, gains, shifts),
        cost=cost(5),
    )


def merged(parts, heads):
    cols = heads * HD
    row, col = (iota((LANES, cols), d) for d in (0, 1))
    spread = zero_one(row // 3 == col // HD)
    marks = [dot(p[:, cols:], spread) for p in parts]
    top = functools.reduce(jnp.maximum, marks)
    expos = [jnp.exp(m - top) for m in marks]
    total = sum(expos)
    mixed = sum(e * p[:, :cols].astype(F32) for p, e in zip(parts, expos)) / total
    row, col = (iota((cols, LANES), d) for d in (0, 1))
    packed = [
        dot(piece, zero_one((row % HD == 0) & (col == 3 * (row // HD) + i)))
        for i, piece in enumerate(pieces(top + jnp.log(total)))
    ]
    return mixed, sum(packed)


def pair_kernel(heads, *refs):
    count = (len(refs) - 1) // 2
    for j, (mine, out) in enumerate(zip(refs[:count], refs[count + 1 :])):
        mixed, marks = merged([mine[...], refs[count][j]], heads)
        out[...] = jnp.concatenate([mixed.astype(BF), marks.astype(BF)], axis=1)


def pair_merge(parts, other, heads):
    return local_call(
        functools.partial(pair_kernel, heads),
        "pair_merge",
        tuple(shaped(*p.shape) for p in parts),
        [VMEM] * (len(parts) + 1),
        (VMEM,) * len(parts),
        (*parts, other),
        cost=cost(3),
        room=ROOM,
    )


def merge_kernel(heads, counts, thumb, *refs):
    parts, (low, full, lse) = refs[:-3], refs[-3:]
    cols = heads * HD
    rows = lse.shape[0]
    mixed, marks = merged([p[...] for p in parts], heads)
    lse[...] = (-marks).astype(BF)
    image = iota((rows, cols), 0) < counts[0] * TILE
    full[:rows, :] = jnp.where(image, mixed, thumb[:rows, :])
    full[rows:, :] = thumb[rows:, :]
    low[...] = full[...].astype(BF)


def merge(count, parts, thumb, heads):
    size, cols = thumb.shape
    return local_call(
        functools.partial(merge_kernel, heads),
        "merge",
        (shaped(size, cols), shaped(size, cols, dtype=F32), shaped(parts[0].shape[0], LANES)),
        [SMEM] + [VMEM] * (1 + len(parts)),
        (VMEM,) * 3,
        (count, thumb, *parts),
        cost=cost(3),
    )


def fold_kernel(*refs):
    count = (len(refs) - 1) // 2
    for j, (mine, out) in enumerate(zip(refs[:count], refs[count + 1 :])):
        out[...] = (mine[...].astype(F32) + refs[count][j].astype(F32)).astype(BF)


def fold(parts, other):
    return local_call(
        fold_kernel,
        "fold",
        tuple(shaped(*p.shape) for p in parts),
        [VMEM] * (len(parts) + 1),
        (VMEM,) * len(parts),
        (*parts, other),
        cost=cost(2),
        room=ROOM,
    )


ROOT = 0.7978845608028654
CUBE = 0.044715


def ff_kernel(
    heads, tokens, outer, low, low_far, full, lse, out_weight, out_far, up, up_bias, down, far_one,
    far_two, gains, shifts, mixed, grad_mid, grad_low, packed, hidden_out, act_out, pre_out, small,
):
    size, model = tokens.shape
    passes = outer.shape[0]
    cols = heads * HD
    chunk = far_one.shape[1]
    units = up.shape[1]
    rows = packed.shape[0]
    branch = dot(low[...], out_weight[...]) + dot(low_far[...], out_far[...])
    middle = tokens[...].astype(F32) + (branch + shifts[1:2, :])
    xhat, factor = standard(middle)
    hidden = (xhat * gains[1:2, :] + shifts[2:3, :]).astype(BF)
    hidden_out[...] = hidden

    def one_chunk(up_part, bias, down_part, keep):
        v = dot(hidden, up_part) + bias
        t = jnp.tanh(ROOT * (v + CUBE * (v * v * v)))
        act = (0.5 * v * (1.0 + t)).astype(BF)
        slope = 0.5 * (1.0 + t) + 0.5 * v * (1.0 - t * t) * (ROOT * (1.0 + 3.0 * CUBE * (v * v)))
        two = []
        for p in range(passes):
            pre = (dot_nt(outer[p], down_part) * slope).astype(BF)
            if keep is not None:
                pre_out[p, :, keep] = pre
            two.append(dot_nt(pre, up_part))
        if keep is not None:
            act_out[:, keep] = act
        return dot(act, down_part), two

    def far_chunk(ref):
        told = ref[2 * chunk : 2 * chunk + 16, :].astype(F32)
        bias = told[0:1] + told[1:2] + told[2:3]
        return one_chunk(ref[:chunk, :], bias, ref[chunk : 2 * chunk, :], None)

    done = []
    for i in range(units // chunk):
        at = slice(i * chunk, (i + 1) * chunk)
        done.append(one_chunk(up[:, at], up_bias[:, at], down[at, :], at))
    done += [far_chunk(far_one), far_chunk(far_two)]

    def tree(parts):
        half = len(parts) // 2
        return sum(parts[:half]) + sum(parts[half:])

    output = tree([d[0] for d in done])
    mixed[...] = (middle + (output + shifts[3:4, :])).astype(BF)
    small[...] = jnp.zeros(small.shape, F32)
    lane = iota((rows, LANES), 1)
    stats = jnp.zeros((rows, LANES), F32)
    for p in range(passes):
        two = tree([d[1][p] for d in done])
        c = outer[p].astype(F32)
        mid = c + norm_back(two, gains[1:2, :], xhat, factor)
        mid_low = mid.astype(BF)
        grad_mid[p] = mid
        grad_low[p] = mid_low
        att = dot_nt(mid_low, out_weight[...]).astype(BF)
        packed[:, p * cols : (p + 1) * cols] = att[:rows, :]
        pre_out_p = pre_out[p].astype(F32)
        bias = jnp.sum(pre_out_p, axis=0, keepdims=True)
        small[p, 0:1, :] = jnp.sum(two * xhat, axis=0, keepdims=True)
        small[p, 1:2, :] = jnp.sum(two, axis=0, keepdims=True)
        small[p, 2:3, :] = jnp.sum(mid_low.astype(F32), axis=0, keepdims=True)
        small[p, 3:4, :] = jnp.sum(c, axis=0, keepdims=True)
        for i in range(units // model):
            small[p, 4 + i : 5 + i, :] = bias[:, i * model : (i + 1) * model]
        product = att[:rows, :].astype(F32) * full[:rows, :]
        for h in range(heads):
            delta = jnp.sum(product[:, h * HD : (h + 1) * HD], axis=-1, keepdims=True)
            for i, piece in enumerate(pieces(-delta)):
                stats = jnp.where(lane == 3 * heads * (p + 1) + 3 * h + i, piece.astype(F32), stats)
    packed[:, passes * cols :] = (stats + lse[...].astype(F32)).astype(BF)


def feed_forward(
    tokens, outer, low, low_far, full, lse, out_weight, out_far, up, up_bias, down, far_one, far_two,
    gains, shifts, rows, heads,
):
    size, model = tokens.shape
    passes = outer.shape[0]
    units = up.shape[1]
    return local_call(
        functools.partial(ff_kernel, heads),
        "feed_forward",
        (
            shaped(size, model),
            shaped(passes, size, model, dtype=F32),
            shaped(passes, size, model),
            shaped(rows, passes * heads * HD + LANES),
            shaped(size, model),
            shaped(size, units),
            shaped(passes, size, units),
            shaped(passes, 8, model, dtype=F32),
        ),
        [VMEM] * 15,
        (VMEM,) * 8,
        (
            tokens, outer, low, low_far, full, lse, out_weight, out_far, up, up_bias, down, far_one,
            far_two, gains, shifts,
        ),
        cost=cost(12),
        room=32,
    )


def thumb_back_kernel(heads, counts, x, mid_low, out_weight, out):
    width = heads * LANES
    size = x.shape[0]
    passes = mid_low.shape[0]
    visible = same_tile(size - TILE)
    outside = iota((size - TILE, HD), 0) + TILE >= counts[0] * TILE
    grads = [dot_nt(mid_low[p], out_weight[...]).astype(BF) for p in range(passes)]
    out[:, :, :TILE, :] = jnp.zeros((*out.shape[:2], TILE, out.shape[3]), BF)
    for h in range(heads):
        q = x[TILE:, h * LANES : (h + 1) * LANES]
        k = x[TILE:, width + h * LANES : width + (h + 1) * LANES]
        v = x[TILE:, 2 * width + h * LANES : 2 * width + h * LANES + HD]
        s = jnp.where(visible, dot_nt(q, k), FAR)
        e = jnp.exp(s - jnp.max(s, axis=-1, keepdims=True))
        w = e / jnp.sum(e, axis=-1, keepdims=True)
        w_low = w.astype(BF)
        for p in range(passes):
            g = grads[p][TILE:, h * HD : (h + 1) * HD]
            gw = dot_nt(g, v)
            ds = (w * (gw - jnp.sum(w * gw, axis=-1, keepdims=True))).astype(BF)
            dq = dot(ds, k[:, :HD]) * SCALE
            dk = dot_tn(ds, q)[:, :HD]
            dv = dot_tn(w_low, g)
            for c, piece in enumerate((dq, dk, dv)):
                at = c * LANES + (h % 2) * HD
                out[h // 2, p, TILE:, at : at + HD] = jnp.where(outside, piece, 0.0).astype(BF)


def thumbs_back(count, x, mid_low, out_weight, heads):
    passes, size, _ = mid_low.shape
    return local_call(
        functools.partial(thumb_back_kernel, heads),
        "thumbs_back",
        shaped(heads // 2, passes, size, 3 * LANES),
        [SMEM] + [VMEM] * 3,
        VMEM,
        (count, x, mid_low, out_weight),
        cost=cost(6),
    )


def early_at(units, model, low):
    ends = [model, 2 * model, 2 * model + units, 2 * model + units + low]
    return [slice(b - w, b) for b, w in zip(ends, (model, model, units, low))]


def early_cuts(parts, units, model, low):
    high, wide, turns = units // parts // 2, model // parts, model // low
    narrow = low * turns // parts
    for i in range(parts):
        yield (
            (slice(2 * i * high, (2 * i + 1) * high), slice(0, model)),
            (slice((2 * i + 1) * high, (2 * i + 2) * high), slice(0, model)),
            (slice(i * wide, (i + 1) * wide), slice(0, units)),
            (
                slice(i // turns * narrow, (i // turns + 1) * narrow),
                slice(i % turns * low, (i % turns + 1) * low),
            ),
        )


def weight_kernel(place, act, outer, hidden, pre, low, mid_low, keep, give):
    units, model, cols = act.shape[1], hidden.shape[1], low.shape[1]
    core = place[0]
    for turn, out in ((core, keep), (1 - core, give)):
        down = dot_tn(act[...], outer[turn]).astype(BF)
        up = dot_tn(hidden[...], pre[turn]).astype(BF)
        proj = dot_tn(low[...], mid_low[turn]).astype(BF)
        for i, cut in enumerate(early_cuts(keep.shape[0], units, model, cols)):
            for value, (rows, lanes), at in zip(
                (down, down, up, proj), cut, early_at(units, model, cols)
            ):
                out[i, :, at] = value[rows, lanes]


def weight_grads(core, act, outer, hidden, pre, low, mid_low, parts):
    units, model = act.shape[1], outer.shape[2]
    out = shaped(parts, model // parts, 2 * model + units + low.shape[1])
    return local_call(
        weight_kernel,
        "weight_grads",
        (out, out),
        [SMEM] + [VMEM] * 6,
        (VMEM,) * 2,
        (core, act, outer, hidden, pre, low, mid_low),
        cost=cost(8),
        room=24,
    )


def reverse_kernel(rows, groups, heads, passes, counts, place, *refs):
    grads, kept = refs[:groups], refs[groups : groups + 5]
    own, thumb, weights, columns, small = refs[groups + 5 : groups + 10]
    at = groups + 10
    out_q, give_q, at = refs[at : at + groups // 2], refs[at + groups // 2], at + groups // 2 + 1
    out_kv, at = refs[at : at + groups // 2], at + groups // 2
    keep, give = refs[at : at + 2]
    (
        stage, xq, xk, qx, kx, vx, packed, gx, kt, dq_t, dv, dk, low_q, low_kv, total, sums,
        starts, sems,
    ) = refs[at + 2 :]
    couples = heads // 2
    sources = [*grads, *kept[2:], *kept[:2]]
    targets = [*[stage.at[g] for g in range(groups)], qx, kx, vx, xq, xk]
    copies = [
        pltpu.make_async_copy(f, t, sems.at[i]) for i, (f, t) in enumerate(zip(sources, targets))
    ]
    for copy in copies:
        copy.start()
    cols = heads * HD
    wide = passes * LANES
    q_counts = [counts[g] for g in range(groups)]
    k_counts = [counts[groups + g] for g in range(groups)]
    start = jnp.int32(0)
    for g in range(groups):
        copies[g].wait()
        packed[rows_at(start, rows), :] = stage[g]
        start = start + q_counts[g] * TILE
    q_total, k_total = start, sum(k_counts) * TILE
    tail_lane = iota((BLOCK, packed.shape[1]), 1) - passes * cols
    empty = (tail_lane >= 0) & (tail_lane < 3 * heads) & (tail_lane % 3 == 0)
    packed[rows_at(q_total, BLOCK), :] = jnp.where(empty, FAR, 0.0).astype(BF)
    q_blocks = (q_total + BLOCK - 1) // BLOCK
    k_blocks = (k_total + BLOCK - 1) // BLOCK
    spans = range(groups * TILE // BLOCK, groups * rows // BLOCK + 1)

    row, col = (iota((LANES, heads * LANES), d) for d in (0, 1))
    head, lane = col // LANES, col % LANES
    to_marks = zero_one((lane > HD) & (lane < HD + 4) & (row == 3 * head + lane - HD - 1))
    row, col = (iota((LANES, heads * wide), d) for d in (0, 1))
    head, turn, lane = col // wide, col % wide // LANES, col % LANES
    to_deltas = zero_one(
        (lane >= HD) & (lane < HD + 3) & (row == 3 * heads * (turn + 1) + 3 * head + lane - HD)
    )
    for copy in copies[groups : groups + 3]:
        copy.wait()

    @pl.loop(0, q_blocks)
    def _(b):
        here = rows_at(b * BLOCK, BLOCK, BLOCK)
        stats = packed[here, passes * cols :]
        marks = dot(stats, to_marks)
        deltas = dot(stats, to_deltas).astype(BF)
        for h in range(heads):
            more = marks[:, h * LANES : (h + 1) * LANES]
            qx[h, here, :] = (qx[h, here, :].astype(F32) + more).astype(BF)
            for p in range(passes):
                at = p * cols + h * HD
                mine = (h * passes + p) * LANES
                gx[h, here, p * LANES : (p + 1) * LANES] = jnp.concatenate(
                    [packed[here, at : at + HD], deltas[:, mine + HD : mine + LANES]], axis=1
                )

    @pl.loop(0, k_blocks)
    def _(b):
        here = rows_at(b * BLOCK, BLOCK, BLOCK)
        for h in range(heads):
            kt[h, b] = jnp.transpose(kx[h, here, :].astype(F32))[:HD, :].astype(BF)

    def reverse_all(blocks):
        span = blocks * BLOCK

        @pl.loop(0, couples)
        def _(pair):
            dv[:, :span, :] = jnp.zeros((2, span, wide), F32)
            dk[:, :, :span, :] = jnp.zeros((passes, 2, span, LANES), F32)

            @pl.loop(0, q_blocks)
            def _(b):
                here = rows_at(b * BLOCK, BLOCK, BLOCK)
                for i in range(2):
                    h = 2 * pair + i
                    q, g = qx[h, here, :], gx[h, here, :]
                    k_t = jnp.concatenate([kt[h, j] for j in range(blocks)], axis=1)
                    w = jnp.exp(dot_nt(kx[h, :span, :], q))
                    dv[i, :span, :] += dot(w.astype(BF), g)
                    for p in range(passes):
                        ds = dot_nt(vx[h, :span, :], g[:, p * LANES : (p + 1) * LANES])
                        ds = (w * ds).astype(BF)
                        dk[p, i, :span, :] += dot(ds, q)
                        dq_t[p, i * HD : (i + 1) * HD, :] = dot(k_t, ds)
                for p in range(passes):
                    piece = jnp.transpose(dq_t[p]) * SCALE
                    low_q[pair, here, p * LANES : (p + 1) * LANES] = piece.astype(BF)

            for p in range(passes):
                for c, both in enumerate(
                    (
                        [dk[p, i, :span, :HD] for i in range(2)],
                        [dv[i, :span, p * LANES : p * LANES + HD] for i in range(2)],
                    )
                ):
                    lane = (2 * p + c) * LANES
                    low_kv[pair, :span, lane : lane + LANES] = jnp.concatenate(both, axis=1).astype(BF)

    for blocks in spans:
        pl.when(k_blocks == blocks)(functools.partial(reverse_all, blocks))

    start = jnp.int32(0)
    for g in range(groups):
        starts[g] = start
        start = start + k_counts[g] * TILE
    for g in range(groups):
        here = rows_at(starts[place[1 + g]], rows)
        out_kv[g // 2][g % 2] = jnp.concatenate([low_kv[i, here, :] for i in range(couples)], axis=1)
    start = jnp.int32(0)
    for g in range(groups):
        here = rows_at(start, rows)
        value = jnp.concatenate([low_q[i, here, :] for i in range(couples)], axis=1)
        if g < groups // 2:
            out_q[g][...] = value
        else:
            give_q[g - groups // 2] = value
        start = start + q_counts[g] * TILE

    copies[groups + 3].wait()
    copies[groups + 4].wait()

    def key_sums(blocks):
        span = blocks * BLOCK
        for i in range(couples):
            flat = low_kv[i, :span, :]
            total[i, :, wide:] = dot_tn(xk[:span, :], flat)
            sums[i, :, wide:] = dot(jnp.ones((8, span), BF), flat)

    for blocks in spans:
        pl.when(k_blocks == blocks)(functools.partial(key_sums, blocks))

    total[:, :, :wide] = jnp.zeros((couples, total.shape[1], wide), F32)
    sums[:, :, :wide] = jnp.zeros((couples, 8, wide), F32)

    @pl.loop(0, q_blocks)
    def _(b):
        here = rows_at(b * BLOCK, BLOCK, BLOCK)
        for i in range(couples):
            total[i, :, :wide] += dot_tn(xq[here, :], low_q[i, here, :])
            sums[i, :, :wide] += dot(jnp.ones((8, BLOCK), BF), low_q[i, here, :])

    model = total.shape[1]
    gain, shift = columns[:, 0:1], columns[:, 1:2]
    ones = jnp.ones((8, own.shape[0]), BF)
    for p in range(passes):
        whole = []
        for i in range(couples):
            mine = thumb[i, p]
            part = dot_tn(own[...], mine)
            part_sum = dot(ones, mine)[0:1, :]
            q_at = slice(p * LANES, (p + 1) * LANES)
            kv_at = slice((passes + 2 * p) * LANES, (passes + 2 * p + 2) * LANES)
            part += jnp.concatenate([total[i, :, q_at], total[i, :, kv_at]], axis=1)
            part_sum += jnp.concatenate([sums[i, 0:1, q_at], sums[i, 0:1, kv_at]], axis=1)
            w = weights[i].astype(F32)
            gain_one = jnp.sum(w * part, axis=1, keepdims=True)
            shift_one = jnp.sum(w * part_sum, axis=1, keepdims=True)
            lane = iota((model, LANES), 1)
            tall = jnp.where(lane == 0, gain_one, jnp.where(lane == 1, shift_one, 0.0))
            flat = jnp.concatenate(
                [jnp.zeros((2, LANES), F32)]
                + [part_sum[:, c * LANES : (c + 1) * LANES] for c in range(3)]
                + [jnp.zeros((LANES - 5, LANES), F32)],
                axis=0,
            )
            tall = jnp.concatenate([tall[:LANES] + jnp.transpose(flat), tall[LANES:]], axis=0)
            if i == 0:
                turned = jnp.concatenate(
                    [
                        jnp.zeros((8, model), F32),
                        small[p],
                        jnp.zeros((LANES - 16, model), F32),
                    ],
                    axis=0,
                )
                tall = tall + jnp.transpose(turned)
            whole += [part * gain + shift * part_sum, tall]
        whole = jnp.concatenate(whole, axis=1).astype(BF)

        @pl.when(place[0] == p)
        def _():
            keep[...] = whole

        @pl.when(place[0] != p)
        def _():
            give[...] = whole


def reverse(counts, place, grads, kept, own, thumb, weights, columns, small, rows, heads):
    groups = len(grads)
    couples, passes = thumb.shape[:2]
    model = own.shape[1]
    room = rows * groups + BLOCK
    cols = heads * HD
    wide = passes * LANES
    half = groups // 2
    late = shaped(model, couples * 4 * LANES)
    q, kv = shaped(rows, couples * wide), shaped(2, rows, couples * 2 * wide)
    out = (*[q] * half, shaped(half, rows, couples * wide), *[kv] * half, late, late)
    return local_call(
        functools.partial(reverse_kernel, rows, groups, heads, passes),
        "reverse",
        out,
        [SMEM, SMEM] + [ANY] * (groups + 5) + [VMEM] * 5,
        (VMEM,) * len(out),
        (counts, place, *grads, *kept, own, thumb, weights, columns, small),
        [
            pltpu.VMEM((groups, rows, passes * cols + LANES), BF),
            pltpu.VMEM((room, model), BF),
            pltpu.VMEM((room, model), BF),
            pltpu.VMEM((heads, room, LANES), BF),
            pltpu.VMEM((heads, room, LANES), BF),
            pltpu.VMEM((heads, room, LANES), BF),
            pltpu.VMEM((room, passes * cols + LANES), BF),
            pltpu.VMEM((heads, room, wide), BF),
            pltpu.VMEM((heads, room // BLOCK, HD, BLOCK), BF),
            pltpu.VMEM((passes, LANES, BLOCK), F32),
            pltpu.VMEM((2, room, wide), F32),
            pltpu.VMEM((passes, 2, room, LANES), F32),
            pltpu.VMEM((couples, room, wide), BF),
            pltpu.VMEM((couples, room, 2 * wide), BF),
            pltpu.VMEM((couples, model, 3 * wide), F32),
            pltpu.VMEM((couples, 8, 3 * wide), F32),
            pltpu.SMEM((groups,), jnp.int32),
            pltpu.SemaphoreType.DMA((groups + 5,)),
        ],
        cost(45),
        ROOM,
    )


def grad_one_kernel(near, counts, *refs):
    from_q, from_kv, (thumb, weights, mine, other) = refs[:near], refs[near:-4], refs[-4:]
    couples, passes, size, _ = thumb.shape
    rows = from_q[0].shape[0]
    sum_q = sum(r[...].astype(F32) for r in from_q)
    sum_kv = [sum(r[f].astype(F32) for r in from_kv) for f in range(2)]
    image = iota((rows, 3 * LANES), 0) < counts[0] * TILE
    for p in range(passes):
        parts = []
        for i in range(couples):
            at = (passes * i + p) * LANES
            there = slice(2 * at, 2 * at + 2 * LANES)
            far = jnp.concatenate([sum_q[:, at : at + LANES], sum_kv[0][:, there]], axis=1)
            flat = jnp.concatenate(
                [jnp.where(image, far.astype(BF), thumb[i, p, :rows]), thumb[i, p, rows:]], axis=0
            )
            parts.append(
                (
                    dot_nt(flat, weights[i]),
                    dot_nt(sum_kv[1][:, there].astype(BF), weights[i, :, LANES:]),
                )
            )
        mine[p] = sum(a for a, _ in parts).astype(BF)
        other[p] = sum(b for _, b in parts).astype(BF)


def grad_one(count, from_q, from_kv, thumb, weights):
    near = len(from_q)
    passes, size, _ = thumb.shape[1:]
    model = weights.shape[1]
    return local_call(
        functools.partial(grad_one_kernel, near),
        "grad_one",
        (shaped(passes, size, model), shaped(passes, from_q[0].shape[0], model)),
        [SMEM] + [VMEM] * (near + len(from_kv) + 2),
        (VMEM,) * 2,
        (count, *from_q, *from_kv, thumb, weights),
        cost=cost(5),
        room=ROOM,
    )


def close_kernel(counts, tokens, mid, mine, head, side, cross, gains, out):
    xhat, factor = standard(tokens[...].astype(F32))
    rows = side.shape[1]
    image = iota(side.shape[1:], 0) < counts[0] * TILE
    for p in range(mid.shape[0]):
        grad = mine[p].astype(F32) + head[p].astype(F32)
        more = jnp.where(image, side[p].astype(F32) + cross[p].astype(F32), 0.0)
        grad = jnp.concatenate([grad[:rows] + more, grad[rows:]], axis=0)
        out[p] = mid[p] + norm_back(grad, gains[0:1, :], xhat, factor)


def close(count, tokens, mid, mine, head, side, cross, gains):
    return local_call(
        close_kernel,
        "close",
        shaped(*mid.shape, dtype=F32),
        [SMEM] + [VMEM] * 7,
        VMEM,
        (count, tokens, mid, mine, head, side, cross, gains),
        cost=cost(4),
        room=ROOM,
    )


def early_kernel(lines, place, *refs):
    own, far, (down, up, proj) = refs[:lines], refs[lines : 2 * lines], refs[2 * lines :]
    core, z, y = place[0], place[9], place[10]
    (units, model), low = down.shape[1:], proj.shape[1]
    steps, rows = own[0].shape[:2]
    lane_down, lane_next, lane_up, lane_proj = early_at(units, model, low)
    turns = model // low
    for out, parts in ((core, own), (1 - core, far)):
        for d, ref in enumerate(parts):
            for j in range(steps):
                i = (z + steps - j) % steps * lines + (y + lines - d) % lines
                at = pl.multiple_of(2 * rows * i, 2 * rows)
                down[out, pl.ds(at, rows), :] = ref[j, :, lane_down].astype(F32)
                down[out, pl.ds(at + rows, rows), :] = ref[j, :, lane_next].astype(F32)
                up[out, rows_at(rows * i, rows, rows), :] = ref[j, :, lane_up].astype(F32)
                here = rows_at(i // turns * rows, rows, rows)
                value = ref[j, :, lane_proj].astype(F32)
                for t in range(turns):

                    @pl.when(i % turns == t)
                    def _(value=value, here=here, t=t):
                        proj[out, here, t * low : (t + 1) * low] = value


def early_out(place, own, far, units, low):
    model = len(own) * own[0].shape[0] * own[0].shape[1]
    return local_call(
        functools.partial(early_kernel, len(own)),
        "early_out",
        (
            shaped(2, units, model, dtype=F32),
            shaped(2, model, units, dtype=F32),
            shaped(2, low, model, dtype=F32),
        ),
        [SMEM] + [VMEM] * (2 * len(own)),
        (VMEM,) * 3,
        (place, *own, *far),
        cost=cost(8),
        room=ROOM,
    )


def late_kernel(place, own, far, grad_in, in_bias, up_bias, gains, shifts):
    core = place[0]
    for turn, ref in ((core, own), (1 - core, far)):
        turned = []
        for pair in range(2):
            at = 4 * LANES * pair
            for c in range(3):
                grad_in[turn, c, :, pair * LANES : (pair + 1) * LANES] = ref[
                    :, at + c * LANES : at + (c + 1) * LANES
                ].astype(F32)
            turned.append(jnp.transpose(ref[:, at + 3 * LANES : at + 4 * LANES].astype(F32)))
        a, b = turned
        in_bias[turn] = jnp.concatenate(
            [
                jnp.concatenate([a[2:3, :LANES], b[2:3, :LANES]], axis=1),
                jnp.concatenate([a[4:5, :LANES], b[4:5, :LANES]], axis=1),
            ],
            axis=0,
        )
        up_bias[turn] = jnp.concatenate([a[12:13], a[13:14]], axis=1)
        gains[turn] = jnp.concatenate([a[0:1] + b[0:1], a[8:9]], axis=0)
        shifts[turn] = jnp.concatenate([a[1:2] + b[1:2], a[10:11], a[9:10], a[11:12]], axis=0)


def late_out(core, own, far, units):
    model = own.shape[0]
    return local_call(
        late_kernel,
        "late_out",
        (
            shaped(2, 3, model, 2 * LANES, dtype=F32),
            shaped(2, 2, 2 * LANES, dtype=F32),
            shaped(2, 1, units, dtype=F32),
            shaped(2, 2, model, dtype=F32),
            shaped(2, 4, model, dtype=F32),
        ),
        [SMEM] + [VMEM] * 2,
        (VMEM,) * 5,
        (core, own, far),
        cost=cost(4),
        room=ROOM,
    )


def gather_near(array):
    mine = [array] + [shift_by(array, "y", d) for d in range(1, lax.axis_size("y"))]
    return mine + [shift_by(a, "c", 1) for a in mine]


def return_near(parts):
    return [parts[0]] + [shift_by(p, "y", -j) for j, p in enumerate(parts) if j > 0]


def offsets(size):
    return [(step, flip) for step in range(size) for flip in range(2)]


def return_far(parts):
    return [parts[0]] + [shift_by(p, "z", step) for step, p in enumerate(parts) if step > 0]


PLANE = ("z", "y")


def core_sum(keep, give):
    return (keep.astype(F32) + shift_by(give, "c", 1).astype(F32)).astype(BF)


def crossed(array):
    n = lax.axis_size(("xl", "h"))
    return lax.ppermute(array, ("xl", "h"), [(i, n - 1 - i) for i in range(n)])


def across(low):
    done = low.astype(F32) + shift_by(low, "xl", 1).astype(F32)
    size = 4 * LANES
    ones = jnp.concatenate([low[:, i + 3 * LANES : i + size] for i in range(0, low.shape[1], size)], axis=1)
    more = shift_by(ones, "h", 1).astype(F32) + crossed(ones).astype(F32)
    more = jnp.where(jnp.arange(more.shape[1]) % LANES < 2, more, 0.0)
    nothing = jnp.zeros((low.shape[0], 3 * LANES), F32)
    laid = [[nothing, more[:, i : i + LANES]] for i in range(0, more.shape[1], LANES)]
    return (done + jnp.concatenate(sum(laid, []), axis=1)).astype(BF)


def tied(arrays, others):
    return lax.optimization_barrier((arrays, others))


def local(
    tokens,
    cotangents,
    segment_ids,
    in_weights,
    in_biases,
    out_weight,
    up_weight,
    up_biases,
    down_weight,
    gains,
    shifts,
):
    size, model = tokens.shape
    cols = in_weights.shape[2]
    heads = cols // HD
    rows = size - TILE
    units = up_weight.shape[1]
    c = lax.axis_index("c")

    told, copies, count = front(tokens, segment_ids, lax.axis_size(("z", "xl")))
    far = lax.all_to_all(copies, ("z", "xl"), 0, 0, tiled=True)
    near = gather_near(told)
    core = c.astype(jnp.int32).reshape(1)
    z, xl, z_size = lax.axis_index("z"), lax.axis_index("xl"), lax.axis_size("z")
    routes = [((z + step) % z_size) * 2 + (xl ^ flip) for step, flip in offsets(z_size)]
    place = jnp.stack([c, *routes, z, lax.axis_index("y")]).astype(jnp.int32)
    plane = lax.axis_size(PLANE)

    weights, biases, pairs, columns, bundle = prepare(
        core, in_weights, in_biases, gains, shifts, up_weight, down_weight, up_biases[None], heads
    )
    out_far = crossed(out_weight)
    far_one = crossed(bundle)
    far_two = shift_by(far_one, "c", 1)

    *parts, give, xq, xk, qx, kx, vx, counts = attend(
        near, far, weights, biases, gains, shifts, rows, heads
    )
    thumb_out, xhat, x = thumbs(tokens, weights, biases, gains, shifts, heads)
    parts = pair_merge(parts, shift_by(give, "c", 1), heads)
    low, full, lse = merge(count, return_near(parts), thumb_out, heads)
    low_far = shift_by(low, "h", 1)
    mixed, grad_mid, mid_low, packed, hidden, act, pre, small = feed_forward(
        tokens, cotangents, low, low_far, full, lse, out_weight, out_far, up_weight, up_biases[None],
        down_weight, far_one, far_two, gains, shifts, rows, heads,
    )
    grads = gather_near(packed)
    keep, give = weight_grads(core, act, cotangents, hidden, pre, low, mid_low, plane)
    mid_low, (keep, give) = tied(mid_low, (keep, give))
    thumb = thumbs_back(count, x, mid_low, out_weight, heads)
    early = core_sum(keep, give)

    grads, (early, thumb) = tied(grads, (early, thumb))
    early = lax.all_to_all(early, PLANE, 0, 0, tiled=True)
    *out, keep, give = reverse(
        counts, place, grads, (xq, xk, qx, kx, vx), xhat, thumb, pairs, columns, small, rows, heads
    )
    half = len(near) // 2
    out_q, give_q, out_kv = out[:half], out[half], out[half + 1 :]
    early = jnp.sum(early.astype(F32), axis=0).astype(BF)
    early_side = shift_by(early, "xl", 1)
    late, early_side = tied(core_sum(keep, give), early_side)
    late = late.reshape(plane, -1, late.shape[1])
    late = lax.all_to_all(late, PLANE, 0, 0, tiled=True)
    from_kv = return_far(out_kv)
    from_q = return_near(fold(out_q, shift_by(give_q, "c", 1)))

    early = (early.astype(F32) + early_side.astype(F32)).astype(BF)
    early = jnp.stack([early] + [shift_by(early, "z", d) for d in range(1, z_size)])
    late, early = tied(late, early)
    early = [early] + [shift_by(early, "y", d) for d in range(1, lax.axis_size("y"))]
    late = across(jnp.sum(late.astype(F32), axis=0).astype(BF))
    late, (from_kv, early[1]) = tied(late, (from_kv, early[1]))
    late = jnp.broadcast_to(late[None], (plane, *late.shape))
    late = lax.all_to_all(late, PLANE, 0, 0, tiled=True).reshape(model, -1)

    mine, other = grad_one(count, from_q, from_kv, thumb, pairs)
    grad_tokens = close(
        count, tokens, grad_mid, mine, shift_by(mine, "h", 1), shift_by(other, "xl", 1),
        crossed(other), gains,
    )
    early_far = [shift_by(e, "c", 1) for e in early]
    grad_down, grad_up, grad_out = early_out(place, early, early_far, units, cols)
    grad_in, in_bias, up_bias, grad_gains, grad_shifts = late_out(
        core, late, shift_by(late, "c", 1), units
    )
    return (
        mixed,
        grad_tokens,
        grad_in,
        in_bias,
        grad_out,
        grad_up,
        up_bias.reshape(2, units),
        grad_down,
        grad_gains,
        grad_shifts,
    )


def solution(mesh):
    fine = Mesh(mesh.devices.reshape(4, 2, 4, 2, 2), ("z", "xl", "y", "c", "h"))
    blk = ("z", "xl", "y", "c")
    return jax.shard_map(
        local,
        mesh=fine,
        in_specs=(
            P(blk, None),
            P(None, blk, None),
            P(blk),
            P(None, None, "h"),
            P(None, "h"),
            P("h", None),
            P(None, "h"),
            P("h"),
            P("h", None),
            P(),
            P(),
        ),
        out_specs=(
            P(blk, None),
            P(None, blk, None),
            P(None, None, None, "h"),
            P(None, None, "h"),
            P(None, "h", None),
            P(None, None, "h"),
            P(None, "h"),
            P(None, "h", None),
            P(),
            P(),
        ),
        check_vma=False,
    )
```

```python
import functools

import jax
import jax.numpy as jnp
from jax import lax
from jax.experimental import pallas as pl
from jax.experimental.pallas import tpu as pltpu
from jax.sharding import Mesh
from jax.sharding import PartitionSpec as P

HD = 64
LANES = 128
TILE = 64
BLOCK = 256
EPS = 1e-06
SCALE = 0.125
FAR = -1e30
BF = jnp.bfloat16
F32 = jnp.float32
MIB = 1024 * 1024
ROOM = 56

NT = (((1,), (1,)), ((), ()))
TN = (((0,), (0,)), ((), ()))


def shift_by(array, axis, step):
    size = lax.axis_size(axis)
    return lax.ppermute(array, axis, [(i, (i + step) % size) for i in range(size)])


def dot(a, b):
    return jnp.dot(a, b, preferred_element_type=F32)


def dot_nt(a, b):
    return lax.dot_general(a, b, NT, preferred_element_type=F32)


def dot_tn(a, b):
    return lax.dot_general(a, b, TN, preferred_element_type=F32)


def standard(field):
    center = field - jnp.mean(field, axis=-1, keepdims=True)
    factor = lax.rsqrt(jnp.mean(center * center, axis=-1, keepdims=True) + EPS)
    return center * factor, factor


def norm_back(grad, gain, xhat, factor):
    h = grad * gain
    mean = jnp.mean(h, axis=-1, keepdims=True)
    return factor * (h - mean - xhat * jnp.mean(h * xhat, axis=-1, keepdims=True))


def pieces(value):
    high = value.astype(BF)
    rest = value - high.astype(F32)
    middle = rest.astype(BF)
    low = (rest - middle.astype(F32)).astype(BF)
    return high, middle, low


def zero_one(mask):
    return jnp.where(mask, 1.0, 0.0).astype(BF)


def iota(shape, dim):
    return lax.broadcasted_iota(jnp.int32, shape, dim)


VMEM = pl.BlockSpec(memory_space=pltpu.VMEM)
ANY = pl.BlockSpec(memory_space=pl.ANY)
SMEM = pl.BlockSpec(memory_space=pltpu.SMEM)


def local_call(body, name, out, ins, outs, args, scratch=(), cost=None, room=16):
    return pl.pallas_call(
        body,
        out_shape=out,
        in_specs=ins,
        out_specs=outs,
        scratch_shapes=scratch,
        cost_estimate=cost,
        compiler_params=pltpu.CompilerParams(vmem_limit_bytes=room * MIB),
        name=name,
    )(*args)


def shaped(*shape, dtype=BF):
    return jax.ShapeDtypeStruct(shape, dtype)


def cost(micros):
    return pl.CostEstimate(flops=int(micros * 1e9), bytes_accessed=0, transcendentals=0)


def front_kernel(tokens, ids, told, copies, number):
    rows = told.shape[0] - 16
    marks = jnp.where(ids[...] == 0, 1.0, 0.0)
    tiles = jnp.sum(marks).astype(jnp.int32) // TILE
    number[0] = tiles
    told[:rows, :] = tokens[:rows, :]
    told[rows:, :] = jnp.full((16, told.shape[1]), tiles.astype(F32), F32).astype(BF)
    for g in range(copies.shape[0]):
        copies[g] = told[...]


def front(tokens, ids, copies):
    size, model = tokens.shape
    told = size - TILE + 16
    return local_call(
        front_kernel,
        "front",
        (shaped(told, model), shaped(copies, told, model), shaped(1, dtype=jnp.int32)),
        [VMEM, VMEM],
        (VMEM, VMEM, SMEM),
        (tokens, ids.reshape(-1, LANES)),
        room=ROOM,
    )


def prepare_kernel(
    heads, place, in_weights, in_biases, gains, shifts, up, down, bias,
    weights, biases, pairs, columns, out,
):
    core = place[0]
    half = out.shape[1]
    at = pl.ds(pl.multiple_of(core * half, half), half)
    out[:half, :] = up[:, at]
    out[half : 2 * half, :] = down[at, :]
    mine = jnp.where(core == 0, bias[:, :half], bias[:, half:])
    row = iota((16, half), 0)
    rows = jnp.zeros((16, half), F32)
    for i, piece in enumerate(pieces(mine)):
        rows = jnp.where(row == i, piece.astype(F32), rows)
    out[2 * half :, :] = rows.astype(BF)

    model, cols = in_weights.shape[1:]
    width = heads * LANES
    row, col = (iota((cols, width), d) for d in (0, 1))
    spread = zero_one((row // HD == col // LANES) & (row % HD == col % LANES))
    lane = iota((1, width), 1) % LANES
    gap = jnp.zeros((1, HD), F32)

    def apart(line):
        return jnp.concatenate(
            sum([[line[:, h * HD : (h + 1) * HD], gap] for h in range(heads)], []), axis=1
        )

    extra = [
        apart(in_biases[0:1, :] * SCALE) + jnp.where(lane == HD, 1.0, 0.0),
        jnp.where((lane > HD) & (lane < HD + 4), 1.0, 0.0),
        apart(in_biases[1:2, :]) + jnp.where((lane >= HD) & (lane < HD + 3), 1.0, 0.0),
    ]
    for i in range(3):
        factor = SCALE if i == 0 else 1.0
        weights[:, i * width : (i + 1) * width] = (dot(in_weights[i], spread) * factor).astype(BF)
        biases[:, i * width : (i + 1) * width] = extra[i]
        for pair in range(heads // 2):
            pairs[pair, :, i * LANES : (i + 1) * LANES] = in_weights[
                i, :, pair * LANES : (pair + 1) * LANES
            ]
    tall = jnp.concatenate(
        [gains[0:1, :], shifts[0:1, :], jnp.zeros((LANES - 2, model), F32)], axis=0
    )
    columns[...] = jnp.transpose(tall)


def prepare(core, in_weights, in_biases, gains, shifts, up, down, bias, heads):
    model = up.shape[0]
    width = 3 * heads * LANES
    return local_call(
        functools.partial(prepare_kernel, heads),
        "prepare",
        (
            shaped(model, width),
            shaped(1, width, dtype=F32),
            shaped(heads // 2, model, 3 * LANES),
            shaped(model, LANES, dtype=F32),
            shaped(2 * model + 16, model),
        ),
        [SMEM] + [VMEM] * 7,
        (VMEM,) * 5,
        (core, in_weights, in_biases, gains, shifts, up, down, bias),
        cost=cost(4),
        room=ROOM,
    )


def count_of(ref, rows):
    return jnp.max(ref[rows : rows + 16, :LANES].astype(F32)).astype(jnp.int32)


def rows_at(start, rows, step=TILE):
    return pl.ds(pl.multiple_of(start, step), rows)


def attend_kernel(rows, groups, heads, *refs):
    near, far = refs[:groups], refs[groups]
    weights, biases, gains, shifts = refs[groups + 1 : groups + 5]
    at = groups + 5 + groups // 2
    out, give = refs[groups + 5 : at], refs[at]
    kept, counts, place = refs[at + 1 : at + 6], refs[at + 6], refs[at + 7]
    (xq, xk, qx, kx, vx), sems = refs[at + 8 : at + 13], refs[at + 13]
    model = xq.shape[1]
    q_counts = [count_of(r, rows) for r in near]
    k_counts = [count_of(far.at[g], rows) for g in range(groups)]
    for g in range(groups):
        counts[g] = q_counts[g]
        counts[groups + g] = k_counts[g]

    def compact(numbers, read, target):
        start = jnp.int32(0)
        for g, n in enumerate(numbers):
            target[rows_at(start, rows), :] = read(g)
            start = start + n * TILE
        target[rows_at(start, BLOCK), :] = jnp.zeros((BLOCK, model), BF)
        return start

    q_total = compact(q_counts, lambda g: near[g][:rows, :], xq)
    k_total = compact(k_counts, lambda g: far[g, :rows, :], xk)
    q_blocks = (q_total + BLOCK - 1) // BLOCK
    k_blocks = (k_total + BLOCK - 1) // BLOCK
    width = heads * LANES

    def hidden(ref, here):
        clean = standard(ref[here, :].astype(F32))[0].astype(BF)
        ref[here, :] = clean
        return (clean.astype(F32) * gains[0:1, :] + shifts[0:1, :]).astype(BF)

    @pl.loop(0, q_blocks)
    def _(b):
        here = rows_at(b * BLOCK, BLOCK, BLOCK)
        q = (dot(hidden(xq, here), weights[:, :width]) + biases[:, :width]).astype(BF)
        for h in range(heads):
            qx[h, here, :] = q[:, h * LANES : (h + 1) * LANES]

    @pl.loop(0, k_blocks)
    def _(b):
        here = rows_at(b * BLOCK, BLOCK, BLOCK)
        both = dot(hidden(xk, here), weights[:, width:]) + biases[:, width:]
        unseen = (iota((BLOCK, width), 0) + b * BLOCK >= k_total) & (
            iota((BLOCK, width), 1) % LANES == HD
        )
        k = jnp.where(unseen, FAR, both[:, :width]).astype(BF)
        v = both[:, width:].astype(BF)
        for h in range(heads):
            kx[h, here, :] = k[:, h * LANES : (h + 1) * LANES]
            vx[h, here, :] = v[:, h * LANES : (h + 1) * LANES]

    copies = [
        pltpu.make_async_copy(held, to, sems.at[i])
        for i, (held, to) in enumerate(zip((xq, xk, qx, kx, vx), kept))
    ]
    for copy in copies:
        copy.start()

    def attend_all(span):
        @pl.loop(0, q_blocks)
        def _(b):
            here = rows_at(b * BLOCK, BLOCK, BLOCK)
            lane = iota((BLOCK, LANES), 1)
            for h in range(heads):
                s = dot_nt(qx[h, here, :], kx[h, :span, :])
                top = jnp.max(s, axis=-1, keepdims=True)
                o = dot(jnp.exp(s - top).astype(BF), vx[h, :span, :])
                total = o[:, HD : HD + 1]
                o = o / total
                for i, piece in enumerate(pieces(top + jnp.log(total))):
                    o = jnp.where(lane == HD + i, piece.astype(F32), o)
                place[h, here, :] = o.astype(BF)

    for blocks in range(groups * TILE // BLOCK, groups * rows // BLOCK + 1):
        pl.when(k_blocks == blocks)(functools.partial(attend_all, blocks * BLOCK))

    gather = [
        (iota((LANES, LANES), 0) - HD + 3 * h == iota((LANES, LANES), 1))
        & (iota((LANES, LANES), 0) >= HD)
        & (iota((LANES, LANES), 0) < HD + 3)
        for h in range(heads)
    ]
    gather = [jnp.where(m, 1.0, 0.0).astype(BF) for m in gather]
    start = jnp.int32(0)
    for g in range(groups):
        mine = [place[h, rows_at(start, rows), :] for h in range(heads)]
        stats = sum(dot(m, s) for m, s in zip(mine, gather)).astype(BF)
        value = jnp.concatenate([m[:, :HD] for m in mine] + [stats], axis=1)
        if g < groups // 2:
            out[g][...] = value
        else:
            give[g - groups // 2] = value
        start = start + q_counts[g] * TILE
    for copy in copies:
        copy.wait()


def attend(near, far, weights, biases, gains, shifts, rows, heads):
    groups = len(near)
    model = near[0].shape[1]
    room = rows * groups + BLOCK
    parts = heads * HD + LANES
    kept = [(room, model)] * 2 + [(heads, room, LANES)] * 3
    return local_call(
        functools.partial(attend_kernel, rows, groups, heads),
        "attend",
        (
            *[shaped(rows, parts)] * (groups // 2),
            shaped(groups // 2, rows, parts),
            *[shaped(*k) for k in kept],
            shaped(2 * groups, dtype=jnp.int32),
        ),
        [VMEM] * (groups + 5),
        (*[VMEM] * (groups // 2 + 1), *[ANY] * 5, SMEM),
        (*near, far, weights, biases, gains, shifts),
        [
            pltpu.VMEM((heads, room, LANES), BF),
            *[pltpu.VMEM(k, BF) for k in kept],
            pltpu.SemaphoreType.DMA((5,)),
        ],
        cost(15),
        ROOM,
    )


def same_tile(rows):
    return iota((rows, rows), 0) // TILE == iota((rows, rows), 1) // TILE


def thumb_kernel(heads, tokens, weights, biases, gains, shifts, out, xhat, x):
    width = heads * LANES
    size = tokens.shape[0]
    clean = standard(tokens[...].astype(F32))[0].astype(BF)
    xhat[...] = clean
    hidden = (clean.astype(F32) * gains[0:1, :] + shifts[0:1, :]).astype(BF)
    x[...] = (dot(hidden, weights[...]) + biases[...]).astype(BF)
    visible = same_tile(size - TILE)
    out[:TILE, :] = jnp.zeros((TILE, heads * HD), F32)
    for h in range(heads):
        q = x[TILE:, h * LANES : (h + 1) * LANES]
        k = x[TILE:, width + h * LANES : width + (h + 1) * LANES]
        v = x[TILE:, 2 * width + h * LANES : 2 * width + (h + 1) * LANES]
        s = jnp.where(visible, dot_nt(q, k), FAR)
        e = jnp.exp(s - jnp.max(s, axis=-1, keepdims=True))
        o = dot(e.astype(BF), v)[:, :HD] / jnp.sum(e, axis=-1, keepdims=True)
        out[TILE:, h * HD : (h + 1) * HD] = o


def thumbs(tokens, weights, biases, gains, shifts, heads):
    size, model = tokens.shape
    return local_call(
        functools.partial(thumb_kernel, heads),
        "thumbs",
        (
            shaped(size, heads * HD, dtype=F32),
            shaped(size, model),
            shaped(size, 3 * heads * LANES),
        ),
        [VMEM] * 5,
        (VMEM,) * 3,
        (tokens, weights, biases, gains, shifts),
        cost=cost(5),
    )


def merged(parts, heads):
    cols = heads * HD
    row, col = (iota((LANES, cols), d) for d in (0, 1))
    spread = zero_one(row // 3 == col // HD)
    marks = [dot(p[:, cols:], spread) for p in parts]
    top = functools.reduce(jnp.maximum, marks)
    expos = [jnp.exp(m - top) for m in marks]
    total = sum(expos)
    mixed = sum(e * p[:, :cols].astype(F32) for p, e in zip(parts, expos)) / total
    row, col = (iota((cols, LANES), d) for d in (0, 1))
    packed = [
        dot(piece, zero_one((row % HD == 0) & (col == 3 * (row // HD) + i)))
        for i, piece in enumerate(pieces(top + jnp.log(total)))
    ]
    return mixed, sum(packed)


def pair_kernel(heads, *refs):
    count = (len(refs) - 1) // 2
    for j, (mine, out) in enumerate(zip(refs[:count], refs[count + 1 :])):
        mixed, marks = merged([mine[...], refs[count][j]], heads)
        out[...] = jnp.concatenate([mixed.astype(BF), marks.astype(BF)], axis=1)


def pair_merge(parts, other, heads):
    return local_call(
        functools.partial(pair_kernel, heads),
        "pair_merge",
        tuple(shaped(*p.shape) for p in parts),
        [VMEM] * (len(parts) + 1),
        (VMEM,) * len(parts),
        (*parts, other),
        cost=cost(3),
        room=ROOM,
    )


def merge_kernel(heads, counts, thumb, *refs):
    parts, (low, full, lse) = refs[:-3], refs[-3:]
    cols = heads * HD
    rows = lse.shape[0]
    mixed, marks = merged([p[...] for p in parts], heads)
    lse[...] = (-marks).astype(BF)
    image = iota((rows, cols), 0) < counts[0] * TILE
    full[:rows, :] = jnp.where(image, mixed, thumb[:rows, :])
    full[rows:, :] = thumb[rows:, :]
    low[...] = full[...].astype(BF)


def merge(count, parts, thumb, heads):
    size, cols = thumb.shape
    return local_call(
        functools.partial(merge_kernel, heads),
        "merge",
        (shaped(size, cols), shaped(size, cols, dtype=F32), shaped(parts[0].shape[0], LANES)),
        [SMEM] + [VMEM] * (1 + len(parts)),
        (VMEM,) * 3,
        (count, thumb, *parts),
        cost=cost(3),
    )


def fold_kernel(*refs):
    count = (len(refs) - 1) // 2
    for j, (mine, out) in enumerate(zip(refs[:count], refs[count + 1 :])):
        out[...] = (mine[...].astype(F32) + refs[count][j].astype(F32)).astype(BF)


def fold(parts, other):
    return local_call(
        fold_kernel,
        "fold",
        tuple(shaped(*p.shape) for p in parts),
        [VMEM] * (len(parts) + 1),
        (VMEM,) * len(parts),
        (*parts, other),
        cost=cost(2),
        room=ROOM,
    )


ROOT = 0.7978845608028654
CUBE = 0.044715


def ff_kernel(
    heads, tokens, outer, low, low_far, full, lse, out_weight, out_far, up, up_bias, down, far_one,
    far_two, gains, shifts, mixed, grad_mid, grad_low, packed, hidden_out, act_out, pre_out, small,
):
    size, model = tokens.shape
    passes = outer.shape[0]
    cols = heads * HD
    chunk = far_one.shape[1]
    units = up.shape[1]
    rows = packed.shape[0]
    branch = dot(low[...], out_weight[...]) + dot(low_far[...], out_far[...])
    middle = tokens[...].astype(F32) + (branch + shifts[1:2, :])
    xhat, factor = standard(middle)
    hidden = (xhat * gains[1:2, :] + shifts[2:3, :]).astype(BF)
    hidden_out[...] = hidden

    def one_chunk(up_part, bias, down_part, keep):
        v = dot(hidden, up_part) + bias
        t = jnp.tanh(ROOT * (v + CUBE * (v * v * v)))
        act = (0.5 * v * (1.0 + t)).astype(BF)
        slope = 0.5 * (1.0 + t) + 0.5 * v * (1.0 - t * t) * (ROOT * (1.0 + 3.0 * CUBE * (v * v)))
        two = []
        for p in range(passes):
            pre = (dot_nt(outer[p], down_part) * slope).astype(BF)
            if keep is not None:
                pre_out[p, :, keep] = pre
            two.append(dot_nt(pre, up_part))
        if keep is not None:
            act_out[:, keep] = act
        return dot(act, down_part), two

    def far_chunk(ref):
        told = ref[2 * chunk : 2 * chunk + 16, :].astype(F32)
        bias = told[0:1] + told[1:2] + told[2:3]
        return one_chunk(ref[:chunk, :], bias, ref[chunk : 2 * chunk, :], None)

    done = []
    for i in range(units // chunk):
        at = slice(i * chunk, (i + 1) * chunk)
        done.append(one_chunk(up[:, at], up_bias[:, at], down[at, :], at))
    done += [far_chunk(far_one), far_chunk(far_two)]

    def tree(parts):
        half = len(parts) // 2
        return sum(parts[:half]) + sum(parts[half:])

    output = tree([d[0] for d in done])
    mixed[...] = (middle + (output + shifts[3:4, :])).astype(BF)
    small[...] = jnp.zeros(small.shape, F32)
    lane = iota((rows, LANES), 1)
    stats = jnp.zeros((rows, LANES), F32)
    for p in range(passes):
        two = tree([d[1][p] for d in done])
        c = outer[p].astype(F32)
        mid = c + norm_back(two, gains[1:2, :], xhat, factor)
        mid_low = mid.astype(BF)
        grad_mid[p] = mid
        grad_low[p] = mid_low
        att = dot_nt(mid_low, out_weight[...]).astype(BF)
        packed[:, p * cols : (p + 1) * cols] = att[:rows, :]
        pre_out_p = pre_out[p].astype(F32)
        bias = jnp.sum(pre_out_p, axis=0, keepdims=True)
        small[p, 0:1, :] = jnp.sum(two * xhat, axis=0, keepdims=True)
        small[p, 1:2, :] = jnp.sum(two, axis=0, keepdims=True)
        small[p, 2:3, :] = jnp.sum(mid_low.astype(F32), axis=0, keepdims=True)
        small[p, 3:4, :] = jnp.sum(c, axis=0, keepdims=True)
        for i in range(units // model):
            small[p, 4 + i : 5 + i, :] = bias[:, i * model : (i + 1) * model]
        product = att[:rows, :].astype(F32) * full[:rows, :]
        for h in range(heads):
            delta = jnp.sum(product[:, h * HD : (h + 1) * HD], axis=-1, keepdims=True)
            for i, piece in enumerate(pieces(-delta)):
                stats = jnp.where(lane == 3 * heads * (p + 1) + 3 * h + i, piece.astype(F32), stats)
    packed[:, passes * cols :] = (stats + lse[...].astype(F32)).astype(BF)


def feed_forward(
    tokens, outer, low, low_far, full, lse, out_weight, out_far, up, up_bias, down, far_one, far_two,
    gains, shifts, rows, heads,
):
    size, model = tokens.shape
    passes = outer.shape[0]
    units = up.shape[1]
    return local_call(
        functools.partial(ff_kernel, heads),
        "feed_forward",
        (
            shaped(size, model),
            shaped(passes, size, model, dtype=F32),
            shaped(passes, size, model),
            shaped(rows, passes * heads * HD + LANES),
            shaped(size, model),
            shaped(size, units),
            shaped(passes, size, units),
            shaped(passes, 8, model, dtype=F32),
        ),
        [VMEM] * 15,
        (VMEM,) * 8,
        (
            tokens, outer, low, low_far, full, lse, out_weight, out_far, up, up_bias, down, far_one,
            far_two, gains, shifts,
        ),
        cost=cost(12),
        room=32,
    )


def thumb_back_kernel(heads, counts, x, mid_low, out_weight, out):
    width = heads * LANES
    size = x.shape[0]
    passes = mid_low.shape[0]
    visible = same_tile(size - TILE)
    outside = iota((size - TILE, HD), 0) + TILE >= counts[0] * TILE
    grads = [dot_nt(mid_low[p], out_weight[...]).astype(BF) for p in range(passes)]
    out[:, :, :TILE, :] = jnp.zeros((*out.shape[:2], TILE, out.shape[3]), BF)
    for h in range(heads):
        q = x[TILE:, h * LANES : (h + 1) * LANES]
        k = x[TILE:, width + h * LANES : width + (h + 1) * LANES]
        v = x[TILE:, 2 * width + h * LANES : 2 * width + h * LANES + HD]
        s = jnp.where(visible, dot_nt(q, k), FAR)
        e = jnp.exp(s - jnp.max(s, axis=-1, keepdims=True))
        w = e / jnp.sum(e, axis=-1, keepdims=True)
        w_low = w.astype(BF)
        for p in range(passes):
            g = grads[p][TILE:, h * HD : (h + 1) * HD]
            gw = dot_nt(g, v)
            ds = (w * (gw - jnp.sum(w * gw, axis=-1, keepdims=True))).astype(BF)
            dq = dot(ds, k[:, :HD]) * SCALE
            dk = dot_tn(ds, q)[:, :HD]
            dv = dot_tn(w_low, g)
            for c, piece in enumerate((dq, dk, dv)):
                at = c * LANES + (h % 2) * HD
                out[h // 2, p, TILE:, at : at + HD] = jnp.where(outside, piece, 0.0).astype(BF)


def thumbs_back(count, x, mid_low, out_weight, heads):
    passes, size, _ = mid_low.shape
    return local_call(
        functools.partial(thumb_back_kernel, heads),
        "thumbs_back",
        shaped(heads // 2, passes, size, 3 * LANES),
        [SMEM] + [VMEM] * 3,
        VMEM,
        (count, x, mid_low, out_weight),
        cost=cost(6),
    )


def early_at(units, model, low):
    ends = [model, 2 * model, 2 * model + units, 2 * model + units + low]
    return [slice(b - w, b) for b, w in zip(ends, (model, model, units, low))]


def early_cuts(parts, units, model, low):
    high, wide, turns = units // parts // 2, model // parts, model // low
    narrow = low * turns // parts
    for i in range(parts):
        yield (
            (slice(2 * i * high, (2 * i + 1) * high), slice(0, model)),
            (slice((2 * i + 1) * high, (2 * i + 2) * high), slice(0, model)),
            (slice(i * wide, (i + 1) * wide), slice(0, units)),
            (
                slice(i // turns * narrow, (i // turns + 1) * narrow),
                slice(i % turns * low, (i % turns + 1) * low),
            ),
        )


def weight_kernel(place, act, outer, hidden, pre, low, mid_low, keep, give):
    units, model, cols = act.shape[1], hidden.shape[1], low.shape[1]
    core = place[0]
    for turn, out in ((core, keep), (1 - core, give)):
        down = dot_tn(act[...], outer[turn]).astype(BF)
        up = dot_tn(hidden[...], pre[turn]).astype(BF)
        proj = dot_tn(low[...], mid_low[turn]).astype(BF)
        for i, cut in enumerate(early_cuts(keep.shape[0], units, model, cols)):
            for value, (rows, lanes), at in zip(
                (down, down, up, proj), cut, early_at(units, model, cols)
            ):
                out[i, :, at] = value[rows, lanes]


def weight_grads(core, act, outer, hidden, pre, low, mid_low, parts):
    units, model = act.shape[1], outer.shape[2]
    out = shaped(parts, model // parts, 2 * model + units + low.shape[1])
    return local_call(
        weight_kernel,
        "weight_grads",
        (out, out),
        [SMEM] + [VMEM] * 6,
        (VMEM,) * 2,
        (core, act, outer, hidden, pre, low, mid_low),
        cost=cost(8),
        room=24,
    )


def reverse_kernel(rows, groups, heads, passes, counts, place, *refs):
    grads, kept = refs[:groups], refs[groups : groups + 5]
    own, thumb, weights, columns, small = refs[groups + 5 : groups + 10]
    at = groups + 10
    out_q, give_q, at = refs[at : at + groups // 2], refs[at + groups // 2], at + groups // 2 + 1
    out_kv, at = refs[at : at + groups // 2], at + groups // 2
    keep, give = refs[at : at + 2]
    (
        stage, xq, xk, qx, kx, vx, packed, gx, kt, dq_t, dv, dk, low_q, low_kv, total, sums,
        starts, sems,
    ) = refs[at + 2 :]
    couples = heads // 2
    sources = [*grads, *kept[2:], *kept[:2]]
    targets = [*[stage.at[g] for g in range(groups)], qx, kx, vx, xq, xk]
    copies = [
        pltpu.make_async_copy(f, t, sems.at[i]) for i, (f, t) in enumerate(zip(sources, targets))
    ]
    for copy in copies:
        copy.start()
    cols = heads * HD
    wide = passes * LANES
    q_counts = [counts[g] for g in range(groups)]
    k_counts = [counts[groups + g] for g in range(groups)]
    start = jnp.int32(0)
    for g in range(groups):
        copies[g].wait()
        packed[rows_at(start, rows), :] = stage[g]
        start = start + q_counts[g] * TILE
    q_total, k_total = start, sum(k_counts) * TILE
    tail_lane = iota((BLOCK, packed.shape[1]), 1) - passes * cols
    empty = (tail_lane >= 0) & (tail_lane < 3 * heads) & (tail_lane % 3 == 0)
    packed[rows_at(q_total, BLOCK), :] = jnp.where(empty, FAR, 0.0).astype(BF)
    q_blocks = (q_total + BLOCK - 1) // BLOCK
    k_blocks = (k_total + BLOCK - 1) // BLOCK
    spans = range(groups * TILE // BLOCK, groups * rows // BLOCK + 1)

    row, col = (iota((LANES, heads * LANES), d) for d in (0, 1))
    head, lane = col // LANES, col % LANES
    to_marks = zero_one((lane > HD) & (lane < HD + 4) & (row == 3 * head + lane - HD - 1))
    row, col = (iota((LANES, heads * wide), d) for d in (0, 1))
    head, turn, lane = col // wide, col % wide // LANES, col % LANES
    to_deltas = zero_one(
        (lane >= HD) & (lane < HD + 3) & (row == 3 * heads * (turn + 1) + 3 * head + lane - HD)
    )
    for copy in copies[groups : groups + 3]:
        copy.wait()

    @pl.loop(0, q_blocks)
    def _(b):
        here = rows_at(b * BLOCK, BLOCK, BLOCK)
        stats = packed[here, passes * cols :]
        marks = dot(stats, to_marks)
        deltas = dot(stats, to_deltas).astype(BF)
        for h in range(heads):
            more = marks[:, h * LANES : (h + 1) * LANES]
            qx[h, here, :] = (qx[h, here, :].astype(F32) + more).astype(BF)
            for p in range(passes):
                at = p * cols + h * HD
                mine = (h * passes + p) * LANES
                gx[h, here, p * LANES : (p + 1) * LANES] = jnp.concatenate(
                    [packed[here, at : at + HD], deltas[:, mine + HD : mine + LANES]], axis=1
                )

    @pl.loop(0, k_blocks)
    def _(b):
        here = rows_at(b * BLOCK, BLOCK, BLOCK)
        for h in range(heads):
            kt[h, b] = jnp.transpose(kx[h, here, :].astype(F32))[:HD, :].astype(BF)

    def reverse_all(blocks):
        span = blocks * BLOCK

        @pl.loop(0, couples)
        def _(pair):
            dv[:, :span, :] = jnp.zeros((2, span, wide), F32)
            dk[:, :, :span, :] = jnp.zeros((passes, 2, span, LANES), F32)

            @pl.loop(0, q_blocks)
            def _(b):
                here = rows_at(b * BLOCK, BLOCK, BLOCK)
                for i in range(2):
                    h = 2 * pair + i
                    q, g = qx[h, here, :], gx[h, here, :]
                    k_t = jnp.concatenate([kt[h, j] for j in range(blocks)], axis=1)
                    w = jnp.exp(dot_nt(kx[h, :span, :], q))
                    dv[i, :span, :] += dot(w.astype(BF), g)
                    for p in range(passes):
                        ds = dot_nt(vx[h, :span, :], g[:, p * LANES : (p + 1) * LANES])
                        ds = (w * ds).astype(BF)
                        dk[p, i, :span, :] += dot(ds, q)
                        dq_t[p, i * HD : (i + 1) * HD, :] = dot(k_t, ds)
                for p in range(passes):
                    piece = jnp.transpose(dq_t[p]) * SCALE
                    low_q[pair, here, p * LANES : (p + 1) * LANES] = piece.astype(BF)

            for p in range(passes):
                for c, both in enumerate(
                    (
                        [dk[p, i, :span, :HD] for i in range(2)],
                        [dv[i, :span, p * LANES : p * LANES + HD] for i in range(2)],
                    )
                ):
                    lane = (2 * p + c) * LANES
                    low_kv[pair, :span, lane : lane + LANES] = jnp.concatenate(both, axis=1).astype(BF)

    for blocks in spans:
        pl.when(k_blocks == blocks)(functools.partial(reverse_all, blocks))

    start = jnp.int32(0)
    for g in range(groups):
        starts[g] = start
        start = start + k_counts[g] * TILE
    for g in range(groups):
        here = rows_at(starts[place[1 + g]], rows)
        out_kv[g // 2][g % 2] = jnp.concatenate([low_kv[i, here, :] for i in range(couples)], axis=1)
    start = jnp.int32(0)
    for g in range(groups):
        here = rows_at(start, rows)
        value = jnp.concatenate([low_q[i, here, :] for i in range(couples)], axis=1)
        if g < groups // 2:
            out_q[g][...] = value
        else:
            give_q[g - groups // 2] = value
        start = start + q_counts[g] * TILE

    copies[groups + 3].wait()
    copies[groups + 4].wait()

    def key_sums(blocks):
        span = blocks * BLOCK
        for i in range(couples):
            flat = low_kv[i, :span, :]
            total[i, :, wide:] = dot_tn(xk[:span, :], flat)
            sums[i, :, wide:] = dot(jnp.ones((8, span), BF), flat)

    for blocks in spans:
        pl.when(k_blocks == blocks)(functools.partial(key_sums, blocks))

    total[:, :, :wide] = jnp.zeros((couples, total.shape[1], wide), F32)
    sums[:, :, :wide] = jnp.zeros((couples, 8, wide), F32)

    @pl.loop(0, q_blocks)
    def _(b):
        here = rows_at(b * BLOCK, BLOCK, BLOCK)
        for i in range(couples):
            total[i, :, :wide] += dot_tn(xq[here, :], low_q[i, here, :])
            sums[i, :, :wide] += dot(jnp.ones((8, BLOCK), BF), low_q[i, here, :])

    model = total.shape[1]
    gain, shift = columns[:, 0:1], columns[:, 1:2]
    ones = jnp.ones((8, own.shape[0]), BF)
    for p in range(passes):
        whole = []
        for i in range(couples):
            mine = thumb[i, p]
            part = dot_tn(own[...], mine)
            part_sum = dot(ones, mine)[0:1, :]
            q_at = slice(p * LANES, (p + 1) * LANES)
            kv_at = slice((passes + 2 * p) * LANES, (passes + 2 * p + 2) * LANES)
            part += jnp.concatenate([total[i, :, q_at], total[i, :, kv_at]], axis=1)
            part_sum += jnp.concatenate([sums[i, 0:1, q_at], sums[i, 0:1, kv_at]], axis=1)
            w = weights[i].astype(F32)
            gain_one = jnp.sum(w * part, axis=1, keepdims=True)
            shift_one = jnp.sum(w * part_sum, axis=1, keepdims=True)
            lane = iota((model, LANES), 1)
            tall = jnp.where(lane == 0, gain_one, jnp.where(lane == 1, shift_one, 0.0))
            flat = jnp.concatenate(
                [jnp.zeros((2, LANES), F32)]
                + [part_sum[:, c * LANES : (c + 1) * LANES] for c in range(3)]
                + [jnp.zeros((LANES - 5, LANES), F32)],
                axis=0,
            )
            tall = jnp.concatenate([tall[:LANES] + jnp.transpose(flat), tall[LANES:]], axis=0)
            if i == 0:
                turned = jnp.concatenate(
                    [
                        jnp.zeros((8, model), F32),
                        small[p],
                        jnp.zeros((LANES - 16, model), F32),
                    ],
                    axis=0,
                )
                tall = tall + jnp.transpose(turned)
            whole += [part * gain + shift * part_sum, tall]
        whole = jnp.concatenate(whole, axis=1).astype(BF)

        @pl.when(place[0] == p)
        def _():
            keep[...] = whole

        @pl.when(place[0] != p)
        def _():
            give[...] = whole


def reverse(counts, place, grads, kept, own, thumb, weights, columns, small, rows, heads):
    groups = len(grads)
    couples, passes = thumb.shape[:2]
    model = own.shape[1]
    room = rows * groups + BLOCK
    cols = heads * HD
    wide = passes * LANES
    half = groups // 2
    late = shaped(model, couples * 4 * LANES)
    q, kv = shaped(rows, couples * wide), shaped(2, rows, couples * 2 * wide)
    out = (*[q] * half, shaped(half, rows, couples * wide), *[kv] * half, late, late)
    return local_call(
        functools.partial(reverse_kernel, rows, groups, heads, passes),
        "reverse",
        out,
        [SMEM, SMEM] + [ANY] * (groups + 5) + [VMEM] * 5,
        (VMEM,) * len(out),
        (counts, place, *grads, *kept, own, thumb, weights, columns, small),
        [
            pltpu.VMEM((groups, rows, passes * cols + LANES), BF),
            pltpu.VMEM((room, model), BF),
            pltpu.VMEM((room, model), BF),
            pltpu.VMEM((heads, room, LANES), BF),
            pltpu.VMEM((heads, room, LANES), BF),
            pltpu.VMEM((heads, room, LANES), BF),
            pltpu.VMEM((room, passes * cols + LANES), BF),
            pltpu.VMEM((heads, room, wide), BF),
            pltpu.VMEM((heads, room // BLOCK, HD, BLOCK), BF),
            pltpu.VMEM((passes, LANES, BLOCK), F32),
            pltpu.VMEM((2, room, wide), F32),
            pltpu.VMEM((passes, 2, room, LANES), F32),
            pltpu.VMEM((couples, room, wide), BF),
            pltpu.VMEM((couples, room, 2 * wide), BF),
            pltpu.VMEM((couples, model, 3 * wide), F32),
            pltpu.VMEM((couples, 8, 3 * wide), F32),
            pltpu.SMEM((groups,), jnp.int32),
            pltpu.SemaphoreType.DMA((groups + 5,)),
        ],
        cost(45),
        ROOM,
    )


def grad_one_kernel(near, counts, *refs):
    from_q, from_kv, (thumb, weights, mine, other) = refs[:near], refs[near:-4], refs[-4:]
    couples, passes, size, _ = thumb.shape
    rows = from_q[0].shape[0]
    sum_q = sum(r[...].astype(F32) for r in from_q)
    sum_kv = [sum(r[f].astype(F32) for r in from_kv) for f in range(2)]
    image = iota((rows, 3 * LANES), 0) < counts[0] * TILE
    for p in range(passes):
        parts = []
        for i in range(couples):
            at = (passes * i + p) * LANES
            there = slice(2 * at, 2 * at + 2 * LANES)
            far = jnp.concatenate([sum_q[:, at : at + LANES], sum_kv[0][:, there]], axis=1)
            flat = jnp.concatenate(
                [jnp.where(image, far.astype(BF), thumb[i, p, :rows]), thumb[i, p, rows:]], axis=0
            )
            parts.append(
                (
                    dot_nt(flat, weights[i]),
                    dot_nt(sum_kv[1][:, there].astype(BF), weights[i, :, LANES:]),
                )
            )
        mine[p] = sum(a for a, _ in parts).astype(BF)
        other[p] = sum(b for _, b in parts).astype(BF)


def grad_one(count, from_q, from_kv, thumb, weights):
    near = len(from_q)
    passes, size, _ = thumb.shape[1:]
    model = weights.shape[1]
    return local_call(
        functools.partial(grad_one_kernel, near),
        "grad_one",
        (shaped(passes, size, model), shaped(passes, from_q[0].shape[0], model)),
        [SMEM] + [VMEM] * (near + len(from_kv) + 2),
        (VMEM,) * 2,
        (count, *from_q, *from_kv, thumb, weights),
        cost=cost(5),
        room=ROOM,
    )


def close_kernel(counts, tokens, mid, mine, head, side, cross, gains, out):
    xhat, factor = standard(tokens[...].astype(F32))
    rows = side.shape[1]
    image = iota(side.shape[1:], 0) < counts[0] * TILE
    for p in range(mid.shape[0]):
        grad = mine[p].astype(F32) + head[p].astype(F32)
        more = jnp.where(image, side[p].astype(F32) + cross[p].astype(F32), 0.0)
        grad = jnp.concatenate([grad[:rows] + more, grad[rows:]], axis=0)
        out[p] = mid[p] + norm_back(grad, gains[0:1, :], xhat, factor)


def close(count, tokens, mid, mine, head, side, cross, gains):
    return local_call(
        close_kernel,
        "close",
        shaped(*mid.shape, dtype=F32),
        [SMEM] + [VMEM] * 7,
        VMEM,
        (count, tokens, mid, mine, head, side, cross, gains),
        cost=cost(4),
        room=ROOM,
    )


def early_kernel(lines, place, *refs):
    own, far, (down, up, proj) = refs[:lines], refs[lines : 2 * lines], refs[2 * lines :]
    core, z, y = place[0], place[9], place[10]
    (units, model), low = down.shape[1:], proj.shape[1]
    steps, rows = own[0].shape[:2]
    lane_down, lane_next, lane_up, lane_proj = early_at(units, model, low)
    turns = model // low
    for out, parts in ((core, own), (1 - core, far)):
        for d, ref in enumerate(parts):
            for j in range(steps):
                i = (z + steps - j) % steps * lines + (y + lines - d) % lines
                at = pl.multiple_of(2 * rows * i, 2 * rows)
                down[out, pl.ds(at, rows), :] = ref[j, :, lane_down].astype(F32)
                down[out, pl.ds(at + rows, rows), :] = ref[j, :, lane_next].astype(F32)
                up[out, rows_at(rows * i, rows, rows), :] = ref[j, :, lane_up].astype(F32)
                here = rows_at(i // turns * rows, rows, rows)
                value = ref[j, :, lane_proj].astype(F32)
                for t in range(turns):

                    @pl.when(i % turns == t)
                    def _(value=value, here=here, t=t):
                        proj[out, here, t * low : (t + 1) * low] = value


def early_out(place, own, far, units, low):
    model = len(own) * own[0].shape[0] * own[0].shape[1]
    return local_call(
        functools.partial(early_kernel, len(own)),
        "early_out",
        (
            shaped(2, units, model, dtype=F32),
            shaped(2, model, units, dtype=F32),
            shaped(2, low, model, dtype=F32),
        ),
        [SMEM] + [VMEM] * (2 * len(own)),
        (VMEM,) * 3,
        (place, *own, *far),
        cost=cost(8),
        room=ROOM,
    )


def late_kernel(place, own, far, grad_in, in_bias, up_bias, gains, shifts):
    core = place[0]
    for turn, ref in ((core, own), (1 - core, far)):
        turned = []
        for pair in range(2):
            at = 4 * LANES * pair
            for c in range(3):
                grad_in[turn, c, :, pair * LANES : (pair + 1) * LANES] = ref[
                    :, at + c * LANES : at + (c + 1) * LANES
                ].astype(F32)
            turned.append(jnp.transpose(ref[:, at + 3 * LANES : at + 4 * LANES].astype(F32)))
        a, b = turned
        in_bias[turn] = jnp.concatenate(
            [
                jnp.concatenate([a[2:3, :LANES], b[2:3, :LANES]], axis=1),
                jnp.concatenate([a[4:5, :LANES], b[4:5, :LANES]], axis=1),
            ],
            axis=0,
        )
        up_bias[turn] = jnp.concatenate([a[12:13], a[13:14]], axis=1)
        gains[turn] = jnp.concatenate([a[0:1] + b[0:1], a[8:9]], axis=0)
        shifts[turn] = jnp.concatenate([a[1:2] + b[1:2], a[10:11], a[9:10], a[11:12]], axis=0)


def late_out(core, own, far, units):
    model = own.shape[0]
    return local_call(
        late_kernel,
        "late_out",
        (
            shaped(2, 3, model, 2 * LANES, dtype=F32),
            shaped(2, 2, 2 * LANES, dtype=F32),
            shaped(2, 1, units, dtype=F32),
            shaped(2, 2, model, dtype=F32),
            shaped(2, 4, model, dtype=F32),
        ),
        [SMEM] + [VMEM] * 2,
        (VMEM,) * 5,
        (core, own, far),
        cost=cost(4),
        room=ROOM,
    )


def gather_near(array):
    mine = [array] + [shift_by(array, "y", d) for d in range(1, lax.axis_size("y"))]
    return mine + [shift_by(a, "c", 1) for a in mine]


def return_near(parts):
    return [parts[0]] + [shift_by(p, "y", -j) for j, p in enumerate(parts) if j > 0]


def offsets(size):
    return [(step, flip) for step in range(size) for flip in range(2)]


def return_far(parts):
    return [parts[0]] + [shift_by(p, "z", step) for step, p in enumerate(parts) if step > 0]


PLANE = ("z", "y")


def core_sum(keep, give):
    return (keep.astype(F32) + shift_by(give, "c", 1).astype(F32)).astype(BF)


def crossed(array):
    n = lax.axis_size(("xl", "h"))
    return lax.ppermute(array, ("xl", "h"), [(i, n - 1 - i) for i in range(n)])


def across(low):
    done = low.astype(F32) + shift_by(low, "xl", 1).astype(F32)
    size = 4 * LANES
    ones = jnp.concatenate([low[:, i + 3 * LANES : i + size] for i in range(0, low.shape[1], size)], axis=1)
    more = shift_by(ones, "h", 1).astype(F32) + crossed(ones).astype(F32)
    more = jnp.where(jnp.arange(more.shape[1]) % LANES < 2, more, 0.0)
    nothing = jnp.zeros((low.shape[0], 3 * LANES), F32)
    laid = [[nothing, more[:, i : i + LANES]] for i in range(0, more.shape[1], LANES)]
    return (done + jnp.concatenate(sum(laid, []), axis=1)).astype(BF)


def tied(arrays, others):
    return lax.optimization_barrier((arrays, others))


def local(
    tokens,
    cotangents,
    segment_ids,
    in_weights,
    in_biases,
    out_weight,
    up_weight,
    up_biases,
    down_weight,
    gains,
    shifts,
):
    size, model = tokens.shape
    cols = in_weights.shape[2]
    heads = cols // HD
    rows = size - TILE
    units = up_weight.shape[1]
    c = lax.axis_index("c")

    told, copies, count = front(tokens, segment_ids, lax.axis_size(("z", "xl")))
    far = lax.all_to_all(copies, ("z", "xl"), 0, 0, tiled=True)
    near = gather_near(told)
    core = c.astype(jnp.int32).reshape(1)
    z, xl, z_size = lax.axis_index("z"), lax.axis_index("xl"), lax.axis_size("z")
    routes = [((z + step) % z_size) * 2 + (xl ^ flip) for step, flip in offsets(z_size)]
    place = jnp.stack([c, *routes, z, lax.axis_index("y")]).astype(jnp.int32)
    plane = lax.axis_size(PLANE)

    weights, biases, pairs, columns, bundle = prepare(
        core, in_weights, in_biases, gains, shifts, up_weight, down_weight, up_biases[None], heads
    )
    out_far = crossed(out_weight)
    far_one = crossed(bundle)
    far_two = shift_by(far_one, "c", 1)

    weights, (out_far, columns, place) = tied(weights, (out_far, columns, place))
    *parts, give, xq, xk, qx, kx, vx, counts = attend(
        near, far, weights, biases, gains, shifts, rows, heads
    )
    thumb_out, xhat, x = thumbs(tokens, weights, biases, gains, shifts, heads)
    parts = pair_merge(parts, shift_by(give, "c", 1), heads)
    low, full, lse = merge(count, return_near(parts), thumb_out, heads)
    low_far = shift_by(low, "h", 1)
    mixed, grad_mid, mid_low, packed, hidden, act, pre, small = feed_forward(
        tokens, cotangents, low, low_far, full, lse, out_weight, out_far, up_weight, up_biases[None],
        down_weight, far_one, far_two, gains, shifts, rows, heads,
    )
    grads = gather_near(packed)
    keep, give = weight_grads(core, act, cotangents, hidden, pre, low, mid_low, plane)
    mid_low, (keep, give) = tied(mid_low, (keep, give))
    thumb = thumbs_back(count, x, mid_low, out_weight, heads)
    early = core_sum(keep, give)

    grads, (early, thumb) = tied(grads, (early, thumb))
    early = lax.all_to_all(early, PLANE, 0, 0, tiled=True)
    *out, keep, give = reverse(
        counts, place, grads, (xq, xk, qx, kx, vx), xhat, thumb, pairs, columns, small, rows, heads
    )
    half = len(near) // 2
    out_q, give_q, out_kv = out[:half], out[half], out[half + 1 :]
    early = jnp.sum(early.astype(F32), axis=0).astype(BF)
    early = (early.astype(F32) + shift_by(early, "xl", 1).astype(F32)).astype(BF)
    early = jnp.stack([early] + [shift_by(early, "z", d) for d in range(1, z_size)])
    from_kv = return_far(out_kv)
    out_q = fold(out_q, shift_by(give_q, "c", 1))
    late = core_sum(keep, give)
    late, (early, from_kv, out_q) = tied(late, (early, from_kv, out_q))

    late = late.reshape(plane, -1, late.shape[1])
    late = lax.all_to_all(late, PLANE, 0, 0, tiled=True)
    from_q = return_near(out_q)
    early = [early] + [shift_by(early, "y", d) for d in range(1, lax.axis_size("y"))]
    late = across(jnp.sum(late.astype(F32), axis=0).astype(BF))
    late, early = tied(late, early)
    late = jnp.broadcast_to(late[None], (plane, *late.shape))
    late = lax.all_to_all(late, PLANE, 0, 0, tiled=True).reshape(model, -1)

    mine, other = grad_one(count, from_q, from_kv, thumb, pairs)
    grad_tokens = close(
        count, tokens, grad_mid, mine, shift_by(mine, "h", 1), shift_by(other, "xl", 1),
        crossed(other), gains,
    )
    early_far = [shift_by(e, "c", 1) for e in early]
    grad_down, grad_up, grad_out = early_out(place, early, early_far, units, cols)
    grad_in, in_bias, up_bias, grad_gains, grad_shifts = late_out(
        core, late, shift_by(late, "c", 1), units
    )
    return (
        mixed,
        grad_tokens,
        grad_in,
        in_bias,
        grad_out,
        grad_up,
        up_bias.reshape(2, units),
        grad_down,
        grad_gains,
        grad_shifts,
    )


def solution(mesh):
    fine = Mesh(mesh.devices.reshape(4, 2, 4, 2, 2), ("z", "xl", "y", "c", "h"))
    blk = ("z", "xl", "y", "c")
    return jax.shard_map(
        local,
        mesh=fine,
        in_specs=(
            P(blk, None),
            P(None, blk, None),
            P(blk),
            P(None, None, "h"),
            P(None, "h"),
            P("h", None),
            P(None, "h"),
            P("h"),
            P("h", None),
            P(),
            P(),
        ),
        out_specs=(
            P(blk, None),
            P(None, blk, None),
            P(None, None, None, "h"),
            P(None, None, "h"),
            P(None, "h", None),
            P(None, None, "h"),
            P(None, "h"),
            P(None, "h", None),
            P(),
            P(),
        ),
        check_vma=False,
    )
```

```python
import functools

import jax
import jax.numpy as jnp
from jax import lax
from jax.experimental import pallas as pl
from jax.experimental.pallas import tpu as pltpu
from jax.sharding import Mesh
from jax.sharding import PartitionSpec as P

HD = 64
LANES = 128
TILE = 64
BLOCK = 256
EPS = 1e-06
SCALE = 0.125
FAR = -1e30
BF = jnp.bfloat16
F32 = jnp.float32
MIB = 1024 * 1024
ROOM = 56

NT = (((1,), (1,)), ((), ()))
TN = (((0,), (0,)), ((), ()))


def shift_by(array, axis, step):
    size = lax.axis_size(axis)
    return lax.ppermute(array, axis, [(i, (i + step) % size) for i in range(size)])


def dot(a, b):
    return jnp.dot(a, b, preferred_element_type=F32)


def dot_nt(a, b):
    return lax.dot_general(a, b, NT, preferred_element_type=F32)


def dot_tn(a, b):
    return lax.dot_general(a, b, TN, preferred_element_type=F32)


def standard(field):
    center = field - jnp.mean(field, axis=-1, keepdims=True)
    factor = lax.rsqrt(jnp.mean(center * center, axis=-1, keepdims=True) + EPS)
    return center * factor, factor


def norm_back(grad, gain, xhat, factor):
    h = grad * gain
    mean = jnp.mean(h, axis=-1, keepdims=True)
    return factor * (h - mean - xhat * jnp.mean(h * xhat, axis=-1, keepdims=True))


def pieces(value):
    high = value.astype(BF)
    rest = value - high.astype(F32)
    middle = rest.astype(BF)
    low = (rest - middle.astype(F32)).astype(BF)
    return high, middle, low


def zero_one(mask):
    return jnp.where(mask, 1.0, 0.0).astype(BF)


def iota(shape, dim):
    return lax.broadcasted_iota(jnp.int32, shape, dim)


VMEM = pl.BlockSpec(memory_space=pltpu.VMEM)
ANY = pl.BlockSpec(memory_space=pl.ANY)
SMEM = pl.BlockSpec(memory_space=pltpu.SMEM)


def local_call(body, name, out, ins, outs, args, scratch=(), cost=None, room=16):
    return pl.pallas_call(
        body,
        out_shape=out,
        in_specs=ins,
        out_specs=outs,
        scratch_shapes=scratch,
        cost_estimate=cost,
        compiler_params=pltpu.CompilerParams(vmem_limit_bytes=room * MIB),
        name=name,
    )(*args)


def shaped(*shape, dtype=BF):
    return jax.ShapeDtypeStruct(shape, dtype)


def cost(micros):
    return pl.CostEstimate(flops=int(micros * 1e9), bytes_accessed=0, transcendentals=0)


def front_kernel(tokens, ids, told, copies, number):
    rows = told.shape[0] - 16
    marks = jnp.where(ids[...] == 0, 1.0, 0.0)
    tiles = jnp.sum(marks).astype(jnp.int32) // TILE
    number[0] = tiles
    told[:rows, :] = tokens[:rows, :]
    told[rows:, :] = jnp.full((16, told.shape[1]), tiles.astype(F32), F32).astype(BF)
    for g in range(copies.shape[0]):
        copies[g] = told[...]


def front(tokens, ids, copies):
    size, model = tokens.shape
    told = size - TILE + 16
    return local_call(
        front_kernel,
        "front",
        (shaped(told, model), shaped(copies, told, model), shaped(1, dtype=jnp.int32)),
        [VMEM, VMEM],
        (VMEM, VMEM, SMEM),
        (tokens, ids.reshape(-1, LANES)),
        room=ROOM,
    )


def prepare_kernel(
    heads, place, in_weights, in_biases, gains, shifts, up, down, bias,
    weights, biases, pairs, columns, out,
):
    core = place[0]
    half = out.shape[1]
    at = pl.ds(pl.multiple_of(core * half, half), half)
    out[:half, :] = up[:, at]
    out[half : 2 * half, :] = down[at, :]
    mine = jnp.where(core == 0, bias[:, :half], bias[:, half:])
    row = iota((16, half), 0)
    rows = jnp.zeros((16, half), F32)
    for i, piece in enumerate(pieces(mine)):
        rows = jnp.where(row == i, piece.astype(F32), rows)
    out[2 * half :, :] = rows.astype(BF)

    model, cols = in_weights.shape[1:]
    width = heads * LANES
    row, col = (iota((cols, width), d) for d in (0, 1))
    spread = zero_one((row // HD == col // LANES) & (row % HD == col % LANES))
    lane = iota((1, width), 1) % LANES
    gap = jnp.zeros((1, HD), F32)

    def apart(line):
        return jnp.concatenate(
            sum([[line[:, h * HD : (h + 1) * HD], gap] for h in range(heads)], []), axis=1
        )

    extra = [
        apart(in_biases[0:1, :] * SCALE) + jnp.where(lane == HD, 1.0, 0.0),
        jnp.where((lane > HD) & (lane < HD + 4), 1.0, 0.0),
        apart(in_biases[1:2, :]) + jnp.where((lane >= HD) & (lane < HD + 3), 1.0, 0.0),
    ]
    for i in range(3):
        factor = SCALE if i == 0 else 1.0
        weights[:, i * width : (i + 1) * width] = (dot(in_weights[i], spread) * factor).astype(BF)
        biases[:, i * width : (i + 1) * width] = extra[i]
        for pair in range(heads // 2):
            pairs[pair, :, i * LANES : (i + 1) * LANES] = in_weights[
                i, :, pair * LANES : (pair + 1) * LANES
            ]
    tall = jnp.concatenate(
        [gains[0:1, :], shifts[0:1, :], jnp.zeros((LANES - 2, model), F32)], axis=0
    )
    columns[...] = jnp.transpose(tall)


def prepare(core, in_weights, in_biases, gains, shifts, up, down, bias, heads):
    model = up.shape[0]
    width = 3 * heads * LANES
    return local_call(
        functools.partial(prepare_kernel, heads),
        "prepare",
        (
            shaped(model, width),
            shaped(1, width, dtype=F32),
            shaped(heads // 2, model, 3 * LANES),
            shaped(model, LANES, dtype=F32),
            shaped(2 * model + 16, model),
        ),
        [SMEM] + [VMEM] * 7,
        (VMEM,) * 5,
        (core, in_weights, in_biases, gains, shifts, up, down, bias),
        cost=cost(4),
        room=ROOM,
    )


def count_of(ref, rows):
    return jnp.max(ref[rows : rows + 16, :LANES].astype(F32)).astype(jnp.int32)


def rows_at(start, rows, step=TILE):
    return pl.ds(pl.multiple_of(start, step), rows)


def attend_kernel(rows, groups, heads, *refs):
    near, far = refs[:groups], refs[groups]
    weights, biases, gains, shifts = refs[groups + 1 : groups + 5]
    at = groups + 5 + groups // 2
    out, give = refs[groups + 5 : at], refs[at]
    kept, counts, place = refs[at + 1 : at + 6], refs[at + 6], refs[at + 7]
    (xq, xk, qx, kx, vx), sems = refs[at + 8 : at + 13], refs[at + 13]
    model = xq.shape[1]
    q_counts = [count_of(r, rows) for r in near]
    k_counts = [count_of(far.at[g], rows) for g in range(groups)]
    for g in range(groups):
        counts[g] = q_counts[g]
        counts[groups + g] = k_counts[g]

    def compact(numbers, read, target):
        start = jnp.int32(0)
        for g, n in enumerate(numbers):
            target[rows_at(start, rows), :] = read(g)
            start = start + n * TILE
        target[rows_at(start, BLOCK), :] = jnp.zeros((BLOCK, model), BF)
        return start

    q_total = compact(q_counts, lambda g: near[g][:rows, :], xq)
    k_total = compact(k_counts, lambda g: far[g, :rows, :], xk)
    q_blocks = (q_total + BLOCK - 1) // BLOCK
    k_blocks = (k_total + BLOCK - 1) // BLOCK
    width = heads * LANES

    def hidden(ref, here):
        clean = standard(ref[here, :].astype(F32))[0].astype(BF)
        ref[here, :] = clean
        return (clean.astype(F32) * gains[0:1, :] + shifts[0:1, :]).astype(BF)

    @pl.loop(0, q_blocks)
    def _(b):
        here = rows_at(b * BLOCK, BLOCK, BLOCK)
        q = (dot(hidden(xq, here), weights[:, :width]) + biases[:, :width]).astype(BF)
        for h in range(heads):
            qx[h, here, :] = q[:, h * LANES : (h + 1) * LANES]

    @pl.loop(0, k_blocks)
    def _(b):
        here = rows_at(b * BLOCK, BLOCK, BLOCK)
        both = dot(hidden(xk, here), weights[:, width:]) + biases[:, width:]
        unseen = (iota((BLOCK, width), 0) + b * BLOCK >= k_total) & (
            iota((BLOCK, width), 1) % LANES == HD
        )
        k = jnp.where(unseen, FAR, both[:, :width]).astype(BF)
        v = both[:, width:].astype(BF)
        for h in range(heads):
            kx[h, here, :] = k[:, h * LANES : (h + 1) * LANES]
            vx[h, here, :] = v[:, h * LANES : (h + 1) * LANES]

    copies = [
        pltpu.make_async_copy(held, to, sems.at[i])
        for i, (held, to) in enumerate(zip((xq, xk, qx, kx, vx), kept))
    ]
    for copy in copies:
        copy.start()

    def attend_all(span):
        @pl.loop(0, q_blocks)
        def _(b):
            here = rows_at(b * BLOCK, BLOCK, BLOCK)
            lane = iota((BLOCK, LANES), 1)
            for h in range(heads):
                s = dot_nt(qx[h, here, :], kx[h, :span, :])
                top = jnp.max(s, axis=-1, keepdims=True)
                o = dot(jnp.exp(s - top).astype(BF), vx[h, :span, :])
                total = o[:, HD : HD + 1]
                o = o / total
                for i, piece in enumerate(pieces(top + jnp.log(total))):
                    o = jnp.where(lane == HD + i, piece.astype(F32), o)
                place[h, here, :] = o.astype(BF)

    for blocks in range(groups * TILE // BLOCK, groups * rows // BLOCK + 1):
        pl.when(k_blocks == blocks)(functools.partial(attend_all, blocks * BLOCK))

    gather = [
        (iota((LANES, LANES), 0) - HD + 3 * h == iota((LANES, LANES), 1))
        & (iota((LANES, LANES), 0) >= HD)
        & (iota((LANES, LANES), 0) < HD + 3)
        for h in range(heads)
    ]
    gather = [jnp.where(m, 1.0, 0.0).astype(BF) for m in gather]
    start = jnp.int32(0)
    for g in range(groups):
        mine = [place[h, rows_at(start, rows), :] for h in range(heads)]
        stats = sum(dot(m, s) for m, s in zip(mine, gather)).astype(BF)
        value = jnp.concatenate([m[:, :HD] for m in mine] + [stats], axis=1)
        if g < groups // 2:
            out[g][...] = value
        else:
            give[g - groups // 2] = value
        start = start + q_counts[g] * TILE
    for copy in copies:
        copy.wait()


def attend(near, far, weights, biases, gains, shifts, rows, heads):
    groups = len(near)
    model = near[0].shape[1]
    room = rows * groups + BLOCK
    parts = heads * HD + LANES
    kept = [(room, model)] * 2 + [(heads, room, LANES)] * 3
    return local_call(
        functools.partial(attend_kernel, rows, groups, heads),
        "attend",
        (
            *[shaped(rows, parts)] * (groups // 2),
            shaped(groups // 2, rows, parts),
            *[shaped(*k) for k in kept],
            shaped(2 * groups, dtype=jnp.int32),
        ),
        [VMEM] * (groups + 5),
        (*[VMEM] * (groups // 2 + 1), *[ANY] * 5, SMEM),
        (*near, far, weights, biases, gains, shifts),
        [
            pltpu.VMEM((heads, room, LANES), BF),
            *[pltpu.VMEM(k, BF) for k in kept],
            pltpu.SemaphoreType.DMA((5,)),
        ],
        cost(15),
        ROOM,
    )


def same_tile(rows):
    return iota((rows, rows), 0) // TILE == iota((rows, rows), 1) // TILE


def thumb_kernel(heads, tokens, weights, biases, gains, shifts, out, xhat, x):
    width = heads * LANES
    size = tokens.shape[0]
    clean = standard(tokens[...].astype(F32))[0].astype(BF)
    xhat[...] = clean
    hidden = (clean.astype(F32) * gains[0:1, :] + shifts[0:1, :]).astype(BF)
    x[...] = (dot(hidden, weights[...]) + biases[...]).astype(BF)
    visible = same_tile(size - TILE)
    out[:TILE, :] = jnp.zeros((TILE, heads * HD), F32)
    for h in range(heads):
        q = x[TILE:, h * LANES : (h + 1) * LANES]
        k = x[TILE:, width + h * LANES : width + (h + 1) * LANES]
        v = x[TILE:, 2 * width + h * LANES : 2 * width + (h + 1) * LANES]
        s = jnp.where(visible, dot_nt(q, k), FAR)
        e = jnp.exp(s - jnp.max(s, axis=-1, keepdims=True))
        o = dot(e.astype(BF), v)[:, :HD] / jnp.sum(e, axis=-1, keepdims=True)
        out[TILE:, h * HD : (h + 1) * HD] = o


def thumbs(tokens, weights, biases, gains, shifts, heads):
    size, model = tokens.shape
    return local_call(
        functools.partial(thumb_kernel, heads),
        "thumbs",
        (
            shaped(size, heads * HD, dtype=F32),
            shaped(size, model),
            shaped(size, 3 * heads * LANES),
        ),
        [VMEM] * 5,
        (VMEM,) * 3,
        (tokens, weights, biases, gains, shifts),
        cost=cost(5),
    )


def merged(parts, heads):
    cols = heads * HD
    row, col = (iota((LANES, cols), d) for d in (0, 1))
    spread = zero_one(row // 3 == col // HD)
    marks = [dot(p[:, cols:], spread) for p in parts]
    top = functools.reduce(jnp.maximum, marks)
    expos = [jnp.exp(m - top) for m in marks]
    total = sum(expos)
    mixed = sum(e * p[:, :cols].astype(F32) for p, e in zip(parts, expos)) / total
    row, col = (iota((cols, LANES), d) for d in (0, 1))
    packed = [
        dot(piece, zero_one((row % HD == 0) & (col == 3 * (row // HD) + i)))
        for i, piece in enumerate(pieces(top + jnp.log(total)))
    ]
    return mixed, sum(packed)


def pair_kernel(heads, *refs):
    count = (len(refs) - 1) // 2
    for j, (mine, out) in enumerate(zip(refs[:count], refs[count + 1 :])):
        mixed, marks = merged([mine[...], refs[count][j]], heads)
        out[...] = jnp.concatenate([mixed.astype(BF), marks.astype(BF)], axis=1)


def pair_merge(parts, other, heads):
    return local_call(
        functools.partial(pair_kernel, heads),
        "pair_merge",
        tuple(shaped(*p.shape) for p in parts),
        [VMEM] * (len(parts) + 1),
        (VMEM,) * len(parts),
        (*parts, other),
        cost=cost(3),
        room=ROOM,
    )


def merge_kernel(heads, counts, thumb, *refs):
    parts, (low, full, lse) = refs[:-3], refs[-3:]
    cols = heads * HD
    rows = lse.shape[0]
    mixed, marks = merged([p[...] for p in parts], heads)
    lse[...] = (-marks).astype(BF)
    image = iota((rows, cols), 0) < counts[0] * TILE
    full[:rows, :] = jnp.where(image, mixed, thumb[:rows, :])
    full[rows:, :] = thumb[rows:, :]
    low[...] = full[...].astype(BF)


def merge(count, parts, thumb, heads):
    size, cols = thumb.shape
    return local_call(
        functools.partial(merge_kernel, heads),
        "merge",
        (shaped(size, cols), shaped(size, cols, dtype=F32), shaped(parts[0].shape[0], LANES)),
        [SMEM] + [VMEM] * (1 + len(parts)),
        (VMEM,) * 3,
        (count, thumb, *parts),
        cost=cost(3),
    )


def fold_kernel(*refs):
    count = (len(refs) - 1) // 2
    for j, (mine, out) in enumerate(zip(refs[:count], refs[count + 1 :])):
        out[...] = (mine[...].astype(F32) + refs[count][j].astype(F32)).astype(BF)


def fold(parts, other):
    return local_call(
        fold_kernel,
        "fold",
        tuple(shaped(*p.shape) for p in parts),
        [VMEM] * (len(parts) + 1),
        (VMEM,) * len(parts),
        (*parts, other),
        cost=cost(2),
        room=ROOM,
    )


ROOT = 0.7978845608028654
CUBE = 0.044715


def ff_kernel(
    heads, tokens, outer, low, low_far, full, lse, out_weight, out_far, up, up_bias, down, far_one,
    far_two, gains, shifts, mixed, grad_mid, grad_low, packed, hidden_out, act_out, pre_out, small,
):
    size, model = tokens.shape
    passes = outer.shape[0]
    cols = heads * HD
    chunk = far_one.shape[1]
    units = up.shape[1]
    rows = packed.shape[0]
    branch = dot(low[...], out_weight[...]) + dot(low_far[...], out_far[...])
    middle = tokens[...].astype(F32) + (branch + shifts[1:2, :])
    xhat, factor = standard(middle)
    hidden = (xhat * gains[1:2, :] + shifts[2:3, :]).astype(BF)
    hidden_out[...] = hidden

    def one_chunk(up_part, bias, down_part, keep):
        v = dot(hidden, up_part) + bias
        t = jnp.tanh(ROOT * (v + CUBE * (v * v * v)))
        act = (0.5 * v * (1.0 + t)).astype(BF)
        slope = 0.5 * (1.0 + t) + 0.5 * v * (1.0 - t * t) * (ROOT * (1.0 + 3.0 * CUBE * (v * v)))
        two = []
        for p in range(passes):
            pre = (dot_nt(outer[p], down_part) * slope).astype(BF)
            if keep is not None:
                pre_out[p, :, keep] = pre
            two.append(dot_nt(pre, up_part))
        if keep is not None:
            act_out[:, keep] = act
        return dot(act, down_part), two

    def far_chunk(ref):
        told = ref[2 * chunk : 2 * chunk + 16, :].astype(F32)
        bias = told[0:1] + told[1:2] + told[2:3]
        return one_chunk(ref[:chunk, :], bias, ref[chunk : 2 * chunk, :], None)

    done = []
    for i in range(units // chunk):
        at = slice(i * chunk, (i + 1) * chunk)
        done.append(one_chunk(up[:, at], up_bias[:, at], down[at, :], at))
    done += [far_chunk(far_one), far_chunk(far_two)]

    def tree(parts):
        half = len(parts) // 2
        return sum(parts[:half]) + sum(parts[half:])

    output = tree([d[0] for d in done])
    mixed[...] = (middle + (output + shifts[3:4, :])).astype(BF)
    small[...] = jnp.zeros(small.shape, F32)
    lane = iota((rows, LANES), 1)
    stats = jnp.zeros((rows, LANES), F32)
    for p in range(passes):
        two = tree([d[1][p] for d in done])
        c = outer[p].astype(F32)
        mid = c + norm_back(two, gains[1:2, :], xhat, factor)
        mid_low = mid.astype(BF)
        grad_mid[p] = mid
        grad_low[p] = mid_low
        att = dot_nt(mid_low, out_weight[...]).astype(BF)
        packed[:, p * cols : (p + 1) * cols] = att[:rows, :]
        pre_out_p = pre_out[p].astype(F32)
        bias = jnp.sum(pre_out_p, axis=0, keepdims=True)
        small[p, 0:1, :] = jnp.sum(two * xhat, axis=0, keepdims=True)
        small[p, 1:2, :] = jnp.sum(two, axis=0, keepdims=True)
        small[p, 2:3, :] = jnp.sum(mid_low.astype(F32), axis=0, keepdims=True)
        small[p, 3:4, :] = jnp.sum(c, axis=0, keepdims=True)
        for i in range(units // model):
            small[p, 4 + i : 5 + i, :] = bias[:, i * model : (i + 1) * model]
        product = att[:rows, :].astype(F32) * full[:rows, :]
        for h in range(heads):
            delta = jnp.sum(product[:, h * HD : (h + 1) * HD], axis=-1, keepdims=True)
            for i, piece in enumerate(pieces(-delta)):
                stats = jnp.where(lane == 3 * heads * (p + 1) + 3 * h + i, piece.astype(F32), stats)
    packed[:, passes * cols :] = (stats + lse[...].astype(F32)).astype(BF)


def feed_forward(
    tokens, outer, low, low_far, full, lse, out_weight, out_far, up, up_bias, down, far_one, far_two,
    gains, shifts, rows, heads,
):
    size, model = tokens.shape
    passes = outer.shape[0]
    units = up.shape[1]
    return local_call(
        functools.partial(ff_kernel, heads),
        "feed_forward",
        (
            shaped(size, model),
            shaped(passes, size, model, dtype=F32),
            shaped(passes, size, model),
            shaped(rows, passes * heads * HD + LANES),
            shaped(size, model),
            shaped(size, units),
            shaped(passes, size, units),
            shaped(passes, 8, model, dtype=F32),
        ),
        [VMEM] * 15,
        (VMEM,) * 8,
        (
            tokens, outer, low, low_far, full, lse, out_weight, out_far, up, up_bias, down, far_one,
            far_two, gains, shifts,
        ),
        cost=cost(12),
        room=32,
    )


def thumb_back_kernel(heads, counts, x, mid_low, out_weight, out):
    width = heads * LANES
    size = x.shape[0]
    passes = mid_low.shape[0]
    visible = same_tile(size - TILE)
    outside = iota((size - TILE, HD), 0) + TILE >= counts[0] * TILE
    grads = [dot_nt(mid_low[p], out_weight[...]).astype(BF) for p in range(passes)]
    out[:, :, :TILE, :] = jnp.zeros((*out.shape[:2], TILE, out.shape[3]), BF)
    for h in range(heads):
        q = x[TILE:, h * LANES : (h + 1) * LANES]
        k = x[TILE:, width + h * LANES : width + (h + 1) * LANES]
        v = x[TILE:, 2 * width + h * LANES : 2 * width + h * LANES + HD]
        s = jnp.where(visible, dot_nt(q, k), FAR)
        e = jnp.exp(s - jnp.max(s, axis=-1, keepdims=True))
        w = e / jnp.sum(e, axis=-1, keepdims=True)
        w_low = w.astype(BF)
        for p in range(passes):
            g = grads[p][TILE:, h * HD : (h + 1) * HD]
            gw = dot_nt(g, v)
            ds = (w * (gw - jnp.sum(w * gw, axis=-1, keepdims=True))).astype(BF)
            dq = dot(ds, k[:, :HD]) * SCALE
            dk = dot_tn(ds, q)[:, :HD]
            dv = dot_tn(w_low, g)
            for c, piece in enumerate((dq, dk, dv)):
                at = c * LANES + (h % 2) * HD
                out[h // 2, p, TILE:, at : at + HD] = jnp.where(outside, piece, 0.0).astype(BF)


def thumbs_back(count, x, mid_low, out_weight, heads):
    passes, size, _ = mid_low.shape
    return local_call(
        functools.partial(thumb_back_kernel, heads),
        "thumbs_back",
        shaped(heads // 2, passes, size, 3 * LANES),
        [SMEM] + [VMEM] * 3,
        VMEM,
        (count, x, mid_low, out_weight),
        cost=cost(6),
    )


def early_at(units, model, low):
    ends = [model, 2 * model, 2 * model + units, 2 * model + units + low]
    return [slice(b - w, b) for b, w in zip(ends, (model, model, units, low))]


def early_cuts(parts, units, model, low):
    high, wide, turns = units // parts // 2, model // parts, model // low
    narrow = low * turns // parts
    for i in range(parts):
        yield (
            (slice(2 * i * high, (2 * i + 1) * high), slice(0, model)),
            (slice((2 * i + 1) * high, (2 * i + 2) * high), slice(0, model)),
            (slice(i * wide, (i + 1) * wide), slice(0, units)),
            (
                slice(i // turns * narrow, (i // turns + 1) * narrow),
                slice(i % turns * low, (i % turns + 1) * low),
            ),
        )


def weight_kernel(place, act, outer, hidden, pre, low, mid_low, keep, give):
    units, model, cols = act.shape[1], hidden.shape[1], low.shape[1]
    core = place[0]
    for turn, out in ((core, keep), (1 - core, give)):
        down = dot_tn(act[...], outer[turn]).astype(BF)
        up = dot_tn(hidden[...], pre[turn]).astype(BF)
        proj = dot_tn(low[...], mid_low[turn]).astype(BF)
        for i, cut in enumerate(early_cuts(keep.shape[0], units, model, cols)):
            for value, (rows, lanes), at in zip(
                (down, down, up, proj), cut, early_at(units, model, cols)
            ):
                out[i, :, at] = value[rows, lanes]


def weight_grads(core, act, outer, hidden, pre, low, mid_low, parts):
    units, model = act.shape[1], outer.shape[2]
    out = shaped(parts, model // parts, 2 * model + units + low.shape[1])
    return local_call(
        weight_kernel,
        "weight_grads",
        (out, out),
        [SMEM] + [VMEM] * 6,
        (VMEM,) * 2,
        (core, act, outer, hidden, pre, low, mid_low),
        cost=cost(8),
        room=24,
    )


def reverse_kernel(rows, groups, heads, passes, counts, place, *refs):
    grads, kept = refs[:groups], refs[groups : groups + 5]
    own, thumb, weights, columns, small = refs[groups + 5 : groups + 10]
    at = groups + 10
    out_q, give_q, at = refs[at : at + groups // 2], refs[at + groups // 2], at + groups // 2 + 1
    out_kv, at = refs[at : at + groups // 2], at + groups // 2
    keep, give = refs[at : at + 2]
    (
        stage, xq, xk, qx, kx, vx, packed, gx, kt, dq_t, dv, dk, low_q, low_kv, total, sums,
        starts, sems,
    ) = refs[at + 2 :]
    couples = heads // 2
    sources = [*grads, *kept[2:], *kept[:2]]
    targets = [*[stage.at[g] for g in range(groups)], qx, kx, vx, xq, xk]
    copies = [
        pltpu.make_async_copy(f, t, sems.at[i]) for i, (f, t) in enumerate(zip(sources, targets))
    ]
    for copy in copies:
        copy.start()
    cols = heads * HD
    wide = passes * LANES
    q_counts = [counts[g] for g in range(groups)]
    k_counts = [counts[groups + g] for g in range(groups)]
    start = jnp.int32(0)
    for g in range(groups):
        copies[g].wait()
        packed[rows_at(start, rows), :] = stage[g]
        start = start + q_counts[g] * TILE
    q_total, k_total = start, sum(k_counts) * TILE
    tail_lane = iota((BLOCK, packed.shape[1]), 1) - passes * cols
    empty = (tail_lane >= 0) & (tail_lane < 3 * heads) & (tail_lane % 3 == 0)
    packed[rows_at(q_total, BLOCK), :] = jnp.where(empty, FAR, 0.0).astype(BF)
    q_blocks = (q_total + BLOCK - 1) // BLOCK
    k_blocks = (k_total + BLOCK - 1) // BLOCK
    spans = range(groups * TILE // BLOCK, groups * rows // BLOCK + 1)

    row, col = (iota((LANES, heads * LANES), d) for d in (0, 1))
    head, lane = col // LANES, col % LANES
    to_marks = zero_one((lane > HD) & (lane < HD + 4) & (row == 3 * head + lane - HD - 1))
    row, col = (iota((LANES, heads * wide), d) for d in (0, 1))
    head, turn, lane = col // wide, col % wide // LANES, col % LANES
    to_deltas = zero_one(
        (lane >= HD) & (lane < HD + 3) & (row == 3 * heads * (turn + 1) + 3 * head + lane - HD)
    )
    for copy in copies[groups : groups + 3]:
        copy.wait()

    @pl.loop(0, q_blocks)
    def _(b):
        here = rows_at(b * BLOCK, BLOCK, BLOCK)
        stats = packed[here, passes * cols :]
        marks = dot(stats, to_marks)
        deltas = dot(stats, to_deltas).astype(BF)
        for h in range(heads):
            more = marks[:, h * LANES : (h + 1) * LANES]
            qx[h, here, :] = (qx[h, here, :].astype(F32) + more).astype(BF)
            for p in range(passes):
                at = p * cols + h * HD
                mine = (h * passes + p) * LANES
                gx[h, here, p * LANES : (p + 1) * LANES] = jnp.concatenate(
                    [packed[here, at : at + HD], deltas[:, mine + HD : mine + LANES]], axis=1
                )

    @pl.loop(0, k_blocks)
    def _(b):
        here = rows_at(b * BLOCK, BLOCK, BLOCK)
        for h in range(heads):
            kt[h, b] = jnp.transpose(kx[h, here, :].astype(F32))[:HD, :].astype(BF)

    def reverse_all(blocks):
        span = blocks * BLOCK

        @pl.loop(0, couples)
        def _(pair):
            dv[:, :span, :] = jnp.zeros((2, span, wide), F32)
            dk[:, :, :span, :] = jnp.zeros((passes, 2, span, LANES), F32)

            @pl.loop(0, q_blocks)
            def _(b):
                here = rows_at(b * BLOCK, BLOCK, BLOCK)
                for i in range(2):
                    h = 2 * pair + i
                    q, g = qx[h, here, :], gx[h, here, :]
                    k_t = jnp.concatenate([kt[h, j] for j in range(blocks)], axis=1)
                    w = jnp.exp(dot_nt(kx[h, :span, :], q))
                    dv[i, :span, :] += dot(w.astype(BF), g)
                    for p in range(passes):
                        ds = dot_nt(vx[h, :span, :], g[:, p * LANES : (p + 1) * LANES])
                        ds = (w * ds).astype(BF)
                        dk[p, i, :span, :] += dot(ds, q)
                        dq_t[p, i * HD : (i + 1) * HD, :] = dot(k_t, ds)
                for p in range(passes):
                    piece = jnp.transpose(dq_t[p]) * SCALE
                    low_q[pair, here, p * LANES : (p + 1) * LANES] = piece.astype(BF)

            for p in range(passes):
                for c, both in enumerate(
                    (
                        [dk[p, i, :span, :HD] for i in range(2)],
                        [dv[i, :span, p * LANES : p * LANES + HD] for i in range(2)],
                    )
                ):
                    lane = (2 * p + c) * LANES
                    low_kv[pair, :span, lane : lane + LANES] = jnp.concatenate(both, axis=1).astype(BF)

    for blocks in spans:
        pl.when(k_blocks == blocks)(functools.partial(reverse_all, blocks))

    start = jnp.int32(0)
    for g in range(groups):
        starts[g] = start
        start = start + k_counts[g] * TILE
    for g in range(groups):
        here = rows_at(starts[place[1 + g]], rows)
        out_kv[g // 2][g % 2] = jnp.concatenate([low_kv[i, here, :] for i in range(couples)], axis=1)
    start = jnp.int32(0)
    for g in range(groups):
        here = rows_at(start, rows)
        value = jnp.concatenate([low_q[i, here, :] for i in range(couples)], axis=1)
        if g < groups // 2:
            out_q[g][...] = value
        else:
            give_q[g - groups // 2] = value
        start = start + q_counts[g] * TILE

    copies[groups + 3].wait()
    copies[groups + 4].wait()

    def key_sums(blocks):
        span = blocks * BLOCK
        for i in range(couples):
            flat = low_kv[i, :span, :]
            total[i, :, wide:] = dot_tn(xk[:span, :], flat)
            sums[i, :, wide:] = dot(jnp.ones((8, span), BF), flat)

    for blocks in spans:
        pl.when(k_blocks == blocks)(functools.partial(key_sums, blocks))

    total[:, :, :wide] = jnp.zeros((couples, total.shape[1], wide), F32)
    sums[:, :, :wide] = jnp.zeros((couples, 8, wide), F32)

    @pl.loop(0, q_blocks)
    def _(b):
        here = rows_at(b * BLOCK, BLOCK, BLOCK)
        for i in range(couples):
            total[i, :, :wide] += dot_tn(xq[here, :], low_q[i, here, :])
            sums[i, :, :wide] += dot(jnp.ones((8, BLOCK), BF), low_q[i, here, :])

    model = total.shape[1]
    gain, shift = columns[:, 0:1], columns[:, 1:2]
    ones = jnp.ones((8, own.shape[0]), BF)
    for p in range(passes):
        whole = []
        for i in range(couples):
            mine = thumb[i, p]
            part = dot_tn(own[...], mine)
            part_sum = dot(ones, mine)[0:1, :]
            q_at = slice(p * LANES, (p + 1) * LANES)
            kv_at = slice((passes + 2 * p) * LANES, (passes + 2 * p + 2) * LANES)
            part += jnp.concatenate([total[i, :, q_at], total[i, :, kv_at]], axis=1)
            part_sum += jnp.concatenate([sums[i, 0:1, q_at], sums[i, 0:1, kv_at]], axis=1)
            w = weights[i].astype(F32)
            gain_one = jnp.sum(w * part, axis=1, keepdims=True)
            shift_one = jnp.sum(w * part_sum, axis=1, keepdims=True)
            lane = iota((model, LANES), 1)
            tall = jnp.where(lane == 0, gain_one, jnp.where(lane == 1, shift_one, 0.0))
            flat = jnp.concatenate(
                [jnp.zeros((2, LANES), F32)]
                + [part_sum[:, c * LANES : (c + 1) * LANES] for c in range(3)]
                + [jnp.zeros((LANES - 5, LANES), F32)],
                axis=0,
            )
            tall = jnp.concatenate([tall[:LANES] + jnp.transpose(flat), tall[LANES:]], axis=0)
            if i == 0:
                turned = jnp.concatenate(
                    [
                        jnp.zeros((8, model), F32),
                        small[p],
                        jnp.zeros((LANES - 16, model), F32),
                    ],
                    axis=0,
                )
                tall = tall + jnp.transpose(turned)
            whole += [part * gain + shift * part_sum, tall]
        whole = jnp.concatenate(whole, axis=1).astype(BF)

        @pl.when(place[0] == p)
        def _():
            keep[...] = whole

        @pl.when(place[0] != p)
        def _():
            give[...] = whole


def reverse(counts, place, grads, kept, own, thumb, weights, columns, small, rows, heads):
    groups = len(grads)
    couples, passes = thumb.shape[:2]
    model = own.shape[1]
    room = rows * groups + BLOCK
    cols = heads * HD
    wide = passes * LANES
    half = groups // 2
    late = shaped(model, couples * 4 * LANES)
    q, kv = shaped(rows, couples * wide), shaped(2, rows, couples * 2 * wide)
    out = (*[q] * half, shaped(half, rows, couples * wide), *[kv] * half, late, late)
    return local_call(
        functools.partial(reverse_kernel, rows, groups, heads, passes),
        "reverse",
        out,
        [SMEM, SMEM] + [ANY] * (groups + 5) + [VMEM] * 5,
        (VMEM,) * len(out),
        (counts, place, *grads, *kept, own, thumb, weights, columns, small),
        [
            pltpu.VMEM((groups, rows, passes * cols + LANES), BF),
            pltpu.VMEM((room, model), BF),
            pltpu.VMEM((room, model), BF),
            pltpu.VMEM((heads, room, LANES), BF),
            pltpu.VMEM((heads, room, LANES), BF),
            pltpu.VMEM((heads, room, LANES), BF),
            pltpu.VMEM((room, passes * cols + LANES), BF),
            pltpu.VMEM((heads, room, wide), BF),
            pltpu.VMEM((heads, room // BLOCK, HD, BLOCK), BF),
            pltpu.VMEM((passes, LANES, BLOCK), F32),
            pltpu.VMEM((2, room, wide), F32),
            pltpu.VMEM((passes, 2, room, LANES), F32),
            pltpu.VMEM((couples, room, wide), BF),
            pltpu.VMEM((couples, room, 2 * wide), BF),
            pltpu.VMEM((couples, model, 3 * wide), F32),
            pltpu.VMEM((couples, 8, 3 * wide), F32),
            pltpu.SMEM((groups,), jnp.int32),
            pltpu.SemaphoreType.DMA((groups + 5,)),
        ],
        cost(45),
        ROOM,
    )


def grad_one_kernel(near, counts, *refs):
    from_q, from_kv, (thumb, weights, mine, other) = refs[:near], refs[near:-4], refs[-4:]
    couples, passes, size, _ = thumb.shape
    rows = from_q[0].shape[0]
    sum_q = sum(r[...].astype(F32) for r in from_q)
    sum_kv = [sum(r[f].astype(F32) for r in from_kv) for f in range(2)]
    image = iota((rows, 3 * LANES), 0) < counts[0] * TILE
    for p in range(passes):
        parts = []
        for i in range(couples):
            at = (passes * i + p) * LANES
            there = slice(2 * at, 2 * at + 2 * LANES)
            far = jnp.concatenate([sum_q[:, at : at + LANES], sum_kv[0][:, there]], axis=1)
            flat = jnp.concatenate(
                [jnp.where(image, far.astype(BF), thumb[i, p, :rows]), thumb[i, p, rows:]], axis=0
            )
            parts.append(
                (
                    dot_nt(flat, weights[i]),
                    dot_nt(sum_kv[1][:, there].astype(BF), weights[i, :, LANES:]),
                )
            )
        mine[p] = sum(a for a, _ in parts).astype(BF)
        other[p] = sum(b for _, b in parts).astype(BF)


def grad_one(count, from_q, from_kv, thumb, weights):
    near = len(from_q)
    passes, size, _ = thumb.shape[1:]
    model = weights.shape[1]
    return local_call(
        functools.partial(grad_one_kernel, near),
        "grad_one",
        (shaped(passes, size, model), shaped(passes, from_q[0].shape[0], model)),
        [SMEM] + [VMEM] * (near + len(from_kv) + 2),
        (VMEM,) * 2,
        (count, *from_q, *from_kv, thumb, weights),
        cost=cost(5),
        room=ROOM,
    )


def close_kernel(counts, tokens, mid, mine, head, side, cross, gains, out):
    xhat, factor = standard(tokens[...].astype(F32))
    rows = side.shape[1]
    image = iota(side.shape[1:], 0) < counts[0] * TILE
    for p in range(mid.shape[0]):
        grad = mine[p].astype(F32) + head[p].astype(F32)
        more = jnp.where(image, side[p].astype(F32) + cross[p].astype(F32), 0.0)
        grad = jnp.concatenate([grad[:rows] + more, grad[rows:]], axis=0)
        out[p] = mid[p] + norm_back(grad, gains[0:1, :], xhat, factor)


def close(count, tokens, mid, mine, head, side, cross, gains):
    return local_call(
        close_kernel,
        "close",
        shaped(*mid.shape, dtype=F32),
        [SMEM] + [VMEM] * 7,
        VMEM,
        (count, tokens, mid, mine, head, side, cross, gains),
        cost=cost(4),
        room=ROOM,
    )


def early_kernel(lines, far, place, *refs):
    parts, refs = refs[:lines], refs[lines:]
    out, (down, up, proj, sems) = refs[-7:-4], refs[-4:]
    turn, y = place[0], place[10]
    turn = 1 - turn if far else turn
    (units, model), low = down.shape, proj.shape[0]
    steps, rows = parts[0].shape[:2]
    lane_down, lane_next, lane_up, lane_proj = early_at(units, model, low)
    turns = model // low
    for d, ref in enumerate(parts):
        for j in range(steps):
            i = j * lines + (y + lines - d) % lines
            at = pl.multiple_of(2 * rows * i, 2 * rows)
            down[pl.ds(at, rows), :] = ref[j, :, lane_down].astype(F32)
            down[pl.ds(at + rows, rows), :] = ref[j, :, lane_next].astype(F32)
            up[rows_at(rows * i, rows, rows), :] = ref[j, :, lane_up].astype(F32)
            here = rows_at(i // turns * rows, rows, rows)
            value = ref[j, :, lane_proj].astype(F32)
            for t in range(turns):

                @pl.when(i % turns == t)
                def _(value=value, here=here, t=t):
                    proj[here, t * low : (t + 1) * low] = value

    copies = [
        pltpu.make_async_copy(held, to.at[turn], sems.at[n])
        for n, (held, to) in enumerate(zip((down, up, proj), out))
    ]
    for copy in copies:
        copy.start()
    for copy in copies:
        copy.wait()


def early_out(place, parts, before, units, low):
    model = len(parts) * parts[0].shape[0] * parts[0].shape[1]
    shapes = (units, model), (model, units), (low, model)
    return pl.pallas_call(
        functools.partial(early_kernel, len(parts), bool(before)),
        out_shape=tuple(shaped(2, *s, dtype=F32) for s in shapes),
        in_specs=[SMEM] + [VMEM] * len(parts) + [ANY] * len(before),
        out_specs=(ANY,) * 3,
        scratch_shapes=[
            *[pltpu.VMEM(s, F32) for s in shapes],
            pltpu.SemaphoreType.DMA((3,)),
        ],
        input_output_aliases={1 + len(parts) + i: i for i in range(len(before))},
        cost_estimate=cost(5),
        compiler_params=pltpu.CompilerParams(vmem_limit_bytes=ROOM * MIB),
        name="early_far" if before else "early_own",
    )(place, *parts, *before)


def late_kernel(far, place, ref, *refs):
    out, (grad_in, *small), sems = refs[-11:-6], refs[-6:-1], refs[-1]
    in_bias, up_bias, gains, shifts = small
    turn = 1 - place[0] if far else place[0]
    turned = []
    for pair in range(2):
        at = 4 * LANES * pair
        for c in range(3):
            grad_in[c, :, pair * LANES : (pair + 1) * LANES] = ref[
                :, at + c * LANES : at + (c + 1) * LANES
            ].astype(F32)
        turned.append(jnp.transpose(ref[:, at + 3 * LANES : at + 4 * LANES].astype(F32)))
    a, b = turned
    in_bias[...] = jnp.concatenate(
        [
            jnp.concatenate([a[2:3, :LANES], b[2:3, :LANES]], axis=1),
            jnp.concatenate([a[4:5, :LANES], b[4:5, :LANES]], axis=1),
        ],
        axis=0,
    )
    up_bias[...] = jnp.concatenate([a[12:13], a[13:14]], axis=1)
    gains[...] = jnp.concatenate([a[0:1] + b[0:1], a[8:9]], axis=0)
    shifts[...] = jnp.concatenate([a[1:2] + b[1:2], a[10:11], a[9:10], a[11:12]], axis=0)
    copies = [
        pltpu.make_async_copy(held, to.at[turn], sems.at[n])
        for n, (held, to) in enumerate(zip((grad_in, *small), out))
    ]
    for copy in copies:
        copy.start()
    for copy in copies:
        copy.wait()


def late_out(place, part, before, units):
    model = part.shape[0]
    shapes = (3, model, 2 * LANES), (2, 2 * LANES), (1, units), (2, model), (4, model)
    return pl.pallas_call(
        functools.partial(late_kernel, bool(before)),
        out_shape=tuple(shaped(2, *s, dtype=F32) for s in shapes),
        in_specs=[SMEM, VMEM] + [ANY] * len(before),
        out_specs=(ANY,) * 5,
        scratch_shapes=[
            *[pltpu.VMEM(s, F32) for s in shapes],
            pltpu.SemaphoreType.DMA((5,)),
        ],
        input_output_aliases={2 + i: i for i in range(len(before))},
        cost_estimate=cost(3),
        compiler_params=pltpu.CompilerParams(vmem_limit_bytes=ROOM * MIB),
        name="late_far" if before else "late_own",
    )(place, part, *before)


def gather_near(array):
    mine = [array] + [shift_by(array, "y", d) for d in range(1, lax.axis_size("y"))]
    return mine + [shift_by(a, "c", 1) for a in mine]


def return_near(parts):
    return [parts[0]] + [shift_by(p, "y", -j) for j, p in enumerate(parts) if j > 0]


def offsets(size):
    return [(step, flip) for step in range(size) for flip in range(2)]


def return_far(parts):
    return [parts[0]] + [shift_by(p, "z", step) for step, p in enumerate(parts) if step > 0]


PLANE = ("z", "y")


def core_sum(keep, give):
    return (keep.astype(F32) + shift_by(give, "c", 1).astype(F32)).astype(BF)


def crossed(array):
    n = lax.axis_size(("xl", "h"))
    return lax.ppermute(array, ("xl", "h"), [(i, n - 1 - i) for i in range(n)])


def across(low):
    done = low.astype(F32) + shift_by(low, "xl", 1).astype(F32)
    size = 4 * LANES
    ones = jnp.concatenate([low[:, i + 3 * LANES : i + size] for i in range(0, low.shape[1], size)], axis=1)
    more = shift_by(ones, "h", 1).astype(F32) + crossed(ones).astype(F32)
    more = jnp.where(jnp.arange(more.shape[1]) % LANES < 2, more, 0.0)
    nothing = jnp.zeros((low.shape[0], 3 * LANES), F32)
    laid = [[nothing, more[:, i : i + LANES]] for i in range(0, more.shape[1], LANES)]
    return (done + jnp.concatenate(sum(laid, []), axis=1)).astype(BF)


def tied(arrays, others):
    return lax.optimization_barrier((arrays, others))


def local(
    tokens,
    cotangents,
    segment_ids,
    in_weights,
    in_biases,
    out_weight,
    up_weight,
    up_biases,
    down_weight,
    gains,
    shifts,
):
    size, model = tokens.shape
    cols = in_weights.shape[2]
    heads = cols // HD
    rows = size - TILE
    units = up_weight.shape[1]
    c = lax.axis_index("c")

    told, copies, count = front(tokens, segment_ids, lax.axis_size(("z", "xl")))
    far = lax.all_to_all(copies, ("z", "xl"), 0, 0, tiled=True)
    near = gather_near(told)
    core = c.astype(jnp.int32).reshape(1)
    z, xl, z_size = lax.axis_index("z"), lax.axis_index("xl"), lax.axis_size("z")
    routes = [((z + step) % z_size) * 2 + (xl ^ flip) for step, flip in offsets(z_size)]
    place = jnp.stack([c, *routes, z, lax.axis_index("y")]).astype(jnp.int32)
    plane = lax.axis_size(PLANE)

    weights, biases, pairs, columns, bundle = prepare(
        core, in_weights, in_biases, gains, shifts, up_weight, down_weight, up_biases[None], heads
    )
    out_far = crossed(out_weight)
    far_one = crossed(bundle)
    far_two = shift_by(far_one, "c", 1)

    weights, (out_far, columns, place) = tied(weights, (out_far, columns, place))
    *parts, give, xq, xk, qx, kx, vx, counts = attend(
        near, far, weights, biases, gains, shifts, rows, heads
    )
    thumb_out, xhat, x = thumbs(tokens, weights, biases, gains, shifts, heads)
    parts = pair_merge(parts, shift_by(give, "c", 1), heads)
    low, full, lse = merge(count, return_near(parts), thumb_out, heads)
    low_far = shift_by(low, "h", 1)
    mixed, grad_mid, mid_low, packed, hidden, act, pre, small = feed_forward(
        tokens, cotangents, low, low_far, full, lse, out_weight, out_far, up_weight, up_biases[None],
        down_weight, far_one, far_two, gains, shifts, rows, heads,
    )
    grads = gather_near(packed)
    keep, give = weight_grads(core, act, cotangents, hidden, pre, low, mid_low, plane)
    mid_low, (keep, give) = tied(mid_low, (keep, give))
    thumb = thumbs_back(count, x, mid_low, out_weight, heads)
    early = core_sum(keep, give)

    grads, (early, thumb) = tied(grads, (early, thumb))
    early = lax.all_to_all(early, PLANE, 0, 0, tiled=True)
    *out, keep, give = reverse(
        counts, place, grads, (xq, xk, qx, kx, vx), xhat, thumb, pairs, columns, small, rows, heads
    )
    half = len(near) // 2
    out_q, give_q, out_kv = out[:half], out[half], out[half + 1 :]
    early = jnp.sum(early.astype(F32), axis=0).astype(BF)
    early = (early.astype(F32) + shift_by(early, "xl", 1).astype(F32)).astype(BF)
    early = jnp.broadcast_to(early[None], (z_size, *early.shape))
    late, early = tied(core_sum(keep, give), early)
    early = lax.all_to_all(early, "z", 0, 0, tiled=True)
    from_kv = return_far(out_kv)
    out_q = fold(out_q, shift_by(give_q, "c", 1))
    late, (early, from_kv[1], from_kv[-1], out_q) = tied(
        late, (early, from_kv[1], from_kv[-1], out_q)
    )
    late = late.reshape(plane, -1, late.shape[1])
    late = lax.all_to_all(late, PLANE, 0, 0, tiled=True)
    from_q = return_near(out_q)
    early = [early] + [shift_by(early, "y", d) for d in range(1, lax.axis_size("y"))]
    late = across(jnp.sum(late.astype(F32), axis=0).astype(BF))
    late, (from_kv, early, from_q) = tied(late, (from_kv, early, from_q))
    late = jnp.broadcast_to(late[None], (plane, *late.shape))
    late = lax.all_to_all(late, PLANE, 0, 0, tiled=True).reshape(model, -1)

    mine, other = grad_one(count, from_q, from_kv, thumb, pairs)
    grad_tokens = close(
        count, tokens, grad_mid, mine, shift_by(mine, "h", 1), shift_by(other, "xl", 1),
        crossed(other), gains,
    )
    early_far = [shift_by(e, "c", 1) for e in early]
    done = early_out(place, early, (), units, cols)
    grad_down, grad_up, grad_out = early_out(place, early_far, done, units, cols)
    done = late_out(place, late, (), units)
    grad_in, in_bias, up_bias, grad_gains, grad_shifts = late_out(
        place, shift_by(late, "c", 1), done, units
    )
    return (
        mixed,
        grad_tokens,
        grad_in,
        in_bias,
        grad_out,
        grad_up,
        up_bias.reshape(2, units),
        grad_down,
        grad_gains,
        grad_shifts,
    )


def solution(mesh):
    fine = Mesh(mesh.devices.reshape(4, 2, 4, 2, 2), ("z", "xl", "y", "c", "h"))
    blk = ("z", "xl", "y", "c")
    return jax.shard_map(
        local,
        mesh=fine,
        in_specs=(
            P(blk, None),
            P(None, blk, None),
            P(blk),
            P(None, None, "h"),
            P(None, "h"),
            P("h", None),
            P(None, "h"),
            P("h"),
            P("h", None),
            P(),
            P(),
        ),
        out_specs=(
            P(blk, None),
            P(None, blk, None),
            P(None, None, None, "h"),
            P(None, None, "h"),
            P(None, "h", None),
            P(None, None, "h"),
            P(None, "h"),
            P(None, "h", None),
            P(),
            P(),
        ),
        check_vma=False,
    )
```

```python
import functools

import jax
import jax.numpy as jnp
from jax import lax
from jax.experimental import pallas as pl
from jax.experimental.pallas import tpu as pltpu
from jax.sharding import Mesh
from jax.sharding import PartitionSpec as P

HD = 64
LANES = 128
TILE = 64
BLOCK = 256
EPS = 1e-06
SCALE = 0.125
FAR = -1e30
BF = jnp.bfloat16
F32 = jnp.float32
MIB = 1024 * 1024
ROOM = 56

NT = (((1,), (1,)), ((), ()))
TN = (((0,), (0,)), ((), ()))


def shift_by(array, axis, step):
    size = lax.axis_size(axis)
    return lax.ppermute(array, axis, [(i, (i + step) % size) for i in range(size)])


def dot(a, b):
    return jnp.dot(a, b, preferred_element_type=F32)


def dot_nt(a, b):
    return lax.dot_general(a, b, NT, preferred_element_type=F32)


def dot_tn(a, b):
    return lax.dot_general(a, b, TN, preferred_element_type=F32)


def standard(field):
    center = field - jnp.mean(field, axis=-1, keepdims=True)
    factor = lax.rsqrt(jnp.mean(center * center, axis=-1, keepdims=True) + EPS)
    return center * factor, factor


def norm_back(grad, gain, xhat, factor):
    h = grad * gain
    mean = jnp.mean(h, axis=-1, keepdims=True)
    return factor * (h - mean - xhat * jnp.mean(h * xhat, axis=-1, keepdims=True))


def pieces(value):
    high = value.astype(BF)
    rest = value - high.astype(F32)
    middle = rest.astype(BF)
    low = (rest - middle.astype(F32)).astype(BF)
    return high, middle, low


def zero_one(mask):
    return jnp.where(mask, 1.0, 0.0).astype(BF)


def iota(shape, dim):
    return lax.broadcasted_iota(jnp.int32, shape, dim)


VMEM = pl.BlockSpec(memory_space=pltpu.VMEM)
ANY = pl.BlockSpec(memory_space=pl.ANY)
SMEM = pl.BlockSpec(memory_space=pltpu.SMEM)


def local_call(body, name, out, ins, outs, args, scratch=(), cost=None, room=16):
    return pl.pallas_call(
        body,
        out_shape=out,
        in_specs=ins,
        out_specs=outs,
        scratch_shapes=scratch,
        cost_estimate=cost,
        compiler_params=pltpu.CompilerParams(vmem_limit_bytes=room * MIB),
        name=name,
    )(*args)


def shaped(*shape, dtype=BF):
    return jax.ShapeDtypeStruct(shape, dtype)


def cost(micros):
    return pl.CostEstimate(flops=int(micros * 1e9), bytes_accessed=0, transcendentals=0)


def front_kernel(tokens, ids, told, copies, number):
    rows = told.shape[0] - 16
    marks = jnp.where(ids[...] == 0, 1.0, 0.0)
    tiles = jnp.sum(marks).astype(jnp.int32) // TILE
    number[0] = tiles
    told[:rows, :] = tokens[:rows, :]
    told[rows:, :] = jnp.full((16, told.shape[1]), tiles.astype(F32), F32).astype(BF)
    for g in range(copies.shape[0]):
        copies[g] = told[...]


def front(tokens, ids, copies):
    size, model = tokens.shape
    told = size - TILE + 16
    return local_call(
        front_kernel,
        "front",
        (shaped(told, model), shaped(copies, told, model), shaped(1, dtype=jnp.int32)),
        [VMEM, VMEM],
        (VMEM, VMEM, SMEM),
        (tokens, ids.reshape(-1, LANES)),
        room=ROOM,
    )


def prepare_kernel(
    heads, place, in_weights, in_biases, gains, shifts, up, down, bias,
    weights, biases, pairs, columns, out,
):
    core = place[0]
    half = out.shape[1]
    at = pl.ds(pl.multiple_of(core * half, half), half)
    out[:half, :] = up[:, at]
    out[half : 2 * half, :] = down[at, :]
    mine = jnp.where(core == 0, bias[:, :half], bias[:, half:])
    row = iota((16, half), 0)
    rows = jnp.zeros((16, half), F32)
    for i, piece in enumerate(pieces(mine)):
        rows = jnp.where(row == i, piece.astype(F32), rows)
    out[2 * half :, :] = rows.astype(BF)

    model, cols = in_weights.shape[1:]
    width = heads * LANES
    row, col = (iota((cols, width), d) for d in (0, 1))
    spread = zero_one((row // HD == col // LANES) & (row % HD == col % LANES))
    lane = iota((1, width), 1) % LANES
    gap = jnp.zeros((1, HD), F32)

    def apart(line):
        return jnp.concatenate(
            sum([[line[:, h * HD : (h + 1) * HD], gap] for h in range(heads)], []), axis=1
        )

    extra = [
        apart(in_biases[0:1, :] * SCALE) + jnp.where(lane == HD, 1.0, 0.0),
        jnp.where((lane > HD) & (lane < HD + 4), 1.0, 0.0),
        apart(in_biases[1:2, :]) + jnp.where((lane >= HD) & (lane < HD + 3), 1.0, 0.0),
    ]
    for i in range(3):
        factor = SCALE if i == 0 else 1.0
        weights[:, i * width : (i + 1) * width] = (dot(in_weights[i], spread) * factor).astype(BF)
        biases[:, i * width : (i + 1) * width] = extra[i]
        for pair in range(heads // 2):
            pairs[pair, :, i * LANES : (i + 1) * LANES] = in_weights[
                i, :, pair * LANES : (pair + 1) * LANES
            ]
    tall = jnp.concatenate(
        [gains[0:1, :], shifts[0:1, :], jnp.zeros((LANES - 2, model), F32)], axis=0
    )
    columns[...] = jnp.transpose(tall)


def prepare(core, in_weights, in_biases, gains, shifts, up, down, bias, heads):
    model = up.shape[0]
    width = 3 * heads * LANES
    return local_call(
        functools.partial(prepare_kernel, heads),
        "prepare",
        (
            shaped(model, width),
            shaped(1, width, dtype=F32),
            shaped(heads // 2, model, 3 * LANES),
            shaped(model, LANES, dtype=F32),
            shaped(2 * model + 16, model),
        ),
        [SMEM] + [VMEM] * 7,
        (VMEM,) * 5,
        (core, in_weights, in_biases, gains, shifts, up, down, bias),
        cost=cost(4),
        room=ROOM,
    )


def count_of(ref, rows):
    return jnp.max(ref[rows : rows + 16, :LANES].astype(F32)).astype(jnp.int32)


def rows_at(start, rows, step=TILE):
    return pl.ds(pl.multiple_of(start, step), rows)


def attend_kernel(rows, groups, heads, *refs):
    near, far = refs[:groups], refs[groups]
    weights, biases, gains, shifts = refs[groups + 1 : groups + 5]
    at = groups + 5 + groups // 2
    out, give = refs[groups + 5 : at], refs[at]
    kept, counts, place = refs[at + 1 : at + 6], refs[at + 6], refs[at + 7]
    (xq, xk, qx, kx, vx), sems = refs[at + 8 : at + 13], refs[at + 13]
    model = xq.shape[1]
    q_counts = [count_of(r, rows) for r in near]
    k_counts = [count_of(far.at[g], rows) for g in range(groups)]
    for g in range(groups):
        counts[g] = q_counts[g]
        counts[groups + g] = k_counts[g]

    def compact(numbers, read, target):
        start = jnp.int32(0)
        for g, n in enumerate(numbers):
            target[rows_at(start, rows), :] = read(g)
            start = start + n * TILE
        target[rows_at(start, BLOCK), :] = jnp.zeros((BLOCK, model), BF)
        return start

    q_total = compact(q_counts, lambda g: near[g][:rows, :], xq)
    k_total = compact(k_counts, lambda g: far[g, :rows, :], xk)
    q_blocks = (q_total + BLOCK - 1) // BLOCK
    k_blocks = (k_total + BLOCK - 1) // BLOCK
    width = heads * LANES

    def hidden(ref, here):
        clean = standard(ref[here, :].astype(F32))[0].astype(BF)
        ref[here, :] = clean
        return (clean.astype(F32) * gains[0:1, :] + shifts[0:1, :]).astype(BF)

    @pl.loop(0, q_blocks)
    def _(b):
        here = rows_at(b * BLOCK, BLOCK, BLOCK)
        q = (dot(hidden(xq, here), weights[:, :width]) + biases[:, :width]).astype(BF)
        for h in range(heads):
            qx[h, here, :] = q[:, h * LANES : (h + 1) * LANES]

    @pl.loop(0, k_blocks)
    def _(b):
        here = rows_at(b * BLOCK, BLOCK, BLOCK)
        both = dot(hidden(xk, here), weights[:, width:]) + biases[:, width:]
        unseen = (iota((BLOCK, width), 0) + b * BLOCK >= k_total) & (
            iota((BLOCK, width), 1) % LANES == HD
        )
        k = jnp.where(unseen, FAR, both[:, :width]).astype(BF)
        v = both[:, width:].astype(BF)
        for h in range(heads):
            kx[h, here, :] = k[:, h * LANES : (h + 1) * LANES]
            vx[h, here, :] = v[:, h * LANES : (h + 1) * LANES]

    copies = [
        pltpu.make_async_copy(held, to, sems.at[i])
        for i, (held, to) in enumerate(zip((xq, xk, qx, kx, vx), kept))
    ]
    for copy in copies:
        copy.start()

    def attend_all(span):
        @pl.loop(0, q_blocks)
        def _(b):
            here = rows_at(b * BLOCK, BLOCK, BLOCK)
            lane = iota((BLOCK, LANES), 1)
            for h in range(heads):
                s = dot_nt(qx[h, here, :], kx[h, :span, :])
                top = jnp.max(s, axis=-1, keepdims=True)
                o = dot(jnp.exp(s - top).astype(BF), vx[h, :span, :])
                total = o[:, HD : HD + 1]
                o = o / total
                for i, piece in enumerate(pieces(top + jnp.log(total))):
                    o = jnp.where(lane == HD + i, piece.astype(F32), o)
                place[h, here, :] = o.astype(BF)

    for blocks in range(groups * TILE // BLOCK, groups * rows // BLOCK + 1):
        pl.when(k_blocks == blocks)(functools.partial(attend_all, blocks * BLOCK))

    gather = [
        (iota((LANES, LANES), 0) - HD + 3 * h == iota((LANES, LANES), 1))
        & (iota((LANES, LANES), 0) >= HD)
        & (iota((LANES, LANES), 0) < HD + 3)
        for h in range(heads)
    ]
    gather = [jnp.where(m, 1.0, 0.0).astype(BF) for m in gather]
    start = jnp.int32(0)
    for g in range(groups):
        mine = [place[h, rows_at(start, rows), :] for h in range(heads)]
        stats = sum(dot(m, s) for m, s in zip(mine, gather)).astype(BF)
        value = jnp.concatenate([m[:, :HD] for m in mine] + [stats], axis=1)
        if g < groups // 2:
            out[g][...] = value
        else:
            give[g - groups // 2] = value
        start = start + q_counts[g] * TILE
    for copy in copies:
        copy.wait()


def attend(near, far, weights, biases, gains, shifts, rows, heads):
    groups = len(near)
    model = near[0].shape[1]
    room = rows * groups + BLOCK
    parts = heads * HD + LANES
    kept = [(room, model)] * 2 + [(heads, room, LANES)] * 3
    return local_call(
        functools.partial(attend_kernel, rows, groups, heads),
        "attend",
        (
            *[shaped(rows, parts)] * (groups // 2),
            shaped(groups // 2, rows, parts),
            *[shaped(*k) for k in kept],
            shaped(2 * groups, dtype=jnp.int32),
        ),
        [VMEM] * (groups + 5),
        (*[VMEM] * (groups // 2 + 1), *[ANY] * 5, SMEM),
        (*near, far, weights, biases, gains, shifts),
        [
            pltpu.VMEM((heads, room, LANES), BF),
            *[pltpu.VMEM(k, BF) for k in kept],
            pltpu.SemaphoreType.DMA((5,)),
        ],
        cost(15),
        ROOM,
    )


def same_tile(rows):
    return iota((rows, rows), 0) // TILE == iota((rows, rows), 1) // TILE


def thumb_kernel(heads, tokens, weights, biases, gains, shifts, out, xhat, x):
    width = heads * LANES
    size = tokens.shape[0]
    clean = standard(tokens[...].astype(F32))[0].astype(BF)
    xhat[...] = clean
    hidden = (clean.astype(F32) * gains[0:1, :] + shifts[0:1, :]).astype(BF)
    x[...] = (dot(hidden, weights[...]) + biases[...]).astype(BF)
    visible = same_tile(size - TILE)
    out[:TILE, :] = jnp.zeros((TILE, heads * HD), F32)
    for h in range(heads):
        q = x[TILE:, h * LANES : (h + 1) * LANES]
        k = x[TILE:, width + h * LANES : width + (h + 1) * LANES]
        v = x[TILE:, 2 * width + h * LANES : 2 * width + (h + 1) * LANES]
        s = jnp.where(visible, dot_nt(q, k), FAR)
        e = jnp.exp(s - jnp.max(s, axis=-1, keepdims=True))
        o = dot(e.astype(BF), v)[:, :HD] / jnp.sum(e, axis=-1, keepdims=True)
        out[TILE:, h * HD : (h + 1) * HD] = o


def thumbs(tokens, weights, biases, gains, shifts, heads):
    size, model = tokens.shape
    return local_call(
        functools.partial(thumb_kernel, heads),
        "thumbs",
        (
            shaped(size, heads * HD, dtype=F32),
            shaped(size, model),
            shaped(size, 3 * heads * LANES),
        ),
        [VMEM] * 5,
        (VMEM,) * 3,
        (tokens, weights, biases, gains, shifts),
        cost=cost(5),
    )


def merged(parts, heads):
    cols = heads * HD
    row, col = (iota((LANES, cols), d) for d in (0, 1))
    spread = zero_one(row // 3 == col // HD)
    marks = [dot(p[:, cols:], spread) for p in parts]
    top = functools.reduce(jnp.maximum, marks)
    expos = [jnp.exp(m - top) for m in marks]
    total = sum(expos)
    mixed = sum(e * p[:, :cols].astype(F32) for p, e in zip(parts, expos)) / total
    row, col = (iota((cols, LANES), d) for d in (0, 1))
    packed = [
        dot(piece, zero_one((row % HD == 0) & (col == 3 * (row // HD) + i)))
        for i, piece in enumerate(pieces(top + jnp.log(total)))
    ]
    return mixed, sum(packed)


def pair_kernel(heads, *refs):
    count = (len(refs) - 1) // 2
    for j, (mine, out) in enumerate(zip(refs[:count], refs[count + 1 :])):
        mixed, marks = merged([mine[...], refs[count][j]], heads)
        out[...] = jnp.concatenate([mixed.astype(BF), marks.astype(BF)], axis=1)


def pair_merge(parts, other, heads):
    return local_call(
        functools.partial(pair_kernel, heads),
        "pair_merge",
        tuple(shaped(*p.shape) for p in parts),
        [VMEM] * (len(parts) + 1),
        (VMEM,) * len(parts),
        (*parts, other),
        cost=cost(3),
        room=ROOM,
    )


def merge_kernel(heads, counts, thumb, *refs):
    parts, (low, full, lse) = refs[:-3], refs[-3:]
    cols = heads * HD
    rows = lse.shape[0]
    mixed, marks = merged([p[...] for p in parts], heads)
    lse[...] = (-marks).astype(BF)
    image = iota((rows, cols), 0) < counts[0] * TILE
    full[:rows, :] = jnp.where(image, mixed, thumb[:rows, :])
    full[rows:, :] = thumb[rows:, :]
    low[...] = full[...].astype(BF)


def merge(count, parts, thumb, heads):
    size, cols = thumb.shape
    return local_call(
        functools.partial(merge_kernel, heads),
        "merge",
        (shaped(size, cols), shaped(size, cols, dtype=F32), shaped(parts[0].shape[0], LANES)),
        [SMEM] + [VMEM] * (1 + len(parts)),
        (VMEM,) * 3,
        (count, thumb, *parts),
        cost=cost(3),
    )


def fold_kernel(*refs):
    count = (len(refs) - 1) // 2
    for j, (mine, out) in enumerate(zip(refs[:count], refs[count + 1 :])):
        out[...] = (mine[...].astype(F32) + refs[count][j].astype(F32)).astype(BF)


def fold(parts, other):
    return local_call(
        fold_kernel,
        "fold",
        tuple(shaped(*p.shape) for p in parts),
        [VMEM] * (len(parts) + 1),
        (VMEM,) * len(parts),
        (*parts, other),
        cost=cost(2),
        room=ROOM,
    )


ROOT = 0.7978845608028654
CUBE = 0.044715


def ff_kernel(
    heads, tokens, outer, low, low_far, full, lse, out_weight, out_far, up, up_bias, down, far_one,
    far_two, gains, shifts, mixed, grad_mid, grad_low, packed, hidden_out, act_out, pre_out, small,
):
    size, model = tokens.shape
    passes = outer.shape[0]
    cols = heads * HD
    chunk = far_one.shape[1]
    units = up.shape[1]
    rows = packed.shape[0]
    branch = dot(low[...], out_weight[...]) + dot(low_far[...], out_far[...])
    middle = tokens[...].astype(F32) + (branch + shifts[1:2, :])
    xhat, factor = standard(middle)
    hidden = (xhat * gains[1:2, :] + shifts[2:3, :]).astype(BF)
    hidden_out[...] = hidden

    def one_chunk(up_part, bias, down_part, keep):
        v = dot(hidden, up_part) + bias
        t = jnp.tanh(ROOT * (v + CUBE * (v * v * v)))
        act = (0.5 * v * (1.0 + t)).astype(BF)
        slope = 0.5 * (1.0 + t) + 0.5 * v * (1.0 - t * t) * (ROOT * (1.0 + 3.0 * CUBE * (v * v)))
        two = []
        for p in range(passes):
            pre = (dot_nt(outer[p], down_part) * slope).astype(BF)
            if keep is not None:
                pre_out[p, :, keep] = pre
            two.append(dot_nt(pre, up_part))
        if keep is not None:
            act_out[:, keep] = act
        return dot(act, down_part), two

    def far_chunk(ref):
        told = ref[2 * chunk : 2 * chunk + 16, :].astype(F32)
        bias = told[0:1] + told[1:2] + told[2:3]
        return one_chunk(ref[:chunk, :], bias, ref[chunk : 2 * chunk, :], None)

    done = []
    for i in range(units // chunk):
        at = slice(i * chunk, (i + 1) * chunk)
        done.append(one_chunk(up[:, at], up_bias[:, at], down[at, :], at))
    done += [far_chunk(far_one), far_chunk(far_two)]

    def tree(parts):
        half = len(parts) // 2
        return sum(parts[:half]) + sum(parts[half:])

    output = tree([d[0] for d in done])
    mixed[...] = (middle + (output + shifts[3:4, :])).astype(BF)
    small[...] = jnp.zeros(small.shape, F32)
    lane = iota((rows, LANES), 1)
    stats = jnp.zeros((rows, LANES), F32)
    for p in range(passes):
        two = tree([d[1][p] for d in done])
        c = outer[p].astype(F32)
        mid = c + norm_back(two, gains[1:2, :], xhat, factor)
        mid_low = mid.astype(BF)
        grad_mid[p] = mid
        grad_low[p] = mid_low
        att = dot_nt(mid_low, out_weight[...]).astype(BF)
        packed[:, p * cols : (p + 1) * cols] = att[:rows, :]
        pre_out_p = pre_out[p].astype(F32)
        bias = jnp.sum(pre_out_p, axis=0, keepdims=True)
        small[p, 0:1, :] = jnp.sum(two * xhat, axis=0, keepdims=True)
        small[p, 1:2, :] = jnp.sum(two, axis=0, keepdims=True)
        small[p, 2:3, :] = jnp.sum(mid_low.astype(F32), axis=0, keepdims=True)
        small[p, 3:4, :] = jnp.sum(c, axis=0, keepdims=True)
        for i in range(units // model):
            small[p, 4 + i : 5 + i, :] = bias[:, i * model : (i + 1) * model]
        product = att[:rows, :].astype(F32) * full[:rows, :]
        for h in range(heads):
            delta = jnp.sum(product[:, h * HD : (h + 1) * HD], axis=-1, keepdims=True)
            for i, piece in enumerate(pieces(-delta)):
                stats = jnp.where(lane == 3 * heads * (p + 1) + 3 * h + i, piece.astype(F32), stats)
    packed[:, passes * cols :] = (stats + lse[...].astype(F32)).astype(BF)


def feed_forward(
    tokens, outer, low, low_far, full, lse, out_weight, out_far, up, up_bias, down, far_one, far_two,
    gains, shifts, rows, heads,
):
    size, model = tokens.shape
    passes = outer.shape[0]
    units = up.shape[1]
    return local_call(
        functools.partial(ff_kernel, heads),
        "feed_forward",
        (
            shaped(size, model),
            shaped(passes, size, model, dtype=F32),
            shaped(passes, size, model),
            shaped(rows, passes * heads * HD + LANES),
            shaped(size, model),
            shaped(size, units),
            shaped(passes, size, units),
            shaped(passes, 8, model, dtype=F32),
        ),
        [VMEM] * 15,
        (VMEM,) * 8,
        (
            tokens, outer, low, low_far, full, lse, out_weight, out_far, up, up_bias, down, far_one,
            far_two, gains, shifts,
        ),
        cost=cost(12),
        room=32,
    )


def thumb_back_kernel(heads, counts, x, mid_low, out_weight, out):
    width = heads * LANES
    size = x.shape[0]
    passes = mid_low.shape[0]
    visible = same_tile(size - TILE)
    outside = iota((size - TILE, HD), 0) + TILE >= counts[0] * TILE
    grads = [dot_nt(mid_low[p], out_weight[...]).astype(BF) for p in range(passes)]
    out[:, :, :TILE, :] = jnp.zeros((*out.shape[:2], TILE, out.shape[3]), BF)
    for h in range(heads):
        q = x[TILE:, h * LANES : (h + 1) * LANES]
        k = x[TILE:, width + h * LANES : width + (h + 1) * LANES]
        v = x[TILE:, 2 * width + h * LANES : 2 * width + h * LANES + HD]
        s = jnp.where(visible, dot_nt(q, k), FAR)
        e = jnp.exp(s - jnp.max(s, axis=-1, keepdims=True))
        w = e / jnp.sum(e, axis=-1, keepdims=True)
        w_low = w.astype(BF)
        for p in range(passes):
            g = grads[p][TILE:, h * HD : (h + 1) * HD]
            gw = dot_nt(g, v)
            ds = (w * (gw - jnp.sum(w * gw, axis=-1, keepdims=True))).astype(BF)
            dq = dot(ds, k[:, :HD]) * SCALE
            dk = dot_tn(ds, q)[:, :HD]
            dv = dot_tn(w_low, g)
            for c, piece in enumerate((dq, dk, dv)):
                at = c * LANES + (h % 2) * HD
                out[h // 2, p, TILE:, at : at + HD] = jnp.where(outside, piece, 0.0).astype(BF)


def thumbs_back(count, x, mid_low, out_weight, heads):
    passes, size, _ = mid_low.shape
    return local_call(
        functools.partial(thumb_back_kernel, heads),
        "thumbs_back",
        shaped(heads // 2, passes, size, 3 * LANES),
        [SMEM] + [VMEM] * 3,
        VMEM,
        (count, x, mid_low, out_weight),
        cost=cost(6),
    )


def early_at(units, model, low):
    ends = [model, 2 * model, 2 * model + units, 2 * model + units + low]
    return [slice(b - w, b) for b, w in zip(ends, (model, model, units, low))]


def early_cuts(parts, units, model, low):
    high, wide, turns = units // parts // 2, model // parts, model // low
    narrow = low * turns // parts
    for i in range(parts):
        yield (
            (slice(2 * i * high, (2 * i + 1) * high), slice(0, model)),
            (slice((2 * i + 1) * high, (2 * i + 2) * high), slice(0, model)),
            (slice(i * wide, (i + 1) * wide), slice(0, units)),
            (
                slice(i // turns * narrow, (i // turns + 1) * narrow),
                slice(i % turns * low, (i % turns + 1) * low),
            ),
        )


def weight_kernel(place, act, outer, hidden, pre, low, mid_low, keep, give):
    units, model, cols = act.shape[1], hidden.shape[1], low.shape[1]
    core = place[0]
    for turn, out in ((core, keep), (1 - core, give)):
        down = dot_tn(act[...], outer[turn]).astype(BF)
        up = dot_tn(hidden[...], pre[turn]).astype(BF)
        proj = dot_tn(low[...], mid_low[turn]).astype(BF)
        for i, cut in enumerate(early_cuts(keep.shape[0], units, model, cols)):
            for value, (rows, lanes), at in zip(
                (down, down, up, proj), cut, early_at(units, model, cols)
            ):
                out[i, :, at] = value[rows, lanes]


def weight_grads(core, act, outer, hidden, pre, low, mid_low, parts):
    units, model = act.shape[1], outer.shape[2]
    out = shaped(parts, model // parts, 2 * model + units + low.shape[1])
    return local_call(
        weight_kernel,
        "weight_grads",
        (out, out),
        [SMEM] + [VMEM] * 6,
        (VMEM,) * 2,
        (core, act, outer, hidden, pre, low, mid_low),
        cost=cost(8),
        room=24,
    )


def reverse_kernel(rows, groups, heads, passes, counts, place, *refs):
    grads, kept = refs[:groups], refs[groups : groups + 5]
    own, thumb, weights, columns, small = refs[groups + 5 : groups + 10]
    at = groups + 10
    out_q, give_q, at = refs[at : at + groups // 2], refs[at + groups // 2], at + groups // 2 + 1
    out_kv, at = refs[at : at + groups // 2], at + groups // 2
    keep, give = refs[at : at + 2]
    (
        stage, xq, xk, qx, kx, vx, packed, gx, kt, dq_t, dv, dk, low_q, low_kv, total, sums,
        starts, sems,
    ) = refs[at + 2 :]
    couples = heads // 2
    sources = [*grads, *kept[2:], *kept[:2]]
    targets = [*[stage.at[g] for g in range(groups)], qx, kx, vx, xq, xk]
    copies = [
        pltpu.make_async_copy(f, t, sems.at[i]) for i, (f, t) in enumerate(zip(sources, targets))
    ]
    for copy in copies:
        copy.start()
    cols = heads * HD
    wide = passes * LANES
    q_counts = [counts[g] for g in range(groups)]
    k_counts = [counts[groups + g] for g in range(groups)]
    start = jnp.int32(0)
    for g in range(groups):
        copies[g].wait()
        packed[rows_at(start, rows), :] = stage[g]
        start = start + q_counts[g] * TILE
    q_total, k_total = start, sum(k_counts) * TILE
    tail_lane = iota((BLOCK, packed.shape[1]), 1) - passes * cols
    empty = (tail_lane >= 0) & (tail_lane < 3 * heads) & (tail_lane % 3 == 0)
    packed[rows_at(q_total, BLOCK), :] = jnp.where(empty, FAR, 0.0).astype(BF)
    q_blocks = (q_total + BLOCK - 1) // BLOCK
    k_blocks = (k_total + BLOCK - 1) // BLOCK
    spans = range(groups * TILE // BLOCK, groups * rows // BLOCK + 1)

    row, col = (iota((LANES, heads * LANES), d) for d in (0, 1))
    head, lane = col // LANES, col % LANES
    to_marks = zero_one((lane > HD) & (lane < HD + 4) & (row == 3 * head + lane - HD - 1))
    row, col = (iota((LANES, heads * wide), d) for d in (0, 1))
    head, turn, lane = col // wide, col % wide // LANES, col % LANES
    to_deltas = zero_one(
        (lane >= HD) & (lane < HD + 3) & (row == 3 * heads * (turn + 1) + 3 * head + lane - HD)
    )
    for copy in copies[groups : groups + 3]:
        copy.wait()

    @pl.loop(0, q_blocks)
    def _(b):
        here = rows_at(b * BLOCK, BLOCK, BLOCK)
        stats = packed[here, passes * cols :]
        marks = dot(stats, to_marks)
        deltas = dot(stats, to_deltas).astype(BF)
        for h in range(heads):
            more = marks[:, h * LANES : (h + 1) * LANES]
            qx[h, here, :] = (qx[h, here, :].astype(F32) + more).astype(BF)
            for p in range(passes):
                at = p * cols + h * HD
                mine = (h * passes + p) * LANES
                gx[h, here, p * LANES : (p + 1) * LANES] = jnp.concatenate(
                    [packed[here, at : at + HD], deltas[:, mine + HD : mine + LANES]], axis=1
                )

    @pl.loop(0, k_blocks)
    def _(b):
        here = rows_at(b * BLOCK, BLOCK, BLOCK)
        for h in range(heads):
            kt[h, b] = jnp.transpose(kx[h, here, :].astype(F32))[:HD, :].astype(BF)

    def reverse_all(blocks):
        span = blocks * BLOCK

        @pl.loop(0, couples)
        def _(pair):
            dv[:, :span, :] = jnp.zeros((2, span, wide), F32)
            dk[:, :, :span, :] = jnp.zeros((passes, 2, span, LANES), F32)

            @pl.loop(0, q_blocks)
            def _(b):
                here = rows_at(b * BLOCK, BLOCK, BLOCK)
                for i in range(2):
                    h = 2 * pair + i
                    q, g = qx[h, here, :], gx[h, here, :]
                    k_t = jnp.concatenate([kt[h, j] for j in range(blocks)], axis=1)
                    w = jnp.exp(dot_nt(kx[h, :span, :], q))
                    dv[i, :span, :] += dot(w.astype(BF), g)
                    for p in range(passes):
                        ds = dot_nt(vx[h, :span, :], g[:, p * LANES : (p + 1) * LANES])
                        ds = (w * ds).astype(BF)
                        dk[p, i, :span, :] += dot(ds, q)
                        dq_t[p, i * HD : (i + 1) * HD, :] = dot(k_t, ds)
                for p in range(passes):
                    piece = jnp.transpose(dq_t[p]) * SCALE
                    low_q[pair, here, p * LANES : (p + 1) * LANES] = piece.astype(BF)

            for p in range(passes):
                for c, both in enumerate(
                    (
                        [dk[p, i, :span, :HD] for i in range(2)],
                        [dv[i, :span, p * LANES : p * LANES + HD] for i in range(2)],
                    )
                ):
                    lane = (2 * p + c) * LANES
                    low_kv[pair, :span, lane : lane + LANES] = jnp.concatenate(both, axis=1).astype(BF)

    for blocks in spans:
        pl.when(k_blocks == blocks)(functools.partial(reverse_all, blocks))

    start = jnp.int32(0)
    for g in range(groups):
        starts[g] = start
        start = start + k_counts[g] * TILE
    for g in range(groups):
        here = rows_at(starts[place[1 + g]], rows)
        out_kv[g // 2][g % 2] = jnp.concatenate([low_kv[i, here, :] for i in range(couples)], axis=1)
    start = jnp.int32(0)
    for g in range(groups):
        here = rows_at(start, rows)
        value = jnp.concatenate([low_q[i, here, :] for i in range(couples)], axis=1)
        if g < groups // 2:
            out_q[g][...] = value
        else:
            give_q[g - groups // 2] = value
        start = start + q_counts[g] * TILE

    copies[groups + 3].wait()
    copies[groups + 4].wait()

    def key_sums(blocks):
        span = blocks * BLOCK
        for i in range(couples):
            flat = low_kv[i, :span, :]
            total[i, :, wide:] = dot_tn(xk[:span, :], flat)
            sums[i, :, wide:] = dot(jnp.ones((8, span), BF), flat)

    for blocks in spans:
        pl.when(k_blocks == blocks)(functools.partial(key_sums, blocks))

    total[:, :, :wide] = jnp.zeros((couples, total.shape[1], wide), F32)
    sums[:, :, :wide] = jnp.zeros((couples, 8, wide), F32)

    @pl.loop(0, q_blocks)
    def _(b):
        here = rows_at(b * BLOCK, BLOCK, BLOCK)
        for i in range(couples):
            total[i, :, :wide] += dot_tn(xq[here, :], low_q[i, here, :])
            sums[i, :, :wide] += dot(jnp.ones((8, BLOCK), BF), low_q[i, here, :])

    model = total.shape[1]
    gain, shift = columns[:, 0:1], columns[:, 1:2]
    ones = jnp.ones((8, own.shape[0]), BF)
    for p in range(passes):
        whole = []
        for i in range(couples):
            mine = thumb[i, p]
            part = dot_tn(own[...], mine)
            part_sum = dot(ones, mine)[0:1, :]
            q_at = slice(p * LANES, (p + 1) * LANES)
            kv_at = slice((passes + 2 * p) * LANES, (passes + 2 * p + 2) * LANES)
            part += jnp.concatenate([total[i, :, q_at], total[i, :, kv_at]], axis=1)
            part_sum += jnp.concatenate([sums[i, 0:1, q_at], sums[i, 0:1, kv_at]], axis=1)
            w = weights[i].astype(F32)
            gain_one = jnp.sum(w * part, axis=1, keepdims=True)
            shift_one = jnp.sum(w * part_sum, axis=1, keepdims=True)
            lane = iota((model, LANES), 1)
            tall = jnp.where(lane == 0, gain_one, jnp.where(lane == 1, shift_one, 0.0))
            flat = jnp.concatenate(
                [jnp.zeros((2, LANES), F32)]
                + [part_sum[:, c * LANES : (c + 1) * LANES] for c in range(3)]
                + [jnp.zeros((LANES - 5, LANES), F32)],
                axis=0,
            )
            tall = jnp.concatenate([tall[:LANES] + jnp.transpose(flat), tall[LANES:]], axis=0)
            if i == 0:
                turned = jnp.concatenate(
                    [
                        jnp.zeros((8, model), F32),
                        small[p],
                        jnp.zeros((LANES - 16, model), F32),
                    ],
                    axis=0,
                )
                tall = tall + jnp.transpose(turned)
            whole += [part * gain + shift * part_sum, tall]
        whole = jnp.concatenate(whole, axis=1).astype(BF)

        @pl.when(place[0] == p)
        def _():
            keep[...] = whole

        @pl.when(place[0] != p)
        def _():
            give[...] = whole


def reverse(counts, place, grads, kept, own, thumb, weights, columns, small, rows, heads):
    groups = len(grads)
    couples, passes = thumb.shape[:2]
    model = own.shape[1]
    room = rows * groups + BLOCK
    cols = heads * HD
    wide = passes * LANES
    half = groups // 2
    late = shaped(model, couples * 4 * LANES)
    q, kv = shaped(rows, couples * wide), shaped(2, rows, couples * 2 * wide)
    out = (*[q] * half, shaped(half, rows, couples * wide), *[kv] * half, late, late)
    return local_call(
        functools.partial(reverse_kernel, rows, groups, heads, passes),
        "reverse",
        out,
        [SMEM, SMEM] + [ANY] * (groups + 5) + [VMEM] * 5,
        (VMEM,) * len(out),
        (counts, place, *grads, *kept, own, thumb, weights, columns, small),
        [
            pltpu.VMEM((groups, rows, passes * cols + LANES), BF),
            pltpu.VMEM((room, model), BF),
            pltpu.VMEM((room, model), BF),
            pltpu.VMEM((heads, room, LANES), BF),
            pltpu.VMEM((heads, room, LANES), BF),
            pltpu.VMEM((heads, room, LANES), BF),
            pltpu.VMEM((room, passes * cols + LANES), BF),
            pltpu.VMEM((heads, room, wide), BF),
            pltpu.VMEM((heads, room // BLOCK, HD, BLOCK), BF),
            pltpu.VMEM((passes, LANES, BLOCK), F32),
            pltpu.VMEM((2, room, wide), F32),
            pltpu.VMEM((passes, 2, room, LANES), F32),
            pltpu.VMEM((couples, room, wide), BF),
            pltpu.VMEM((couples, room, 2 * wide), BF),
            pltpu.VMEM((couples, model, 3 * wide), F32),
            pltpu.VMEM((couples, 8, 3 * wide), F32),
            pltpu.SMEM((groups,), jnp.int32),
            pltpu.SemaphoreType.DMA((groups + 5,)),
        ],
        cost(45),
        ROOM,
    )


def grad_one_kernel(near, counts, *refs):
    from_q, from_kv, (thumb, weights, mine, other) = refs[:near], refs[near:-4], refs[-4:]
    couples, passes, size, _ = thumb.shape
    rows = from_q[0].shape[0]
    sum_q = sum(r[...].astype(F32) for r in from_q)
    sum_kv = [sum(r[f].astype(F32) for r in from_kv) for f in range(2)]
    image = iota((rows, 3 * LANES), 0) < counts[0] * TILE
    for p in range(passes):
        parts = []
        for i in range(couples):
            at = (passes * i + p) * LANES
            there = slice(2 * at, 2 * at + 2 * LANES)
            far = jnp.concatenate([sum_q[:, at : at + LANES], sum_kv[0][:, there]], axis=1)
            flat = jnp.concatenate(
                [jnp.where(image, far.astype(BF), thumb[i, p, :rows]), thumb[i, p, rows:]], axis=0
            )
            parts.append(
                (
                    dot_nt(flat, weights[i]),
                    dot_nt(sum_kv[1][:, there].astype(BF), weights[i, :, LANES:]),
                )
            )
        mine[p] = sum(a for a, _ in parts).astype(BF)
        other[p] = sum(b for _, b in parts).astype(BF)


def grad_one(count, from_q, from_kv, thumb, weights):
    near = len(from_q)
    passes, size, _ = thumb.shape[1:]
    model = weights.shape[1]
    return local_call(
        functools.partial(grad_one_kernel, near),
        "grad_one",
        (shaped(passes, size, model), shaped(passes, from_q[0].shape[0], model)),
        [SMEM] + [VMEM] * (near + len(from_kv) + 2),
        (VMEM,) * 2,
        (count, *from_q, *from_kv, thumb, weights),
        cost=cost(5),
        room=ROOM,
    )


def close_kernel(counts, tokens, mid, mine, head, side, cross, gains, out):
    xhat, factor = standard(tokens[...].astype(F32))
    rows = side.shape[1]
    image = iota(side.shape[1:], 0) < counts[0] * TILE
    for p in range(mid.shape[0]):
        grad = mine[p].astype(F32) + head[p].astype(F32)
        more = jnp.where(image, side[p].astype(F32) + cross[p].astype(F32), 0.0)
        grad = jnp.concatenate([grad[:rows] + more, grad[rows:]], axis=0)
        out[p] = mid[p] + norm_back(grad, gains[0:1, :], xhat, factor)


def close(count, tokens, mid, mine, head, side, cross, gains):
    return local_call(
        close_kernel,
        "close",
        shaped(*mid.shape, dtype=F32),
        [SMEM] + [VMEM] * 7,
        VMEM,
        (count, tokens, mid, mine, head, side, cross, gains),
        cost=cost(4),
        room=ROOM,
    )


def early_kernel(lines, far, place, *refs):
    parts, refs = refs[:lines], refs[lines:]
    out, (down, up, proj, sems) = refs[-7:-4], refs[-4:]
    turn, y = place[0], place[10]
    turn = 1 - turn if far else turn
    (units, model), low = down.shape, proj.shape[0]
    steps, rows = parts[0].shape[:2]
    lane_down, lane_next, lane_up, lane_proj = early_at(units, model, low)
    turns = model // low
    for d, ref in enumerate(parts):
        for j in range(steps):
            i = j * lines + (y + lines - d) % lines
            at = pl.multiple_of(2 * rows * i, 2 * rows)
            down[pl.ds(at, rows), :] = ref[j, :, lane_down].astype(F32)
            down[pl.ds(at + rows, rows), :] = ref[j, :, lane_next].astype(F32)
            up[rows_at(rows * i, rows, rows), :] = ref[j, :, lane_up].astype(F32)
            here = rows_at(i // turns * rows, rows, rows)
            value = ref[j, :, lane_proj].astype(F32)
            for t in range(turns):

                @pl.when(i % turns == t)
                def _(value=value, here=here, t=t):
                    proj[here, t * low : (t + 1) * low] = value

    copies = [
        pltpu.make_async_copy(held, to.at[turn], sems.at[n])
        for n, (held, to) in enumerate(zip((down, up, proj), out))
    ]
    for copy in copies:
        copy.start()
    for copy in copies:
        copy.wait()


def early_out(place, parts, before, units, low):
    model = len(parts) * parts[0].shape[0] * parts[0].shape[1]
    shapes = (units, model), (model, units), (low, model)
    return pl.pallas_call(
        functools.partial(early_kernel, len(parts), bool(before)),
        out_shape=tuple(shaped(2, *s, dtype=F32) for s in shapes),
        in_specs=[SMEM] + [VMEM] * len(parts) + [ANY] * len(before),
        out_specs=(ANY,) * 3,
        scratch_shapes=[
            *[pltpu.VMEM(s, F32) for s in shapes],
            pltpu.SemaphoreType.DMA((3,)),
        ],
        input_output_aliases={1 + len(parts) + i: i for i in range(len(before))},
        cost_estimate=cost(5),
        compiler_params=pltpu.CompilerParams(vmem_limit_bytes=ROOM * MIB),
        name="early_far" if before else "early_own",
    )(place, *parts, *before)


def late_kernel(far, place, ref, *refs):
    out, (grad_in, *small), sems = refs[-11:-6], refs[-6:-1], refs[-1]
    in_bias, up_bias, gains, shifts = small
    turn = 1 - place[0] if far else place[0]
    turned = []
    for pair in range(2):
        at = 4 * LANES * pair
        for c in range(3):
            grad_in[c, :, pair * LANES : (pair + 1) * LANES] = ref[
                :, at + c * LANES : at + (c + 1) * LANES
            ].astype(F32)
        turned.append(jnp.transpose(ref[:, at + 3 * LANES : at + 4 * LANES].astype(F32)))
    a, b = turned
    in_bias[...] = jnp.concatenate(
        [
            jnp.concatenate([a[2:3, :LANES], b[2:3, :LANES]], axis=1),
            jnp.concatenate([a[4:5, :LANES], b[4:5, :LANES]], axis=1),
        ],
        axis=0,
    )
    up_bias[...] = jnp.concatenate([a[12:13], a[13:14]], axis=1)
    gains[...] = jnp.concatenate([a[0:1] + b[0:1], a[8:9]], axis=0)
    shifts[...] = jnp.concatenate([a[1:2] + b[1:2], a[10:11], a[9:10], a[11:12]], axis=0)
    copies = [
        pltpu.make_async_copy(held, to.at[turn], sems.at[n])
        for n, (held, to) in enumerate(zip((grad_in, *small), out))
    ]
    for copy in copies:
        copy.start()
    for copy in copies:
        copy.wait()


def late_out(place, part, before, units):
    model = part.shape[0]
    shapes = (3, model, 2 * LANES), (2, 2 * LANES), (1, units), (2, model), (4, model)
    return pl.pallas_call(
        functools.partial(late_kernel, bool(before)),
        out_shape=tuple(shaped(2, *s, dtype=F32) for s in shapes),
        in_specs=[SMEM, VMEM] + [ANY] * len(before),
        out_specs=(ANY,) * 5,
        scratch_shapes=[
            *[pltpu.VMEM(s, F32) for s in shapes],
            pltpu.SemaphoreType.DMA((5,)),
        ],
        input_output_aliases={2 + i: i for i in range(len(before))},
        cost_estimate=cost(3),
        compiler_params=pltpu.CompilerParams(vmem_limit_bytes=ROOM * MIB),
        name="late_far" if before else "late_own",
    )(place, part, *before)


def gather_near(array):
    mine = [array] + [shift_by(array, "y", d) for d in range(1, lax.axis_size("y"))]
    return mine + [shift_by(a, "c", 1) for a in mine]


def return_near(parts):
    return [parts[0]] + [shift_by(p, "y", -j) for j, p in enumerate(parts) if j > 0]


def offsets(size):
    return [(step, flip) for step in range(size) for flip in range(2)]


def return_far(parts):
    return [parts[0]] + [shift_by(p, "z", step) for step, p in enumerate(parts) if step > 0]


PLANE = ("z", "y")


def core_sum(keep, give):
    return (keep.astype(F32) + shift_by(give, "c", 1).astype(F32)).astype(BF)


def crossed(array):
    n = lax.axis_size(("xl", "h"))
    return lax.ppermute(array, ("xl", "h"), [(i, n - 1 - i) for i in range(n)])


def across(low):
    done = low.astype(F32) + shift_by(low, "xl", 1).astype(F32)
    size = 4 * LANES
    ones = jnp.concatenate([low[:, i + 3 * LANES : i + size] for i in range(0, low.shape[1], size)], axis=1)
    more = shift_by(ones, "h", 1).astype(F32) + crossed(ones).astype(F32)
    more = jnp.where(jnp.arange(more.shape[1]) % LANES < 2, more, 0.0)
    nothing = jnp.zeros((low.shape[0], 3 * LANES), F32)
    laid = [[nothing, more[:, i : i + LANES]] for i in range(0, more.shape[1], LANES)]
    return (done + jnp.concatenate(sum(laid, []), axis=1)).astype(BF)


def tied(arrays, others):
    return lax.optimization_barrier((arrays, others))


def local(
    tokens,
    cotangents,
    segment_ids,
    in_weights,
    in_biases,
    out_weight,
    up_weight,
    up_biases,
    down_weight,
    gains,
    shifts,
):
    size, model = tokens.shape
    cols = in_weights.shape[2]
    heads = cols // HD
    rows = size - TILE
    units = up_weight.shape[1]
    c = lax.axis_index("c")

    told, copies, count = front(tokens, segment_ids, lax.axis_size(("z", "xl")))
    far = lax.all_to_all(copies, ("z", "xl"), 0, 0, tiled=True)
    near = gather_near(told)
    core = c.astype(jnp.int32).reshape(1)
    z, xl, z_size = lax.axis_index("z"), lax.axis_index("xl"), lax.axis_size("z")
    routes = [((z + step) % z_size) * 2 + (xl ^ flip) for step, flip in offsets(z_size)]
    place = jnp.stack([c, *routes, z, lax.axis_index("y")]).astype(jnp.int32)
    plane = lax.axis_size(PLANE)

    weights, biases, pairs, columns, bundle = prepare(
        core, in_weights, in_biases, gains, shifts, up_weight, down_weight, up_biases[None], heads
    )
    out_far = crossed(out_weight)
    far_one = crossed(bundle)
    far_two = shift_by(far_one, "c", 1)

    weights, (out_far, columns, place) = tied(weights, (out_far, columns, place))
    *parts, give, xq, xk, qx, kx, vx, counts = attend(
        near, far, weights, biases, gains, shifts, rows, heads
    )
    thumb_out, xhat, x = thumbs(tokens, weights, biases, gains, shifts, heads)
    parts = pair_merge(parts, shift_by(give, "c", 1), heads)
    low, full, lse = merge(count, return_near(parts), thumb_out, heads)
    low_far = shift_by(low, "h", 1)
    mixed, grad_mid, mid_low, packed, hidden, act, pre, small = feed_forward(
        tokens, cotangents, low, low_far, full, lse, out_weight, out_far, up_weight, up_biases[None],
        down_weight, far_one, far_two, gains, shifts, rows, heads,
    )
    grads = gather_near(packed)
    keep, give = weight_grads(core, act, cotangents, hidden, pre, low, mid_low, plane)
    mid_low, (keep, give) = tied(mid_low, (keep, give))
    thumb = thumbs_back(count, x, mid_low, out_weight, heads)
    early = core_sum(keep, give)

    grads, (early, thumb) = tied(grads, (early, thumb))
    early = lax.all_to_all(early, PLANE, 0, 0, tiled=True)
    *out, keep, give = reverse(
        counts, place, grads, (xq, xk, qx, kx, vx), xhat, thumb, pairs, columns, small, rows, heads
    )
    half = len(near) // 2
    out_q, give_q, out_kv = out[:half], out[half], out[half + 1 :]
    early = jnp.sum(early.astype(F32), axis=0).astype(BF)
    early = (early.astype(F32) + shift_by(early, "xl", 1).astype(F32)).astype(BF)
    early = jnp.broadcast_to(early[None], (z_size, *early.shape))
    late, early = tied(core_sum(keep, give), early)
    early = lax.all_to_all(early, "z", 0, 0, tiled=True)
    from_kv = return_far(out_kv)
    out_q = fold(out_q, shift_by(give_q, "c", 1))
    from_q = return_near(out_q)
    late, (early, from_kv, from_q) = tied(late, (early, from_kv, from_q))
    late = late.reshape(plane, -1, late.shape[1])
    late = lax.all_to_all(late, PLANE, 0, 0, tiled=True)
    early = [early] + [shift_by(early, "y", d) for d in range(1, lax.axis_size("y"))]
    mine, other = grad_one(count, from_q, from_kv, thumb, pairs)
    late, (early[1], early[-1], mine, other) = tied(late, (early[1], early[-1], mine, other))
    late = across(jnp.sum(late.astype(F32), axis=0).astype(BF))
    arrived = [shift_by(mine, "h", 1), shift_by(other, "xl", 1), crossed(other)]
    late, (early, arrived) = tied(late, (early, arrived))
    late = jnp.broadcast_to(late[None], (plane, *late.shape))
    late = lax.all_to_all(late, PLANE, 0, 0, tiled=True).reshape(model, -1)

    grad_tokens = close(count, tokens, grad_mid, mine, *arrived, gains)
    early_far = [shift_by(e, "c", 1) for e in early]
    done = early_out(place, early, (), units, cols)
    grad_down, grad_up, grad_out = early_out(place, early_far, done, units, cols)
    done = late_out(place, late, (), units)
    grad_in, in_bias, up_bias, grad_gains, grad_shifts = late_out(
        place, shift_by(late, "c", 1), done, units
    )
    return (
        mixed,
        grad_tokens,
        grad_in,
        in_bias,
        grad_out,
        grad_up,
        up_bias.reshape(2, units),
        grad_down,
        grad_gains,
        grad_shifts,
    )


def solution(mesh):
    fine = Mesh(mesh.devices.reshape(4, 2, 4, 2, 2), ("z", "xl", "y", "c", "h"))
    blk = ("z", "xl", "y", "c")
    return jax.shard_map(
        local,
        mesh=fine,
        in_specs=(
            P(blk, None),
            P(None, blk, None),
            P(blk),
            P(None, None, "h"),
            P(None, "h"),
            P("h", None),
            P(None, "h"),
            P("h"),
            P("h", None),
            P(),
            P(),
        ),
        out_specs=(
            P(blk, None),
            P(None, blk, None),
            P(None, None, None, "h"),
            P(None, None, "h"),
            P(None, "h", None),
            P(None, None, "h"),
            P(None, "h"),
            P(None, "h", None),
            P(),
            P(),
        ),
        check_vma=False,
    )
```

```python
import functools

import jax
import jax.numpy as jnp
from jax import lax
from jax.experimental import pallas as pl
from jax.experimental.pallas import tpu as pltpu
from jax.sharding import Mesh
from jax.sharding import PartitionSpec as P

HD = 64
LANES = 128
TILE = 64
BLOCK = 256
EPS = 1e-06
SCALE = 0.125
FAR = -1e30
BF = jnp.bfloat16
F32 = jnp.float32
MIB = 1024 * 1024
ROOM = 56

NT = (((1,), (1,)), ((), ()))
TN = (((0,), (0,)), ((), ()))


def shift_by(array, axis, step):
    size = lax.axis_size(axis)
    return lax.ppermute(array, axis, [(i, (i + step) % size) for i in range(size)])


def dot(a, b):
    return jnp.dot(a, b, preferred_element_type=F32)


def dot_nt(a, b):
    return lax.dot_general(a, b, NT, preferred_element_type=F32)


def dot_tn(a, b):
    return lax.dot_general(a, b, TN, preferred_element_type=F32)


def standard(field):
    center = field - jnp.mean(field, axis=-1, keepdims=True)
    factor = lax.rsqrt(jnp.mean(center * center, axis=-1, keepdims=True) + EPS)
    return center * factor, factor


def norm_back(grad, gain, xhat, factor):
    h = grad * gain
    mean = jnp.mean(h, axis=-1, keepdims=True)
    return factor * (h - mean - xhat * jnp.mean(h * xhat, axis=-1, keepdims=True))


def pieces(value):
    high = value.astype(BF)
    rest = value - high.astype(F32)
    middle = rest.astype(BF)
    low = (rest - middle.astype(F32)).astype(BF)
    return high, middle, low


def zero_one(mask):
    return jnp.where(mask, 1.0, 0.0).astype(BF)


def iota(shape, dim):
    return lax.broadcasted_iota(jnp.int32, shape, dim)


VMEM = pl.BlockSpec(memory_space=pltpu.VMEM)
ANY = pl.BlockSpec(memory_space=pl.ANY)
SMEM = pl.BlockSpec(memory_space=pltpu.SMEM)


def local_call(body, name, out, ins, outs, args, scratch=(), cost=None, room=16):
    return pl.pallas_call(
        body,
        out_shape=out,
        in_specs=ins,
        out_specs=outs,
        scratch_shapes=scratch,
        cost_estimate=cost,
        compiler_params=pltpu.CompilerParams(vmem_limit_bytes=room * MIB),
        name=name,
    )(*args)


def shaped(*shape, dtype=BF):
    return jax.ShapeDtypeStruct(shape, dtype)


def cost(micros):
    return pl.CostEstimate(flops=int(micros * 1e9), bytes_accessed=0, transcendentals=0)


def front_kernel(tokens, ids, told, copies, number):
    rows = told.shape[0] - 16
    marks = jnp.where(ids[...] == 0, 1.0, 0.0)
    tiles = jnp.sum(marks).astype(jnp.int32) // TILE
    number[0] = tiles
    told[:rows, :] = tokens[:rows, :]
    told[rows:, :] = jnp.full((16, told.shape[1]), tiles.astype(F32), F32).astype(BF)
    for g in range(copies.shape[0]):
        copies[g] = told[...]


def front(tokens, ids, copies):
    size, model = tokens.shape
    told = size - TILE + 16
    return local_call(
        front_kernel,
        "front",
        (shaped(told, model), shaped(copies, told, model), shaped(1, dtype=jnp.int32)),
        [VMEM, VMEM],
        (VMEM, VMEM, SMEM),
        (tokens, ids.reshape(-1, LANES)),
        room=ROOM,
    )


def prepare_kernel(
    heads, place, in_weights, in_biases, gains, shifts, up, down, bias,
    weights, biases, pairs, columns, out,
):
    core = place[0]
    half = out.shape[1]
    at = pl.ds(pl.multiple_of(core * half, half), half)
    out[:half, :] = up[:, at]
    out[half : 2 * half, :] = down[at, :]
    mine = jnp.where(core == 0, bias[:, :half], bias[:, half:])
    row = iota((16, half), 0)
    rows = jnp.zeros((16, half), F32)
    for i, piece in enumerate(pieces(mine)):
        rows = jnp.where(row == i, piece.astype(F32), rows)
    out[2 * half :, :] = rows.astype(BF)

    model, cols = in_weights.shape[1:]
    width = heads * LANES
    row, col = (iota((cols, width), d) for d in (0, 1))
    spread = zero_one((row // HD == col // LANES) & (row % HD == col % LANES))
    lane = iota((1, width), 1) % LANES
    gap = jnp.zeros((1, HD), F32)

    def apart(line):
        return jnp.concatenate(
            sum([[line[:, h * HD : (h + 1) * HD], gap] for h in range(heads)], []), axis=1
        )

    extra = [
        apart(in_biases[0:1, :] * SCALE) + jnp.where(lane == HD, 1.0, 0.0),
        jnp.where((lane > HD) & (lane < HD + 4), 1.0, 0.0),
        apart(in_biases[1:2, :]) + jnp.where((lane >= HD) & (lane < HD + 3), 1.0, 0.0),
    ]
    for i in range(3):
        factor = SCALE if i == 0 else 1.0
        weights[:, i * width : (i + 1) * width] = (dot(in_weights[i], spread) * factor).astype(BF)
        biases[:, i * width : (i + 1) * width] = extra[i]
        for pair in range(heads // 2):
            pairs[pair, :, i * LANES : (i + 1) * LANES] = in_weights[
                i, :, pair * LANES : (pair + 1) * LANES
            ]
    tall = jnp.concatenate(
        [gains[0:1, :], shifts[0:1, :], jnp.zeros((LANES - 2, model), F32)], axis=0
    )
    columns[...] = jnp.transpose(tall)


def prepare(core, in_weights, in_biases, gains, shifts, up, down, bias, heads):
    model = up.shape[0]
    width = 3 * heads * LANES
    return local_call(
        functools.partial(prepare_kernel, heads),
        "prepare",
        (
            shaped(model, width),
            shaped(1, width, dtype=F32),
            shaped(heads // 2, model, 3 * LANES),
            shaped(model, LANES, dtype=F32),
            shaped(2 * model + 16, model),
        ),
        [SMEM] + [VMEM] * 7,
        (VMEM,) * 5,
        (core, in_weights, in_biases, gains, shifts, up, down, bias),
        cost=cost(4),
        room=ROOM,
    )


def count_of(ref, rows):
    return jnp.max(ref[rows : rows + 16, :LANES].astype(F32)).astype(jnp.int32)


def rows_at(start, rows, step=TILE):
    return pl.ds(pl.multiple_of(start, step), rows)


def attend_kernel(rows, groups, heads, *refs):
    near, far = refs[:groups], refs[groups]
    weights, biases, gains, shifts = refs[groups + 1 : groups + 5]
    at = groups + 5 + groups // 2
    out, give = refs[groups + 5 : at], refs[at]
    kept, counts, place = refs[at + 1 : at + 6], refs[at + 6], refs[at + 7]
    (xq, xk, qx, kx, vx), sems = refs[at + 8 : at + 13], refs[at + 13]
    model = xq.shape[1]
    q_counts = [count_of(r, rows) for r in near]
    k_counts = [count_of(far.at[g], rows) for g in range(groups)]
    for g in range(groups):
        counts[g] = q_counts[g]
        counts[groups + g] = k_counts[g]

    def compact(numbers, read, target):
        start = jnp.int32(0)
        for g, n in enumerate(numbers):
            target[rows_at(start, rows), :] = read(g)
            start = start + n * TILE
        target[rows_at(start, BLOCK), :] = jnp.zeros((BLOCK, model), BF)
        return start

    q_total = compact(q_counts, lambda g: near[g][:rows, :], xq)
    k_total = compact(k_counts, lambda g: far[g, :rows, :], xk)
    q_blocks = (q_total + BLOCK - 1) // BLOCK
    k_blocks = (k_total + BLOCK - 1) // BLOCK
    width = heads * LANES

    def hidden(ref, here):
        clean = standard(ref[here, :].astype(F32))[0].astype(BF)
        ref[here, :] = clean
        return (clean.astype(F32) * gains[0:1, :] + shifts[0:1, :]).astype(BF)

    @pl.loop(0, q_blocks)
    def _(b):
        here = rows_at(b * BLOCK, BLOCK, BLOCK)
        q = (dot(hidden(xq, here), weights[:, :width]) + biases[:, :width]).astype(BF)
        for h in range(heads):
            qx[h, here, :] = q[:, h * LANES : (h + 1) * LANES]

    @pl.loop(0, k_blocks)
    def _(b):
        here = rows_at(b * BLOCK, BLOCK, BLOCK)
        both = dot(hidden(xk, here), weights[:, width:]) + biases[:, width:]
        unseen = (iota((BLOCK, width), 0) + b * BLOCK >= k_total) & (
            iota((BLOCK, width), 1) % LANES == HD
        )
        k = jnp.where(unseen, FAR, both[:, :width]).astype(BF)
        v = both[:, width:].astype(BF)
        for h in range(heads):
            kx[h, here, :] = k[:, h * LANES : (h + 1) * LANES]
            vx[h, here, :] = v[:, h * LANES : (h + 1) * LANES]

    copies = [
        pltpu.make_async_copy(held, to, sems.at[i])
        for i, (held, to) in enumerate(zip((xq, xk, qx, kx, vx), kept))
    ]
    for copy in copies:
        copy.start()

    def attend_all(span):
        @pl.loop(0, q_blocks)
        def _(b):
            here = rows_at(b * BLOCK, BLOCK, BLOCK)
            lane = iota((BLOCK, LANES), 1)
            for h in range(heads):
                s = dot_nt(qx[h, here, :], kx[h, :span, :])
                top = jnp.max(s, axis=-1, keepdims=True)
                o = dot(jnp.exp(s - top).astype(BF), vx[h, :span, :])
                total = o[:, HD : HD + 1]
                o = o / total
                for i, piece in enumerate(pieces(top + jnp.log(total))):
                    o = jnp.where(lane == HD + i, piece.astype(F32), o)
                place[h, here, :] = o.astype(BF)

    for blocks in range(groups * TILE // BLOCK, groups * rows // BLOCK + 1):
        pl.when(k_blocks == blocks)(functools.partial(attend_all, blocks * BLOCK))

    gather = [
        (iota((LANES, LANES), 0) - HD + 3 * h == iota((LANES, LANES), 1))
        & (iota((LANES, LANES), 0) >= HD)
        & (iota((LANES, LANES), 0) < HD + 3)
        for h in range(heads)
    ]
    gather = [jnp.where(m, 1.0, 0.0).astype(BF) for m in gather]
    start = jnp.int32(0)
    for g in range(groups):
        mine = [place[h, rows_at(start, rows), :] for h in range(heads)]
        stats = sum(dot(m, s) for m, s in zip(mine, gather)).astype(BF)
        value = jnp.concatenate([m[:, :HD] for m in mine] + [stats], axis=1)
        if g < groups // 2:
            out[g][...] = value
        else:
            give[g - groups // 2] = value
        start = start + q_counts[g] * TILE
    for copy in copies:
        copy.wait()


def attend(near, far, weights, biases, gains, shifts, rows, heads):
    groups = len(near)
    model = near[0].shape[1]
    room = rows * groups + BLOCK
    parts = heads * HD + LANES
    kept = [(room, model)] * 2 + [(heads, room, LANES)] * 3
    return local_call(
        functools.partial(attend_kernel, rows, groups, heads),
        "attend",
        (
            *[shaped(rows, parts)] * (groups // 2),
            shaped(groups // 2, rows, parts),
            *[shaped(*k) for k in kept],
            shaped(2 * groups, dtype=jnp.int32),
        ),
        [VMEM] * (groups + 5),
        (*[VMEM] * (groups // 2 + 1), *[ANY] * 5, SMEM),
        (*near, far, weights, biases, gains, shifts),
        [
            pltpu.VMEM((heads, room, LANES), BF),
            *[pltpu.VMEM(k, BF) for k in kept],
            pltpu.SemaphoreType.DMA((5,)),
        ],
        cost(15),
        ROOM,
    )


def same_tile(rows):
    return iota((rows, rows), 0) // TILE == iota((rows, rows), 1) // TILE


def thumb_kernel(heads, tokens, weights, biases, gains, shifts, out, xhat, x):
    width = heads * LANES
    size = tokens.shape[0]
    clean = standard(tokens[...].astype(F32))[0].astype(BF)
    xhat[...] = clean
    hidden = (clean.astype(F32) * gains[0:1, :] + shifts[0:1, :]).astype(BF)
    x[...] = (dot(hidden, weights[...]) + biases[...]).astype(BF)
    visible = same_tile(size - TILE)
    out[:TILE, :] = jnp.zeros((TILE, heads * HD), F32)
    for h in range(heads):
        q = x[TILE:, h * LANES : (h + 1) * LANES]
        k = x[TILE:, width + h * LANES : width + (h + 1) * LANES]
        v = x[TILE:, 2 * width + h * LANES : 2 * width + (h + 1) * LANES]
        s = jnp.where(visible, dot_nt(q, k), FAR)
        e = jnp.exp(s - jnp.max(s, axis=-1, keepdims=True))
        o = dot(e.astype(BF), v)[:, :HD] / jnp.sum(e, axis=-1, keepdims=True)
        out[TILE:, h * HD : (h + 1) * HD] = o


def thumbs(tokens, weights, biases, gains, shifts, heads):
    size, model = tokens.shape
    return local_call(
        functools.partial(thumb_kernel, heads),
        "thumbs",
        (
            shaped(size, heads * HD, dtype=F32),
            shaped(size, model),
            shaped(size, 3 * heads * LANES),
        ),
        [VMEM] * 5,
        (VMEM,) * 3,
        (tokens, weights, biases, gains, shifts),
        cost=cost(5),
    )


def merged(parts, heads):
    cols = heads * HD
    row, col = (iota((LANES, cols), d) for d in (0, 1))
    spread = zero_one(row // 3 == col // HD)
    marks = [dot(p[:, cols:], spread) for p in parts]
    top = functools.reduce(jnp.maximum, marks)
    expos = [jnp.exp(m - top) for m in marks]
    total = sum(expos)
    mixed = sum(e * p[:, :cols].astype(F32) for p, e in zip(parts, expos)) / total
    row, col = (iota((cols, LANES), d) for d in (0, 1))
    packed = [
        dot(piece, zero_one((row % HD == 0) & (col == 3 * (row // HD) + i)))
        for i, piece in enumerate(pieces(top + jnp.log(total)))
    ]
    return mixed, sum(packed)


def pair_kernel(heads, *refs):
    count = (len(refs) - 1) // 2
    for j, (mine, out) in enumerate(zip(refs[:count], refs[count + 1 :])):
        mixed, marks = merged([mine[...], refs[count][j]], heads)
        out[...] = jnp.concatenate([mixed.astype(BF), marks.astype(BF)], axis=1)


def pair_merge(parts, other, heads):
    return local_call(
        functools.partial(pair_kernel, heads),
        "pair_merge",
        tuple(shaped(*p.shape) for p in parts),
        [VMEM] * (len(parts) + 1),
        (VMEM,) * len(parts),
        (*parts, other),
        cost=cost(3),
        room=ROOM,
    )


def merge_kernel(heads, counts, thumb, *refs):
    parts, (low, full, lse) = refs[:-3], refs[-3:]
    cols = heads * HD
    rows = lse.shape[0]
    mixed, marks = merged([p[...] for p in parts], heads)
    lse[...] = (-marks).astype(BF)
    image = iota((rows, cols), 0) < counts[0] * TILE
    full[:rows, :] = jnp.where(image, mixed, thumb[:rows, :])
    full[rows:, :] = thumb[rows:, :]
    low[...] = full[...].astype(BF)


def merge(count, parts, thumb, heads):
    size, cols = thumb.shape
    return local_call(
        functools.partial(merge_kernel, heads),
        "merge",
        (shaped(size, cols), shaped(size, cols, dtype=F32), shaped(parts[0].shape[0], LANES)),
        [SMEM] + [VMEM] * (1 + len(parts)),
        (VMEM,) * 3,
        (count, thumb, *parts),
        cost=cost(3),
    )


def fold_kernel(*refs):
    count = (len(refs) - 1) // 2
    for j, (mine, out) in enumerate(zip(refs[:count], refs[count + 1 :])):
        out[...] = (mine[...].astype(F32) + refs[count][j].astype(F32)).astype(BF)


def fold(parts, other):
    return local_call(
        fold_kernel,
        "fold",
        tuple(shaped(*p.shape) for p in parts),
        [VMEM] * (len(parts) + 1),
        (VMEM,) * len(parts),
        (*parts, other),
        cost=cost(2),
        room=ROOM,
    )


ROOT = 0.7978845608028654
CUBE = 0.044715


def ff_kernel(
    heads, tokens, outer, low, low_far, full, lse, out_weight, out_far, up, up_bias, down, far_one,
    far_two, gains, shifts, mixed, grad_mid, grad_low, packed, hidden_out, act_out, pre_out, small,
):
    size, model = tokens.shape
    passes = outer.shape[0]
    cols = heads * HD
    chunk = far_one.shape[1]
    units = up.shape[1]
    rows = packed.shape[0]
    branch = dot(low[...], out_weight[...]) + dot(low_far[...], out_far[...])
    middle = tokens[...].astype(F32) + (branch + shifts[1:2, :])
    xhat, factor = standard(middle)
    hidden = (xhat * gains[1:2, :] + shifts[2:3, :]).astype(BF)
    hidden_out[...] = hidden

    def one_chunk(up_part, bias, down_part, keep):
        v = dot(hidden, up_part) + bias
        t = jnp.tanh(ROOT * (v + CUBE * (v * v * v)))
        act = (0.5 * v * (1.0 + t)).astype(BF)
        slope = 0.5 * (1.0 + t) + 0.5 * v * (1.0 - t * t) * (ROOT * (1.0 + 3.0 * CUBE * (v * v)))
        two = []
        for p in range(passes):
            pre = (dot_nt(outer[p], down_part) * slope).astype(BF)
            if keep is not None:
                pre_out[p, :, keep] = pre
            two.append(dot_nt(pre, up_part))
        if keep is not None:
            act_out[:, keep] = act
        return dot(act, down_part), two

    def far_chunk(ref):
        told = ref[2 * chunk : 2 * chunk + 16, :].astype(F32)
        bias = told[0:1] + told[1:2] + told[2:3]
        return one_chunk(ref[:chunk, :], bias, ref[chunk : 2 * chunk, :], None)

    done = []
    for i in range(units // chunk):
        at = slice(i * chunk, (i + 1) * chunk)
        done.append(one_chunk(up[:, at], up_bias[:, at], down[at, :], at))
    done += [far_chunk(far_one), far_chunk(far_two)]

    def tree(parts):
        half = len(parts) // 2
        return sum(parts[:half]) + sum(parts[half:])

    output = tree([d[0] for d in done])
    mixed[...] = (middle + (output + shifts[3:4, :])).astype(BF)
    small[...] = jnp.zeros(small.shape, F32)
    lane = iota((rows, LANES), 1)
    stats = jnp.zeros((rows, LANES), F32)
    for p in range(passes):
        two = tree([d[1][p] for d in done])
        c = outer[p].astype(F32)
        mid = c + norm_back(two, gains[1:2, :], xhat, factor)
        mid_low = mid.astype(BF)
        grad_mid[p] = mid
        grad_low[p] = mid_low
        att = dot_nt(mid_low, out_weight[...]).astype(BF)
        packed[:, p * cols : (p + 1) * cols] = att[:rows, :]
        pre_out_p = pre_out[p].astype(F32)
        bias = jnp.sum(pre_out_p, axis=0, keepdims=True)
        small[p, 0:1, :] = jnp.sum(two * xhat, axis=0, keepdims=True)
        small[p, 1:2, :] = jnp.sum(two, axis=0, keepdims=True)
        small[p, 2:3, :] = jnp.sum(mid_low.astype(F32), axis=0, keepdims=True)
        small[p, 3:4, :] = jnp.sum(c, axis=0, keepdims=True)
        for i in range(units // model):
            small[p, 4 + i : 5 + i, :] = bias[:, i * model : (i + 1) * model]
        product = att[:rows, :].astype(F32) * full[:rows, :]
        for h in range(heads):
            delta = jnp.sum(product[:, h * HD : (h + 1) * HD], axis=-1, keepdims=True)
            for i, piece in enumerate(pieces(-delta)):
                stats = jnp.where(lane == 3 * heads * (p + 1) + 3 * h + i, piece.astype(F32), stats)
    packed[:, passes * cols :] = (stats + lse[...].astype(F32)).astype(BF)


def feed_forward(
    tokens, outer, low, low_far, full, lse, out_weight, out_far, up, up_bias, down, far_one, far_two,
    gains, shifts, rows, heads,
):
    size, model = tokens.shape
    passes = outer.shape[0]
    units = up.shape[1]
    return local_call(
        functools.partial(ff_kernel, heads),
        "feed_forward",
        (
            shaped(size, model),
            shaped(passes, size, model, dtype=F32),
            shaped(passes, size, model),
            shaped(rows, passes * heads * HD + LANES),
            shaped(size, model),
            shaped(size, units),
            shaped(passes, size, units),
            shaped(passes, 8, model, dtype=F32),
        ),
        [VMEM] * 15,
        (VMEM,) * 8,
        (
            tokens, outer, low, low_far, full, lse, out_weight, out_far, up, up_bias, down, far_one,
            far_two, gains, shifts,
        ),
        cost=cost(12),
        room=32,
    )


def thumb_back_kernel(heads, counts, x, mid_low, out_weight, out):
    width = heads * LANES
    size = x.shape[0]
    passes = mid_low.shape[0]
    visible = same_tile(size - TILE)
    outside = iota((size - TILE, HD), 0) + TILE >= counts[0] * TILE
    grads = [dot_nt(mid_low[p], out_weight[...]).astype(BF) for p in range(passes)]
    out[:, :, :TILE, :] = jnp.zeros((*out.shape[:2], TILE, out.shape[3]), BF)
    for h in range(heads):
        q = x[TILE:, h * LANES : (h + 1) * LANES]
        k = x[TILE:, width + h * LANES : width + (h + 1) * LANES]
        v = x[TILE:, 2 * width + h * LANES : 2 * width + h * LANES + HD]
        s = jnp.where(visible, dot_nt(q, k), FAR)
        e = jnp.exp(s - jnp.max(s, axis=-1, keepdims=True))
        w = e / jnp.sum(e, axis=-1, keepdims=True)
        w_low = w.astype(BF)
        for p in range(passes):
            g = grads[p][TILE:, h * HD : (h + 1) * HD]
            gw = dot_nt(g, v)
            ds = (w * (gw - jnp.sum(w * gw, axis=-1, keepdims=True))).astype(BF)
            dq = dot(ds, k[:, :HD]) * SCALE
            dk = dot_tn(ds, q)[:, :HD]
            dv = dot_tn(w_low, g)
            for c, piece in enumerate((dq, dk, dv)):
                at = c * LANES + (h % 2) * HD
                out[h // 2, p, TILE:, at : at + HD] = jnp.where(outside, piece, 0.0).astype(BF)


def thumbs_back(count, x, mid_low, out_weight, heads):
    passes, size, _ = mid_low.shape
    return local_call(
        functools.partial(thumb_back_kernel, heads),
        "thumbs_back",
        shaped(heads // 2, passes, size, 3 * LANES),
        [SMEM] + [VMEM] * 3,
        VMEM,
        (count, x, mid_low, out_weight),
        cost=cost(6),
    )


def early_at(units, model, low):
    ends = [model, 2 * model, 2 * model + units, 2 * model + units + low]
    return [slice(b - w, b) for b, w in zip(ends, (model, model, units, low))]


def early_cuts(parts, units, model, low):
    high, wide, turns = units // parts // 2, model // parts, model // low
    narrow = low * turns // parts
    for i in range(parts):
        yield (
            (slice(2 * i * high, (2 * i + 1) * high), slice(0, model)),
            (slice((2 * i + 1) * high, (2 * i + 2) * high), slice(0, model)),
            (slice(i * wide, (i + 1) * wide), slice(0, units)),
            (
                slice(i // turns * narrow, (i // turns + 1) * narrow),
                slice(i % turns * low, (i % turns + 1) * low),
            ),
        )


def weight_kernel(place, act, outer, hidden, pre, low, mid_low, keep, give):
    units, model, cols = act.shape[1], hidden.shape[1], low.shape[1]
    core = place[0]
    for turn, out in ((core, keep), (1 - core, give)):
        down = dot_tn(act[...], outer[turn]).astype(BF)
        up = dot_tn(hidden[...], pre[turn]).astype(BF)
        proj = dot_tn(low[...], mid_low[turn]).astype(BF)
        for i, cut in enumerate(early_cuts(keep.shape[0], units, model, cols)):
            for value, (rows, lanes), at in zip(
                (down, down, up, proj), cut, early_at(units, model, cols)
            ):
                out[i, :, at] = value[rows, lanes]


def weight_grads(core, act, outer, hidden, pre, low, mid_low, parts):
    units, model = act.shape[1], outer.shape[2]
    out = shaped(parts, model // parts, 2 * model + units + low.shape[1])
    return local_call(
        weight_kernel,
        "weight_grads",
        (out, out),
        [SMEM] + [VMEM] * 6,
        (VMEM,) * 2,
        (core, act, outer, hidden, pre, low, mid_low),
        cost=cost(8),
        room=24,
    )


def reverse_kernel(rows, groups, heads, passes, counts, place, *refs):
    grads, kept = refs[:groups], refs[groups : groups + 5]
    own, thumb, weights, columns, small = refs[groups + 5 : groups + 10]
    at = groups + 10
    out_q, give_q, at = refs[at : at + groups // 2], refs[at + groups // 2], at + groups // 2 + 1
    out_kv, at = refs[at : at + groups // 2], at + groups // 2
    keep, give = refs[at : at + 2]
    (
        stage, xq, xk, qx, kx, vx, packed, gx, kt, dq_t, dv, dk, low_q, low_kv, total, sums,
        starts, sems,
    ) = refs[at + 2 :]
    couples = heads // 2
    sources = [*grads, *kept[2:], *kept[:2]]
    targets = [*[stage.at[g] for g in range(groups)], qx, kx, vx, xq, xk]
    copies = [
        pltpu.make_async_copy(f, t, sems.at[i]) for i, (f, t) in enumerate(zip(sources, targets))
    ]
    for copy in copies:
        copy.start()
    cols = heads * HD
    wide = passes * LANES
    q_counts = [counts[g] for g in range(groups)]
    k_counts = [counts[groups + g] for g in range(groups)]
    start = jnp.int32(0)
    for g in range(groups):
        copies[g].wait()
        packed[rows_at(start, rows), :] = stage[g]
        start = start + q_counts[g] * TILE
    q_total, k_total = start, sum(k_counts) * TILE
    tail_lane = iota((BLOCK, packed.shape[1]), 1) - passes * cols
    empty = (tail_lane >= 0) & (tail_lane < 3 * heads) & (tail_lane % 3 == 0)
    packed[rows_at(q_total, BLOCK), :] = jnp.where(empty, FAR, 0.0).astype(BF)
    q_blocks = (q_total + BLOCK - 1) // BLOCK
    k_blocks = (k_total + BLOCK - 1) // BLOCK
    spans = range(groups * TILE // BLOCK, groups * rows // BLOCK + 1)

    row, col = (iota((LANES, heads * LANES), d) for d in (0, 1))
    head, lane = col // LANES, col % LANES
    to_marks = zero_one((lane > HD) & (lane < HD + 4) & (row == 3 * head + lane - HD - 1))
    row, col = (iota((LANES, heads * wide), d) for d in (0, 1))
    head, turn, lane = col // wide, col % wide // LANES, col % LANES
    to_deltas = zero_one(
        (lane >= HD) & (lane < HD + 3) & (row == 3 * heads * (turn + 1) + 3 * head + lane - HD)
    )
    for copy in copies[groups : groups + 3]:
        copy.wait()

    @pl.loop(0, q_blocks)
    def _(b):
        here = rows_at(b * BLOCK, BLOCK, BLOCK)
        stats = packed[here, passes * cols :]
        marks = dot(stats, to_marks)
        deltas = dot(stats, to_deltas).astype(BF)
        for h in range(heads):
            more = marks[:, h * LANES : (h + 1) * LANES]
            qx[h, here, :] = (qx[h, here, :].astype(F32) + more).astype(BF)
            for p in range(passes):
                at = p * cols + h * HD
                mine = (h * passes + p) * LANES
                gx[h, here, p * LANES : (p + 1) * LANES] = jnp.concatenate(
                    [packed[here, at : at + HD], deltas[:, mine + HD : mine + LANES]], axis=1
                )

    @pl.loop(0, k_blocks)
    def _(b):
        here = rows_at(b * BLOCK, BLOCK, BLOCK)
        for h in range(heads):
            kt[h, b] = jnp.transpose(kx[h, here, :].astype(F32))[:HD, :].astype(BF)

    def reverse_all(blocks):
        span = blocks * BLOCK

        @pl.loop(0, couples)
        def _(pair):
            dv[:, :span, :] = jnp.zeros((2, span, wide), F32)
            dk[:, :, :span, :] = jnp.zeros((passes, 2, span, LANES), F32)

            @pl.loop(0, q_blocks)
            def _(b):
                here = rows_at(b * BLOCK, BLOCK, BLOCK)
                for i in range(2):
                    h = 2 * pair + i
                    q, g = qx[h, here, :], gx[h, here, :]
                    k_t = jnp.concatenate([kt[h, j] for j in range(blocks)], axis=1)
                    w = jnp.exp(dot_nt(kx[h, :span, :], q))
                    dv[i, :span, :] += dot(w.astype(BF), g)
                    for p in range(passes):
                        ds = dot_nt(vx[h, :span, :], g[:, p * LANES : (p + 1) * LANES])
                        ds = (w * ds).astype(BF)
                        dk[p, i, :span, :] += dot(ds, q)
                        dq_t[p, i * HD : (i + 1) * HD, :] = dot(k_t, ds)
                for p in range(passes):
                    piece = jnp.transpose(dq_t[p]) * SCALE
                    low_q[pair, here, p * LANES : (p + 1) * LANES] = piece.astype(BF)

            for p in range(passes):
                for c, both in enumerate(
                    (
                        [dk[p, i, :span, :HD] for i in range(2)],
                        [dv[i, :span, p * LANES : p * LANES + HD] for i in range(2)],
                    )
                ):
                    lane = (2 * p + c) * LANES
                    low_kv[pair, :span, lane : lane + LANES] = jnp.concatenate(both, axis=1).astype(BF)

    for blocks in spans:
        pl.when(k_blocks == blocks)(functools.partial(reverse_all, blocks))

    start = jnp.int32(0)
    for g in range(groups):
        starts[g] = start
        start = start + k_counts[g] * TILE
    for g in range(groups):
        here = rows_at(starts[place[1 + g]], rows)
        out_kv[g // 2][g % 2] = jnp.concatenate([low_kv[i, here, :] for i in range(couples)], axis=1)
    start = jnp.int32(0)
    for g in range(groups):
        here = rows_at(start, rows)
        value = jnp.concatenate([low_q[i, here, :] for i in range(couples)], axis=1)
        if g < groups // 2:
            out_q[g][...] = value
        else:
            give_q[g - groups // 2] = value
        start = start + q_counts[g] * TILE

    copies[groups + 3].wait()
    copies[groups + 4].wait()

    def key_sums(blocks):
        span = blocks * BLOCK
        for i in range(couples):
            flat = low_kv[i, :span, :]
            total[i, :, wide:] = dot_tn(xk[:span, :], flat)
            sums[i, :, wide:] = dot(jnp.ones((8, span), BF), flat)

    for blocks in spans:
        pl.when(k_blocks == blocks)(functools.partial(key_sums, blocks))

    total[:, :, :wide] = jnp.zeros((couples, total.shape[1], wide), F32)
    sums[:, :, :wide] = jnp.zeros((couples, 8, wide), F32)

    @pl.loop(0, q_blocks)
    def _(b):
        here = rows_at(b * BLOCK, BLOCK, BLOCK)
        for i in range(couples):
            total[i, :, :wide] += dot_tn(xq[here, :], low_q[i, here, :])
            sums[i, :, :wide] += dot(jnp.ones((8, BLOCK), BF), low_q[i, here, :])

    model = total.shape[1]
    gain, shift = columns[:, 0:1], columns[:, 1:2]
    ones = jnp.ones((8, own.shape[0]), BF)
    for p in range(passes):
        whole = []
        for i in range(couples):
            mine = thumb[i, p]
            part = dot_tn(own[...], mine)
            part_sum = dot(ones, mine)[0:1, :]
            q_at = slice(p * LANES, (p + 1) * LANES)
            kv_at = slice((passes + 2 * p) * LANES, (passes + 2 * p + 2) * LANES)
            part += jnp.concatenate([total[i, :, q_at], total[i, :, kv_at]], axis=1)
            part_sum += jnp.concatenate([sums[i, 0:1, q_at], sums[i, 0:1, kv_at]], axis=1)
            w = weights[i].astype(F32)
            gain_one = jnp.sum(w * part, axis=1, keepdims=True)
            shift_one = jnp.sum(w * part_sum, axis=1, keepdims=True)
            lane = iota((model, LANES), 1)
            tall = jnp.where(lane == 0, gain_one, jnp.where(lane == 1, shift_one, 0.0))
            flat = jnp.concatenate(
                [jnp.zeros((2, LANES), F32)]
                + [part_sum[:, c * LANES : (c + 1) * LANES] for c in range(3)]
                + [jnp.zeros((LANES - 5, LANES), F32)],
                axis=0,
            )
            tall = jnp.concatenate([tall[:LANES] + jnp.transpose(flat), tall[LANES:]], axis=0)
            if i == 0:
                turned = jnp.concatenate(
                    [
                        jnp.zeros((8, model), F32),
                        small[p],
                        jnp.zeros((LANES - 16, model), F32),
                    ],
                    axis=0,
                )
                tall = tall + jnp.transpose(turned)
            whole += [part * gain + shift * part_sum, tall]
        whole = jnp.concatenate(whole, axis=1).astype(BF)

        @pl.when(place[0] == p)
        def _():
            keep[...] = whole

        @pl.when(place[0] != p)
        def _():
            give[...] = whole


def reverse(counts, place, grads, kept, own, thumb, weights, columns, small, rows, heads):
    groups = len(grads)
    couples, passes = thumb.shape[:2]
    model = own.shape[1]
    room = rows * groups + BLOCK
    cols = heads * HD
    wide = passes * LANES
    half = groups // 2
    late = shaped(model, couples * 4 * LANES)
    q, kv = shaped(rows, couples * wide), shaped(2, rows, couples * 2 * wide)
    out = (*[q] * half, shaped(half, rows, couples * wide), *[kv] * half, late, late)
    return local_call(
        functools.partial(reverse_kernel, rows, groups, heads, passes),
        "reverse",
        out,
        [SMEM, SMEM] + [ANY] * (groups + 5) + [VMEM] * 5,
        (VMEM,) * len(out),
        (counts, place, *grads, *kept, own, thumb, weights, columns, small),
        [
            pltpu.VMEM((groups, rows, passes * cols + LANES), BF),
            pltpu.VMEM((room, model), BF),
            pltpu.VMEM((room, model), BF),
            pltpu.VMEM((heads, room, LANES), BF),
            pltpu.VMEM((heads, room, LANES), BF),
            pltpu.VMEM((heads, room, LANES), BF),
            pltpu.VMEM((room, passes * cols + LANES), BF),
            pltpu.VMEM((heads, room, wide), BF),
            pltpu.VMEM((heads, room // BLOCK, HD, BLOCK), BF),
            pltpu.VMEM((passes, LANES, BLOCK), F32),
            pltpu.VMEM((2, room, wide), F32),
            pltpu.VMEM((passes, 2, room, LANES), F32),
            pltpu.VMEM((couples, room, wide), BF),
            pltpu.VMEM((couples, room, 2 * wide), BF),
            pltpu.VMEM((couples, model, 3 * wide), F32),
            pltpu.VMEM((couples, 8, 3 * wide), F32),
            pltpu.SMEM((groups,), jnp.int32),
            pltpu.SemaphoreType.DMA((groups + 5,)),
        ],
        cost(45),
        ROOM,
    )


def grad_one_kernel(near, counts, *refs):
    from_q, from_kv, (thumb, weights, mine, other) = refs[:near], refs[near:-4], refs[-4:]
    couples, passes, size, _ = thumb.shape
    rows = from_q[0].shape[0]
    sum_q = sum(r[...].astype(F32) for r in from_q)
    sum_kv = [sum(r[f].astype(F32) for r in from_kv) for f in range(2)]
    image = iota((rows, 3 * LANES), 0) < counts[0] * TILE
    for p in range(passes):
        parts = []
        for i in range(couples):
            at = (passes * i + p) * LANES
            there = slice(2 * at, 2 * at + 2 * LANES)
            far = jnp.concatenate([sum_q[:, at : at + LANES], sum_kv[0][:, there]], axis=1)
            flat = jnp.concatenate(
                [jnp.where(image, far.astype(BF), thumb[i, p, :rows]), thumb[i, p, rows:]], axis=0
            )
            parts.append(
                (
                    dot_nt(flat, weights[i]),
                    dot_nt(sum_kv[1][:, there].astype(BF), weights[i, :, LANES:]),
                )
            )
        mine[p] = sum(a for a, _ in parts).astype(BF)
        other[p] = sum(b for _, b in parts).astype(BF)


def grad_one(count, from_q, from_kv, thumb, weights):
    near = len(from_q)
    passes, size, _ = thumb.shape[1:]
    model = weights.shape[1]
    return local_call(
        functools.partial(grad_one_kernel, near),
        "grad_one",
        (shaped(passes, size, model), shaped(passes, from_q[0].shape[0], model)),
        [SMEM] + [VMEM] * (near + len(from_kv) + 2),
        (VMEM,) * 2,
        (count, *from_q, *from_kv, thumb, weights),
        cost=cost(5),
        room=ROOM,
    )


def close_kernel(counts, tokens, mid, mine, head, side, cross, gains, out):
    xhat, factor = standard(tokens[...].astype(F32))
    rows = side.shape[1]
    image = iota(side.shape[1:], 0) < counts[0] * TILE
    for p in range(mid.shape[0]):
        grad = mine[p].astype(F32) + head[p].astype(F32)
        more = jnp.where(image, side[p].astype(F32) + cross[p].astype(F32), 0.0)
        grad = jnp.concatenate([grad[:rows] + more, grad[rows:]], axis=0)
        out[p] = mid[p] + norm_back(grad, gains[0:1, :], xhat, factor)


def close(count, tokens, mid, mine, head, side, cross, gains):
    return local_call(
        close_kernel,
        "close",
        shaped(*mid.shape, dtype=F32),
        [SMEM] + [VMEM] * 7,
        VMEM,
        (count, tokens, mid, mine, head, side, cross, gains),
        cost=cost(4),
        room=ROOM,
    )


def early_kernel(lines, far, place, *refs):
    parts, refs = refs[:lines], refs[lines:]
    out, (down, up, proj, sems) = refs[-7:-4], refs[-4:]
    turn, y = place[0], place[10]
    turn = 1 - turn if far else turn
    (units, model), low = down.shape, proj.shape[0]
    steps, rows = parts[0].shape[:2]
    lane_down, lane_next, lane_up, lane_proj = early_at(units, model, low)
    turns = model // low
    for d, ref in enumerate(parts):
        for j in range(steps):
            i = j * lines + (y + lines - d) % lines
            at = pl.multiple_of(2 * rows * i, 2 * rows)
            down[pl.ds(at, rows), :] = ref[j, :, lane_down].astype(F32)
            down[pl.ds(at + rows, rows), :] = ref[j, :, lane_next].astype(F32)
            up[rows_at(rows * i, rows, rows), :] = ref[j, :, lane_up].astype(F32)
            here = rows_at(i // turns * rows, rows, rows)
            value = ref[j, :, lane_proj].astype(F32)
            for t in range(turns):

                @pl.when(i % turns == t)
                def _(value=value, here=here, t=t):
                    proj[here, t * low : (t + 1) * low] = value

    copies = [
        pltpu.make_async_copy(held, to.at[turn], sems.at[n])
        for n, (held, to) in enumerate(zip((down, up, proj), out))
    ]
    for copy in copies:
        copy.start()
    for copy in copies:
        copy.wait()


def early_out(place, parts, before, units, low):
    model = len(parts) * parts[0].shape[0] * parts[0].shape[1]
    shapes = (units, model), (model, units), (low, model)
    return pl.pallas_call(
        functools.partial(early_kernel, len(parts), bool(before)),
        out_shape=tuple(shaped(2, *s, dtype=F32) for s in shapes),
        in_specs=[SMEM] + [VMEM] * len(parts) + [ANY] * len(before),
        out_specs=(ANY,) * 3,
        scratch_shapes=[
            *[pltpu.VMEM(s, F32) for s in shapes],
            pltpu.SemaphoreType.DMA((3,)),
        ],
        input_output_aliases={1 + len(parts) + i: i for i in range(len(before))},
        cost_estimate=cost(5),
        compiler_params=pltpu.CompilerParams(vmem_limit_bytes=ROOM * MIB),
        name="early_far" if before else "early_own",
    )(place, *parts, *before)


def late_kernel(far, place, ref, *refs):
    out, (grad_in, *small), sems = refs[-11:-6], refs[-6:-1], refs[-1]
    in_bias, up_bias, gains, shifts = small
    turn = 1 - place[0] if far else place[0]
    turned = []
    for pair in range(2):
        at = 4 * LANES * pair
        for c in range(3):
            grad_in[c, :, pair * LANES : (pair + 1) * LANES] = ref[
                :, at + c * LANES : at + (c + 1) * LANES
            ].astype(F32)
        turned.append(jnp.transpose(ref[:, at + 3 * LANES : at + 4 * LANES].astype(F32)))
    a, b = turned
    in_bias[...] = jnp.concatenate(
        [
            jnp.concatenate([a[2:3, :LANES], b[2:3, :LANES]], axis=1),
            jnp.concatenate([a[4:5, :LANES], b[4:5, :LANES]], axis=1),
        ],
        axis=0,
    )
    up_bias[...] = jnp.concatenate([a[12:13], a[13:14]], axis=1)
    gains[...] = jnp.concatenate([a[0:1] + b[0:1], a[8:9]], axis=0)
    shifts[...] = jnp.concatenate([a[1:2] + b[1:2], a[10:11], a[9:10], a[11:12]], axis=0)
    copies = [
        pltpu.make_async_copy(held, to.at[turn], sems.at[n])
        for n, (held, to) in enumerate(zip((grad_in, *small), out))
    ]
    for copy in copies:
        copy.start()
    for copy in copies:
        copy.wait()


def late_out(place, part, before, units):
    model = part.shape[0]
    shapes = (3, model, 2 * LANES), (2, 2 * LANES), (1, units), (2, model), (4, model)
    return pl.pallas_call(
        functools.partial(late_kernel, bool(before)),
        out_shape=tuple(shaped(2, *s, dtype=F32) for s in shapes),
        in_specs=[SMEM, VMEM] + [ANY] * len(before),
        out_specs=(ANY,) * 5,
        scratch_shapes=[
            *[pltpu.VMEM(s, F32) for s in shapes],
            pltpu.SemaphoreType.DMA((5,)),
        ],
        input_output_aliases={2 + i: i for i in range(len(before))},
        cost_estimate=cost(3),
        compiler_params=pltpu.CompilerParams(vmem_limit_bytes=ROOM * MIB),
        name="late_far" if before else "late_own",
    )(place, part, *before)


def gather_near(array):
    mine = [array] + [shift_by(array, "y", d) for d in range(1, lax.axis_size("y"))]
    return mine + [shift_by(a, "c", 1) for a in mine]


def return_near(parts):
    return [parts[0]] + [shift_by(p, "y", -j) for j, p in enumerate(parts) if j > 0]


def offsets(size):
    return [(step, flip) for step in range(size) for flip in range(2)]


def return_far(parts):
    return [parts[0]] + [shift_by(p, "z", step) for step, p in enumerate(parts) if step > 0]


PLANE = ("z", "y")


def core_sum(keep, give):
    return (keep.astype(F32) + shift_by(give, "c", 1).astype(F32)).astype(BF)


def crossed(array):
    n = lax.axis_size(("xl", "h"))
    return lax.ppermute(array, ("xl", "h"), [(i, n - 1 - i) for i in range(n)])


def across(low):
    done = low.astype(F32) + shift_by(low, "xl", 1).astype(F32)
    size = 4 * LANES
    ones = jnp.concatenate([low[:, i + 3 * LANES : i + size] for i in range(0, low.shape[1], size)], axis=1)
    more = shift_by(ones, "h", 1).astype(F32) + crossed(ones).astype(F32)
    more = jnp.where(jnp.arange(more.shape[1]) % LANES < 2, more, 0.0)
    nothing = jnp.zeros((low.shape[0], 3 * LANES), F32)
    laid = [[nothing, more[:, i : i + LANES]] for i in range(0, more.shape[1], LANES)]
    return (done + jnp.concatenate(sum(laid, []), axis=1)).astype(BF)


def tied(arrays, others):
    return lax.optimization_barrier((arrays, others))


def local(
    tokens,
    cotangents,
    segment_ids,
    in_weights,
    in_biases,
    out_weight,
    up_weight,
    up_biases,
    down_weight,
    gains,
    shifts,
):
    size, model = tokens.shape
    cols = in_weights.shape[2]
    heads = cols // HD
    rows = size - TILE
    units = up_weight.shape[1]
    c = lax.axis_index("c")

    told, copies, count = front(tokens, segment_ids, lax.axis_size(("z", "xl")))
    far = lax.all_to_all(copies, ("z", "xl"), 0, 0, tiled=True)
    near = gather_near(told)
    core = c.astype(jnp.int32).reshape(1)
    z, xl, z_size = lax.axis_index("z"), lax.axis_index("xl"), lax.axis_size("z")
    routes = [((z + step) % z_size) * 2 + (xl ^ flip) for step, flip in offsets(z_size)]
    place = jnp.stack([c, *routes, z, lax.axis_index("y")]).astype(jnp.int32)
    plane = lax.axis_size(PLANE)

    weights, biases, pairs, columns, bundle = prepare(
        core, in_weights, in_biases, gains, shifts, up_weight, down_weight, up_biases[None], heads
    )
    out_far = crossed(out_weight)
    far_one = crossed(bundle)
    far_two = shift_by(far_one, "c", 1)

    weights, (out_far, columns, place) = tied(weights, (out_far, columns, place))
    *parts, give, xq, xk, qx, kx, vx, counts = attend(
        near, far, weights, biases, gains, shifts, rows, heads
    )
    thumb_out, xhat, x = thumbs(tokens, weights, biases, gains, shifts, heads)
    parts = pair_merge(parts, shift_by(give, "c", 1), heads)
    low, full, lse = merge(count, return_near(parts), thumb_out, heads)
    low_far = shift_by(low, "h", 1)
    mixed, grad_mid, mid_low, packed, hidden, act, pre, small = feed_forward(
        tokens, cotangents, low, low_far, full, lse, out_weight, out_far, up_weight, up_biases[None],
        down_weight, far_one, far_two, gains, shifts, rows, heads,
    )
    grads = gather_near(packed)
    keep, give = weight_grads(core, act, cotangents, hidden, pre, low, mid_low, plane)
    mid_low, (keep, give) = tied(mid_low, (keep, give))
    thumb = thumbs_back(count, x, mid_low, out_weight, heads)
    early = core_sum(keep, give)

    grads, (early, thumb) = tied(grads, (early, thumb))
    early = lax.all_to_all(early, PLANE, 0, 0, tiled=True)
    *out, keep, give = reverse(
        counts, place, grads, (xq, xk, qx, kx, vx), xhat, thumb, pairs, columns, small, rows, heads
    )
    half = len(near) // 2
    out_q, give_q, out_kv = out[:half], out[half], out[half + 1 :]
    early = jnp.sum(early.astype(F32), axis=0).astype(BF)
    early = (early.astype(F32) + shift_by(early, "xl", 1).astype(F32)).astype(BF)
    early = jnp.broadcast_to(early[None], (z_size, *early.shape))
    late, early = tied(core_sum(keep, give), early)
    early = lax.all_to_all(early, "z", 0, 0, tiled=True)
    from_kv = return_far(out_kv)
    out_q = fold(out_q, shift_by(give_q, "c", 1))
    from_q = return_near(out_q)
    late, (early, from_kv[1], from_kv[-1], from_q) = tied(
        late, (early, from_kv[1], from_kv[-1], from_q)
    )
    late = late.reshape(plane, -1, late.shape[1])
    late = lax.all_to_all(late, PLANE, 0, 0, tiled=True)
    early = [early] + [shift_by(early, "y", d) for d in range(1, lax.axis_size("y"))]
    mine, other = grad_one(count, from_q, from_kv, thumb, pairs)
    late, (early[1], early[-1]) = tied(late, (early[1], early[-1]))
    late = across(jnp.sum(late.astype(F32), axis=0).astype(BF))
    arrived = [shift_by(mine, "h", 1), shift_by(other, "xl", 1), crossed(other)]
    late, (early, mine, other) = tied(late, (early, mine, other))
    late = jnp.broadcast_to(late[None], (plane, *late.shape))
    late = lax.all_to_all(late, PLANE, 0, 0, tiled=True).reshape(model, -1)

    grad_tokens = close(count, tokens, grad_mid, mine, *arrived, gains)
    early_far = [shift_by(e, "c", 1) for e in early]
    done = early_out(place, early, (), units, cols)
    grad_down, grad_up, grad_out = early_out(place, early_far, done, units, cols)
    done = late_out(place, late, (), units)
    grad_in, in_bias, up_bias, grad_gains, grad_shifts = late_out(
        place, shift_by(late, "c", 1), done, units
    )
    return (
        mixed,
        grad_tokens,
        grad_in,
        in_bias,
        grad_out,
        grad_up,
        up_bias.reshape(2, units),
        grad_down,
        grad_gains,
        grad_shifts,
    )


def solution(mesh):
    fine = Mesh(mesh.devices.reshape(4, 2, 4, 2, 2), ("z", "xl", "y", "c", "h"))
    blk = ("z", "xl", "y", "c")
    return jax.shard_map(
        local,
        mesh=fine,
        in_specs=(
            P(blk, None),
            P(None, blk, None),
            P(blk),
            P(None, None, "h"),
            P(None, "h"),
            P("h", None),
            P(None, "h"),
            P("h"),
            P("h", None),
            P(),
            P(),
        ),
        out_specs=(
            P(blk, None),
            P(None, blk, None),
            P(None, None, None, "h"),
            P(None, None, "h"),
            P(None, "h", None),
            P(None, None, "h"),
            P(None, "h"),
            P(None, "h", None),
            P(),
            P(),
        ),
        check_vma=False,
    )
```

```python
import functools

import jax
import jax.numpy as jnp
from jax import lax
from jax.experimental import pallas as pl
from jax.experimental.pallas import tpu as pltpu
from jax.sharding import Mesh
from jax.sharding import PartitionSpec as P

HD = 64
LANES = 128
TILE = 64
BLOCK = 256
EPS = 1e-06
SCALE = 0.125
FAR = -1e30
BF = jnp.bfloat16
F32 = jnp.float32
MIB = 1024 * 1024
ROOM = 56

NT = (((1,), (1,)), ((), ()))
TN = (((0,), (0,)), ((), ()))


def shift_by(array, axis, step):
    size = lax.axis_size(axis)
    return lax.ppermute(array, axis, [(i, (i + step) % size) for i in range(size)])


def dot(a, b):
    return jnp.dot(a, b, preferred_element_type=F32)


def dot_nt(a, b):
    return lax.dot_general(a, b, NT, preferred_element_type=F32)


def dot_tn(a, b):
    return lax.dot_general(a, b, TN, preferred_element_type=F32)


def standard(field):
    center = field - jnp.mean(field, axis=-1, keepdims=True)
    factor = lax.rsqrt(jnp.mean(center * center, axis=-1, keepdims=True) + EPS)
    return center * factor, factor


def norm_back(grad, gain, xhat, factor):
    h = grad * gain
    mean = jnp.mean(h, axis=-1, keepdims=True)
    return factor * (h - mean - xhat * jnp.mean(h * xhat, axis=-1, keepdims=True))


def pieces(value):
    high = value.astype(BF)
    rest = value - high.astype(F32)
    middle = rest.astype(BF)
    low = (rest - middle.astype(F32)).astype(BF)
    return high, middle, low


def zero_one(mask):
    return jnp.where(mask, 1.0, 0.0).astype(BF)


def iota(shape, dim):
    return lax.broadcasted_iota(jnp.int32, shape, dim)


VMEM = pl.BlockSpec(memory_space=pltpu.VMEM)
ANY = pl.BlockSpec(memory_space=pl.ANY)
SMEM = pl.BlockSpec(memory_space=pltpu.SMEM)


def local_call(body, name, out, ins, outs, args, scratch=(), cost=None, room=16):
    return pl.pallas_call(
        body,
        out_shape=out,
        in_specs=ins,
        out_specs=outs,
        scratch_shapes=scratch,
        cost_estimate=cost,
        compiler_params=pltpu.CompilerParams(vmem_limit_bytes=room * MIB),
        name=name,
    )(*args)


def shaped(*shape, dtype=BF):
    return jax.ShapeDtypeStruct(shape, dtype)


def cost(micros):
    return pl.CostEstimate(flops=int(micros * 1e9), bytes_accessed=0, transcendentals=0)


def front_kernel(tokens, ids, told, copies, number):
    rows = told.shape[0] - 16
    marks = jnp.where(ids[...] == 0, 1.0, 0.0)
    tiles = jnp.sum(marks).astype(jnp.int32) // TILE
    number[0] = tiles
    told[:rows, :] = tokens[:rows, :]
    told[rows:, :] = jnp.full((16, told.shape[1]), tiles.astype(F32), F32).astype(BF)
    for g in range(copies.shape[0]):
        copies[g] = told[...]


def front(tokens, ids, copies):
    size, model = tokens.shape
    told = size - TILE + 16
    return local_call(
        front_kernel,
        "front",
        (shaped(told, model), shaped(copies, told, model), shaped(1, dtype=jnp.int32)),
        [VMEM, VMEM],
        (VMEM, VMEM, SMEM),
        (tokens, ids.reshape(-1, LANES)),
        room=ROOM,
    )


def prepare_kernel(
    heads, place, in_weights, in_biases, gains, shifts, up, down, bias,
    weights, biases, pairs, columns, out,
):
    core = place[0]
    half = out.shape[1]
    at = pl.ds(pl.multiple_of(core * half, half), half)
    out[:half, :] = up[:, at]
    out[half : 2 * half, :] = down[at, :]
    mine = jnp.where(core == 0, bias[:, :half], bias[:, half:])
    row = iota((16, half), 0)
    rows = jnp.zeros((16, half), F32)
    for i, piece in enumerate(pieces(mine)):
        rows = jnp.where(row == i, piece.astype(F32), rows)
    out[2 * half :, :] = rows.astype(BF)

    model, cols = in_weights.shape[1:]
    width = heads * LANES
    row, col = (iota((cols, width), d) for d in (0, 1))
    spread = zero_one((row // HD == col // LANES) & (row % HD == col % LANES))
    lane = iota((1, width), 1) % LANES
    gap = jnp.zeros((1, HD), F32)

    def apart(line):
        return jnp.concatenate(
            sum([[line[:, h * HD : (h + 1) * HD], gap] for h in range(heads)], []), axis=1
        )

    extra = [
        apart(in_biases[0:1, :] * SCALE) + jnp.where(lane == HD, 1.0, 0.0),
        jnp.where((lane > HD) & (lane < HD + 4), 1.0, 0.0),
        apart(in_biases[1:2, :]) + jnp.where((lane >= HD) & (lane < HD + 3), 1.0, 0.0),
    ]
    for i in range(3):
        factor = SCALE if i == 0 else 1.0
        weights[:, i * width : (i + 1) * width] = (dot(in_weights[i], spread) * factor).astype(BF)
        biases[:, i * width : (i + 1) * width] = extra[i]
        for pair in range(heads // 2):
            pairs[pair, :, i * LANES : (i + 1) * LANES] = in_weights[
                i, :, pair * LANES : (pair + 1) * LANES
            ]
    tall = jnp.concatenate(
        [gains[0:1, :], shifts[0:1, :], jnp.zeros((LANES - 2, model), F32)], axis=0
    )
    columns[...] = jnp.transpose(tall)


def prepare(core, in_weights, in_biases, gains, shifts, up, down, bias, heads):
    model = up.shape[0]
    width = 3 * heads * LANES
    return local_call(
        functools.partial(prepare_kernel, heads),
        "prepare",
        (
            shaped(model, width),
            shaped(1, width, dtype=F32),
            shaped(heads // 2, model, 3 * LANES),
            shaped(model, LANES, dtype=F32),
            shaped(2 * model + 16, model),
        ),
        [SMEM] + [VMEM] * 7,
        (VMEM,) * 5,
        (core, in_weights, in_biases, gains, shifts, up, down, bias),
        cost=cost(4),
        room=ROOM,
    )


def count_of(ref, rows):
    return jnp.max(ref[rows : rows + 16, :LANES].astype(F32)).astype(jnp.int32)


def rows_at(start, rows, step=TILE):
    return pl.ds(pl.multiple_of(start, step), rows)


def attend_kernel(rows, groups, heads, *refs):
    near, far = refs[:groups], refs[groups]
    weights, biases, gains, shifts = refs[groups + 1 : groups + 5]
    at = groups + 5 + groups // 2
    out, give = refs[groups + 5 : at], refs[at]
    kept, counts, place = refs[at + 1 : at + 6], refs[at + 6], refs[at + 7]
    (xq, xk, qx, kx, vx), sems = refs[at + 8 : at + 13], refs[at + 13]
    model = xq.shape[1]
    q_counts = [count_of(r, rows) for r in near]
    k_counts = [count_of(far.at[g], rows) for g in range(groups)]
    for g in range(groups):
        counts[g] = q_counts[g]
        counts[groups + g] = k_counts[g]

    def compact(numbers, read, target):
        start = jnp.int32(0)
        for g, n in enumerate(numbers):
            target[rows_at(start, rows), :] = read(g)
            start = start + n * TILE
        target[rows_at(start, BLOCK), :] = jnp.zeros((BLOCK, model), BF)
        return start

    q_total = compact(q_counts, lambda g: near[g][:rows, :], xq)
    k_total = compact(k_counts, lambda g: far[g, :rows, :], xk)
    q_blocks = (q_total + BLOCK - 1) // BLOCK
    k_blocks = (k_total + BLOCK - 1) // BLOCK
    width = heads * LANES

    def hidden(ref, here):
        clean = standard(ref[here, :].astype(F32))[0].astype(BF)
        ref[here, :] = clean
        return (clean.astype(F32) * gains[0:1, :] + shifts[0:1, :]).astype(BF)

    @pl.loop(0, q_blocks)
    def _(b):
        here = rows_at(b * BLOCK, BLOCK, BLOCK)
        q = (dot(hidden(xq, here), weights[:, :width]) + biases[:, :width]).astype(BF)
        for h in range(heads):
            qx[h, here, :] = q[:, h * LANES : (h + 1) * LANES]

    @pl.loop(0, k_blocks)
    def _(b):
        here = rows_at(b * BLOCK, BLOCK, BLOCK)
        both = dot(hidden(xk, here), weights[:, width:]) + biases[:, width:]
        unseen = (iota((BLOCK, width), 0) + b * BLOCK >= k_total) & (
            iota((BLOCK, width), 1) % LANES == HD
        )
        k = jnp.where(unseen, FAR, both[:, :width]).astype(BF)
        v = both[:, width:].astype(BF)
        for h in range(heads):
            kx[h, here, :] = k[:, h * LANES : (h + 1) * LANES]
            vx[h, here, :] = v[:, h * LANES : (h + 1) * LANES]

    copies = [
        pltpu.make_async_copy(held, to, sems.at[i])
        for i, (held, to) in enumerate(zip((xq, xk, qx, kx, vx), kept))
    ]
    for copy in copies:
        copy.start()

    def attend_all(span):
        @pl.loop(0, q_blocks)
        def _(b):
            here = rows_at(b * BLOCK, BLOCK, BLOCK)
            lane = iota((BLOCK, LANES), 1)
            for h in range(heads):
                s = dot_nt(qx[h, here, :], kx[h, :span, :])
                top = jnp.max(s, axis=-1, keepdims=True)
                o = dot(jnp.exp(s - top).astype(BF), vx[h, :span, :])
                total = o[:, HD : HD + 1]
                o = o / total
                for i, piece in enumerate(pieces(top + jnp.log(total))):
                    o = jnp.where(lane == HD + i, piece.astype(F32), o)
                place[h, here, :] = o.astype(BF)

    for blocks in range(groups * TILE // BLOCK, groups * rows // BLOCK + 1):
        pl.when(k_blocks == blocks)(functools.partial(attend_all, blocks * BLOCK))

    gather = [
        (iota((LANES, LANES), 0) - HD + 3 * h == iota((LANES, LANES), 1))
        & (iota((LANES, LANES), 0) >= HD)
        & (iota((LANES, LANES), 0) < HD + 3)
        for h in range(heads)
    ]
    gather = [jnp.where(m, 1.0, 0.0).astype(BF) for m in gather]
    start = jnp.int32(0)
    for g in range(groups):
        mine = [place[h, rows_at(start, rows), :] for h in range(heads)]
        stats = sum(dot(m, s) for m, s in zip(mine, gather)).astype(BF)
        value = jnp.concatenate([m[:, :HD] for m in mine] + [stats], axis=1)
        if g < groups // 2:
            out[g][...] = value
        else:
            give[g - groups // 2] = value
        start = start + q_counts[g] * TILE
    for copy in copies:
        copy.wait()


def attend(near, far, weights, biases, gains, shifts, rows, heads):
    groups = len(near)
    model = near[0].shape[1]
    room = rows * groups + BLOCK
    parts = heads * HD + LANES
    kept = [(room, model)] * 2 + [(heads, room, LANES)] * 3
    return local_call(
        functools.partial(attend_kernel, rows, groups, heads),
        "attend",
        (
            *[shaped(rows, parts)] * (groups // 2),
            shaped(groups // 2, rows, parts),
            *[shaped(*k) for k in kept],
            shaped(2 * groups, dtype=jnp.int32),
        ),
        [VMEM] * (groups + 5),
        (*[VMEM] * (groups // 2 + 1), *[ANY] * 5, SMEM),
        (*near, far, weights, biases, gains, shifts),
        [
            pltpu.VMEM((heads, room, LANES), BF),
            *[pltpu.VMEM(k, BF) for k in kept],
            pltpu.SemaphoreType.DMA((5,)),
        ],
        cost(15),
        ROOM,
    )


def same_tile(rows):
    return iota((rows, rows), 0) // TILE == iota((rows, rows), 1) // TILE


def thumb_kernel(heads, tokens, weights, biases, gains, shifts, out, xhat, x):
    width = heads * LANES
    size = tokens.shape[0]
    clean = standard(tokens[...].astype(F32))[0].astype(BF)
    xhat[...] = clean
    hidden = (clean.astype(F32) * gains[0:1, :] + shifts[0:1, :]).astype(BF)
    x[...] = (dot(hidden, weights[...]) + biases[...]).astype(BF)
    visible = same_tile(size - TILE)
    out[:TILE, :] = jnp.zeros((TILE, heads * HD), F32)
    for h in range(heads):
        q = x[TILE:, h * LANES : (h + 1) * LANES]
        k = x[TILE:, width + h * LANES : width + (h + 1) * LANES]
        v = x[TILE:, 2 * width + h * LANES : 2 * width + (h + 1) * LANES]
        s = jnp.where(visible, dot_nt(q, k), FAR)
        e = jnp.exp(s - jnp.max(s, axis=-1, keepdims=True))
        o = dot(e.astype(BF), v)[:, :HD] / jnp.sum(e, axis=-1, keepdims=True)
        out[TILE:, h * HD : (h + 1) * HD] = o


def thumbs(tokens, weights, biases, gains, shifts, heads):
    size, model = tokens.shape
    return local_call(
        functools.partial(thumb_kernel, heads),
        "thumbs",
        (
            shaped(size, heads * HD, dtype=F32),
            shaped(size, model),
            shaped(size, 3 * heads * LANES),
        ),
        [VMEM] * 5,
        (VMEM,) * 3,
        (tokens, weights, biases, gains, shifts),
        cost=cost(5),
    )


def merged(parts, heads):
    cols = heads * HD
    row, col = (iota((LANES, cols), d) for d in (0, 1))
    spread = zero_one(row // 3 == col // HD)
    marks = [dot(p[:, cols:], spread) for p in parts]
    top = functools.reduce(jnp.maximum, marks)
    expos = [jnp.exp(m - top) for m in marks]
    total = sum(expos)
    mixed = sum(e * p[:, :cols].astype(F32) for p, e in zip(parts, expos)) / total
    row, col = (iota((cols, LANES), d) for d in (0, 1))
    packed = [
        dot(piece, zero_one((row % HD == 0) & (col == 3 * (row // HD) + i)))
        for i, piece in enumerate(pieces(top + jnp.log(total)))
    ]
    return mixed, sum(packed)


def pair_kernel(heads, *refs):
    count = (len(refs) - 1) // 2
    for j, (mine, out) in enumerate(zip(refs[:count], refs[count + 1 :])):
        mixed, marks = merged([mine[...], refs[count][j]], heads)
        out[...] = jnp.concatenate([mixed.astype(BF), marks.astype(BF)], axis=1)


def pair_merge(parts, other, heads):
    return local_call(
        functools.partial(pair_kernel, heads),
        "pair_merge",
        tuple(shaped(*p.shape) for p in parts),
        [VMEM] * (len(parts) + 1),
        (VMEM,) * len(parts),
        (*parts, other),
        cost=cost(3),
        room=ROOM,
    )


def merge_kernel(heads, counts, thumb, *refs):
    parts, (low, full, lse) = refs[:-3], refs[-3:]
    cols = heads * HD
    rows = lse.shape[0]
    mixed, marks = merged([p[...] for p in parts], heads)
    lse[...] = (-marks).astype(BF)
    image = iota((rows, cols), 0) < counts[0] * TILE
    full[:rows, :] = jnp.where(image, mixed, thumb[:rows, :])
    full[rows:, :] = thumb[rows:, :]
    low[...] = full[...].astype(BF)


def merge(count, parts, thumb, heads):
    size, cols = thumb.shape
    return local_call(
        functools.partial(merge_kernel, heads),
        "merge",
        (shaped(size, cols), shaped(size, cols, dtype=F32), shaped(parts[0].shape[0], LANES)),
        [SMEM] + [VMEM] * (1 + len(parts)),
        (VMEM,) * 3,
        (count, thumb, *parts),
        cost=cost(3),
    )


def fold_kernel(*refs):
    count = (len(refs) - 1) // 2
    for j, (mine, out) in enumerate(zip(refs[:count], refs[count + 1 :])):
        out[...] = (mine[...].astype(F32) + refs[count][j].astype(F32)).astype(BF)


def fold(parts, other):
    return local_call(
        fold_kernel,
        "fold",
        tuple(shaped(*p.shape) for p in parts),
        [VMEM] * (len(parts) + 1),
        (VMEM,) * len(parts),
        (*parts, other),
        cost=cost(2),
        room=ROOM,
    )


ROOT = 0.7978845608028654
CUBE = 0.044715


def ff_kernel(
    heads, tokens, outer, low, low_far, full, lse, out_weight, out_far, up, up_bias, down, far_one,
    far_two, gains, shifts, mixed, grad_mid, grad_low, packed, hidden_out, act_out, pre_out, small,
):
    size, model = tokens.shape
    passes = outer.shape[0]
    cols = heads * HD
    chunk = far_one.shape[1]
    units = up.shape[1]
    rows = packed.shape[0]
    branch = dot(low[...], out_weight[...]) + dot(low_far[...], out_far[...])
    middle = tokens[...].astype(F32) + (branch + shifts[1:2, :])
    xhat, factor = standard(middle)
    hidden = (xhat * gains[1:2, :] + shifts[2:3, :]).astype(BF)
    hidden_out[...] = hidden

    def one_chunk(up_part, bias, down_part, keep):
        v = dot(hidden, up_part) + bias
        t = jnp.tanh(ROOT * (v + CUBE * (v * v * v)))
        act = (0.5 * v * (1.0 + t)).astype(BF)
        slope = 0.5 * (1.0 + t) + 0.5 * v * (1.0 - t * t) * (ROOT * (1.0 + 3.0 * CUBE * (v * v)))
        two = []
        for p in range(passes):
            pre = (dot_nt(outer[p], down_part) * slope).astype(BF)
            if keep is not None:
                pre_out[p, :, keep] = pre
            two.append(dot_nt(pre, up_part))
        if keep is not None:
            act_out[:, keep] = act
        return dot(act, down_part), two

    def far_chunk(ref):
        told = ref[2 * chunk : 2 * chunk + 16, :].astype(F32)
        bias = told[0:1] + told[1:2] + told[2:3]
        return one_chunk(ref[:chunk, :], bias, ref[chunk : 2 * chunk, :], None)

    done = []
    for i in range(units // chunk):
        at = slice(i * chunk, (i + 1) * chunk)
        done.append(one_chunk(up[:, at], up_bias[:, at], down[at, :], at))
    done += [far_chunk(far_one), far_chunk(far_two)]

    def tree(parts):
        half = len(parts) // 2
        return sum(parts[:half]) + sum(parts[half:])

    output = tree([d[0] for d in done])
    mixed[...] = (middle + (output + shifts[3:4, :])).astype(BF)
    small[...] = jnp.zeros(small.shape, F32)
    lane = iota((rows, LANES), 1)
    stats = jnp.zeros((rows, LANES), F32)
    for p in range(passes):
        two = tree([d[1][p] for d in done])
        c = outer[p].astype(F32)
        mid = c + norm_back(two, gains[1:2, :], xhat, factor)
        mid_low = mid.astype(BF)
        grad_mid[p] = mid
        grad_low[p] = mid_low
        att = dot_nt(mid_low, out_weight[...]).astype(BF)
        packed[:, p * cols : (p + 1) * cols] = att[:rows, :]
        pre_out_p = pre_out[p].astype(F32)
        bias = jnp.sum(pre_out_p, axis=0, keepdims=True)
        small[p, 0:1, :] = jnp.sum(two * xhat, axis=0, keepdims=True)
        small[p, 1:2, :] = jnp.sum(two, axis=0, keepdims=True)
        small[p, 2:3, :] = jnp.sum(mid_low.astype(F32), axis=0, keepdims=True)
        small[p, 3:4, :] = jnp.sum(c, axis=0, keepdims=True)
        for i in range(units // model):
            small[p, 4 + i : 5 + i, :] = bias[:, i * model : (i + 1) * model]
        product = att[:rows, :].astype(F32) * full[:rows, :]
        for h in range(heads):
            delta = jnp.sum(product[:, h * HD : (h + 1) * HD], axis=-1, keepdims=True)
            for i, piece in enumerate(pieces(-delta)):
                stats = jnp.where(lane == 3 * heads * (p + 1) + 3 * h + i, piece.astype(F32), stats)
    packed[:, passes * cols :] = (stats + lse[...].astype(F32)).astype(BF)


def feed_forward(
    tokens, outer, low, low_far, full, lse, out_weight, out_far, up, up_bias, down, far_one, far_two,
    gains, shifts, rows, heads,
):
    size, model = tokens.shape
    passes = outer.shape[0]
    units = up.shape[1]
    return local_call(
        functools.partial(ff_kernel, heads),
        "feed_forward",
        (
            shaped(size, model),
            shaped(passes, size, model, dtype=F32),
            shaped(passes, size, model),
            shaped(rows, passes * heads * HD + LANES),
            shaped(size, model),
            shaped(size, units),
            shaped(passes, size, units),
            shaped(passes, 8, model, dtype=F32),
        ),
        [VMEM] * 15,
        (VMEM,) * 8,
        (
            tokens, outer, low, low_far, full, lse, out_weight, out_far, up, up_bias, down, far_one,
            far_two, gains, shifts,
        ),
        cost=cost(12),
        room=32,
    )


def thumb_back_kernel(heads, counts, x, mid_low, out_weight, out):
    width = heads * LANES
    size = x.shape[0]
    passes = mid_low.shape[0]
    visible = same_tile(size - TILE)
    outside = iota((size - TILE, HD), 0) + TILE >= counts[0] * TILE
    grads = [dot_nt(mid_low[p], out_weight[...]).astype(BF) for p in range(passes)]
    out[:, :, :TILE, :] = jnp.zeros((*out.shape[:2], TILE, out.shape[3]), BF)
    for h in range(heads):
        q = x[TILE:, h * LANES : (h + 1) * LANES]
        k = x[TILE:, width + h * LANES : width + (h + 1) * LANES]
        v = x[TILE:, 2 * width + h * LANES : 2 * width + h * LANES + HD]
        s = jnp.where(visible, dot_nt(q, k), FAR)
        e = jnp.exp(s - jnp.max(s, axis=-1, keepdims=True))
        w = e / jnp.sum(e, axis=-1, keepdims=True)
        w_low = w.astype(BF)
        for p in range(passes):
            g = grads[p][TILE:, h * HD : (h + 1) * HD]
            gw = dot_nt(g, v)
            ds = (w * (gw - jnp.sum(w * gw, axis=-1, keepdims=True))).astype(BF)
            dq = dot(ds, k[:, :HD]) * SCALE
            dk = dot_tn(ds, q)[:, :HD]
            dv = dot_tn(w_low, g)
            for c, piece in enumerate((dq, dk, dv)):
                at = c * LANES + (h % 2) * HD
                out[h // 2, p, TILE:, at : at + HD] = jnp.where(outside, piece, 0.0).astype(BF)


def thumbs_back(count, x, mid_low, out_weight, heads):
    passes, size, _ = mid_low.shape
    return local_call(
        functools.partial(thumb_back_kernel, heads),
        "thumbs_back",
        shaped(heads // 2, passes, size, 3 * LANES),
        [SMEM] + [VMEM] * 3,
        VMEM,
        (count, x, mid_low, out_weight),
        cost=cost(6),
    )


def early_at(units, model, low):
    ends = [model, 2 * model, 2 * model + units, 2 * model + units + low]
    return [slice(b - w, b) for b, w in zip(ends, (model, model, units, low))]


def early_cuts(parts, units, model, low):
    high, wide, turns = units // parts // 2, model // parts, model // low
    narrow = low * turns // parts
    for i in range(parts):
        yield (
            (slice(2 * i * high, (2 * i + 1) * high), slice(0, model)),
            (slice((2 * i + 1) * high, (2 * i + 2) * high), slice(0, model)),
            (slice(i * wide, (i + 1) * wide), slice(0, units)),
            (
                slice(i // turns * narrow, (i // turns + 1) * narrow),
                slice(i % turns * low, (i % turns + 1) * low),
            ),
        )


def weight_kernel(place, act, outer, hidden, pre, low, mid_low, keep, give):
    units, model, cols = act.shape[1], hidden.shape[1], low.shape[1]
    core = place[0]
    for turn, out in ((core, keep), (1 - core, give)):
        down = dot_tn(act[...], outer[turn]).astype(BF)
        up = dot_tn(hidden[...], pre[turn]).astype(BF)
        proj = dot_tn(low[...], mid_low[turn]).astype(BF)
        for i, cut in enumerate(early_cuts(keep.shape[0], units, model, cols)):
            for value, (rows, lanes), at in zip(
                (down, down, up, proj), cut, early_at(units, model, cols)
            ):
                out[i, :, at] = value[rows, lanes]


def weight_grads(core, act, outer, hidden, pre, low, mid_low, parts):
    units, model = act.shape[1], outer.shape[2]
    out = shaped(parts, model // parts, 2 * model + units + low.shape[1])
    return local_call(
        weight_kernel,
        "weight_grads",
        (out, out),
        [SMEM] + [VMEM] * 6,
        (VMEM,) * 2,
        (core, act, outer, hidden, pre, low, mid_low),
        cost=cost(8),
        room=24,
    )


def reverse_kernel(rows, groups, heads, passes, counts, place, *refs):
    grads, kept = refs[:groups], refs[groups : groups + 5]
    own, thumb, weights, columns, small = refs[groups + 5 : groups + 10]
    at = groups + 10
    out_q, give_q, at = refs[at : at + groups // 2], refs[at + groups // 2], at + groups // 2 + 1
    out_kv, at = refs[at : at + groups // 2], at + groups // 2
    keep, give = refs[at : at + 2]
    (
        stage, xq, xk, qx, kx, vx, packed, gx, kt, dq_t, dv, dk, low_q, low_kv, total, sums,
        starts, sems,
    ) = refs[at + 2 :]
    couples = heads // 2
    sources = [*grads, *kept[2:], *kept[:2]]
    targets = [*[stage.at[g] for g in range(groups)], qx, kx, vx, xq, xk]
    copies = [
        pltpu.make_async_copy(f, t, sems.at[i]) for i, (f, t) in enumerate(zip(sources, targets))
    ]
    for copy in copies:
        copy.start()
    cols = heads * HD
    wide = passes * LANES
    q_counts = [counts[g] for g in range(groups)]
    k_counts = [counts[groups + g] for g in range(groups)]
    start = jnp.int32(0)
    for g in range(groups):
        copies[g].wait()
        packed[rows_at(start, rows), :] = stage[g]
        start = start + q_counts[g] * TILE
    q_total, k_total = start, sum(k_counts) * TILE
    tail_lane = iota((BLOCK, packed.shape[1]), 1) - passes * cols
    empty = (tail_lane >= 0) & (tail_lane < 3 * heads) & (tail_lane % 3 == 0)
    packed[rows_at(q_total, BLOCK), :] = jnp.where(empty, FAR, 0.0).astype(BF)
    q_blocks = (q_total + BLOCK - 1) // BLOCK
    k_blocks = (k_total + BLOCK - 1) // BLOCK
    spans = range(groups * TILE // BLOCK, groups * rows // BLOCK + 1)

    row, col = (iota((LANES, heads * LANES), d) for d in (0, 1))
    head, lane = col // LANES, col % LANES
    to_marks = zero_one((lane > HD) & (lane < HD + 4) & (row == 3 * head + lane - HD - 1))
    row, col = (iota((LANES, heads * wide), d) for d in (0, 1))
    head, turn, lane = col // wide, col % wide // LANES, col % LANES
    to_deltas = zero_one(
        (lane >= HD) & (lane < HD + 3) & (row == 3 * heads * (turn + 1) + 3 * head + lane - HD)
    )
    for copy in copies[groups : groups + 3]:
        copy.wait()

    @pl.loop(0, q_blocks)
    def _(b):
        here = rows_at(b * BLOCK, BLOCK, BLOCK)
        stats = packed[here, passes * cols :]
        marks = dot(stats, to_marks)
        deltas = dot(stats, to_deltas).astype(BF)
        for h in range(heads):
            more = marks[:, h * LANES : (h + 1) * LANES]
            qx[h, here, :] = (qx[h, here, :].astype(F32) + more).astype(BF)
            for p in range(passes):
                at = p * cols + h * HD
                mine = (h * passes + p) * LANES
                gx[h, here, p * LANES : (p + 1) * LANES] = jnp.concatenate(
                    [packed[here, at : at + HD], deltas[:, mine + HD : mine + LANES]], axis=1
                )

    @pl.loop(0, k_blocks)
    def _(b):
        here = rows_at(b * BLOCK, BLOCK, BLOCK)
        for h in range(heads):
            kt[h, b] = jnp.transpose(kx[h, here, :].astype(F32))[:HD, :].astype(BF)

    def reverse_all(blocks):
        span = blocks * BLOCK

        @pl.loop(0, couples)
        def _(pair):
            dv[:, :span, :] = jnp.zeros((2, span, wide), F32)
            dk[:, :, :span, :] = jnp.zeros((passes, 2, span, LANES), F32)

            @pl.loop(0, q_blocks)
            def _(b):
                here = rows_at(b * BLOCK, BLOCK, BLOCK)
                for i in range(2):
                    h = 2 * pair + i
                    q, g = qx[h, here, :], gx[h, here, :]
                    k_t = jnp.concatenate([kt[h, j] for j in range(blocks)], axis=1)
                    w = jnp.exp(dot_nt(kx[h, :span, :], q))
                    dv[i, :span, :] += dot(w.astype(BF), g)
                    for p in range(passes):
                        ds = dot_nt(vx[h, :span, :], g[:, p * LANES : (p + 1) * LANES])
                        ds = (w * ds).astype(BF)
                        dk[p, i, :span, :] += dot(ds, q)
                        dq_t[p, i * HD : (i + 1) * HD, :] = dot(k_t, ds)
                for p in range(passes):
                    piece = jnp.transpose(dq_t[p]) * SCALE
                    low_q[pair, here, p * LANES : (p + 1) * LANES] = piece.astype(BF)

            for p in range(passes):
                for c, both in enumerate(
                    (
                        [dk[p, i, :span, :HD] for i in range(2)],
                        [dv[i, :span, p * LANES : p * LANES + HD] for i in range(2)],
                    )
                ):
                    lane = (2 * p + c) * LANES
                    low_kv[pair, :span, lane : lane + LANES] = jnp.concatenate(both, axis=1).astype(BF)

    for blocks in spans:
        pl.when(k_blocks == blocks)(functools.partial(reverse_all, blocks))

    start = jnp.int32(0)
    for g in range(groups):
        starts[g] = start
        start = start + k_counts[g] * TILE
    for g in range(groups):
        here = rows_at(starts[place[1 + g]], rows)
        out_kv[g // 2][g % 2] = jnp.concatenate([low_kv[i, here, :] for i in range(couples)], axis=1)
    start = jnp.int32(0)
    for g in range(groups):
        here = rows_at(start, rows)
        value = jnp.concatenate([low_q[i, here, :] for i in range(couples)], axis=1)
        if g < groups // 2:
            out_q[g][...] = value
        else:
            give_q[g - groups // 2] = value
        start = start + q_counts[g] * TILE

    copies[groups + 3].wait()
    copies[groups + 4].wait()

    def key_sums(blocks):
        span = blocks * BLOCK
        for i in range(couples):
            flat = low_kv[i, :span, :]
            total[i, :, wide:] = dot_tn(xk[:span, :], flat)
            sums[i, :, wide:] = dot(jnp.ones((8, span), BF), flat)

    for blocks in spans:
        pl.when(k_blocks == blocks)(functools.partial(key_sums, blocks))

    total[:, :, :wide] = jnp.zeros((couples, total.shape[1], wide), F32)
    sums[:, :, :wide] = jnp.zeros((couples, 8, wide), F32)

    @pl.loop(0, q_blocks)
    def _(b):
        here = rows_at(b * BLOCK, BLOCK, BLOCK)
        for i in range(couples):
            total[i, :, :wide] += dot_tn(xq[here, :], low_q[i, here, :])
            sums[i, :, :wide] += dot(jnp.ones((8, BLOCK), BF), low_q[i, here, :])

    model = total.shape[1]
    gain, shift = columns[:, 0:1], columns[:, 1:2]
    ones = jnp.ones((8, own.shape[0]), BF)
    for p in range(passes):
        whole = []
        for i in range(couples):
            mine = thumb[i, p]
            part = dot_tn(own[...], mine)
            part_sum = dot(ones, mine)[0:1, :]
            q_at = slice(p * LANES, (p + 1) * LANES)
            kv_at = slice((passes + 2 * p) * LANES, (passes + 2 * p + 2) * LANES)
            part += jnp.concatenate([total[i, :, q_at], total[i, :, kv_at]], axis=1)
            part_sum += jnp.concatenate([sums[i, 0:1, q_at], sums[i, 0:1, kv_at]], axis=1)
            w = weights[i].astype(F32)
            gain_one = jnp.sum(w * part, axis=1, keepdims=True)
            shift_one = jnp.sum(w * part_sum, axis=1, keepdims=True)
            lane = iota((model, LANES), 1)
            tall = jnp.where(lane == 0, gain_one, jnp.where(lane == 1, shift_one, 0.0))
            flat = jnp.concatenate(
                [jnp.zeros((2, LANES), F32)]
                + [part_sum[:, c * LANES : (c + 1) * LANES] for c in range(3)]
                + [jnp.zeros((LANES - 5, LANES), F32)],
                axis=0,
            )
            tall = jnp.concatenate([tall[:LANES] + jnp.transpose(flat), tall[LANES:]], axis=0)
            if i == 0:
                turned = jnp.concatenate(
                    [
                        jnp.zeros((8, model), F32),
                        small[p],
                        jnp.zeros((LANES - 16, model), F32),
                    ],
                    axis=0,
                )
                tall = tall + jnp.transpose(turned)
            whole += [part * gain + shift * part_sum, tall]
        whole = jnp.concatenate(whole, axis=1).astype(BF)

        @pl.when(place[0] == p)
        def _():
            keep[...] = whole

        @pl.when(place[0] != p)
        def _():
            give[...] = whole


def reverse(counts, place, grads, kept, own, thumb, weights, columns, small, rows, heads):
    groups = len(grads)
    couples, passes = thumb.shape[:2]
    model = own.shape[1]
    room = rows * groups + BLOCK
    cols = heads * HD
    wide = passes * LANES
    half = groups // 2
    late = shaped(model, couples * 4 * LANES)
    q, kv = shaped(rows, couples * wide), shaped(2, rows, couples * 2 * wide)
    out = (*[q] * half, shaped(half, rows, couples * wide), *[kv] * half, late, late)
    return local_call(
        functools.partial(reverse_kernel, rows, groups, heads, passes),
        "reverse",
        out,
        [SMEM, SMEM] + [ANY] * (groups + 5) + [VMEM] * 5,
        (VMEM,) * len(out),
        (counts, place, *grads, *kept, own, thumb, weights, columns, small),
        [
            pltpu.VMEM((groups, rows, passes * cols + LANES), BF),
            pltpu.VMEM((room, model), BF),
            pltpu.VMEM((room, model), BF),
            pltpu.VMEM((heads, room, LANES), BF),
            pltpu.VMEM((heads, room, LANES), BF),
            pltpu.VMEM((heads, room, LANES), BF),
            pltpu.VMEM((room, passes * cols + LANES), BF),
            pltpu.VMEM((heads, room, wide), BF),
            pltpu.VMEM((heads, room // BLOCK, HD, BLOCK), BF),
            pltpu.VMEM((passes, LANES, BLOCK), F32),
            pltpu.VMEM((2, room, wide), F32),
            pltpu.VMEM((passes, 2, room, LANES), F32),
            pltpu.VMEM((couples, room, wide), BF),
            pltpu.VMEM((couples, room, 2 * wide), BF),
            pltpu.VMEM((couples, model, 3 * wide), F32),
            pltpu.VMEM((couples, 8, 3 * wide), F32),
            pltpu.SMEM((groups,), jnp.int32),
            pltpu.SemaphoreType.DMA((groups + 5,)),
        ],
        cost(45),
        ROOM,
    )


def grad_one_kernel(near, counts, *refs):
    from_q, from_kv, (thumb, weights, mine, other) = refs[:near], refs[near:-4], refs[-4:]
    couples, passes, size, _ = thumb.shape
    rows = from_q[0].shape[0]
    sum_q = sum(r[...].astype(F32) for r in from_q)
    sum_kv = [sum(r[f].astype(F32) for r in from_kv) for f in range(2)]
    image = iota((rows, 3 * LANES), 0) < counts[0] * TILE
    for p in range(passes):
        parts = []
        for i in range(couples):
            at = (passes * i + p) * LANES
            there = slice(2 * at, 2 * at + 2 * LANES)
            far = jnp.concatenate([sum_q[:, at : at + LANES], sum_kv[0][:, there]], axis=1)
            flat = jnp.concatenate(
                [jnp.where(image, far.astype(BF), thumb[i, p, :rows]), thumb[i, p, rows:]], axis=0
            )
            parts.append(
                (
                    dot_nt(flat, weights[i]),
                    dot_nt(sum_kv[1][:, there].astype(BF), weights[i, :, LANES:]),
                )
            )
        mine[p] = sum(a for a, _ in parts).astype(BF)
        other[p] = sum(b for _, b in parts).astype(BF)


def grad_one(count, from_q, from_kv, thumb, weights):
    near = len(from_q)
    passes, size, _ = thumb.shape[1:]
    model = weights.shape[1]
    return local_call(
        functools.partial(grad_one_kernel, near),
        "grad_one",
        (shaped(passes, size, model), shaped(passes, from_q[0].shape[0], model)),
        [SMEM] + [VMEM] * (near + len(from_kv) + 2),
        (VMEM,) * 2,
        (count, *from_q, *from_kv, thumb, weights),
        cost=cost(5),
        room=ROOM,
    )


def close_kernel(counts, tokens, mid, mine, head, side, cross, gains, out):
    xhat, factor = standard(tokens[...].astype(F32))
    rows = side.shape[1]
    image = iota(side.shape[1:], 0) < counts[0] * TILE
    for p in range(mid.shape[0]):
        grad = mine[p].astype(F32) + head[p].astype(F32)
        more = jnp.where(image, side[p].astype(F32) + cross[p].astype(F32), 0.0)
        grad = jnp.concatenate([grad[:rows] + more, grad[rows:]], axis=0)
        out[p] = mid[p] + norm_back(grad, gains[0:1, :], xhat, factor)


def close(count, tokens, mid, mine, head, side, cross, gains):
    return local_call(
        close_kernel,
        "close",
        shaped(*mid.shape, dtype=F32),
        [SMEM] + [VMEM] * 7,
        VMEM,
        (count, tokens, mid, mine, head, side, cross, gains),
        cost=cost(4),
        room=ROOM,
    )


def early_kernel(lines, far, place, *refs):
    parts, refs = refs[:lines], refs[lines:]
    out, (down, up, proj, sems) = refs[-7:-4], refs[-4:]
    turn, y = place[0], place[10]
    turn = 1 - turn if far else turn
    (units, model), low = down.shape, proj.shape[0]
    steps, rows = parts[0].shape[:2]
    lane_down, lane_next, lane_up, lane_proj = early_at(units, model, low)
    turns = model // low
    for d, ref in enumerate(parts):
        for j in range(steps):
            i = j * lines + (y + lines - d) % lines
            at = pl.multiple_of(2 * rows * i, 2 * rows)
            down[pl.ds(at, rows), :] = ref[j, :, lane_down].astype(F32)
            down[pl.ds(at + rows, rows), :] = ref[j, :, lane_next].astype(F32)
            up[rows_at(rows * i, rows, rows), :] = ref[j, :, lane_up].astype(F32)
            here = rows_at(i // turns * rows, rows, rows)
            value = ref[j, :, lane_proj].astype(F32)
            for t in range(turns):

                @pl.when(i % turns == t)
                def _(value=value, here=here, t=t):
                    proj[here, t * low : (t + 1) * low] = value

    copies = [
        pltpu.make_async_copy(held, to.at[turn], sems.at[n])
        for n, (held, to) in enumerate(zip((down, up, proj), out))
    ]
    for copy in copies:
        copy.start()
    for copy in copies:
        copy.wait()


def early_out(place, parts, before, units, low):
    model = len(parts) * parts[0].shape[0] * parts[0].shape[1]
    shapes = (units, model), (model, units), (low, model)
    return pl.pallas_call(
        functools.partial(early_kernel, len(parts), bool(before)),
        out_shape=tuple(shaped(2, *s, dtype=F32) for s in shapes),
        in_specs=[SMEM] + [VMEM] * len(parts) + [ANY] * len(before),
        out_specs=(ANY,) * 3,
        scratch_shapes=[
            *[pltpu.VMEM(s, F32) for s in shapes],
            pltpu.SemaphoreType.DMA((3,)),
        ],
        input_output_aliases={1 + len(parts) + i: i for i in range(len(before))},
        cost_estimate=cost(5),
        compiler_params=pltpu.CompilerParams(vmem_limit_bytes=ROOM * MIB),
        name="early_far" if before else "early_own",
    )(place, *parts, *before)


def late_kernel(far, place, ref, *refs):
    out, (grad_in, *small), sems = refs[-11:-6], refs[-6:-1], refs[-1]
    in_bias, up_bias, gains, shifts = small
    turn = 1 - place[0] if far else place[0]
    turned = []
    for pair in range(2):
        at = 4 * LANES * pair
        for c in range(3):
            grad_in[c, :, pair * LANES : (pair + 1) * LANES] = ref[
                :, at + c * LANES : at + (c + 1) * LANES
            ].astype(F32)
        turned.append(jnp.transpose(ref[:, at + 3 * LANES : at + 4 * LANES].astype(F32)))
    a, b = turned
    in_bias[...] = jnp.concatenate(
        [
            jnp.concatenate([a[2:3, :LANES], b[2:3, :LANES]], axis=1),
            jnp.concatenate([a[4:5, :LANES], b[4:5, :LANES]], axis=1),
        ],
        axis=0,
    )
    up_bias[...] = jnp.concatenate([a[12:13], a[13:14]], axis=1)
    gains[...] = jnp.concatenate([a[0:1] + b[0:1], a[8:9]], axis=0)
    shifts[...] = jnp.concatenate([a[1:2] + b[1:2], a[10:11], a[9:10], a[11:12]], axis=0)
    copies = [
        pltpu.make_async_copy(held, to.at[turn], sems.at[n])
        for n, (held, to) in enumerate(zip((grad_in, *small), out))
    ]
    for copy in copies:
        copy.start()
    for copy in copies:
        copy.wait()


def late_out(place, part, before, units):
    model = part.shape[0]
    shapes = (3, model, 2 * LANES), (2, 2 * LANES), (1, units), (2, model), (4, model)
    return pl.pallas_call(
        functools.partial(late_kernel, bool(before)),
        out_shape=tuple(shaped(2, *s, dtype=F32) for s in shapes),
        in_specs=[SMEM, VMEM] + [ANY] * len(before),
        out_specs=(ANY,) * 5,
        scratch_shapes=[
            *[pltpu.VMEM(s, F32) for s in shapes],
            pltpu.SemaphoreType.DMA((5,)),
        ],
        input_output_aliases={2 + i: i for i in range(len(before))},
        cost_estimate=cost(3),
        compiler_params=pltpu.CompilerParams(vmem_limit_bytes=ROOM * MIB),
        name="late_far" if before else "late_own",
    )(place, part, *before)


def gather_near(array):
    mine = [array] + [shift_by(array, "y", d) for d in range(1, lax.axis_size("y"))]
    return mine + [shift_by(a, "c", 1) for a in mine]


def return_near(parts):
    return [parts[0]] + [shift_by(p, "y", -j) for j, p in enumerate(parts) if j > 0]


def offsets(size):
    return [(step, flip) for step in range(size) for flip in range(2)]


def return_far(parts):
    return [parts[0]] + [shift_by(p, "z", step) for step, p in enumerate(parts) if step > 0]


PLANE = ("z", "y")


def core_sum(keep, give):
    return (keep.astype(F32) + shift_by(give, "c", 1).astype(F32)).astype(BF)


def crossed(array):
    n = lax.axis_size(("xl", "h"))
    return lax.ppermute(array, ("xl", "h"), [(i, n - 1 - i) for i in range(n)])


def across(low):
    done = low.astype(F32) + shift_by(low, "xl", 1).astype(F32)
    size = 4 * LANES
    ones = jnp.concatenate([low[:, i + 3 * LANES : i + size] for i in range(0, low.shape[1], size)], axis=1)
    more = shift_by(ones, "h", 1).astype(F32) + crossed(ones).astype(F32)
    more = jnp.where(jnp.arange(more.shape[1]) % LANES < 2, more, 0.0)
    nothing = jnp.zeros((low.shape[0], 3 * LANES), F32)
    laid = [[nothing, more[:, i : i + LANES]] for i in range(0, more.shape[1], LANES)]
    return (done + jnp.concatenate(sum(laid, []), axis=1)).astype(BF)


def tied(arrays, others):
    return lax.optimization_barrier((arrays, others))


def local(
    tokens,
    cotangents,
    segment_ids,
    in_weights,
    in_biases,
    out_weight,
    up_weight,
    up_biases,
    down_weight,
    gains,
    shifts,
):
    size, model = tokens.shape
    cols = in_weights.shape[2]
    heads = cols // HD
    rows = size - TILE
    units = up_weight.shape[1]
    c = lax.axis_index("c")

    told, copies, count = front(tokens, segment_ids, lax.axis_size(("z", "xl")))
    far = lax.all_to_all(copies, ("z", "xl"), 0, 0, tiled=True)
    near = gather_near(told)
    core = c.astype(jnp.int32).reshape(1)
    z, xl, z_size = lax.axis_index("z"), lax.axis_index("xl"), lax.axis_size("z")
    routes = [((z + step) % z_size) * 2 + (xl ^ flip) for step, flip in offsets(z_size)]
    place = jnp.stack([c, *routes, z, lax.axis_index("y")]).astype(jnp.int32)
    plane = lax.axis_size(PLANE)

    weights, biases, pairs, columns, bundle = prepare(
        core, in_weights, in_biases, gains, shifts, up_weight, down_weight, up_biases[None], heads
    )
    out_far = crossed(out_weight)
    far_one = crossed(bundle)
    far_two = shift_by(far_one, "c", 1)

    weights, (out_far, columns, place) = tied(weights, (out_far, columns, place))
    *parts, give, xq, xk, qx, kx, vx, counts = attend(
        near, far, weights, biases, gains, shifts, rows, heads
    )
    thumb_out, xhat, x = thumbs(tokens, weights, biases, gains, shifts, heads)
    parts = pair_merge(parts, shift_by(give, "c", 1), heads)
    low, full, lse = merge(count, return_near(parts), thumb_out, heads)
    low_far = shift_by(low, "h", 1)
    mixed, grad_mid, mid_low, packed, hidden, act, pre, small = feed_forward(
        tokens, cotangents, low, low_far, full, lse, out_weight, out_far, up_weight, up_biases[None],
        down_weight, far_one, far_two, gains, shifts, rows, heads,
    )
    grads = gather_near(packed)
    keep, give = weight_grads(core, act, cotangents, hidden, pre, low, mid_low, plane)
    mid_low, (keep, give) = tied(mid_low, (keep, give))
    thumb = thumbs_back(count, x, mid_low, out_weight, heads)
    early = core_sum(keep, give)

    grads, (early, thumb) = tied(grads, (early, thumb))
    early = lax.all_to_all(early, PLANE, 0, 0, tiled=True)
    *out, keep, give = reverse(
        counts, place, grads, (xq, xk, qx, kx, vx), xhat, thumb, pairs, columns, small, rows, heads
    )
    half = len(near) // 2
    out_q, give_q, out_kv = out[:half], out[half], out[half + 1 :]
    early = jnp.sum(early.astype(F32), axis=0).astype(BF)
    early = (early.astype(F32) + shift_by(early, "xl", 1).astype(F32)).astype(BF)
    early = jnp.broadcast_to(early[None], (z_size, *early.shape))
    late, early = tied(core_sum(keep, give), early)
    early = lax.all_to_all(early, "z", 0, 0, tiled=True)
    from_kv = return_far(out_kv)
    out_q = fold(out_q, shift_by(give_q, "c", 1))
    from_q = return_near(out_q)
    late, (early, from_kv[1], from_kv[-1], from_q) = tied(
        late, (early, from_kv[1], from_kv[-1], from_q)
    )
    late = late.reshape(plane, -1, late.shape[1])
    late = lax.all_to_all(late, PLANE, 0, 0, tiled=True)
    early = [early] + [shift_by(early, "y", d) for d in range(1, lax.axis_size("y"))]
    mine, other = grad_one(count, from_q, from_kv, thumb, pairs)
    late, (early[1], early[-1]) = tied(late, (early[1], early[-1]))
    late = across(jnp.sum(late.astype(F32), axis=0).astype(BF))
    arrived = [shift_by(mine, "h", 1), shift_by(other, "xl", 1), crossed(other)]
    late = jnp.broadcast_to(late[None], (plane, *late.shape))
    late = lax.all_to_all(late, PLANE, 0, 0, tiled=True).reshape(model, -1)

    grad_tokens = close(count, tokens, grad_mid, mine, *arrived, gains)
    early_far = [shift_by(e, "c", 1) for e in early]
    done = early_out(place, early, (), units, cols)
    grad_down, grad_up, grad_out = early_out(place, early_far, done, units, cols)
    done = late_out(place, late, (), units)
    grad_in, in_bias, up_bias, grad_gains, grad_shifts = late_out(
        place, shift_by(late, "c", 1), done, units
    )
    return (
        mixed,
        grad_tokens,
        grad_in,
        in_bias,
        grad_out,
        grad_up,
        up_bias.reshape(2, units),
        grad_down,
        grad_gains,
        grad_shifts,
    )


def solution(mesh):
    fine = Mesh(mesh.devices.reshape(4, 2, 4, 2, 2), ("z", "xl", "y", "c", "h"))
    blk = ("z", "xl", "y", "c")
    return jax.shard_map(
        local,
        mesh=fine,
        in_specs=(
            P(blk, None),
            P(None, blk, None),
            P(blk),
            P(None, None, "h"),
            P(None, "h"),
            P("h", None),
            P(None, "h"),
            P("h"),
            P("h", None),
            P(),
            P(),
        ),
        out_specs=(
            P(blk, None),
            P(None, blk, None),
            P(None, None, None, "h"),
            P(None, None, "h"),
            P(None, "h", None),
            P(None, None, "h"),
            P(None, "h"),
            P(None, "h", None),
            P(),
            P(),
        ),
        check_vma=False,
    )
```

```python
import functools

import jax
import jax.numpy as jnp
from jax import lax
from jax.experimental import pallas as pl
from jax.experimental.pallas import tpu as pltpu
from jax.sharding import Mesh
from jax.sharding import PartitionSpec as P

HD = 64
LANES = 128
TILE = 64
BLOCK = 256
EPS = 1e-06
SCALE = 0.125
FAR = -1e30
BF = jnp.bfloat16
F32 = jnp.float32
MIB = 1024 * 1024
ROOM = 56

NT = (((1,), (1,)), ((), ()))
TN = (((0,), (0,)), ((), ()))


def shift_by(array, axis, step):
    size = lax.axis_size(axis)
    return lax.ppermute(array, axis, [(i, (i + step) % size) for i in range(size)])


def dot(a, b):
    return jnp.dot(a, b, preferred_element_type=F32)


def dot_nt(a, b):
    return lax.dot_general(a, b, NT, preferred_element_type=F32)


def dot_tn(a, b):
    return lax.dot_general(a, b, TN, preferred_element_type=F32)


def standard(field):
    center = field - jnp.mean(field, axis=-1, keepdims=True)
    factor = lax.rsqrt(jnp.mean(center * center, axis=-1, keepdims=True) + EPS)
    return center * factor, factor


def norm_back(grad, gain, xhat, factor):
    h = grad * gain
    mean = jnp.mean(h, axis=-1, keepdims=True)
    return factor * (h - mean - xhat * jnp.mean(h * xhat, axis=-1, keepdims=True))


def pieces(value):
    high = value.astype(BF)
    rest = value - high.astype(F32)
    middle = rest.astype(BF)
    low = (rest - middle.astype(F32)).astype(BF)
    return high, middle, low


def zero_one(mask):
    return jnp.where(mask, 1.0, 0.0).astype(BF)


def iota(shape, dim):
    return lax.broadcasted_iota(jnp.int32, shape, dim)


VMEM = pl.BlockSpec(memory_space=pltpu.VMEM)
ANY = pl.BlockSpec(memory_space=pl.ANY)
SMEM = pl.BlockSpec(memory_space=pltpu.SMEM)


def local_call(body, name, out, ins, outs, args, scratch=(), cost=None, room=16):
    return pl.pallas_call(
        body,
        out_shape=out,
        in_specs=ins,
        out_specs=outs,
        scratch_shapes=scratch,
        cost_estimate=cost,
        compiler_params=pltpu.CompilerParams(vmem_limit_bytes=room * MIB),
        name=name,
    )(*args)


def shaped(*shape, dtype=BF):
    return jax.ShapeDtypeStruct(shape, dtype)


def cost(micros):
    return pl.CostEstimate(flops=int(micros * 1e9), bytes_accessed=0, transcendentals=0)


def front_kernel(tokens, ids, told, copies, number):
    rows = told.shape[0] - 16
    marks = jnp.where(ids[...] == 0, 1.0, 0.0)
    tiles = jnp.sum(marks).astype(jnp.int32) // TILE
    number[0] = tiles
    told[:rows, :] = tokens[:rows, :]
    told[rows:, :] = jnp.full((16, told.shape[1]), tiles.astype(F32), F32).astype(BF)
    for g in range(copies.shape[0]):
        copies[g] = told[...]


def front(tokens, ids, copies):
    size, model = tokens.shape
    told = size - TILE + 16
    return local_call(
        front_kernel,
        "front",
        (shaped(told, model), shaped(copies, told, model), shaped(1, dtype=jnp.int32)),
        [VMEM, VMEM],
        (VMEM, VMEM, SMEM),
        (tokens, ids.reshape(-1, LANES)),
        room=ROOM,
    )


def prepare_kernel(
    heads, place, in_weights, in_biases, gains, shifts, up, down, bias,
    weights, biases, pairs, columns, out,
):
    core = place[0]
    half = out.shape[1]
    at = pl.ds(pl.multiple_of(core * half, half), half)
    out[:half, :] = up[:, at]
    out[half : 2 * half, :] = down[at, :]
    mine = jnp.where(core == 0, bias[:, :half], bias[:, half:])
    row = iota((16, half), 0)
    rows = jnp.zeros((16, half), F32)
    for i, piece in enumerate(pieces(mine)):
        rows = jnp.where(row == i, piece.astype(F32), rows)
    out[2 * half :, :] = rows.astype(BF)

    model, cols = in_weights.shape[1:]
    width = heads * LANES
    row, col = (iota((cols, width), d) for d in (0, 1))
    spread = zero_one((row // HD == col // LANES) & (row % HD == col % LANES))
    lane = iota((1, width), 1) % LANES
    gap = jnp.zeros((1, HD), F32)

    def apart(line):
        return jnp.concatenate(
            sum([[line[:, h * HD : (h + 1) * HD], gap] for h in range(heads)], []), axis=1
        )

    extra = [
        apart(in_biases[0:1, :] * SCALE) + jnp.where(lane == HD, 1.0, 0.0),
        jnp.where((lane > HD) & (lane < HD + 4), 1.0, 0.0),
        apart(in_biases[1:2, :]) + jnp.where((lane >= HD) & (lane < HD + 3), 1.0, 0.0),
    ]
    for i in range(3):
        factor = SCALE if i == 0 else 1.0
        weights[:, i * width : (i + 1) * width] = (dot(in_weights[i], spread) * factor).astype(BF)
        biases[:, i * width : (i + 1) * width] = extra[i]
        for pair in range(heads // 2):
            pairs[pair, :, i * LANES : (i + 1) * LANES] = in_weights[
                i, :, pair * LANES : (pair + 1) * LANES
            ]
    tall = jnp.concatenate(
        [gains[0:1, :], shifts[0:1, :], jnp.zeros((LANES - 2, model), F32)], axis=0
    )
    columns[...] = jnp.transpose(tall)


def prepare(core, in_weights, in_biases, gains, shifts, up, down, bias, heads):
    model = up.shape[0]
    width = 3 * heads * LANES
    return local_call(
        functools.partial(prepare_kernel, heads),
        "prepare",
        (
            shaped(model, width),
            shaped(1, width, dtype=F32),
            shaped(heads // 2, model, 3 * LANES),
            shaped(model, LANES, dtype=F32),
            shaped(2 * model + 16, model),
        ),
        [SMEM] + [VMEM] * 7,
        (VMEM,) * 5,
        (core, in_weights, in_biases, gains, shifts, up, down, bias),
        cost=cost(4),
        room=ROOM,
    )


def count_of(ref, rows):
    return jnp.max(ref[rows : rows + 16, :LANES].astype(F32)).astype(jnp.int32)


def rows_at(start, rows, step=TILE):
    return pl.ds(pl.multiple_of(start, step), rows)


def attend_kernel(rows, groups, heads, *refs):
    near, far = refs[:groups], refs[groups]
    weights, biases, gains, shifts = refs[groups + 1 : groups + 5]
    at = groups + 5 + groups // 2
    out, give = refs[groups + 5 : at], refs[at]
    kept, counts, place = refs[at + 1 : at + 6], refs[at + 6], refs[at + 7]
    (xq, xk, qx, kx, vx), sems = refs[at + 8 : at + 13], refs[at + 13]
    model = xq.shape[1]
    q_counts = [count_of(r, rows) for r in near]
    k_counts = [count_of(far.at[g], rows) for g in range(groups)]
    for g in range(groups):
        counts[g] = q_counts[g]
        counts[groups + g] = k_counts[g]

    def compact(numbers, read, target):
        start = jnp.int32(0)
        for g, n in enumerate(numbers):
            target[rows_at(start, rows), :] = read(g)
            start = start + n * TILE
        target[rows_at(start, BLOCK), :] = jnp.zeros((BLOCK, model), BF)
        return start

    q_total = compact(q_counts, lambda g: near[g][:rows, :], xq)
    k_total = compact(k_counts, lambda g: far[g, :rows, :], xk)
    q_blocks = (q_total + BLOCK - 1) // BLOCK
    k_blocks = (k_total + BLOCK - 1) // BLOCK
    width = heads * LANES

    def hidden(ref, here):
        clean = standard(ref[here, :].astype(F32))[0].astype(BF)
        ref[here, :] = clean
        return (clean.astype(F32) * gains[0:1, :] + shifts[0:1, :]).astype(BF)

    @pl.loop(0, q_blocks)
    def _(b):
        here = rows_at(b * BLOCK, BLOCK, BLOCK)
        q = (dot(hidden(xq, here), weights[:, :width]) + biases[:, :width]).astype(BF)
        for h in range(heads):
            qx[h, here, :] = q[:, h * LANES : (h + 1) * LANES]

    @pl.loop(0, k_blocks)
    def _(b):
        here = rows_at(b * BLOCK, BLOCK, BLOCK)
        both = dot(hidden(xk, here), weights[:, width:]) + biases[:, width:]
        unseen = (iota((BLOCK, width), 0) + b * BLOCK >= k_total) & (
            iota((BLOCK, width), 1) % LANES == HD
        )
        k = jnp.where(unseen, FAR, both[:, :width]).astype(BF)
        v = both[:, width:].astype(BF)
        for h in range(heads):
            kx[h, here, :] = k[:, h * LANES : (h + 1) * LANES]
            vx[h, here, :] = v[:, h * LANES : (h + 1) * LANES]

    copies = [
        pltpu.make_async_copy(held, to, sems.at[i])
        for i, (held, to) in enumerate(zip((xq, xk, qx, kx, vx), kept))
    ]
    for copy in copies:
        copy.start()

    def attend_all(span):
        @pl.loop(0, q_blocks)
        def _(b):
            here = rows_at(b * BLOCK, BLOCK, BLOCK)
            lane = iota((BLOCK, LANES), 1)
            for h in range(heads):
                s = dot_nt(qx[h, here, :], kx[h, :span, :])
                top = jnp.max(s, axis=-1, keepdims=True)
                o = dot(jnp.exp(s - top).astype(BF), vx[h, :span, :])
                total = o[:, HD : HD + 1]
                o = o / total
                for i, piece in enumerate(pieces(top + jnp.log(total))):
                    o = jnp.where(lane == HD + i, piece.astype(F32), o)
                place[h, here, :] = o.astype(BF)

    for blocks in range(groups * TILE // BLOCK, groups * rows // BLOCK + 1):
        pl.when(k_blocks == blocks)(functools.partial(attend_all, blocks * BLOCK))

    gather = [
        (iota((LANES, LANES), 0) - HD + 3 * h == iota((LANES, LANES), 1))
        & (iota((LANES, LANES), 0) >= HD)
        & (iota((LANES, LANES), 0) < HD + 3)
        for h in range(heads)
    ]
    gather = [jnp.where(m, 1.0, 0.0).astype(BF) for m in gather]
    start = jnp.int32(0)
    for g in range(groups):
        mine = [place[h, rows_at(start, rows), :] for h in range(heads)]
        stats = sum(dot(m, s) for m, s in zip(mine, gather)).astype(BF)
        value = jnp.concatenate([m[:, :HD] for m in mine] + [stats], axis=1)
        if g < groups // 2:
            out[g][...] = value
        else:
            give[g - groups // 2] = value
        start = start + q_counts[g] * TILE
    for copy in copies:
        copy.wait()


def attend(near, far, weights, biases, gains, shifts, rows, heads):
    groups = len(near)
    model = near[0].shape[1]
    room = rows * groups + BLOCK
    parts = heads * HD + LANES
    kept = [(room, model)] * 2 + [(heads, room, LANES)] * 3
    return local_call(
        functools.partial(attend_kernel, rows, groups, heads),
        "attend",
        (
            *[shaped(rows, parts)] * (groups // 2),
            shaped(groups // 2, rows, parts),
            *[shaped(*k) for k in kept],
            shaped(2 * groups, dtype=jnp.int32),
        ),
        [VMEM] * (groups + 5),
        (*[VMEM] * (groups // 2 + 1), *[ANY] * 5, SMEM),
        (*near, far, weights, biases, gains, shifts),
        [
            pltpu.VMEM((heads, room, LANES), BF),
            *[pltpu.VMEM(k, BF) for k in kept],
            pltpu.SemaphoreType.DMA((5,)),
        ],
        cost(15),
        ROOM,
    )


def same_tile(rows):
    return iota((rows, rows), 0) // TILE == iota((rows, rows), 1) // TILE


def thumb_kernel(heads, tokens, weights, biases, gains, shifts, out, xhat, x):
    width = heads * LANES
    size = tokens.shape[0]
    clean = standard(tokens[...].astype(F32))[0].astype(BF)
    xhat[...] = clean
    hidden = (clean.astype(F32) * gains[0:1, :] + shifts[0:1, :]).astype(BF)
    x[...] = (dot(hidden, weights[...]) + biases[...]).astype(BF)
    visible = same_tile(size - TILE)
    out[:TILE, :] = jnp.zeros((TILE, heads * HD), F32)
    for h in range(heads):
        q = x[TILE:, h * LANES : (h + 1) * LANES]
        k = x[TILE:, width + h * LANES : width + (h + 1) * LANES]
        v = x[TILE:, 2 * width + h * LANES : 2 * width + (h + 1) * LANES]
        s = jnp.where(visible, dot_nt(q, k), FAR)
        e = jnp.exp(s - jnp.max(s, axis=-1, keepdims=True))
        o = dot(e.astype(BF), v)[:, :HD] / jnp.sum(e, axis=-1, keepdims=True)
        out[TILE:, h * HD : (h + 1) * HD] = o


def thumbs(tokens, weights, biases, gains, shifts, heads):
    size, model = tokens.shape
    return local_call(
        functools.partial(thumb_kernel, heads),
        "thumbs",
        (
            shaped(size, heads * HD, dtype=F32),
            shaped(size, model),
            shaped(size, 3 * heads * LANES),
        ),
        [VMEM] * 5,
        (VMEM,) * 3,
        (tokens, weights, biases, gains, shifts),
        cost=cost(5),
    )


def merged(parts, heads):
    cols = heads * HD
    row, col = (iota((LANES, cols), d) for d in (0, 1))
    spread = zero_one(row // 3 == col // HD)
    marks = [dot(p[:, cols:], spread) for p in parts]
    top = functools.reduce(jnp.maximum, marks)
    expos = [jnp.exp(m - top) for m in marks]
    total = sum(expos)
    mixed = sum(e * p[:, :cols].astype(F32) for p, e in zip(parts, expos)) / total
    row, col = (iota((cols, LANES), d) for d in (0, 1))
    packed = [
        dot(piece, zero_one((row % HD == 0) & (col == 3 * (row // HD) + i)))
        for i, piece in enumerate(pieces(top + jnp.log(total)))
    ]
    return mixed, sum(packed)


def pair_kernel(heads, *refs):
    count = (len(refs) - 1) // 2
    for j, (mine, out) in enumerate(zip(refs[:count], refs[count + 1 :])):
        mixed, marks = merged([mine[...], refs[count][j]], heads)
        out[...] = jnp.concatenate([mixed.astype(BF), marks.astype(BF)], axis=1)


def pair_merge(parts, other, heads):
    return local_call(
        functools.partial(pair_kernel, heads),
        "pair_merge",
        tuple(shaped(*p.shape) for p in parts),
        [VMEM] * (len(parts) + 1),
        (VMEM,) * len(parts),
        (*parts, other),
        cost=cost(3),
        room=ROOM,
    )


def merge_kernel(heads, counts, thumb, *refs):
    parts, (low, full, lse) = refs[:-3], refs[-3:]
    cols = heads * HD
    rows = lse.shape[0]
    mixed, marks = merged([p[...] for p in parts], heads)
    lse[...] = (-marks).astype(BF)
    image = iota((rows, cols), 0) < counts[0] * TILE
    full[:rows, :] = jnp.where(image, mixed, thumb[:rows, :])
    full[rows:, :] = thumb[rows:, :]
    low[...] = full[...].astype(BF)


def merge(count, parts, thumb, heads):
    size, cols = thumb.shape
    return local_call(
        functools.partial(merge_kernel, heads),
        "merge",
        (shaped(size, cols), shaped(size, cols, dtype=F32), shaped(parts[0].shape[0], LANES)),
        [SMEM] + [VMEM] * (1 + len(parts)),
        (VMEM,) * 3,
        (count, thumb, *parts),
        cost=cost(3),
    )


def fold_kernel(*refs):
    count = (len(refs) - 1) // 2
    for j, (mine, out) in enumerate(zip(refs[:count], refs[count + 1 :])):
        out[...] = (mine[...].astype(F32) + refs[count][j].astype(F32)).astype(BF)


def fold(parts, other):
    return local_call(
        fold_kernel,
        "fold",
        tuple(shaped(*p.shape) for p in parts),
        [VMEM] * (len(parts) + 1),
        (VMEM,) * len(parts),
        (*parts, other),
        cost=cost(2),
        room=ROOM,
    )


ROOT = 0.7978845608028654
CUBE = 0.044715


def ff_kernel(
    heads, tokens, outer, low, low_far, full, lse, out_weight, out_far, up, up_bias, down, far_one,
    far_two, gains, shifts, mixed, grad_mid, grad_low, packed, hidden_out, act_out, pre_out, small,
):
    size, model = tokens.shape
    passes = outer.shape[0]
    cols = heads * HD
    chunk = far_one.shape[1]
    units = up.shape[1]
    rows = packed.shape[0]
    branch = dot(low[...], out_weight[...]) + dot(low_far[...], out_far[...])
    middle = tokens[...].astype(F32) + (branch + shifts[1:2, :])
    xhat, factor = standard(middle)
    hidden = (xhat * gains[1:2, :] + shifts[2:3, :]).astype(BF)
    hidden_out[...] = hidden

    def one_chunk(up_part, bias, down_part, keep):
        v = dot(hidden, up_part) + bias
        t = jnp.tanh(ROOT * (v + CUBE * (v * v * v)))
        act = (0.5 * v * (1.0 + t)).astype(BF)
        slope = 0.5 * (1.0 + t) + 0.5 * v * (1.0 - t * t) * (ROOT * (1.0 + 3.0 * CUBE * (v * v)))
        two = []
        for p in range(passes):
            pre = (dot_nt(outer[p], down_part) * slope).astype(BF)
            if keep is not None:
                pre_out[p, :, keep] = pre
            two.append(dot_nt(pre, up_part))
        if keep is not None:
            act_out[:, keep] = act
        return dot(act, down_part), two

    def far_chunk(ref):
        told = ref[2 * chunk : 2 * chunk + 16, :].astype(F32)
        bias = told[0:1] + told[1:2] + told[2:3]
        return one_chunk(ref[:chunk, :], bias, ref[chunk : 2 * chunk, :], None)

    done = []
    for i in range(units // chunk):
        at = slice(i * chunk, (i + 1) * chunk)
        done.append(one_chunk(up[:, at], up_bias[:, at], down[at, :], at))
    done += [far_chunk(far_one), far_chunk(far_two)]

    def tree(parts):
        half = len(parts) // 2
        return sum(parts[:half]) + sum(parts[half:])

    output = tree([d[0] for d in done])
    mixed[...] = (middle + (output + shifts[3:4, :])).astype(BF)
    small[...] = jnp.zeros(small.shape, F32)
    lane = iota((rows, LANES), 1)
    stats = jnp.zeros((rows, LANES), F32)
    for p in range(passes):
        two = tree([d[1][p] for d in done])
        c = outer[p].astype(F32)
        mid = c + norm_back(two, gains[1:2, :], xhat, factor)
        mid_low = mid.astype(BF)
        grad_mid[p] = mid
        grad_low[p] = mid_low
        att = dot_nt(mid_low, out_weight[...]).astype(BF)
        packed[:, p * cols : (p + 1) * cols] = att[:rows, :]
        pre_out_p = pre_out[p].astype(F32)
        bias = jnp.sum(pre_out_p, axis=0, keepdims=True)
        small[p, 0:1, :] = jnp.sum(two * xhat, axis=0, keepdims=True)
        small[p, 1:2, :] = jnp.sum(two, axis=0, keepdims=True)
        small[p, 2:3, :] = jnp.sum(mid_low.astype(F32), axis=0, keepdims=True)
        small[p, 3:4, :] = jnp.sum(c, axis=0, keepdims=True)
        for i in range(units // model):
            small[p, 4 + i : 5 + i, :] = bias[:, i * model : (i + 1) * model]
        product = att[:rows, :].astype(F32) * full[:rows, :]
        for h in range(heads):
            delta = jnp.sum(product[:, h * HD : (h + 1) * HD], axis=-1, keepdims=True)
            for i, piece in enumerate(pieces(-delta)):
                stats = jnp.where(lane == 3 * heads * (p + 1) + 3 * h + i, piece.astype(F32), stats)
    packed[:, passes * cols :] = (stats + lse[...].astype(F32)).astype(BF)


def feed_forward(
    tokens, outer, low, low_far, full, lse, out_weight, out_far, up, up_bias, down, far_one, far_two,
    gains, shifts, rows, heads,
):
    size, model = tokens.shape
    passes = outer.shape[0]
    units = up.shape[1]
    return local_call(
        functools.partial(ff_kernel, heads),
        "feed_forward",
        (
            shaped(size, model),
            shaped(passes, size, model, dtype=F32),
            shaped(passes, size, model),
            shaped(rows, passes * heads * HD + LANES),
            shaped(size, model),
            shaped(size, units),
            shaped(passes, size, units),
            shaped(passes, 8, model, dtype=F32),
        ),
        [VMEM] * 15,
        (VMEM,) * 8,
        (
            tokens, outer, low, low_far, full, lse, out_weight, out_far, up, up_bias, down, far_one,
            far_two, gains, shifts,
        ),
        cost=cost(12),
        room=32,
    )


def thumb_back_kernel(heads, counts, x, mid_low, out_weight, out):
    width = heads * LANES
    size = x.shape[0]
    passes = mid_low.shape[0]
    visible = same_tile(size - TILE)
    outside = iota((size - TILE, HD), 0) + TILE >= counts[0] * TILE
    grads = [dot_nt(mid_low[p], out_weight[...]).astype(BF) for p in range(passes)]
    out[:, :, :TILE, :] = jnp.zeros((*out.shape[:2], TILE, out.shape[3]), BF)
    for h in range(heads):
        q = x[TILE:, h * LANES : (h + 1) * LANES]
        k = x[TILE:, width + h * LANES : width + (h + 1) * LANES]
        v = x[TILE:, 2 * width + h * LANES : 2 * width + h * LANES + HD]
        s = jnp.where(visible, dot_nt(q, k), FAR)
        e = jnp.exp(s - jnp.max(s, axis=-1, keepdims=True))
        w = e / jnp.sum(e, axis=-1, keepdims=True)
        w_low = w.astype(BF)
        for p in range(passes):
            g = grads[p][TILE:, h * HD : (h + 1) * HD]
            gw = dot_nt(g, v)
            ds = (w * (gw - jnp.sum(w * gw, axis=-1, keepdims=True))).astype(BF)
            dq = dot(ds, k[:, :HD]) * SCALE
            dk = dot_tn(ds, q)[:, :HD]
            dv = dot_tn(w_low, g)
            for c, piece in enumerate((dq, dk, dv)):
                at = c * LANES + (h % 2) * HD
                out[h // 2, p, TILE:, at : at + HD] = jnp.where(outside, piece, 0.0).astype(BF)


def thumbs_back(count, x, mid_low, out_weight, heads):
    passes, size, _ = mid_low.shape
    return local_call(
        functools.partial(thumb_back_kernel, heads),
        "thumbs_back",
        shaped(heads // 2, passes, size, 3 * LANES),
        [SMEM] + [VMEM] * 3,
        VMEM,
        (count, x, mid_low, out_weight),
        cost=cost(6),
    )


def early_at(units, model, low):
    ends = [model, 2 * model, 2 * model + units, 2 * model + units + low]
    return [slice(b - w, b) for b, w in zip(ends, (model, model, units, low))]


def early_cuts(parts, units, model, low):
    high, wide, turns = units // parts // 2, model // parts, model // low
    narrow = low * turns // parts
    for i in range(parts):
        yield (
            (slice(2 * i * high, (2 * i + 1) * high), slice(0, model)),
            (slice((2 * i + 1) * high, (2 * i + 2) * high), slice(0, model)),
            (slice(i * wide, (i + 1) * wide), slice(0, units)),
            (
                slice(i // turns * narrow, (i // turns + 1) * narrow),
                slice(i % turns * low, (i % turns + 1) * low),
            ),
        )


def weight_kernel(place, act, outer, hidden, pre, low, mid_low, keep, give):
    units, model, cols = act.shape[1], hidden.shape[1], low.shape[1]
    core = place[0]
    for turn, out in ((core, keep), (1 - core, give)):
        down = dot_tn(act[...], outer[turn]).astype(BF)
        up = dot_tn(hidden[...], pre[turn]).astype(BF)
        proj = dot_tn(low[...], mid_low[turn]).astype(BF)
        for i, cut in enumerate(early_cuts(keep.shape[0], units, model, cols)):
            for value, (rows, lanes), at in zip(
                (down, down, up, proj), cut, early_at(units, model, cols)
            ):
                out[i, :, at] = value[rows, lanes]


def weight_grads(core, act, outer, hidden, pre, low, mid_low, parts):
    units, model = act.shape[1], outer.shape[2]
    out = shaped(parts, model // parts, 2 * model + units + low.shape[1])
    return local_call(
        weight_kernel,
        "weight_grads",
        (out, out),
        [SMEM] + [VMEM] * 6,
        (VMEM,) * 2,
        (core, act, outer, hidden, pre, low, mid_low),
        cost=cost(8),
        room=24,
    )


def reverse_kernel(rows, groups, heads, passes, counts, place, *refs):
    grads, kept = refs[:groups], refs[groups : groups + 5]
    own, thumb, weights, columns, small = refs[groups + 5 : groups + 10]
    at = groups + 10
    out_q, give_q, at = refs[at : at + groups // 2], refs[at + groups // 2], at + groups // 2 + 1
    out_kv, at = refs[at : at + groups // 2], at + groups // 2
    keep, give = refs[at : at + 2]
    (
        stage, xq, xk, qx, kx, vx, packed, gx, kt, dq_t, dv, dk, low_q, low_kv, total, sums,
        starts, sems,
    ) = refs[at + 2 :]
    couples = heads // 2
    sources = [*grads, *kept[2:], *kept[:2]]
    targets = [*[stage.at[g] for g in range(groups)], qx, kx, vx, xq, xk]
    copies = [
        pltpu.make_async_copy(f, t, sems.at[i]) for i, (f, t) in enumerate(zip(sources, targets))
    ]
    for copy in copies:
        copy.start()
    cols = heads * HD
    wide = passes * LANES
    q_counts = [counts[g] for g in range(groups)]
    k_counts = [counts[groups + g] for g in range(groups)]
    start = jnp.int32(0)
    for g in range(groups):
        copies[g].wait()
        packed[rows_at(start, rows), :] = stage[g]
        start = start + q_counts[g] * TILE
    q_total, k_total = start, sum(k_counts) * TILE
    tail_lane = iota((BLOCK, packed.shape[1]), 1) - passes * cols
    empty = (tail_lane >= 0) & (tail_lane < 3 * heads) & (tail_lane % 3 == 0)
    packed[rows_at(q_total, BLOCK), :] = jnp.where(empty, FAR, 0.0).astype(BF)
    q_blocks = (q_total + BLOCK - 1) // BLOCK
    k_blocks = (k_total + BLOCK - 1) // BLOCK
    spans = range(groups * TILE // BLOCK, groups * rows // BLOCK + 1)

    row, col = (iota((LANES, heads * LANES), d) for d in (0, 1))
    head, lane = col // LANES, col % LANES
    to_marks = zero_one((lane > HD) & (lane < HD + 4) & (row == 3 * head + lane - HD - 1))
    row, col = (iota((LANES, heads * wide), d) for d in (0, 1))
    head, turn, lane = col // wide, col % wide // LANES, col % LANES
    to_deltas = zero_one(
        (lane >= HD) & (lane < HD + 3) & (row == 3 * heads * (turn + 1) + 3 * head + lane - HD)
    )
    for copy in copies[groups : groups + 3]:
        copy.wait()

    @pl.loop(0, q_blocks)
    def _(b):
        here = rows_at(b * BLOCK, BLOCK, BLOCK)
        stats = packed[here, passes * cols :]
        marks = dot(stats, to_marks)
        deltas = dot(stats, to_deltas).astype(BF)
        for h in range(heads):
            more = marks[:, h * LANES : (h + 1) * LANES]
            qx[h, here, :] = (qx[h, here, :].astype(F32) + more).astype(BF)
            for p in range(passes):
                at = p * cols + h * HD
                mine = (h * passes + p) * LANES
                gx[h, here, p * LANES : (p + 1) * LANES] = jnp.concatenate(
                    [packed[here, at : at + HD], deltas[:, mine + HD : mine + LANES]], axis=1
                )

    @pl.loop(0, k_blocks)
    def _(b):
        here = rows_at(b * BLOCK, BLOCK, BLOCK)
        for h in range(heads):
            kt[h, b] = jnp.transpose(kx[h, here, :].astype(F32))[:HD, :].astype(BF)

    def reverse_all(blocks):
        span = blocks * BLOCK

        @pl.loop(0, couples)
        def _(pair):
            dv[:, :span, :] = jnp.zeros((2, span, wide), F32)
            dk[:, :, :span, :] = jnp.zeros((passes, 2, span, LANES), F32)

            @pl.loop(0, q_blocks)
            def _(b):
                here = rows_at(b * BLOCK, BLOCK, BLOCK)
                for i in range(2):
                    h = 2 * pair + i
                    q, g = qx[h, here, :], gx[h, here, :]
                    k_t = jnp.concatenate([kt[h, j] for j in range(blocks)], axis=1)
                    w = jnp.exp(dot_nt(kx[h, :span, :], q))
                    dv[i, :span, :] += dot(w.astype(BF), g)
                    for p in range(passes):
                        ds = dot_nt(vx[h, :span, :], g[:, p * LANES : (p + 1) * LANES])
                        ds = (w * ds).astype(BF)
                        dk[p, i, :span, :] += dot(ds, q)
                        dq_t[p, i * HD : (i + 1) * HD, :] = dot(k_t, ds)
                for p in range(passes):
                    piece = jnp.transpose(dq_t[p]) * SCALE
                    low_q[pair, here, p * LANES : (p + 1) * LANES] = piece.astype(BF)

            for p in range(passes):
                for c, both in enumerate(
                    (
                        [dk[p, i, :span, :HD] for i in range(2)],
                        [dv[i, :span, p * LANES : p * LANES + HD] for i in range(2)],
                    )
                ):
                    lane = (2 * p + c) * LANES
                    low_kv[pair, :span, lane : lane + LANES] = jnp.concatenate(both, axis=1).astype(BF)

    for blocks in spans:
        pl.when(k_blocks == blocks)(functools.partial(reverse_all, blocks))

    start = jnp.int32(0)
    for g in range(groups):
        starts[g] = start
        start = start + k_counts[g] * TILE
    for g in range(groups):
        here = rows_at(starts[place[1 + g]], rows)
        out_kv[g // 2][g % 2] = jnp.concatenate([low_kv[i, here, :] for i in range(couples)], axis=1)
    start = jnp.int32(0)
    for g in range(groups):
        here = rows_at(start, rows)
        value = jnp.concatenate([low_q[i, here, :] for i in range(couples)], axis=1)
        if g < groups // 2:
            out_q[g][...] = value
        else:
            give_q[g - groups // 2] = value
        start = start + q_counts[g] * TILE

    copies[groups + 3].wait()
    copies[groups + 4].wait()

    def key_sums(blocks):
        span = blocks * BLOCK
        for i in range(couples):
            flat = low_kv[i, :span, :]
            total[i, :, wide:] = dot_tn(xk[:span, :], flat)
            sums[i, :, wide:] = dot(jnp.ones((8, span), BF), flat)

    for blocks in spans:
        pl.when(k_blocks == blocks)(functools.partial(key_sums, blocks))

    total[:, :, :wide] = jnp.zeros((couples, total.shape[1], wide), F32)
    sums[:, :, :wide] = jnp.zeros((couples, 8, wide), F32)

    @pl.loop(0, q_blocks)
    def _(b):
        here = rows_at(b * BLOCK, BLOCK, BLOCK)
        for i in range(couples):
            total[i, :, :wide] += dot_tn(xq[here, :], low_q[i, here, :])
            sums[i, :, :wide] += dot(jnp.ones((8, BLOCK), BF), low_q[i, here, :])

    model = total.shape[1]
    gain, shift = columns[:, 0:1], columns[:, 1:2]
    ones = jnp.ones((8, own.shape[0]), BF)
    for p in range(passes):
        whole = []
        for i in range(couples):
            mine = thumb[i, p]
            part = dot_tn(own[...], mine)
            part_sum = dot(ones, mine)[0:1, :]
            q_at = slice(p * LANES, (p + 1) * LANES)
            kv_at = slice((passes + 2 * p) * LANES, (passes + 2 * p + 2) * LANES)
            part += jnp.concatenate([total[i, :, q_at], total[i, :, kv_at]], axis=1)
            part_sum += jnp.concatenate([sums[i, 0:1, q_at], sums[i, 0:1, kv_at]], axis=1)
            w = weights[i].astype(F32)
            gain_one = jnp.sum(w * part, axis=1, keepdims=True)
            shift_one = jnp.sum(w * part_sum, axis=1, keepdims=True)
            lane = iota((model, LANES), 1)
            tall = jnp.where(lane == 0, gain_one, jnp.where(lane == 1, shift_one, 0.0))
            flat = jnp.concatenate(
                [jnp.zeros((2, LANES), F32)]
                + [part_sum[:, c * LANES : (c + 1) * LANES] for c in range(3)]
                + [jnp.zeros((LANES - 5, LANES), F32)],
                axis=0,
            )
            tall = jnp.concatenate([tall[:LANES] + jnp.transpose(flat), tall[LANES:]], axis=0)
            if i == 0:
                turned = jnp.concatenate(
                    [
                        jnp.zeros((8, model), F32),
                        small[p],
                        jnp.zeros((LANES - 16, model), F32),
                    ],
                    axis=0,
                )
                tall = tall + jnp.transpose(turned)
            whole += [part * gain + shift * part_sum, tall]
        whole = jnp.concatenate(whole, axis=1).astype(BF)

        @pl.when(place[0] == p)
        def _():
            keep[...] = whole

        @pl.when(place[0] != p)
        def _():
            give[...] = whole


def reverse(counts, place, grads, kept, own, thumb, weights, columns, small, rows, heads):
    groups = len(grads)
    couples, passes = thumb.shape[:2]
    model = own.shape[1]
    room = rows * groups + BLOCK
    cols = heads * HD
    wide = passes * LANES
    half = groups // 2
    late = shaped(model, couples * 4 * LANES)
    q, kv = shaped(rows, couples * wide), shaped(2, rows, couples * 2 * wide)
    out = (*[q] * half, shaped(half, rows, couples * wide), *[kv] * half, late, late)
    return local_call(
        functools.partial(reverse_kernel, rows, groups, heads, passes),
        "reverse",
        out,
        [SMEM, SMEM] + [ANY] * (groups + 5) + [VMEM] * 5,
        (VMEM,) * len(out),
        (counts, place, *grads, *kept, own, thumb, weights, columns, small),
        [
            pltpu.VMEM((groups, rows, passes * cols + LANES), BF),
            pltpu.VMEM((room, model), BF),
            pltpu.VMEM((room, model), BF),
            pltpu.VMEM((heads, room, LANES), BF),
            pltpu.VMEM((heads, room, LANES), BF),
            pltpu.VMEM((heads, room, LANES), BF),
            pltpu.VMEM((room, passes * cols + LANES), BF),
            pltpu.VMEM((heads, room, wide), BF),
            pltpu.VMEM((heads, room // BLOCK, HD, BLOCK), BF),
            pltpu.VMEM((passes, LANES, BLOCK), F32),
            pltpu.VMEM((2, room, wide), F32),
            pltpu.VMEM((passes, 2, room, LANES), F32),
            pltpu.VMEM((couples, room, wide), BF),
            pltpu.VMEM((couples, room, 2 * wide), BF),
            pltpu.VMEM((couples, model, 3 * wide), F32),
            pltpu.VMEM((couples, 8, 3 * wide), F32),
            pltpu.SMEM((groups,), jnp.int32),
            pltpu.SemaphoreType.DMA((groups + 5,)),
        ],
        cost(45),
        ROOM,
    )


def grad_one_kernel(near, counts, *refs):
    from_q, from_kv, (thumb, weights, mine, other) = refs[:near], refs[near:-4], refs[-4:]
    couples, passes, size, _ = thumb.shape
    rows = from_q[0].shape[0]
    sum_q = sum(r[...].astype(F32) for r in from_q)
    sum_kv = [sum(r[f].astype(F32) for r in from_kv) for f in range(2)]
    image = iota((rows, 3 * LANES), 0) < counts[0] * TILE
    for p in range(passes):
        parts = []
        for i in range(couples):
            at = (passes * i + p) * LANES
            there = slice(2 * at, 2 * at + 2 * LANES)
            far = jnp.concatenate([sum_q[:, at : at + LANES], sum_kv[0][:, there]], axis=1)
            flat = jnp.concatenate(
                [jnp.where(image, far.astype(BF), thumb[i, p, :rows]), thumb[i, p, rows:]], axis=0
            )
            parts.append(
                (
                    dot_nt(flat, weights[i]),
                    dot_nt(sum_kv[1][:, there].astype(BF), weights[i, :, LANES:]),
                )
            )
        mine[p] = sum(a for a, _ in parts).astype(BF)
        other[p] = sum(b for _, b in parts).astype(BF)


def grad_one(count, from_q, from_kv, thumb, weights):
    near = len(from_q)
    passes, size, _ = thumb.shape[1:]
    model = weights.shape[1]
    return local_call(
        functools.partial(grad_one_kernel, near),
        "grad_one",
        (shaped(passes, size, model), shaped(passes, from_q[0].shape[0], model)),
        [SMEM] + [VMEM] * (near + len(from_kv) + 2),
        (VMEM,) * 2,
        (count, *from_q, *from_kv, thumb, weights),
        cost=cost(5),
        room=ROOM,
    )


def close_kernel(counts, tokens, mid, mine, head, side, cross, gains, out):
    xhat, factor = standard(tokens[...].astype(F32))
    rows = side.shape[1]
    image = iota(side.shape[1:], 0) < counts[0] * TILE
    for p in range(mid.shape[0]):
        grad = mine[p].astype(F32) + head[p].astype(F32)
        more = jnp.where(image, side[p].astype(F32) + cross[p].astype(F32), 0.0)
        grad = jnp.concatenate([grad[:rows] + more, grad[rows:]], axis=0)
        out[p] = mid[p] + norm_back(grad, gains[0:1, :], xhat, factor)


def close(count, tokens, mid, mine, head, side, cross, gains):
    return local_call(
        close_kernel,
        "close",
        shaped(*mid.shape, dtype=F32),
        [SMEM] + [VMEM] * 7,
        VMEM,
        (count, tokens, mid, mine, head, side, cross, gains),
        cost=cost(4),
        room=ROOM,
    )


def early_kernel(lines, far, place, *refs):
    parts, refs = refs[:lines], refs[lines:]
    out, (down, up, proj, sems) = refs[-7:-4], refs[-4:]
    turn, y = place[0], place[10]
    turn = 1 - turn if far else turn
    (units, model), low = down.shape, proj.shape[0]
    steps, rows = parts[0].shape[:2]
    lane_down, lane_next, lane_up, lane_proj = early_at(units, model, low)
    turns = model // low
    for d, ref in enumerate(parts):
        for j in range(steps):
            i = j * lines + (y + lines - d) % lines
            at = pl.multiple_of(2 * rows * i, 2 * rows)
            down[pl.ds(at, rows), :] = ref[j, :, lane_down].astype(F32)
            down[pl.ds(at + rows, rows), :] = ref[j, :, lane_next].astype(F32)
            up[rows_at(rows * i, rows, rows), :] = ref[j, :, lane_up].astype(F32)
            here = rows_at(i // turns * rows, rows, rows)
            value = ref[j, :, lane_proj].astype(F32)
            for t in range(turns):

                @pl.when(i % turns == t)
                def _(value=value, here=here, t=t):
                    proj[here, t * low : (t + 1) * low] = value

    copies = [
        pltpu.make_async_copy(held, to.at[turn], sems.at[n])
        for n, (held, to) in enumerate(zip((down, up, proj), out))
    ]
    for copy in copies:
        copy.start()
    for copy in copies:
        copy.wait()


def early_out(place, parts, before, units, low):
    model = len(parts) * parts[0].shape[0] * parts[0].shape[1]
    shapes = (units, model), (model, units), (low, model)
    return pl.pallas_call(
        functools.partial(early_kernel, len(parts), bool(before)),
        out_shape=tuple(shaped(2, *s, dtype=F32) for s in shapes),
        in_specs=[SMEM] + [VMEM] * len(parts) + [ANY] * len(before),
        out_specs=(ANY,) * 3,
        scratch_shapes=[
            *[pltpu.VMEM(s, F32) for s in shapes],
            pltpu.SemaphoreType.DMA((3,)),
        ],
        input_output_aliases={1 + len(parts) + i: i for i in range(len(before))},
        cost_estimate=cost(5),
        compiler_params=pltpu.CompilerParams(vmem_limit_bytes=ROOM * MIB),
        name="early_far" if before else "early_own",
    )(place, *parts, *before)


def late_kernel(far, place, ref, *refs):
    out, (grad_in, *small), sems = refs[-11:-6], refs[-6:-1], refs[-1]
    in_bias, up_bias, gains, shifts = small
    turn = 1 - place[0] if far else place[0]
    turned = []
    for pair in range(2):
        at = 4 * LANES * pair
        for c in range(3):
            grad_in[c, :, pair * LANES : (pair + 1) * LANES] = ref[
                :, at + c * LANES : at + (c + 1) * LANES
            ].astype(F32)
        turned.append(jnp.transpose(ref[:, at + 3 * LANES : at + 4 * LANES].astype(F32)))
    a, b = turned
    in_bias[...] = jnp.concatenate(
        [
            jnp.concatenate([a[2:3, :LANES], b[2:3, :LANES]], axis=1),
            jnp.concatenate([a[4:5, :LANES], b[4:5, :LANES]], axis=1),
        ],
        axis=0,
    )
    up_bias[...] = jnp.concatenate([a[12:13], a[13:14]], axis=1)
    gains[...] = jnp.concatenate([a[0:1] + b[0:1], a[8:9]], axis=0)
    shifts[...] = jnp.concatenate([a[1:2] + b[1:2], a[10:11], a[9:10], a[11:12]], axis=0)
    copies = [
        pltpu.make_async_copy(held, to.at[turn], sems.at[n])
        for n, (held, to) in enumerate(zip((grad_in, *small), out))
    ]
    for copy in copies:
        copy.start()
    for copy in copies:
        copy.wait()


def late_out(place, part, before, units):
    model = part.shape[0]
    shapes = (3, model, 2 * LANES), (2, 2 * LANES), (1, units), (2, model), (4, model)
    return pl.pallas_call(
        functools.partial(late_kernel, bool(before)),
        out_shape=tuple(shaped(2, *s, dtype=F32) for s in shapes),
        in_specs=[SMEM, VMEM] + [ANY] * len(before),
        out_specs=(ANY,) * 5,
        scratch_shapes=[
            *[pltpu.VMEM(s, F32) for s in shapes],
            pltpu.SemaphoreType.DMA((5,)),
        ],
        input_output_aliases={2 + i: i for i in range(len(before))},
        cost_estimate=cost(3),
        compiler_params=pltpu.CompilerParams(vmem_limit_bytes=ROOM * MIB),
        name="late_far" if before else "late_own",
    )(place, part, *before)


def gather_near(array):
    mine = [array] + [shift_by(array, "y", d) for d in range(1, lax.axis_size("y"))]
    return mine + [shift_by(a, "c", 1) for a in mine]


def return_near(parts):
    return [parts[0]] + [shift_by(p, "y", -j) for j, p in enumerate(parts) if j > 0]


def offsets(size):
    return [(step, flip) for step in range(size) for flip in range(2)]


def return_far(parts):
    return [parts[0]] + [shift_by(p, "z", step) for step, p in enumerate(parts) if step > 0]


PLANE = ("z", "y")


def core_sum(keep, give):
    return (keep.astype(F32) + shift_by(give, "c", 1).astype(F32)).astype(BF)


def crossed(array):
    n = lax.axis_size(("xl", "h"))
    return lax.ppermute(array, ("xl", "h"), [(i, n - 1 - i) for i in range(n)])


def across(low):
    done = low.astype(F32) + shift_by(low, "xl", 1).astype(F32)
    size = 4 * LANES
    ones = jnp.concatenate([low[:, i + 3 * LANES : i + size] for i in range(0, low.shape[1], size)], axis=1)
    more = shift_by(ones, "h", 1).astype(F32) + crossed(ones).astype(F32)
    more = jnp.where(jnp.arange(more.shape[1]) % LANES < 2, more, 0.0)
    nothing = jnp.zeros((low.shape[0], 3 * LANES), F32)
    laid = [[nothing, more[:, i : i + LANES]] for i in range(0, more.shape[1], LANES)]
    return (done + jnp.concatenate(sum(laid, []), axis=1)).astype(BF)


def tied(arrays, others):
    return lax.optimization_barrier((arrays, others))


def local(
    tokens,
    cotangents,
    segment_ids,
    in_weights,
    in_biases,
    out_weight,
    up_weight,
    up_biases,
    down_weight,
    gains,
    shifts,
):
    size, model = tokens.shape
    cols = in_weights.shape[2]
    heads = cols // HD
    rows = size - TILE
    units = up_weight.shape[1]
    c = lax.axis_index("c")

    told, copies, count = front(tokens, segment_ids, lax.axis_size(("z", "xl")))
    far = lax.all_to_all(copies, ("z", "xl"), 0, 0, tiled=True)
    near = gather_near(told)
    core = c.astype(jnp.int32).reshape(1)
    z, xl, z_size = lax.axis_index("z"), lax.axis_index("xl"), lax.axis_size("z")
    routes = [((z + step) % z_size) * 2 + (xl ^ flip) for step, flip in offsets(z_size)]
    place = jnp.stack([c, *routes, z, lax.axis_index("y")]).astype(jnp.int32)
    plane = lax.axis_size(PLANE)

    weights, biases, pairs, columns, bundle = prepare(
        core, in_weights, in_biases, gains, shifts, up_weight, down_weight, up_biases[None], heads
    )
    out_far = crossed(out_weight)
    far_one = crossed(bundle)
    far_two = shift_by(far_one, "c", 1)

    weights, (out_far, columns, place) = tied(weights, (out_far, columns, place))
    *parts, give, xq, xk, qx, kx, vx, counts = attend(
        near, far, weights, biases, gains, shifts, rows, heads
    )
    thumb_out, xhat, x = thumbs(tokens, weights, biases, gains, shifts, heads)
    parts = pair_merge(parts, shift_by(give, "c", 1), heads)
    low, full, lse = merge(count, return_near(parts), thumb_out, heads)
    low_far = shift_by(low, "h", 1)
    mixed, grad_mid, mid_low, packed, hidden, act, pre, small = feed_forward(
        tokens, cotangents, low, low_far, full, lse, out_weight, out_far, up_weight, up_biases[None],
        down_weight, far_one, far_two, gains, shifts, rows, heads,
    )
    grads = gather_near(packed)
    keep, give = weight_grads(core, act, cotangents, hidden, pre, low, mid_low, plane)
    mid_low, (keep, give) = tied(mid_low, (keep, give))
    thumb = thumbs_back(count, x, mid_low, out_weight, heads)
    early = core_sum(keep, give)

    grads, (early, thumb) = tied(grads, (early, thumb))
    early = lax.all_to_all(early, PLANE, 0, 0, tiled=True)
    *out, keep, give = reverse(
        counts, place, grads, (xq, xk, qx, kx, vx), xhat, thumb, pairs, columns, small, rows, heads
    )
    half = len(near) // 2
    out_q, give_q, out_kv = out[:half], out[half], out[half + 1 :]
    early = jnp.sum(early.astype(F32), axis=0).astype(BF)
    early = (early.astype(F32) + shift_by(early, "xl", 1).astype(F32)).astype(BF)
    early = jnp.broadcast_to(early[None], (z_size, *early.shape))
    late, early = tied(core_sum(keep, give), early)
    early = lax.all_to_all(early, "z", 0, 0, tiled=True)
    from_kv = return_far(out_kv)
    out_q = fold(out_q, shift_by(give_q, "c", 1))
    from_q = return_near(out_q)
    late, (early, from_kv[1], from_kv[-1], from_q) = tied(
        late, (early, from_kv[1], from_kv[-1], from_q)
    )
    late = late.reshape(plane, -1, late.shape[1])
    late = lax.all_to_all(late, PLANE, 0, 0, tiled=True)
    early = [early] + [shift_by(early, "y", d) for d in range(1, lax.axis_size("y"))]
    mine, other = grad_one(count, from_q, from_kv, thumb, pairs)
    late, (early[1], early[-1]) = tied(late, (early[1], early[-1]))
    late = across(jnp.sum(late.astype(F32), axis=0).astype(BF))
    arrived = [shift_by(mine, "h", 1), shift_by(other, "xl", 1), crossed(other)]
    late = jnp.broadcast_to(late[None], (plane, *late.shape))
    late = lax.all_to_all(late, PLANE, 0, 0, tiled=True).reshape(model, -1)

    early_far = [shift_by(e, "c", 1) for e in early]
    early = early_out(place, early, (), units, cols)
    late_far = shift_by(late, "c", 1)
    late = late_out(place, late, (), units)
    arrived, (early, late) = tied(arrived, (early, late))
    grad_tokens = close(count, tokens, grad_mid, mine, *arrived, gains)
    grad_down, grad_up, grad_out = early_out(place, early_far, early, units, cols)
    grad_in, in_bias, up_bias, grad_gains, grad_shifts = late_out(place, late_far, late, units)
    return (
        mixed,
        grad_tokens,
        grad_in,
        in_bias,
        grad_out,
        grad_up,
        up_bias.reshape(2, units),
        grad_down,
        grad_gains,
        grad_shifts,
    )


def solution(mesh):
    fine = Mesh(mesh.devices.reshape(4, 2, 4, 2, 2), ("z", "xl", "y", "c", "h"))
    blk = ("z", "xl", "y", "c")
    return jax.shard_map(
        local,
        mesh=fine,
        in_specs=(
            P(blk, None),
            P(None, blk, None),
            P(blk),
            P(None, None, "h"),
            P(None, "h"),
            P("h", None),
            P(None, "h"),
            P("h"),
            P("h", None),
            P(),
            P(),
        ),
        out_specs=(
            P(blk, None),
            P(None, blk, None),
            P(None, None, None, "h"),
            P(None, None, "h"),
            P(None, "h", None),
            P(None, None, "h"),
            P(None, "h"),
            P(None, "h", None),
            P(),
            P(),
        ),
        check_vma=False,
    )
```

```python
import functools

import jax
import jax.numpy as jnp
from jax import lax
from jax.experimental import pallas as pl
from jax.experimental.pallas import tpu as pltpu
from jax.sharding import Mesh
from jax.sharding import PartitionSpec as P

HD = 64
LANES = 128
TILE = 64
BLOCK = 256
EPS = 1e-06
SCALE = 0.125
FAR = -1e30
BF = jnp.bfloat16
F32 = jnp.float32
MIB = 1024 * 1024
ROOM = 56

NT = (((1,), (1,)), ((), ()))
TN = (((0,), (0,)), ((), ()))


def shift_by(array, axis, step):
    size = lax.axis_size(axis)
    return lax.ppermute(array, axis, [(i, (i + step) % size) for i in range(size)])


def dot(a, b):
    return jnp.dot(a, b, preferred_element_type=F32)


def dot_nt(a, b):
    return lax.dot_general(a, b, NT, preferred_element_type=F32)


def dot_tn(a, b):
    return lax.dot_general(a, b, TN, preferred_element_type=F32)


def standard(field):
    center = field - jnp.mean(field, axis=-1, keepdims=True)
    factor = lax.rsqrt(jnp.mean(center * center, axis=-1, keepdims=True) + EPS)
    return center * factor, factor


def norm_back(grad, gain, xhat, factor):
    h = grad * gain
    mean = jnp.mean(h, axis=-1, keepdims=True)
    return factor * (h - mean - xhat * jnp.mean(h * xhat, axis=-1, keepdims=True))


def pieces(value):
    high = value.astype(BF)
    rest = value - high.astype(F32)
    middle = rest.astype(BF)
    low = (rest - middle.astype(F32)).astype(BF)
    return high, middle, low


def zero_one(mask):
    return jnp.where(mask, 1.0, 0.0).astype(BF)


def iota(shape, dim):
    return lax.broadcasted_iota(jnp.int32, shape, dim)


VMEM = pl.BlockSpec(memory_space=pltpu.VMEM)
ANY = pl.BlockSpec(memory_space=pl.ANY)
SMEM = pl.BlockSpec(memory_space=pltpu.SMEM)


def local_call(body, name, out, ins, outs, args, scratch=(), cost=None, room=16):
    return pl.pallas_call(
        body,
        out_shape=out,
        in_specs=ins,
        out_specs=outs,
        scratch_shapes=scratch,
        cost_estimate=cost,
        compiler_params=pltpu.CompilerParams(vmem_limit_bytes=room * MIB),
        name=name,
    )(*args)


def shaped(*shape, dtype=BF):
    return jax.ShapeDtypeStruct(shape, dtype)


def cost(micros):
    return pl.CostEstimate(flops=int(micros * 1e9), bytes_accessed=0, transcendentals=0)


def front_kernel(tokens, ids, told, copies, number):
    rows = told.shape[0] - 16
    marks = jnp.where(ids[...] == 0, 1.0, 0.0)
    tiles = jnp.sum(marks).astype(jnp.int32) // TILE
    number[0] = tiles
    told[:rows, :] = tokens[:rows, :]
    told[rows:, :] = jnp.full((16, told.shape[1]), tiles.astype(F32), F32).astype(BF)
    for g in range(copies.shape[0]):
        copies[g] = told[...]


def front(tokens, ids, copies):
    size, model = tokens.shape
    told = size - TILE + 16
    return local_call(
        front_kernel,
        "front",
        (shaped(told, model), shaped(copies, told, model), shaped(1, dtype=jnp.int32)),
        [VMEM, VMEM],
        (VMEM, VMEM, SMEM),
        (tokens, ids.reshape(-1, LANES)),
        room=ROOM,
    )


def prepare_kernel(
    heads, place, in_weights, in_biases, gains, shifts, up, down, bias,
    weights, biases, pairs, columns, out,
):
    core = place[0]
    half = out.shape[1]
    at = pl.ds(pl.multiple_of(core * half, half), half)
    out[:half, :] = up[:, at]
    out[half : 2 * half, :] = down[at, :]
    mine = jnp.where(core == 0, bias[:, :half], bias[:, half:])
    row = iota((16, half), 0)
    rows = jnp.zeros((16, half), F32)
    for i, piece in enumerate(pieces(mine)):
        rows = jnp.where(row == i, piece.astype(F32), rows)
    out[2 * half :, :] = rows.astype(BF)

    model, cols = in_weights.shape[1:]
    width = heads * LANES
    row, col = (iota((cols, width), d) for d in (0, 1))
    spread = zero_one((row // HD == col // LANES) & (row % HD == col % LANES))
    lane = iota((1, width), 1) % LANES
    gap = jnp.zeros((1, HD), F32)

    def apart(line):
        return jnp.concatenate(
            sum([[line[:, h * HD : (h + 1) * HD], gap] for h in range(heads)], []), axis=1
        )

    extra = [
        apart(in_biases[0:1, :] * SCALE) + jnp.where(lane == HD, 1.0, 0.0),
        jnp.where((lane > HD) & (lane < HD + 4), 1.0, 0.0),
        apart(in_biases[1:2, :]) + jnp.where((lane >= HD) & (lane < HD + 3), 1.0, 0.0),
    ]
    for i in range(3):
        factor = SCALE if i == 0 else 1.0
        weights[:, i * width : (i + 1) * width] = (dot(in_weights[i], spread) * factor).astype(BF)
        biases[:, i * width : (i + 1) * width] = extra[i]
        for pair in range(heads // 2):
            pairs[pair, :, i * LANES : (i + 1) * LANES] = in_weights[
                i, :, pair * LANES : (pair + 1) * LANES
            ]
    tall = jnp.concatenate(
        [gains[0:1, :], shifts[0:1, :], jnp.zeros((LANES - 2, model), F32)], axis=0
    )
    columns[...] = jnp.transpose(tall)


def prepare(core, in_weights, in_biases, gains, shifts, up, down, bias, heads):
    model = up.shape[0]
    width = 3 * heads * LANES
    return local_call(
        functools.partial(prepare_kernel, heads),
        "prepare",
        (
            shaped(model, width),
            shaped(1, width, dtype=F32),
            shaped(heads // 2, model, 3 * LANES),
            shaped(model, LANES, dtype=F32),
            shaped(2 * model + 16, model),
        ),
        [SMEM] + [VMEM] * 7,
        (VMEM,) * 5,
        (core, in_weights, in_biases, gains, shifts, up, down, bias),
        cost=cost(4),
        room=ROOM,
    )


def count_of(ref, rows):
    return jnp.max(ref[rows : rows + 16, :LANES].astype(F32)).astype(jnp.int32)


def rows_at(start, rows, step=TILE):
    return pl.ds(pl.multiple_of(start, step), rows)


def attend_kernel(rows, groups, heads, *refs):
    near, far = refs[:groups], refs[groups]
    weights, biases, gains, shifts = refs[groups + 1 : groups + 5]
    at = groups + 5 + groups // 2
    out, give = refs[groups + 5 : at], refs[at]
    kept, counts, place = refs[at + 1 : at + 6], refs[at + 6], refs[at + 7]
    (xq, xk, qx, kx, vx), sems = refs[at + 8 : at + 13], refs[at + 13]
    model = xq.shape[1]
    q_counts = [count_of(r, rows) for r in near]
    k_counts = [count_of(far.at[g], rows) for g in range(groups)]
    for g in range(groups):
        counts[g] = q_counts[g]
        counts[groups + g] = k_counts[g]

    def compact(numbers, read, target):
        start = jnp.int32(0)
        for g, n in enumerate(numbers):
            target[rows_at(start, rows), :] = read(g)
            start = start + n * TILE
        target[rows_at(start, BLOCK), :] = jnp.zeros((BLOCK, model), BF)
        return start

    q_total = compact(q_counts, lambda g: near[g][:rows, :], xq)
    k_total = compact(k_counts, lambda g: far[g, :rows, :], xk)
    q_blocks = (q_total + BLOCK - 1) // BLOCK
    k_blocks = (k_total + BLOCK - 1) // BLOCK
    width = heads * LANES

    def hidden(ref, here):
        clean = standard(ref[here, :].astype(F32))[0].astype(BF)
        ref[here, :] = clean
        return (clean.astype(F32) * gains[0:1, :] + shifts[0:1, :]).astype(BF)

    @pl.loop(0, q_blocks)
    def _(b):
        here = rows_at(b * BLOCK, BLOCK, BLOCK)
        q = (dot(hidden(xq, here), weights[:, :width]) + biases[:, :width]).astype(BF)
        for h in range(heads):
            qx[h, here, :] = q[:, h * LANES : (h + 1) * LANES]

    @pl.loop(0, k_blocks)
    def _(b):
        here = rows_at(b * BLOCK, BLOCK, BLOCK)
        both = dot(hidden(xk, here), weights[:, width:]) + biases[:, width:]
        unseen = (iota((BLOCK, width), 0) + b * BLOCK >= k_total) & (
            iota((BLOCK, width), 1) % LANES == HD
        )
        k = jnp.where(unseen, FAR, both[:, :width]).astype(BF)
        v = both[:, width:].astype(BF)
        for h in range(heads):
            kx[h, here, :] = k[:, h * LANES : (h + 1) * LANES]
            vx[h, here, :] = v[:, h * LANES : (h + 1) * LANES]

    copies = [
        pltpu.make_async_copy(held, to, sems.at[i])
        for i, (held, to) in enumerate(zip((xq, xk, qx, kx, vx), kept))
    ]
    for copy in copies:
        copy.start()

    def attend_all(span):
        @pl.loop(0, q_blocks)
        def _(b):
            here = rows_at(b * BLOCK, BLOCK, BLOCK)
            lane = iota((BLOCK, LANES), 1)
            for h in range(heads):
                s = dot_nt(qx[h, here, :], kx[h, :span, :])
                top = jnp.max(s, axis=-1, keepdims=True)
                o = dot(jnp.exp(s - top).astype(BF), vx[h, :span, :])
                total = o[:, HD : HD + 1]
                o = o / total
                for i, piece in enumerate(pieces(top + jnp.log(total))):
                    o = jnp.where(lane == HD + i, piece.astype(F32), o)
                place[h, here, :] = o.astype(BF)

    for blocks in range(groups * TILE // BLOCK, groups * rows // BLOCK + 1):
        pl.when(k_blocks == blocks)(functools.partial(attend_all, blocks * BLOCK))

    gather = [
        (iota((LANES, LANES), 0) - HD + 3 * h == iota((LANES, LANES), 1))
        & (iota((LANES, LANES), 0) >= HD)
        & (iota((LANES, LANES), 0) < HD + 3)
        for h in range(heads)
    ]
    gather = [jnp.where(m, 1.0, 0.0).astype(BF) for m in gather]
    start = jnp.int32(0)
    for g in range(groups):
        mine = [place[h, rows_at(start, rows), :] for h in range(heads)]
        stats = sum(dot(m, s) for m, s in zip(mine, gather)).astype(BF)
        value = jnp.concatenate([m[:, :HD] for m in mine] + [stats], axis=1)
        if g < groups // 2:
            out[g][...] = value
        else:
            give[g - groups // 2] = value
        start = start + q_counts[g] * TILE
    for copy in copies:
        copy.wait()


def attend(near, far, weights, biases, gains, shifts, rows, heads):
    groups = len(near)
    model = near[0].shape[1]
    room = rows * groups + BLOCK
    parts = heads * HD + LANES
    kept = [(room, model)] * 2 + [(heads, room, LANES)] * 3
    return local_call(
        functools.partial(attend_kernel, rows, groups, heads),
        "attend",
        (
            *[shaped(rows, parts)] * (groups // 2),
            shaped(groups // 2, rows, parts),
            *[shaped(*k) for k in kept],
            shaped(2 * groups, dtype=jnp.int32),
        ),
        [VMEM] * (groups + 5),
        (*[VMEM] * (groups // 2 + 1), *[ANY] * 5, SMEM),
        (*near, far, weights, biases, gains, shifts),
        [
            pltpu.VMEM((heads, room, LANES), BF),
            *[pltpu.VMEM(k, BF) for k in kept],
            pltpu.SemaphoreType.DMA((5,)),
        ],
        cost(15),
        ROOM,
    )


def same_tile(rows):
    return iota((rows, rows), 0) // TILE == iota((rows, rows), 1) // TILE


def thumb_kernel(heads, tokens, weights, biases, gains, shifts, out, xhat, x):
    width = heads * LANES
    size = tokens.shape[0]
    clean = standard(tokens[...].astype(F32))[0].astype(BF)
    xhat[...] = clean
    hidden = (clean.astype(F32) * gains[0:1, :] + shifts[0:1, :]).astype(BF)
    x[...] = (dot(hidden, weights[...]) + biases[...]).astype(BF)
    visible = same_tile(size - TILE)
    out[:TILE, :] = jnp.zeros((TILE, heads * HD), F32)
    for h in range(heads):
        q = x[TILE:, h * LANES : (h + 1) * LANES]
        k = x[TILE:, width + h * LANES : width + (h + 1) * LANES]
        v = x[TILE:, 2 * width + h * LANES : 2 * width + (h + 1) * LANES]
        s = jnp.where(visible, dot_nt(q, k), FAR)
        e = jnp.exp(s - jnp.max(s, axis=-1, keepdims=True))
        o = dot(e.astype(BF), v)[:, :HD] / jnp.sum(e, axis=-1, keepdims=True)
        out[TILE:, h * HD : (h + 1) * HD] = o


def thumbs(tokens, weights, biases, gains, shifts, heads):
    size, model = tokens.shape
    return local_call(
        functools.partial(thumb_kernel, heads),
        "thumbs",
        (
            shaped(size, heads * HD, dtype=F32),
            shaped(size, model),
            shaped(size, 3 * heads * LANES),
        ),
        [VMEM] * 5,
        (VMEM,) * 3,
        (tokens, weights, biases, gains, shifts),
        cost=cost(5),
    )


def merged(parts, heads):
    cols = heads * HD
    row, col = (iota((LANES, cols), d) for d in (0, 1))
    spread = zero_one(row // 3 == col // HD)
    marks = [dot(p[:, cols:], spread) for p in parts]
    top = functools.reduce(jnp.maximum, marks)
    expos = [jnp.exp(m - top) for m in marks]
    total = sum(expos)
    mixed = sum(e * p[:, :cols].astype(F32) for p, e in zip(parts, expos)) / total
    row, col = (iota((cols, LANES), d) for d in (0, 1))
    packed = [
        dot(piece, zero_one((row % HD == 0) & (col == 3 * (row // HD) + i)))
        for i, piece in enumerate(pieces(top + jnp.log(total)))
    ]
    return mixed, sum(packed)


def pair_kernel(heads, *refs):
    count = (len(refs) - 1) // 2
    for j, (mine, out) in enumerate(zip(refs[:count], refs[count + 1 :])):
        mixed, marks = merged([mine[...], refs[count][j]], heads)
        out[...] = jnp.concatenate([mixed.astype(BF), marks.astype(BF)], axis=1)


def pair_merge(parts, other, heads):
    return local_call(
        functools.partial(pair_kernel, heads),
        "pair_merge",
        tuple(shaped(*p.shape) for p in parts),
        [VMEM] * (len(parts) + 1),
        (VMEM,) * len(parts),
        (*parts, other),
        cost=cost(3),
        room=ROOM,
    )


def merge_kernel(heads, counts, thumb, *refs):
    parts, (low, full, lse) = refs[:-3], refs[-3:]
    cols = heads * HD
    rows = lse.shape[0]
    mixed, marks = merged([p[...] for p in parts], heads)
    lse[...] = (-marks).astype(BF)
    image = iota((rows, cols), 0) < counts[0] * TILE
    full[:rows, :] = jnp.where(image, mixed, thumb[:rows, :])
    full[rows:, :] = thumb[rows:, :]
    low[...] = full[...].astype(BF)


def merge(count, parts, thumb, heads):
    size, cols = thumb.shape
    return local_call(
        functools.partial(merge_kernel, heads),
        "merge",
        (shaped(size, cols), shaped(size, cols, dtype=F32), shaped(parts[0].shape[0], LANES)),
        [SMEM] + [VMEM] * (1 + len(parts)),
        (VMEM,) * 3,
        (count, thumb, *parts),
        cost=cost(3),
    )


def fold_kernel(*refs):
    count = (len(refs) - 1) // 2
    for j, (mine, out) in enumerate(zip(refs[:count], refs[count + 1 :])):
        out[...] = (mine[...].astype(F32) + refs[count][j].astype(F32)).astype(BF)


def fold(parts, other):
    return local_call(
        fold_kernel,
        "fold",
        tuple(shaped(*p.shape) for p in parts),
        [VMEM] * (len(parts) + 1),
        (VMEM,) * len(parts),
        (*parts, other),
        cost=cost(2),
        room=ROOM,
    )


ROOT = 0.7978845608028654
CUBE = 0.044715


def ff_kernel(
    heads, tokens, outer, low, low_far, full, lse, out_weight, out_far, up, up_bias, down, far_one,
    far_two, gains, shifts, mixed, grad_mid, grad_low, packed, hidden_out, act_out, pre_out, small,
):
    size, model = tokens.shape
    passes = outer.shape[0]
    cols = heads * HD
    chunk = far_one.shape[1]
    units = up.shape[1]
    rows = packed.shape[0]
    branch = dot(low[...], out_weight[...]) + dot(low_far[...], out_far[...])
    middle = tokens[...].astype(F32) + (branch + shifts[1:2, :])
    xhat, factor = standard(middle)
    hidden = (xhat * gains[1:2, :] + shifts[2:3, :]).astype(BF)
    hidden_out[...] = hidden

    def one_chunk(up_part, bias, down_part, keep):
        v = dot(hidden, up_part) + bias
        t = jnp.tanh(ROOT * (v + CUBE * (v * v * v)))
        act = (0.5 * v * (1.0 + t)).astype(BF)
        slope = 0.5 * (1.0 + t) + 0.5 * v * (1.0 - t * t) * (ROOT * (1.0 + 3.0 * CUBE * (v * v)))
        two = []
        for p in range(passes):
            pre = (dot_nt(outer[p], down_part) * slope).astype(BF)
            if keep is not None:
                pre_out[p, :, keep] = pre
            two.append(dot_nt(pre, up_part))
        if keep is not None:
            act_out[:, keep] = act
        return dot(act, down_part), two

    def far_chunk(ref):
        told = ref[2 * chunk : 2 * chunk + 16, :].astype(F32)
        bias = told[0:1] + told[1:2] + told[2:3]
        return one_chunk(ref[:chunk, :], bias, ref[chunk : 2 * chunk, :], None)

    done = []
    for i in range(units // chunk):
        at = slice(i * chunk, (i + 1) * chunk)
        done.append(one_chunk(up[:, at], up_bias[:, at], down[at, :], at))
    done += [far_chunk(far_one), far_chunk(far_two)]

    def tree(parts):
        half = len(parts) // 2
        return sum(parts[:half]) + sum(parts[half:])

    output = tree([d[0] for d in done])
    mixed[...] = (middle + (output + shifts[3:4, :])).astype(BF)
    small[...] = jnp.zeros(small.shape, F32)
    lane = iota((rows, LANES), 1)
    stats = jnp.zeros((rows, LANES), F32)
    for p in range(passes):
        two = tree([d[1][p] for d in done])
        c = outer[p].astype(F32)
        mid = c + norm_back(two, gains[1:2, :], xhat, factor)
        mid_low = mid.astype(BF)
        grad_mid[p] = mid
        grad_low[p] = mid_low
        att = dot_nt(mid_low, out_weight[...]).astype(BF)
        packed[:, p * cols : (p + 1) * cols] = att[:rows, :]
        pre_out_p = pre_out[p].astype(F32)
        bias = jnp.sum(pre_out_p, axis=0, keepdims=True)
        small[p, 0:1, :] = jnp.sum(two * xhat, axis=0, keepdims=True)
        small[p, 1:2, :] = jnp.sum(two, axis=0, keepdims=True)
        small[p, 2:3, :] = jnp.sum(mid_low.astype(F32), axis=0, keepdims=True)
        small[p, 3:4, :] = jnp.sum(c, axis=0, keepdims=True)
        for i in range(units // model):
            small[p, 4 + i : 5 + i, :] = bias[:, i * model : (i + 1) * model]
        product = att[:rows, :].astype(F32) * full[:rows, :]
        for h in range(heads):
            delta = jnp.sum(product[:, h * HD : (h + 1) * HD], axis=-1, keepdims=True)
            for i, piece in enumerate(pieces(-delta)):
                stats = jnp.where(lane == 3 * heads * (p + 1) + 3 * h + i, piece.astype(F32), stats)
    packed[:, passes * cols :] = (stats + lse[...].astype(F32)).astype(BF)


def feed_forward(
    tokens, outer, low, low_far, full, lse, out_weight, out_far, up, up_bias, down, far_one, far_two,
    gains, shifts, rows, heads,
):
    size, model = tokens.shape
    passes = outer.shape[0]
    units = up.shape[1]
    return local_call(
        functools.partial(ff_kernel, heads),
        "feed_forward",
        (
            shaped(size, model),
            shaped(passes, size, model, dtype=F32),
            shaped(passes, size, model),
            shaped(rows, passes * heads * HD + LANES),
            shaped(size, model),
            shaped(size, units),
            shaped(passes, size, units),
            shaped(passes, 8, model, dtype=F32),
        ),
        [VMEM] * 15,
        (VMEM,) * 8,
        (
            tokens, outer, low, low_far, full, lse, out_weight, out_far, up, up_bias, down, far_one,
            far_two, gains, shifts,
        ),
        cost=cost(12),
        room=32,
    )


def thumb_back_kernel(heads, counts, x, mid_low, out_weight, out):
    width = heads * LANES
    size = x.shape[0]
    passes = mid_low.shape[0]
    visible = same_tile(size - TILE)
    outside = iota((size - TILE, HD), 0) + TILE >= counts[0] * TILE
    grads = [dot_nt(mid_low[p], out_weight[...]).astype(BF) for p in range(passes)]
    out[:, :, :TILE, :] = jnp.zeros((*out.shape[:2], TILE, out.shape[3]), BF)
    for h in range(heads):
        q = x[TILE:, h * LANES : (h + 1) * LANES]
        k = x[TILE:, width + h * LANES : width + (h + 1) * LANES]
        v = x[TILE:, 2 * width + h * LANES : 2 * width + h * LANES + HD]
        s = jnp.where(visible, dot_nt(q, k), FAR)
        e = jnp.exp(s - jnp.max(s, axis=-1, keepdims=True))
        w = e / jnp.sum(e, axis=-1, keepdims=True)
        w_low = w.astype(BF)
        for p in range(passes):
            g = grads[p][TILE:, h * HD : (h + 1) * HD]
            gw = dot_nt(g, v)
            ds = (w * (gw - jnp.sum(w * gw, axis=-1, keepdims=True))).astype(BF)
            dq = dot(ds, k[:, :HD]) * SCALE
            dk = dot_tn(ds, q)[:, :HD]
            dv = dot_tn(w_low, g)
            for c, piece in enumerate((dq, dk, dv)):
                at = c * LANES + (h % 2) * HD
                out[h // 2, p, TILE:, at : at + HD] = jnp.where(outside, piece, 0.0).astype(BF)


def thumbs_back(count, x, mid_low, out_weight, heads):
    passes, size, _ = mid_low.shape
    return local_call(
        functools.partial(thumb_back_kernel, heads),
        "thumbs_back",
        shaped(heads // 2, passes, size, 3 * LANES),
        [SMEM] + [VMEM] * 3,
        VMEM,
        (count, x, mid_low, out_weight),
        cost=cost(6),
    )


def early_at(units, model, low):
    ends = [model, 2 * model, 2 * model + units, 2 * model + units + low]
    return [slice(b - w, b) for b, w in zip(ends, (model, model, units, low))]


def early_cuts(parts, units, model, low):
    high, wide, turns = units // parts // 2, model // parts, model // low
    narrow = low * turns // parts
    for i in range(parts):
        yield (
            (slice(2 * i * high, (2 * i + 1) * high), slice(0, model)),
            (slice((2 * i + 1) * high, (2 * i + 2) * high), slice(0, model)),
            (slice(i * wide, (i + 1) * wide), slice(0, units)),
            (
                slice(i // turns * narrow, (i // turns + 1) * narrow),
                slice(i % turns * low, (i % turns + 1) * low),
            ),
        )


def weight_kernel(place, act, outer, hidden, pre, low, mid_low, keep, give):
    units, model, cols = act.shape[1], hidden.shape[1], low.shape[1]
    core = place[0]
    for turn, out in ((core, keep), (1 - core, give)):
        down = dot_tn(act[...], outer[turn]).astype(BF)
        up = dot_tn(hidden[...], pre[turn]).astype(BF)
        proj = dot_tn(low[...], mid_low[turn]).astype(BF)
        for i, cut in enumerate(early_cuts(keep.shape[0], units, model, cols)):
            for value, (rows, lanes), at in zip(
                (down, down, up, proj), cut, early_at(units, model, cols)
            ):
                out[i, :, at] = value[rows, lanes]


def weight_grads(core, act, outer, hidden, pre, low, mid_low, parts):
    units, model = act.shape[1], outer.shape[2]
    out = shaped(parts, model // parts, 2 * model + units + low.shape[1])
    return local_call(
        weight_kernel,
        "weight_grads",
        (out, out),
        [SMEM] + [VMEM] * 6,
        (VMEM,) * 2,
        (core, act, outer, hidden, pre, low, mid_low),
        cost=cost(8),
        room=24,
    )


def reverse_kernel(rows, groups, heads, passes, counts, place, *refs):
    grads, kept = refs[:groups], refs[groups : groups + 5]
    own, thumb, weights, columns, small = refs[groups + 5 : groups + 10]
    at = groups + 10
    out_q, give_q, at = refs[at : at + groups // 2], refs[at + groups // 2], at + groups // 2 + 1
    out_kv, at = refs[at : at + groups // 2], at + groups // 2
    keep, give = refs[at : at + 2]
    (
        stage, xq, xk, qx, kx, vx, packed, gx, kt, dq_t, dv, dk, low_q, low_kv, total, sums,
        starts, sems,
    ) = refs[at + 2 :]
    couples = heads // 2
    sources = [*grads, *kept[2:], *kept[:2]]
    targets = [*[stage.at[g] for g in range(groups)], qx, kx, vx, xq, xk]
    copies = [
        pltpu.make_async_copy(f, t, sems.at[i]) for i, (f, t) in enumerate(zip(sources, targets))
    ]
    for copy in copies:
        copy.start()
    cols = heads * HD
    wide = passes * LANES
    q_counts = [counts[g] for g in range(groups)]
    k_counts = [counts[groups + g] for g in range(groups)]
    start = jnp.int32(0)
    for g in range(groups):
        copies[g].wait()
        packed[rows_at(start, rows), :] = stage[g]
        start = start + q_counts[g] * TILE
    q_total, k_total = start, sum(k_counts) * TILE
    tail_lane = iota((BLOCK, packed.shape[1]), 1) - passes * cols
    empty = (tail_lane >= 0) & (tail_lane < 3 * heads) & (tail_lane % 3 == 0)
    packed[rows_at(q_total, BLOCK), :] = jnp.where(empty, FAR, 0.0).astype(BF)
    q_blocks = (q_total + BLOCK - 1) // BLOCK
    k_blocks = (k_total + BLOCK - 1) // BLOCK
    spans = range(groups * TILE // BLOCK, groups * rows // BLOCK + 1)

    row, col = (iota((LANES, heads * LANES), d) for d in (0, 1))
    head, lane = col // LANES, col % LANES
    to_marks = zero_one((lane > HD) & (lane < HD + 4) & (row == 3 * head + lane - HD - 1))
    row, col = (iota((LANES, heads * wide), d) for d in (0, 1))
    head, turn, lane = col // wide, col % wide // LANES, col % LANES
    to_deltas = zero_one(
        (lane >= HD) & (lane < HD + 3) & (row == 3 * heads * (turn + 1) + 3 * head + lane - HD)
    )
    for copy in copies[groups : groups + 3]:
        copy.wait()

    @pl.loop(0, q_blocks)
    def _(b):
        here = rows_at(b * BLOCK, BLOCK, BLOCK)
        stats = packed[here, passes * cols :]
        marks = dot(stats, to_marks)
        deltas = dot(stats, to_deltas).astype(BF)
        for h in range(heads):
            more = marks[:, h * LANES : (h + 1) * LANES]
            qx[h, here, :] = (qx[h, here, :].astype(F32) + more).astype(BF)
            for p in range(passes):
                at = p * cols + h * HD
                mine = (h * passes + p) * LANES
                gx[h, here, p * LANES : (p + 1) * LANES] = jnp.concatenate(
                    [packed[here, at : at + HD], deltas[:, mine + HD : mine + LANES]], axis=1
                )

    @pl.loop(0, k_blocks)
    def _(b):
        here = rows_at(b * BLOCK, BLOCK, BLOCK)
        for h in range(heads):
            kt[h, b] = jnp.transpose(kx[h, here, :].astype(F32))[:HD, :].astype(BF)

    def reverse_all(blocks):
        span = blocks * BLOCK

        @pl.loop(0, couples)
        def _(pair):
            dv[:, :span, :] = jnp.zeros((2, span, wide), F32)
            dk[:, :, :span, :] = jnp.zeros((passes, 2, span, LANES), F32)

            @pl.loop(0, q_blocks)
            def _(b):
                here = rows_at(b * BLOCK, BLOCK, BLOCK)
                for i in range(2):
                    h = 2 * pair + i
                    q, g = qx[h, here, :], gx[h, here, :]
                    k_t = jnp.concatenate([kt[h, j] for j in range(blocks)], axis=1)
                    w = jnp.exp(dot_nt(kx[h, :span, :], q))
                    dv[i, :span, :] += dot(w.astype(BF), g)
                    for p in range(passes):
                        ds = dot_nt(vx[h, :span, :], g[:, p * LANES : (p + 1) * LANES])
                        ds = (w * ds).astype(BF)
                        dk[p, i, :span, :] += dot(ds, q)
                        dq_t[p, i * HD : (i + 1) * HD, :] = dot(k_t, ds)
                for p in range(passes):
                    piece = jnp.transpose(dq_t[p]) * SCALE
                    low_q[pair, here, p * LANES : (p + 1) * LANES] = piece.astype(BF)

            for p in range(passes):
                for c, both in enumerate(
                    (
                        [dk[p, i, :span, :HD] for i in range(2)],
                        [dv[i, :span, p * LANES : p * LANES + HD] for i in range(2)],
                    )
                ):
                    lane = (2 * p + c) * LANES
                    low_kv[pair, :span, lane : lane + LANES] = jnp.concatenate(both, axis=1).astype(BF)

    for blocks in spans:
        pl.when(k_blocks == blocks)(functools.partial(reverse_all, blocks))

    start = jnp.int32(0)
    for g in range(groups):
        starts[g] = start
        start = start + k_counts[g] * TILE
    for g in range(groups):
        here = rows_at(starts[place[1 + g]], rows)
        out_kv[g // 2][g % 2] = jnp.concatenate([low_kv[i, here, :] for i in range(couples)], axis=1)
    start = jnp.int32(0)
    for g in range(groups):
        here = rows_at(start, rows)
        value = jnp.concatenate([low_q[i, here, :] for i in range(couples)], axis=1)
        if g < groups // 2:
            out_q[g][...] = value
        else:
            give_q[g - groups // 2] = value
        start = start + q_counts[g] * TILE

    copies[groups + 3].wait()
    copies[groups + 4].wait()

    def key_sums(blocks):
        span = blocks * BLOCK
        for i in range(couples):
            flat = low_kv[i, :span, :]
            total[i, :, wide:] = dot_tn(xk[:span, :], flat)
            sums[i, :, wide:] = dot(jnp.ones((8, span), BF), flat)

    for blocks in spans:
        pl.when(k_blocks == blocks)(functools.partial(key_sums, blocks))

    total[:, :, :wide] = jnp.zeros((couples, total.shape[1], wide), F32)
    sums[:, :, :wide] = jnp.zeros((couples, 8, wide), F32)

    @pl.loop(0, q_blocks)
    def _(b):
        here = rows_at(b * BLOCK, BLOCK, BLOCK)
        for i in range(couples):
            total[i, :, :wide] += dot_tn(xq[here, :], low_q[i, here, :])
            sums[i, :, :wide] += dot(jnp.ones((8, BLOCK), BF), low_q[i, here, :])

    model = total.shape[1]
    gain, shift = columns[:, 0:1], columns[:, 1:2]
    ones = jnp.ones((8, own.shape[0]), BF)
    for p in range(passes):
        whole = []
        for i in range(couples):
            mine = thumb[i, p]
            part = dot_tn(own[...], mine)
            part_sum = dot(ones, mine)[0:1, :]
            q_at = slice(p * LANES, (p + 1) * LANES)
            kv_at = slice((passes + 2 * p) * LANES, (passes + 2 * p + 2) * LANES)
            part += jnp.concatenate([total[i, :, q_at], total[i, :, kv_at]], axis=1)
            part_sum += jnp.concatenate([sums[i, 0:1, q_at], sums[i, 0:1, kv_at]], axis=1)
            w = weights[i].astype(F32)
            gain_one = jnp.sum(w * part, axis=1, keepdims=True)
            shift_one = jnp.sum(w * part_sum, axis=1, keepdims=True)
            lane = iota((model, LANES), 1)
            tall = jnp.where(lane == 0, gain_one, jnp.where(lane == 1, shift_one, 0.0))
            flat = jnp.concatenate(
                [jnp.zeros((2, LANES), F32)]
                + [part_sum[:, c * LANES : (c + 1) * LANES] for c in range(3)]
                + [jnp.zeros((LANES - 5, LANES), F32)],
                axis=0,
            )
            tall = jnp.concatenate([tall[:LANES] + jnp.transpose(flat), tall[LANES:]], axis=0)
            if i == 0:
                turned = jnp.concatenate(
                    [
                        jnp.zeros((8, model), F32),
                        small[p],
                        jnp.zeros((LANES - 16, model), F32),
                    ],
                    axis=0,
                )
                tall = tall + jnp.transpose(turned)
            whole += [part * gain + shift * part_sum, tall]
        whole = jnp.concatenate(whole, axis=1).astype(BF)

        @pl.when(place[0] == p)
        def _():
            keep[...] = whole

        @pl.when(place[0] != p)
        def _():
            give[...] = whole


def reverse(counts, place, grads, kept, own, thumb, weights, columns, small, rows, heads):
    groups = len(grads)
    couples, passes = thumb.shape[:2]
    model = own.shape[1]
    room = rows * groups + BLOCK
    cols = heads * HD
    wide = passes * LANES
    half = groups // 2
    late = shaped(model, couples * 4 * LANES)
    q, kv = shaped(rows, couples * wide), shaped(2, rows, couples * 2 * wide)
    out = (*[q] * half, shaped(half, rows, couples * wide), *[kv] * half, late, late)
    return local_call(
        functools.partial(reverse_kernel, rows, groups, heads, passes),
        "reverse",
        out,
        [SMEM, SMEM] + [ANY] * (groups + 5) + [VMEM] * 5,
        (VMEM,) * len(out),
        (counts, place, *grads, *kept, own, thumb, weights, columns, small),
        [
            pltpu.VMEM((groups, rows, passes * cols + LANES), BF),
            pltpu.VMEM((room, model), BF),
            pltpu.VMEM((room, model), BF),
            pltpu.VMEM((heads, room, LANES), BF),
            pltpu.VMEM((heads, room, LANES), BF),
            pltpu.VMEM((heads, room, LANES), BF),
            pltpu.VMEM((room, passes * cols + LANES), BF),
            pltpu.VMEM((heads, room, wide), BF),
            pltpu.VMEM((heads, room // BLOCK, HD, BLOCK), BF),
            pltpu.VMEM((passes, LANES, BLOCK), F32),
            pltpu.VMEM((2, room, wide), F32),
            pltpu.VMEM((passes, 2, room, LANES), F32),
            pltpu.VMEM((couples, room, wide), BF),
            pltpu.VMEM((couples, room, 2 * wide), BF),
            pltpu.VMEM((couples, model, 3 * wide), F32),
            pltpu.VMEM((couples, 8, 3 * wide), F32),
            pltpu.SMEM((groups,), jnp.int32),
            pltpu.SemaphoreType.DMA((groups + 5,)),
        ],
        cost(45),
        ROOM,
    )


def grad_one_kernel(near, counts, *refs):
    from_q, from_kv, (thumb, weights, mine, other) = refs[:near], refs[near:-4], refs[-4:]
    couples, passes, size, _ = thumb.shape
    rows = from_q[0].shape[0]
    sum_q = sum(r[...].astype(F32) for r in from_q)
    sum_kv = [sum(r[f].astype(F32) for r in from_kv) for f in range(2)]
    image = iota((rows, 3 * LANES), 0) < counts[0] * TILE
    for p in range(passes):
        parts = []
        for i in range(couples):
            at = (passes * i + p) * LANES
            there = slice(2 * at, 2 * at + 2 * LANES)
            far = jnp.concatenate([sum_q[:, at : at + LANES], sum_kv[0][:, there]], axis=1)
            flat = jnp.concatenate(
                [jnp.where(image, far.astype(BF), thumb[i, p, :rows]), thumb[i, p, rows:]], axis=0
            )
            parts.append(
                (
                    dot_nt(flat, weights[i]),
                    dot_nt(sum_kv[1][:, there].astype(BF), weights[i, :, LANES:]),
                )
            )
        mine[p] = sum(a for a, _ in parts).astype(BF)
        other[p] = sum(b for _, b in parts).astype(BF)


def grad_one(count, from_q, from_kv, thumb, weights):
    near = len(from_q)
    passes, size, _ = thumb.shape[1:]
    model = weights.shape[1]
    return local_call(
        functools.partial(grad_one_kernel, near),
        "grad_one",
        (shaped(passes, size, model), shaped(passes, from_q[0].shape[0], model)),
        [SMEM] + [VMEM] * (near + len(from_kv) + 2),
        (VMEM,) * 2,
        (count, *from_q, *from_kv, thumb, weights),
        cost=cost(5),
        room=ROOM,
    )


def close_kernel(counts, tokens, mid, mine, head, side, cross, gains, out):
    xhat, factor = standard(tokens[...].astype(F32))
    rows = side.shape[1]
    image = iota(side.shape[1:], 0) < counts[0] * TILE
    for p in range(mid.shape[0]):
        grad = mine[p].astype(F32) + head[p].astype(F32)
        more = jnp.where(image, side[p].astype(F32) + cross[p].astype(F32), 0.0)
        grad = jnp.concatenate([grad[:rows] + more, grad[rows:]], axis=0)
        out[p] = mid[p] + norm_back(grad, gains[0:1, :], xhat, factor)


def close(count, tokens, mid, mine, head, side, cross, gains):
    return local_call(
        close_kernel,
        "close",
        shaped(*mid.shape, dtype=F32),
        [SMEM] + [VMEM] * 7,
        VMEM,
        (count, tokens, mid, mine, head, side, cross, gains),
        cost=cost(4),
        room=ROOM,
    )


def early_kernel(lines, far, place, *refs):
    parts, refs = refs[:lines], refs[lines:]
    out, (down, up, proj, sems) = refs[-7:-4], refs[-4:]
    turn, y = place[0], place[10]
    turn = 1 - turn if far else turn
    (units, model), low = down.shape, proj.shape[0]
    steps, rows = parts[0].shape[:2]
    lane_down, lane_next, lane_up, lane_proj = early_at(units, model, low)
    turns = model // low
    for d, ref in enumerate(parts):
        for j in range(steps):
            i = j * lines + (y + lines - d) % lines
            at = pl.multiple_of(2 * rows * i, 2 * rows)
            down[pl.ds(at, rows), :] = ref[j, :, lane_down].astype(F32)
            down[pl.ds(at + rows, rows), :] = ref[j, :, lane_next].astype(F32)
            up[rows_at(rows * i, rows, rows), :] = ref[j, :, lane_up].astype(F32)
            here = rows_at(i // turns * rows, rows, rows)
            value = ref[j, :, lane_proj].astype(F32)
            for t in range(turns):

                @pl.when(i % turns == t)
                def _(value=value, here=here, t=t):
                    proj[here, t * low : (t + 1) * low] = value

    copies = [
        pltpu.make_async_copy(held, to.at[turn], sems.at[n])
        for n, (held, to) in enumerate(zip((down, up, proj), out))
    ]
    for copy in copies:
        copy.start()
    for copy in copies:
        copy.wait()


def early_out(place, parts, before, units, low):
    model = len(parts) * parts[0].shape[0] * parts[0].shape[1]
    shapes = (units, model), (model, units), (low, model)
    return pl.pallas_call(
        functools.partial(early_kernel, len(parts), bool(before)),
        out_shape=tuple(shaped(2, *s, dtype=F32) for s in shapes),
        in_specs=[SMEM] + [VMEM] * len(parts) + [ANY] * len(before),
        out_specs=(ANY,) * 3,
        scratch_shapes=[
            *[pltpu.VMEM(s, F32) for s in shapes],
            pltpu.SemaphoreType.DMA((3,)),
        ],
        input_output_aliases={1 + len(parts) + i: i for i in range(len(before))},
        cost_estimate=cost(5),
        compiler_params=pltpu.CompilerParams(vmem_limit_bytes=ROOM * MIB),
        name="early_far" if before else "early_own",
    )(place, *parts, *before)


def late_kernel(far, place, ref, *refs):
    out, (grad_in, *small), sems = refs[-11:-6], refs[-6:-1], refs[-1]
    in_bias, up_bias, gains, shifts = small
    turn = 1 - place[0] if far else place[0]
    turned = []
    for pair in range(2):
        at = 4 * LANES * pair
        for c in range(3):
            grad_in[c, :, pair * LANES : (pair + 1) * LANES] = ref[
                :, at + c * LANES : at + (c + 1) * LANES
            ].astype(F32)
        turned.append(jnp.transpose(ref[:, at + 3 * LANES : at + 4 * LANES].astype(F32)))
    a, b = turned
    in_bias[...] = jnp.concatenate(
        [
            jnp.concatenate([a[2:3, :LANES], b[2:3, :LANES]], axis=1),
            jnp.concatenate([a[4:5, :LANES], b[4:5, :LANES]], axis=1),
        ],
        axis=0,
    )
    up_bias[...] = jnp.concatenate([a[12:13], a[13:14]], axis=1)
    gains[...] = jnp.concatenate([a[0:1] + b[0:1], a[8:9]], axis=0)
    shifts[...] = jnp.concatenate([a[1:2] + b[1:2], a[10:11], a[9:10], a[11:12]], axis=0)
    copies = [
        pltpu.make_async_copy(held, to.at[turn], sems.at[n])
        for n, (held, to) in enumerate(zip((grad_in, *small), out))
    ]
    for copy in copies:
        copy.start()
    for copy in copies:
        copy.wait()


def late_out(place, part, before, units):
    model = part.shape[0]
    shapes = (3, model, 2 * LANES), (2, 2 * LANES), (1, units), (2, model), (4, model)
    return pl.pallas_call(
        functools.partial(late_kernel, bool(before)),
        out_shape=tuple(shaped(2, *s, dtype=F32) for s in shapes),
        in_specs=[SMEM, VMEM] + [ANY] * len(before),
        out_specs=(ANY,) * 5,
        scratch_shapes=[
            *[pltpu.VMEM(s, F32) for s in shapes],
            pltpu.SemaphoreType.DMA((5,)),
        ],
        input_output_aliases={2 + i: i for i in range(len(before))},
        cost_estimate=cost(3),
        compiler_params=pltpu.CompilerParams(vmem_limit_bytes=ROOM * MIB),
        name="late_far" if before else "late_own",
    )(place, part, *before)


def gather_near(array):
    mine = [array] + [shift_by(array, "y", d) for d in range(1, lax.axis_size("y"))]
    return mine + [shift_by(a, "c", 1) for a in mine]


def return_near(parts):
    return [parts[0]] + [shift_by(p, "y", -j) for j, p in enumerate(parts) if j > 0]


def offsets(size):
    return [(step, flip) for step in range(size) for flip in range(2)]


def return_far(parts):
    return [parts[0]] + [shift_by(p, "z", step) for step, p in enumerate(parts) if step > 0]


PLANE = ("z", "y")


def core_sum(keep, give):
    return (keep.astype(F32) + shift_by(give, "c", 1).astype(F32)).astype(BF)


def crossed(array):
    n = lax.axis_size(("xl", "h"))
    return lax.ppermute(array, ("xl", "h"), [(i, n - 1 - i) for i in range(n)])


def across(low):
    done = low.astype(F32) + shift_by(low, "xl", 1).astype(F32)
    size = 4 * LANES
    ones = jnp.concatenate([low[:, i + 3 * LANES : i + size] for i in range(0, low.shape[1], size)], axis=1)
    more = shift_by(ones, "h", 1).astype(F32) + crossed(ones).astype(F32)
    more = jnp.where(jnp.arange(more.shape[1]) % LANES < 2, more, 0.0)
    nothing = jnp.zeros((low.shape[0], 3 * LANES), F32)
    laid = [[nothing, more[:, i : i + LANES]] for i in range(0, more.shape[1], LANES)]
    return (done + jnp.concatenate(sum(laid, []), axis=1)).astype(BF)


def tied(arrays, others):
    return lax.optimization_barrier((arrays, others))


def local(
    tokens,
    cotangents,
    segment_ids,
    in_weights,
    in_biases,
    out_weight,
    up_weight,
    up_biases,
    down_weight,
    gains,
    shifts,
):
    size, model = tokens.shape
    cols = in_weights.shape[2]
    heads = cols // HD
    rows = size - TILE
    units = up_weight.shape[1]
    c = lax.axis_index("c")

    told, copies, count = front(tokens, segment_ids, lax.axis_size(("z", "xl")))
    far = lax.all_to_all(copies, ("z", "xl"), 0, 0, tiled=True)
    near = gather_near(told)
    core = c.astype(jnp.int32).reshape(1)
    z, xl, z_size = lax.axis_index("z"), lax.axis_index("xl"), lax.axis_size("z")
    routes = [((z + step) % z_size) * 2 + (xl ^ flip) for step, flip in offsets(z_size)]
    place = jnp.stack([c, *routes, z, lax.axis_index("y")]).astype(jnp.int32)
    plane = lax.axis_size(PLANE)

    weights, biases, pairs, columns, bundle = prepare(
        core, in_weights, in_biases, gains, shifts, up_weight, down_weight, up_biases[None], heads
    )
    out_far = crossed(out_weight)
    far_one = crossed(bundle)
    far_two = shift_by(far_one, "c", 1)

    weights, (out_far, columns, place) = tied(weights, (out_far, columns, place))
    *parts, give, xq, xk, qx, kx, vx, counts = attend(
        near, far, weights, biases, gains, shifts, rows, heads
    )
    thumb_out, xhat, x = thumbs(tokens, weights, biases, gains, shifts, heads)
    parts = pair_merge(parts, shift_by(give, "c", 1), heads)
    low, full, lse = merge(count, return_near(parts), thumb_out, heads)
    low_far = shift_by(low, "h", 1)
    mixed, grad_mid, mid_low, packed, hidden, act, pre, small = feed_forward(
        tokens, cotangents, low, low_far, full, lse, out_weight, out_far, up_weight, up_biases[None],
        down_weight, far_one, far_two, gains, shifts, rows, heads,
    )
    grads = gather_near(packed)
    keep, give = weight_grads(core, act, cotangents, hidden, pre, low, mid_low, plane)
    mid_low, (keep, give) = tied(mid_low, (keep, give))
    thumb = thumbs_back(count, x, mid_low, out_weight, heads)
    early = core_sum(keep, give)

    grads, (early, thumb) = tied(grads, (early, thumb))
    early = lax.all_to_all(early, PLANE, 0, 0, tiled=True)
    *out, keep, give = reverse(
        counts, place, grads, (xq, xk, qx, kx, vx), xhat, thumb, pairs, columns, small, rows, heads
    )
    half = len(near) // 2
    out_q, give_q, out_kv = out[:half], out[half], out[half + 1 :]
    early = jnp.sum(early.astype(F32), axis=0).astype(BF)
    early = (early.astype(F32) + shift_by(early, "xl", 1).astype(F32)).astype(BF)
    early = jnp.broadcast_to(early[None], (z_size, *early.shape))
    late, early = tied(core_sum(keep, give), early)
    early = lax.all_to_all(early, "z", 0, 0, tiled=True)
    from_kv = return_far(out_kv)
    out_q = fold(out_q, shift_by(give_q, "c", 1))
    from_q = return_near(out_q)
    late, (early, from_kv, from_q) = tied(late, (early, from_kv, from_q))
    late = late.reshape(plane, -1, late.shape[1])
    late = lax.all_to_all(late, PLANE, 0, 0, tiled=True)
    early = [early] + [shift_by(early, "y", d) for d in range(1, lax.axis_size("y"))]
    mine, other = grad_one(count, from_q, from_kv, thumb, pairs)
    arrived = [shift_by(mine, "h", 1), shift_by(other, "xl", 1), crossed(other)]
    late, (early[1], arrived[1], arrived[2]) = tied(late, (early[1], arrived[1], arrived[2]))
    late = across(jnp.sum(late.astype(F32), axis=0).astype(BF))
    late = jnp.broadcast_to(late[None], (plane, *late.shape))
    late = lax.all_to_all(late, PLANE, 0, 0, tiled=True).reshape(model, -1)

    early_far = [shift_by(e, "c", 1) for e in early]
    early = early_out(place, early, (), units, cols)
    late_far = shift_by(late, "c", 1)
    late = late_out(place, late, (), units)
    arrived, (early, late) = tied(arrived, (early, late))
    grad_tokens = close(count, tokens, grad_mid, mine, *arrived, gains)
    grad_down, grad_up, grad_out = early_out(place, early_far, early, units, cols)
    grad_in, in_bias, up_bias, grad_gains, grad_shifts = late_out(place, late_far, late, units)
    return (
        mixed,
        grad_tokens,
        grad_in,
        in_bias,
        grad_out,
        grad_up,
        up_bias.reshape(2, units),
        grad_down,
        grad_gains,
        grad_shifts,
    )


def solution(mesh):
    fine = Mesh(mesh.devices.reshape(4, 2, 4, 2, 2), ("z", "xl", "y", "c", "h"))
    blk = ("z", "xl", "y", "c")
    return jax.shard_map(
        local,
        mesh=fine,
        in_specs=(
            P(blk, None),
            P(None, blk, None),
            P(blk),
            P(None, None, "h"),
            P(None, "h"),
            P("h", None),
            P(None, "h"),
            P("h"),
            P("h", None),
            P(),
            P(),
        ),
        out_specs=(
            P(blk, None),
            P(None, blk, None),
            P(None, None, None, "h"),
            P(None, None, "h"),
            P(None, "h", None),
            P(None, None, "h"),
            P(None, "h"),
            P(None, "h", None),
            P(),
            P(),
        ),
        check_vma=False,
    )
```

```python
import functools

import jax
import jax.numpy as jnp
from jax import lax
from jax.experimental import pallas as pl
from jax.experimental.pallas import tpu as pltpu
from jax.sharding import Mesh
from jax.sharding import PartitionSpec as P

HD = 64
LANES = 128
TILE = 64
BLOCK = 256
EPS = 1e-06
SCALE = 0.125
FAR = -1e30
BF = jnp.bfloat16
F32 = jnp.float32
MIB = 1024 * 1024
ROOM = 56

NT = (((1,), (1,)), ((), ()))
TN = (((0,), (0,)), ((), ()))


def shift_by(array, axis, step):
    size = lax.axis_size(axis)
    return lax.ppermute(array, axis, [(i, (i + step) % size) for i in range(size)])


def dot(a, b):
    return jnp.dot(a, b, preferred_element_type=F32)


def dot_nt(a, b):
    return lax.dot_general(a, b, NT, preferred_element_type=F32)


def dot_tn(a, b):
    return lax.dot_general(a, b, TN, preferred_element_type=F32)


def standard(field):
    center = field - jnp.mean(field, axis=-1, keepdims=True)
    factor = lax.rsqrt(jnp.mean(center * center, axis=-1, keepdims=True) + EPS)
    return center * factor, factor


def norm_back(grad, gain, xhat, factor):
    h = grad * gain
    mean = jnp.mean(h, axis=-1, keepdims=True)
    return factor * (h - mean - xhat * jnp.mean(h * xhat, axis=-1, keepdims=True))


def pieces(value):
    high = value.astype(BF)
    rest = value - high.astype(F32)
    middle = rest.astype(BF)
    low = (rest - middle.astype(F32)).astype(BF)
    return high, middle, low


def zero_one(mask):
    return jnp.where(mask, 1.0, 0.0).astype(BF)


def iota(shape, dim):
    return lax.broadcasted_iota(jnp.int32, shape, dim)


VMEM = pl.BlockSpec(memory_space=pltpu.VMEM)
ANY = pl.BlockSpec(memory_space=pl.ANY)
SMEM = pl.BlockSpec(memory_space=pltpu.SMEM)


def local_call(body, name, out, ins, outs, args, scratch=(), cost=None, room=16):
    return pl.pallas_call(
        body,
        out_shape=out,
        in_specs=ins,
        out_specs=outs,
        scratch_shapes=scratch,
        cost_estimate=cost,
        compiler_params=pltpu.CompilerParams(vmem_limit_bytes=room * MIB),
        name=name,
    )(*args)


def shaped(*shape, dtype=BF):
    return jax.ShapeDtypeStruct(shape, dtype)


def cost(micros):
    return pl.CostEstimate(flops=int(micros * 1e9), bytes_accessed=0, transcendentals=0)


def front_kernel(tokens, ids, told, copies, number):
    rows = told.shape[0] - 16
    marks = jnp.where(ids[...] == 0, 1.0, 0.0)
    tiles = jnp.sum(marks).astype(jnp.int32) // TILE
    number[0] = tiles
    told[:rows, :] = tokens[:rows, :]
    told[rows:, :] = jnp.full((16, told.shape[1]), tiles.astype(F32), F32).astype(BF)
    for g in range(copies.shape[0]):
        copies[g] = told[...]


def front(tokens, ids, copies):
    size, model = tokens.shape
    told = size - TILE + 16
    return local_call(
        front_kernel,
        "front",
        (shaped(told, model), shaped(copies, told, model), shaped(1, dtype=jnp.int32)),
        [VMEM, VMEM],
        (VMEM, VMEM, SMEM),
        (tokens, ids.reshape(-1, LANES)),
        room=ROOM,
    )


def prepare_kernel(
    heads, place, in_weights, in_biases, gains, shifts, up, down, bias,
    weights, biases, pairs, columns, out,
):
    core = place[0]
    half = out.shape[1]
    at = pl.ds(pl.multiple_of(core * half, half), half)
    out[:half, :] = up[:, at]
    out[half : 2 * half, :] = down[at, :]
    mine = jnp.where(core == 0, bias[:, :half], bias[:, half:])
    row = iota((16, half), 0)
    rows = jnp.zeros((16, half), F32)
    for i, piece in enumerate(pieces(mine)):
        rows = jnp.where(row == i, piece.astype(F32), rows)
    out[2 * half :, :] = rows.astype(BF)

    model, cols = in_weights.shape[1:]
    width = heads * LANES
    row, col = (iota((cols, width), d) for d in (0, 1))
    spread = zero_one((row // HD == col // LANES) & (row % HD == col % LANES))
    lane = iota((1, width), 1) % LANES
    gap = jnp.zeros((1, HD), F32)

    def apart(line):
        return jnp.concatenate(
            sum([[line[:, h * HD : (h + 1) * HD], gap] for h in range(heads)], []), axis=1
        )

    extra = [
        apart(in_biases[0:1, :] * SCALE) + jnp.where(lane == HD, 1.0, 0.0),
        jnp.where((lane > HD) & (lane < HD + 4), 1.0, 0.0),
        apart(in_biases[1:2, :]) + jnp.where((lane >= HD) & (lane < HD + 3), 1.0, 0.0),
    ]
    for i in range(3):
        factor = SCALE if i == 0 else 1.0
        weights[:, i * width : (i + 1) * width] = (dot(in_weights[i], spread) * factor).astype(BF)
        biases[:, i * width : (i + 1) * width] = extra[i]
        for pair in range(heads // 2):
            pairs[pair, :, i * LANES : (i + 1) * LANES] = in_weights[
                i, :, pair * LANES : (pair + 1) * LANES
            ]
    tall = jnp.concatenate(
        [gains[0:1, :], shifts[0:1, :], jnp.zeros((LANES - 2, model), F32)], axis=0
    )
    columns[...] = jnp.transpose(tall)


def prepare(core, in_weights, in_biases, gains, shifts, up, down, bias, heads):
    model = up.shape[0]
    width = 3 * heads * LANES
    return local_call(
        functools.partial(prepare_kernel, heads),
        "prepare",
        (
            shaped(model, width),
            shaped(1, width, dtype=F32),
            shaped(heads // 2, model, 3 * LANES),
            shaped(model, LANES, dtype=F32),
            shaped(2 * model + 16, model),
        ),
        [SMEM] + [VMEM] * 7,
        (VMEM,) * 5,
        (core, in_weights, in_biases, gains, shifts, up, down, bias),
        cost=cost(4),
        room=ROOM,
    )


def count_of(ref, rows):
    return jnp.max(ref[rows : rows + 16, :LANES].astype(F32)).astype(jnp.int32)


def rows_at(start, rows, step=TILE):
    return pl.ds(pl.multiple_of(start, step), rows)


def attend_kernel(rows, groups, heads, *refs):
    near, far = refs[:groups], refs[groups]
    weights, biases, gains, shifts = refs[groups + 1 : groups + 5]
    at = groups + 5 + groups // 2
    out, give = refs[groups + 5 : at], refs[at]
    kept, counts, place = refs[at + 1 : at + 6], refs[at + 6], refs[at + 7]
    (xq, xk, qx, kx, vx), sems = refs[at + 8 : at + 13], refs[at + 13]
    model = xq.shape[1]
    q_counts = [count_of(r, rows) for r in near]
    k_counts = [count_of(far.at[g], rows) for g in range(groups)]
    for g in range(groups):
        counts[g] = q_counts[g]
        counts[groups + g] = k_counts[g]

    def compact(numbers, read, target):
        start = jnp.int32(0)
        for g, n in enumerate(numbers):
            target[rows_at(start, rows), :] = read(g)
            start = start + n * TILE
        target[rows_at(start, BLOCK), :] = jnp.zeros((BLOCK, model), BF)
        return start

    q_total = compact(q_counts, lambda g: near[g][:rows, :], xq)
    k_total = compact(k_counts, lambda g: far[g, :rows, :], xk)
    q_blocks = (q_total + BLOCK - 1) // BLOCK
    k_blocks = (k_total + BLOCK - 1) // BLOCK
    width = heads * LANES

    def hidden(ref, here):
        clean = standard(ref[here, :].astype(F32))[0].astype(BF)
        ref[here, :] = clean
        return (clean.astype(F32) * gains[0:1, :] + shifts[0:1, :]).astype(BF)

    @pl.loop(0, q_blocks)
    def _(b):
        here = rows_at(b * BLOCK, BLOCK, BLOCK)
        q = (dot(hidden(xq, here), weights[:, :width]) + biases[:, :width]).astype(BF)
        for h in range(heads):
            qx[h, here, :] = q[:, h * LANES : (h + 1) * LANES]

    @pl.loop(0, k_blocks)
    def _(b):
        here = rows_at(b * BLOCK, BLOCK, BLOCK)
        both = dot(hidden(xk, here), weights[:, width:]) + biases[:, width:]
        unseen = (iota((BLOCK, width), 0) + b * BLOCK >= k_total) & (
            iota((BLOCK, width), 1) % LANES == HD
        )
        k = jnp.where(unseen, FAR, both[:, :width]).astype(BF)
        v = both[:, width:].astype(BF)
        for h in range(heads):
            kx[h, here, :] = k[:, h * LANES : (h + 1) * LANES]
            vx[h, here, :] = v[:, h * LANES : (h + 1) * LANES]

    copies = [
        pltpu.make_async_copy(held, to, sems.at[i])
        for i, (held, to) in enumerate(zip((xq, xk, qx, kx, vx), kept))
    ]
    for copy in copies:
        copy.start()

    def attend_all(span):
        @pl.loop(0, q_blocks)
        def _(b):
            here = rows_at(b * BLOCK, BLOCK, BLOCK)
            lane = iota((BLOCK, LANES), 1)
            for h in range(heads):
                s = dot_nt(qx[h, here, :], kx[h, :span, :])
                top = jnp.max(s, axis=-1, keepdims=True)
                o = dot(jnp.exp(s - top).astype(BF), vx[h, :span, :])
                total = o[:, HD : HD + 1]
                o = o / total
                for i, piece in enumerate(pieces(top + jnp.log(total))):
                    o = jnp.where(lane == HD + i, piece.astype(F32), o)
                place[h, here, :] = o.astype(BF)

    for blocks in range(groups * TILE // BLOCK, groups * rows // BLOCK + 1):
        pl.when(k_blocks == blocks)(functools.partial(attend_all, blocks * BLOCK))

    gather = [
        (iota((LANES, LANES), 0) - HD + 3 * h == iota((LANES, LANES), 1))
        & (iota((LANES, LANES), 0) >= HD)
        & (iota((LANES, LANES), 0) < HD + 3)
        for h in range(heads)
    ]
    gather = [jnp.where(m, 1.0, 0.0).astype(BF) for m in gather]
    start = jnp.int32(0)
    for g in range(groups):
        mine = [place[h, rows_at(start, rows), :] for h in range(heads)]
        stats = sum(dot(m, s) for m, s in zip(mine, gather)).astype(BF)
        value = jnp.concatenate([m[:, :HD] for m in mine] + [stats], axis=1)
        if g < groups // 2:
            out[g][...] = value
        else:
            give[g - groups // 2] = value
        start = start + q_counts[g] * TILE
    for copy in copies:
        copy.wait()


def attend(near, far, weights, biases, gains, shifts, rows, heads):
    groups = len(near)
    model = near[0].shape[1]
    room = rows * groups + BLOCK
    parts = heads * HD + LANES
    kept = [(room, model)] * 2 + [(heads, room, LANES)] * 3
    return local_call(
        functools.partial(attend_kernel, rows, groups, heads),
        "attend",
        (
            *[shaped(rows, parts)] * (groups // 2),
            shaped(groups // 2, rows, parts),
            *[shaped(*k) for k in kept],
            shaped(2 * groups, dtype=jnp.int32),
        ),
        [VMEM] * (groups + 5),
        (*[VMEM] * (groups // 2 + 1), *[ANY] * 5, SMEM),
        (*near, far, weights, biases, gains, shifts),
        [
            pltpu.VMEM((heads, room, LANES), BF),
            *[pltpu.VMEM(k, BF) for k in kept],
            pltpu.SemaphoreType.DMA((5,)),
        ],
        cost(15),
        ROOM,
    )


def same_tile(rows):
    return iota((rows, rows), 0) // TILE == iota((rows, rows), 1) // TILE


def thumb_kernel(heads, tokens, weights, biases, gains, shifts, out, xhat, x):
    width = heads * LANES
    size = tokens.shape[0]
    clean = standard(tokens[...].astype(F32))[0].astype(BF)
    xhat[...] = clean
    hidden = (clean.astype(F32) * gains[0:1, :] + shifts[0:1, :]).astype(BF)
    x[...] = (dot(hidden, weights[...]) + biases[...]).astype(BF)
    visible = same_tile(size - TILE)
    out[:TILE, :] = jnp.zeros((TILE, heads * HD), F32)
    for h in range(heads):
        q = x[TILE:, h * LANES : (h + 1) * LANES]
        k = x[TILE:, width + h * LANES : width + (h + 1) * LANES]
        v = x[TILE:, 2 * width + h * LANES : 2 * width + (h + 1) * LANES]
        s = jnp.where(visible, dot_nt(q, k), FAR)
        e = jnp.exp(s - jnp.max(s, axis=-1, keepdims=True))
        o = dot(e.astype(BF), v)[:, :HD] / jnp.sum(e, axis=-1, keepdims=True)
        out[TILE:, h * HD : (h + 1) * HD] = o


def thumbs(tokens, weights, biases, gains, shifts, heads):
    size, model = tokens.shape
    return local_call(
        functools.partial(thumb_kernel, heads),
        "thumbs",
        (
            shaped(size, heads * HD, dtype=F32),
            shaped(size, model),
            shaped(size, 3 * heads * LANES),
        ),
        [VMEM] * 5,
        (VMEM,) * 3,
        (tokens, weights, biases, gains, shifts),
        cost=cost(5),
    )


def merged(parts, heads):
    cols = heads * HD
    row, col = (iota((LANES, cols), d) for d in (0, 1))
    spread = zero_one(row // 3 == col // HD)
    marks = [dot(p[:, cols:], spread) for p in parts]
    top = functools.reduce(jnp.maximum, marks)
    expos = [jnp.exp(m - top) for m in marks]
    total = sum(expos)
    mixed = sum(e * p[:, :cols].astype(F32) for p, e in zip(parts, expos)) / total
    row, col = (iota((cols, LANES), d) for d in (0, 1))
    packed = [
        dot(piece, zero_one((row % HD == 0) & (col == 3 * (row // HD) + i)))
        for i, piece in enumerate(pieces(top + jnp.log(total)))
    ]
    return mixed, sum(packed)


def pair_kernel(heads, *refs):
    count = (len(refs) - 1) // 2
    for j, (mine, out) in enumerate(zip(refs[:count], refs[count + 1 :])):
        mixed, marks = merged([mine[...], refs[count][j]], heads)
        out[...] = jnp.concatenate([mixed.astype(BF), marks.astype(BF)], axis=1)


def pair_merge(parts, other, heads):
    return local_call(
        functools.partial(pair_kernel, heads),
        "pair_merge",
        tuple(shaped(*p.shape) for p in parts),
        [VMEM] * (len(parts) + 1),
        (VMEM,) * len(parts),
        (*parts, other),
        cost=cost(3),
        room=ROOM,
    )


def merge_kernel(heads, counts, thumb, *refs):
    parts, (low, full, lse) = refs[:-3], refs[-3:]
    cols = heads * HD
    rows = lse.shape[0]
    mixed, marks = merged([p[...] for p in parts], heads)
    lse[...] = (-marks).astype(BF)
    image = iota((rows, cols), 0) < counts[0] * TILE
    full[:rows, :] = jnp.where(image, mixed, thumb[:rows, :])
    full[rows:, :] = thumb[rows:, :]
    low[...] = full[...].astype(BF)


def merge(count, parts, thumb, heads):
    size, cols = thumb.shape
    return local_call(
        functools.partial(merge_kernel, heads),
        "merge",
        (shaped(size, cols), shaped(size, cols, dtype=F32), shaped(parts[0].shape[0], LANES)),
        [SMEM] + [VMEM] * (1 + len(parts)),
        (VMEM,) * 3,
        (count, thumb, *parts),
        cost=cost(3),
    )


def fold_kernel(*refs):
    count = (len(refs) - 1) // 2
    for j, (mine, out) in enumerate(zip(refs[:count], refs[count + 1 :])):
        out[...] = (mine[...].astype(F32) + refs[count][j].astype(F32)).astype(BF)


def fold(parts, other):
    return local_call(
        fold_kernel,
        "fold",
        tuple(shaped(*p.shape) for p in parts),
        [VMEM] * (len(parts) + 1),
        (VMEM,) * len(parts),
        (*parts, other),
        cost=cost(2),
        room=ROOM,
    )


ROOT = 0.7978845608028654
CUBE = 0.044715


def ff_kernel(
    heads, tokens, outer, low, low_far, full, lse, out_weight, out_far, up, up_bias, down, far_one,
    far_two, gains, shifts, mixed, grad_mid, grad_low, packed, hidden_out, act_out, pre_out, small,
):
    size, model = tokens.shape
    passes = outer.shape[0]
    cols = heads * HD
    chunk = far_one.shape[1]
    units = up.shape[1]
    rows = packed.shape[0]
    branch = dot(low[...], out_weight[...]) + dot(low_far[...], out_far[...])
    middle = tokens[...].astype(F32) + (branch + shifts[1:2, :])
    xhat, factor = standard(middle)
    hidden = (xhat * gains[1:2, :] + shifts[2:3, :]).astype(BF)
    hidden_out[...] = hidden

    def one_chunk(up_part, bias, down_part, keep):
        v = dot(hidden, up_part) + bias
        t = jnp.tanh(ROOT * (v + CUBE * (v * v * v)))
        act = (0.5 * v * (1.0 + t)).astype(BF)
        slope = 0.5 * (1.0 + t) + 0.5 * v * (1.0 - t * t) * (ROOT * (1.0 + 3.0 * CUBE * (v * v)))
        two = []
        for p in range(passes):
            pre = (dot_nt(outer[p], down_part) * slope).astype(BF)
            if keep is not None:
                pre_out[p, :, keep] = pre
            two.append(dot_nt(pre, up_part))
        if keep is not None:
            act_out[:, keep] = act
        return dot(act, down_part), two

    def far_chunk(ref):
        told = ref[2 * chunk : 2 * chunk + 16, :].astype(F32)
        bias = told[0:1] + told[1:2] + told[2:3]
        return one_chunk(ref[:chunk, :], bias, ref[chunk : 2 * chunk, :], None)

    done = []
    for i in range(units // chunk):
        at = slice(i * chunk, (i + 1) * chunk)
        done.append(one_chunk(up[:, at], up_bias[:, at], down[at, :], at))
    done += [far_chunk(far_one), far_chunk(far_two)]

    def tree(parts):
        half = len(parts) // 2
        return sum(parts[:half]) + sum(parts[half:])

    output = tree([d[0] for d in done])
    mixed[...] = (middle + (output + shifts[3:4, :])).astype(BF)
    small[...] = jnp.zeros(small.shape, F32)
    lane = iota((rows, LANES), 1)
    stats = jnp.zeros((rows, LANES), F32)
    for p in range(passes):
        two = tree([d[1][p] for d in done])
        c = outer[p].astype(F32)
        mid = c + norm_back(two, gains[1:2, :], xhat, factor)
        mid_low = mid.astype(BF)
        grad_mid[p] = mid
        grad_low[p] = mid_low
        att = dot_nt(mid_low, out_weight[...]).astype(BF)
        packed[:, p * cols : (p + 1) * cols] = att[:rows, :]
        pre_out_p = pre_out[p].astype(F32)
        bias = jnp.sum(pre_out_p, axis=0, keepdims=True)
        small[p, 0:1, :] = jnp.sum(two * xhat, axis=0, keepdims=True)
        small[p, 1:2, :] = jnp.sum(two, axis=0, keepdims=True)
        small[p, 2:3, :] = jnp.sum(mid_low.astype(F32), axis=0, keepdims=True)
        small[p, 3:4, :] = jnp.sum(c, axis=0, keepdims=True)
        for i in range(units // model):
            small[p, 4 + i : 5 + i, :] = bias[:, i * model : (i + 1) * model]
        product = att[:rows, :].astype(F32) * full[:rows, :]
        for h in range(heads):
            delta = jnp.sum(product[:, h * HD : (h + 1) * HD], axis=-1, keepdims=True)
            for i, piece in enumerate(pieces(-delta)):
                stats = jnp.where(lane == 3 * heads * (p + 1) + 3 * h + i, piece.astype(F32), stats)
    packed[:, passes * cols :] = (stats + lse[...].astype(F32)).astype(BF)


def feed_forward(
    tokens, outer, low, low_far, full, lse, out_weight, out_far, up, up_bias, down, far_one, far_two,
    gains, shifts, rows, heads,
):
    size, model = tokens.shape
    passes = outer.shape[0]
    units = up.shape[1]
    return local_call(
        functools.partial(ff_kernel, heads),
        "feed_forward",
        (
            shaped(size, model),
            shaped(passes, size, model, dtype=F32),
            shaped(passes, size, model),
            shaped(rows, passes * heads * HD + LANES),
            shaped(size, model),
            shaped(size, units),
            shaped(passes, size, units),
            shaped(passes, 8, model, dtype=F32),
        ),
        [VMEM] * 15,
        (VMEM,) * 8,
        (
            tokens, outer, low, low_far, full, lse, out_weight, out_far, up, up_bias, down, far_one,
            far_two, gains, shifts,
        ),
        cost=cost(12),
        room=32,
    )


def thumb_back_kernel(heads, counts, x, mid_low, out_weight, out):
    width = heads * LANES
    size = x.shape[0]
    passes = mid_low.shape[0]
    visible = same_tile(size - TILE)
    outside = iota((size - TILE, HD), 0) + TILE >= counts[0] * TILE
    grads = [dot_nt(mid_low[p], out_weight[...]).astype(BF) for p in range(passes)]
    out[:, :, :TILE, :] = jnp.zeros((*out.shape[:2], TILE, out.shape[3]), BF)
    for h in range(heads):
        q = x[TILE:, h * LANES : (h + 1) * LANES]
        k = x[TILE:, width + h * LANES : width + (h + 1) * LANES]
        v = x[TILE:, 2 * width + h * LANES : 2 * width + h * LANES + HD]
        s = jnp.where(visible, dot_nt(q, k), FAR)
        e = jnp.exp(s - jnp.max(s, axis=-1, keepdims=True))
        w = e / jnp.sum(e, axis=-1, keepdims=True)
        w_low = w.astype(BF)
        for p in range(passes):
            g = grads[p][TILE:, h * HD : (h + 1) * HD]
            gw = dot_nt(g, v)
            ds = (w * (gw - jnp.sum(w * gw, axis=-1, keepdims=True))).astype(BF)
            dq = dot(ds, k[:, :HD]) * SCALE
            dk = dot_tn(ds, q)[:, :HD]
            dv = dot_tn(w_low, g)
            for c, piece in enumerate((dq, dk, dv)):
                at = c * LANES + (h % 2) * HD
                out[h // 2, p, TILE:, at : at + HD] = jnp.where(outside, piece, 0.0).astype(BF)


def thumbs_back(count, x, mid_low, out_weight, heads):
    passes, size, _ = mid_low.shape
    return local_call(
        functools.partial(thumb_back_kernel, heads),
        "thumbs_back",
        shaped(heads // 2, passes, size, 3 * LANES),
        [SMEM] + [VMEM] * 3,
        VMEM,
        (count, x, mid_low, out_weight),
        cost=cost(6),
    )


def early_at(units, model, low):
    ends = [model, 2 * model, 2 * model + units, 2 * model + units + low]
    return [slice(b - w, b) for b, w in zip(ends, (model, model, units, low))]


def early_cuts(parts, units, model, low):
    high, wide, turns = units // parts // 2, model // parts, model // low
    narrow = low * turns // parts
    for i in range(parts):
        yield (
            (slice(2 * i * high, (2 * i + 1) * high), slice(0, model)),
            (slice((2 * i + 1) * high, (2 * i + 2) * high), slice(0, model)),
            (slice(i * wide, (i + 1) * wide), slice(0, units)),
            (
                slice(i // turns * narrow, (i // turns + 1) * narrow),
                slice(i % turns * low, (i % turns + 1) * low),
            ),
        )


def weight_kernel(place, act, outer, hidden, pre, low, mid_low, keep, give):
    units, model, cols = act.shape[1], hidden.shape[1], low.shape[1]
    core = place[0]
    for turn, out in ((core, keep), (1 - core, give)):
        down = dot_tn(act[...], outer[turn]).astype(BF)
        up = dot_tn(hidden[...], pre[turn]).astype(BF)
        proj = dot_tn(low[...], mid_low[turn]).astype(BF)
        for i, cut in enumerate(early_cuts(keep.shape[0], units, model, cols)):
            for value, (rows, lanes), at in zip(
                (down, down, up, proj), cut, early_at(units, model, cols)
            ):
                out[i, :, at] = value[rows, lanes]


def weight_grads(core, act, outer, hidden, pre, low, mid_low, parts):
    units, model = act.shape[1], outer.shape[2]
    out = shaped(parts, model // parts, 2 * model + units + low.shape[1])
    return local_call(
        weight_kernel,
        "weight_grads",
        (out, out),
        [SMEM] + [VMEM] * 6,
        (VMEM,) * 2,
        (core, act, outer, hidden, pre, low, mid_low),
        cost=cost(8),
        room=24,
    )


def reverse_kernel(rows, groups, heads, passes, counts, place, *refs):
    grads, kept = refs[:groups], refs[groups : groups + 5]
    own, thumb, weights, columns, small = refs[groups + 5 : groups + 10]
    at = groups + 10
    out_q, give_q, at = refs[at : at + groups // 2], refs[at + groups // 2], at + groups // 2 + 1
    out_kv, at = refs[at : at + groups // 2], at + groups // 2
    keep, give = refs[at : at + 2]
    (
        stage, xq, xk, qx, kx, vx, packed, gx, kt, dq_t, dv, dk, low_q, low_kv, total, sums,
        starts, sems,
    ) = refs[at + 2 :]
    couples = heads // 2
    sources = [*grads, *kept[2:], *kept[:2]]
    targets = [*[stage.at[g] for g in range(groups)], qx, kx, vx, xq, xk]
    copies = [
        pltpu.make_async_copy(f, t, sems.at[i]) for i, (f, t) in enumerate(zip(sources, targets))
    ]
    for copy in copies:
        copy.start()
    cols = heads * HD
    wide = passes * LANES
    q_counts = [counts[g] for g in range(groups)]
    k_counts = [counts[groups + g] for g in range(groups)]
    start = jnp.int32(0)
    for g in range(groups):
        copies[g].wait()
        packed[rows_at(start, rows), :] = stage[g]
        start = start + q_counts[g] * TILE
    q_total, k_total = start, sum(k_counts) * TILE
    tail_lane = iota((BLOCK, packed.shape[1]), 1) - passes * cols
    empty = (tail_lane >= 0) & (tail_lane < 3 * heads) & (tail_lane % 3 == 0)
    packed[rows_at(q_total, BLOCK), :] = jnp.where(empty, FAR, 0.0).astype(BF)
    q_blocks = (q_total + BLOCK - 1) // BLOCK
    k_blocks = (k_total + BLOCK - 1) // BLOCK
    spans = range(groups * TILE // BLOCK, groups * rows // BLOCK + 1)

    row, col = (iota((LANES, heads * LANES), d) for d in (0, 1))
    head, lane = col // LANES, col % LANES
    to_marks = zero_one((lane > HD) & (lane < HD + 4) & (row == 3 * head + lane - HD - 1))
    row, col = (iota((LANES, heads * wide), d) for d in (0, 1))
    head, turn, lane = col // wide, col % wide // LANES, col % LANES
    to_deltas = zero_one(
        (lane >= HD) & (lane < HD + 3) & (row == 3 * heads * (turn + 1) + 3 * head + lane - HD)
    )
    for copy in copies[groups : groups + 3]:
        copy.wait()

    @pl.loop(0, q_blocks)
    def _(b):
        here = rows_at(b * BLOCK, BLOCK, BLOCK)
        stats = packed[here, passes * cols :]
        marks = dot(stats, to_marks)
        deltas = dot(stats, to_deltas).astype(BF)
        for h in range(heads):
            more = marks[:, h * LANES : (h + 1) * LANES]
            qx[h, here, :] = (qx[h, here, :].astype(F32) + more).astype(BF)
            for p in range(passes):
                at = p * cols + h * HD
                mine = (h * passes + p) * LANES
                gx[h, here, p * LANES : (p + 1) * LANES] = jnp.concatenate(
                    [packed[here, at : at + HD], deltas[:, mine + HD : mine + LANES]], axis=1
                )

    @pl.loop(0, k_blocks)
    def _(b):
        here = rows_at(b * BLOCK, BLOCK, BLOCK)
        for h in range(heads):
            kt[h, b] = jnp.transpose(kx[h, here, :].astype(F32))[:HD, :].astype(BF)

    def reverse_all(blocks):
        span = blocks * BLOCK

        @pl.loop(0, couples)
        def _(pair):
            dv[:, :span, :] = jnp.zeros((2, span, wide), F32)
            dk[:, :, :span, :] = jnp.zeros((passes, 2, span, LANES), F32)

            @pl.loop(0, q_blocks)
            def _(b):
                here = rows_at(b * BLOCK, BLOCK, BLOCK)
                for i in range(2):
                    h = 2 * pair + i
                    q, g = qx[h, here, :], gx[h, here, :]
                    k_t = jnp.concatenate([kt[h, j] for j in range(blocks)], axis=1)
                    w = jnp.exp(dot_nt(kx[h, :span, :], q))
                    dv[i, :span, :] += dot(w.astype(BF), g)
                    for p in range(passes):
                        ds = dot_nt(vx[h, :span, :], g[:, p * LANES : (p + 1) * LANES])
                        ds = (w * ds).astype(BF)
                        dk[p, i, :span, :] += dot(ds, q)
                        dq_t[p, i * HD : (i + 1) * HD, :] = dot(k_t, ds)
                for p in range(passes):
                    piece = jnp.transpose(dq_t[p]) * SCALE
                    low_q[pair, here, p * LANES : (p + 1) * LANES] = piece.astype(BF)

            for p in range(passes):
                for c, both in enumerate(
                    (
                        [dk[p, i, :span, :HD] for i in range(2)],
                        [dv[i, :span, p * LANES : p * LANES + HD] for i in range(2)],
                    )
                ):
                    lane = (2 * p + c) * LANES
                    low_kv[pair, :span, lane : lane + LANES] = jnp.concatenate(both, axis=1).astype(BF)

    for blocks in spans:
        pl.when(k_blocks == blocks)(functools.partial(reverse_all, blocks))

    start = jnp.int32(0)
    for g in range(groups):
        starts[g] = start
        start = start + k_counts[g] * TILE
    for g in range(groups):
        here = rows_at(starts[place[1 + g]], rows)
        out_kv[g // 2][g % 2] = jnp.concatenate([low_kv[i, here, :] for i in range(couples)], axis=1)
    start = jnp.int32(0)
    for g in range(groups):
        here = rows_at(start, rows)
        value = jnp.concatenate([low_q[i, here, :] for i in range(couples)], axis=1)
        if g < groups // 2:
            out_q[g][...] = value
        else:
            give_q[g - groups // 2] = value
        start = start + q_counts[g] * TILE

    copies[groups + 3].wait()
    copies[groups + 4].wait()

    def key_sums(blocks):
        span = blocks * BLOCK
        for i in range(couples):
            flat = low_kv[i, :span, :]
            total[i, :, wide:] = dot_tn(xk[:span, :], flat)
            sums[i, :, wide:] = dot(jnp.ones((8, span), BF), flat)

    for blocks in spans:
        pl.when(k_blocks == blocks)(functools.partial(key_sums, blocks))

    total[:, :, :wide] = jnp.zeros((couples, total.shape[1], wide), F32)
    sums[:, :, :wide] = jnp.zeros((couples, 8, wide), F32)

    @pl.loop(0, q_blocks)
    def _(b):
        here = rows_at(b * BLOCK, BLOCK, BLOCK)
        for i in range(couples):
            total[i, :, :wide] += dot_tn(xq[here, :], low_q[i, here, :])
            sums[i, :, :wide] += dot(jnp.ones((8, BLOCK), BF), low_q[i, here, :])

    model = total.shape[1]
    gain, shift = columns[:, 0:1], columns[:, 1:2]
    ones = jnp.ones((8, own.shape[0]), BF)
    for p in range(passes):
        whole = []
        for i in range(couples):
            mine = thumb[i, p]
            part = dot_tn(own[...], mine)
            part_sum = dot(ones, mine)[0:1, :]
            q_at = slice(p * LANES, (p + 1) * LANES)
            kv_at = slice((passes + 2 * p) * LANES, (passes + 2 * p + 2) * LANES)
            part += jnp.concatenate([total[i, :, q_at], total[i, :, kv_at]], axis=1)
            part_sum += jnp.concatenate([sums[i, 0:1, q_at], sums[i, 0:1, kv_at]], axis=1)
            w = weights[i].astype(F32)
            gain_one = jnp.sum(w * part, axis=1, keepdims=True)
            shift_one = jnp.sum(w * part_sum, axis=1, keepdims=True)
            lane = iota((model, LANES), 1)
            tall = jnp.where(lane == 0, gain_one, jnp.where(lane == 1, shift_one, 0.0))
            flat = jnp.concatenate(
                [jnp.zeros((2, LANES), F32)]
                + [part_sum[:, c * LANES : (c + 1) * LANES] for c in range(3)]
                + [jnp.zeros((LANES - 5, LANES), F32)],
                axis=0,
            )
            tall = jnp.concatenate([tall[:LANES] + jnp.transpose(flat), tall[LANES:]], axis=0)
            if i == 0:
                turned = jnp.concatenate(
                    [
                        jnp.zeros((8, model), F32),
                        small[p],
                        jnp.zeros((LANES - 16, model), F32),
                    ],
                    axis=0,
                )
                tall = tall + jnp.transpose(turned)
            whole += [part * gain + shift * part_sum, tall]
        whole = jnp.concatenate(whole, axis=1).astype(BF)

        @pl.when(place[0] == p)
        def _():
            keep[...] = whole

        @pl.when(place[0] != p)
        def _():
            give[...] = whole


def reverse(counts, place, grads, kept, own, thumb, weights, columns, small, rows, heads):
    groups = len(grads)
    couples, passes = thumb.shape[:2]
    model = own.shape[1]
    room = rows * groups + BLOCK
    cols = heads * HD
    wide = passes * LANES
    half = groups // 2
    late = shaped(model, couples * 4 * LANES)
    q, kv = shaped(rows, couples * wide), shaped(2, rows, couples * 2 * wide)
    out = (*[q] * half, shaped(half, rows, couples * wide), *[kv] * half, late, late)
    return local_call(
        functools.partial(reverse_kernel, rows, groups, heads, passes),
        "reverse",
        out,
        [SMEM, SMEM] + [ANY] * (groups + 5) + [VMEM] * 5,
        (VMEM,) * len(out),
        (counts, place, *grads, *kept, own, thumb, weights, columns, small),
        [
            pltpu.VMEM((groups, rows, passes * cols + LANES), BF),
            pltpu.VMEM((room, model), BF),
            pltpu.VMEM((room, model), BF),
            pltpu.VMEM((heads, room, LANES), BF),
            pltpu.VMEM((heads, room, LANES), BF),
            pltpu.VMEM((heads, room, LANES), BF),
            pltpu.VMEM((room, passes * cols + LANES), BF),
            pltpu.VMEM((heads, room, wide), BF),
            pltpu.VMEM((heads, room // BLOCK, HD, BLOCK), BF),
            pltpu.VMEM((passes, LANES, BLOCK), F32),
            pltpu.VMEM((2, room, wide), F32),
            pltpu.VMEM((passes, 2, room, LANES), F32),
            pltpu.VMEM((couples, room, wide), BF),
            pltpu.VMEM((couples, room, 2 * wide), BF),
            pltpu.VMEM((couples, model, 3 * wide), F32),
            pltpu.VMEM((couples, 8, 3 * wide), F32),
            pltpu.SMEM((groups,), jnp.int32),
            pltpu.SemaphoreType.DMA((groups + 5,)),
        ],
        cost(45),
        ROOM,
    )


def grad_one_kernel(near, counts, *refs):
    from_q, from_kv, (thumb, weights, mine, other) = refs[:near], refs[near:-4], refs[-4:]
    couples, passes, size, _ = thumb.shape
    rows = from_q[0].shape[0]
    sum_q = sum(r[...].astype(F32) for r in from_q)
    sum_kv = [sum(r[f].astype(F32) for r in from_kv) for f in range(2)]
    image = iota((rows, 3 * LANES), 0) < counts[0] * TILE
    for p in range(passes):
        parts = []
        for i in range(couples):
            at = (passes * i + p) * LANES
            there = slice(2 * at, 2 * at + 2 * LANES)
            far = jnp.concatenate([sum_q[:, at : at + LANES], sum_kv[0][:, there]], axis=1)
            flat = jnp.concatenate(
                [jnp.where(image, far.astype(BF), thumb[i, p, :rows]), thumb[i, p, rows:]], axis=0
            )
            parts.append(
                (
                    dot_nt(flat, weights[i]),
                    dot_nt(sum_kv[1][:, there].astype(BF), weights[i, :, LANES:]),
                )
            )
        mine[p] = sum(a for a, _ in parts).astype(BF)
        other[p] = sum(b for _, b in parts).astype(BF)


def grad_one(count, from_q, from_kv, thumb, weights):
    near = len(from_q)
    passes, size, _ = thumb.shape[1:]
    model = weights.shape[1]
    return local_call(
        functools.partial(grad_one_kernel, near),
        "grad_one",
        (shaped(passes, size, model), shaped(passes, from_q[0].shape[0], model)),
        [SMEM] + [VMEM] * (near + len(from_kv) + 2),
        (VMEM,) * 2,
        (count, *from_q, *from_kv, thumb, weights),
        cost=cost(5),
        room=ROOM,
    )


def close_kernel(counts, tokens, mid, mine, head, side, cross, gains, out):
    xhat, factor = standard(tokens[...].astype(F32))
    rows = side.shape[1]
    image = iota(side.shape[1:], 0) < counts[0] * TILE
    for p in range(mid.shape[0]):
        grad = mine[p].astype(F32) + head[p].astype(F32)
        more = jnp.where(image, side[p].astype(F32) + cross[p].astype(F32), 0.0)
        grad = jnp.concatenate([grad[:rows] + more, grad[rows:]], axis=0)
        out[p] = mid[p] + norm_back(grad, gains[0:1, :], xhat, factor)


def close(count, tokens, mid, mine, head, side, cross, gains):
    return local_call(
        close_kernel,
        "close",
        shaped(*mid.shape, dtype=F32),
        [SMEM] + [VMEM] * 7,
        VMEM,
        (count, tokens, mid, mine, head, side, cross, gains),
        cost=cost(4),
        room=ROOM,
    )


def early_kernel(lines, far, place, *refs):
    parts, refs = refs[:lines], refs[lines:]
    out, (down, up, proj, sems) = refs[-7:-4], refs[-4:]
    turn, y = place[0], place[10]
    turn = 1 - turn if far else turn
    (units, model), low = down.shape, proj.shape[0]
    steps, rows = parts[0].shape[:2]
    lane_down, lane_next, lane_up, lane_proj = early_at(units, model, low)
    turns = model // low
    for d, ref in enumerate(parts):
        for j in range(steps):
            i = j * lines + (y + lines - d) % lines
            at = pl.multiple_of(2 * rows * i, 2 * rows)
            down[pl.ds(at, rows), :] = ref[j, :, lane_down].astype(F32)
            down[pl.ds(at + rows, rows), :] = ref[j, :, lane_next].astype(F32)
            up[rows_at(rows * i, rows, rows), :] = ref[j, :, lane_up].astype(F32)
            here = rows_at(i // turns * rows, rows, rows)
            value = ref[j, :, lane_proj].astype(F32)
            for t in range(turns):

                @pl.when(i % turns == t)
                def _(value=value, here=here, t=t):
                    proj[here, t * low : (t + 1) * low] = value

    copies = [
        pltpu.make_async_copy(held, to.at[turn], sems.at[n])
        for n, (held, to) in enumerate(zip((down, up, proj), out))
    ]
    for copy in copies:
        copy.start()
    for copy in copies:
        copy.wait()


def early_out(place, parts, before, units, low):
    model = len(parts) * parts[0].shape[0] * parts[0].shape[1]
    shapes = (units, model), (model, units), (low, model)
    return pl.pallas_call(
        functools.partial(early_kernel, len(parts), bool(before)),
        out_shape=tuple(shaped(2, *s, dtype=F32) for s in shapes),
        in_specs=[SMEM] + [VMEM] * len(parts) + [ANY] * len(before),
        out_specs=(ANY,) * 3,
        scratch_shapes=[
            *[pltpu.VMEM(s, F32) for s in shapes],
            pltpu.SemaphoreType.DMA((3,)),
        ],
        input_output_aliases={1 + len(parts) + i: i for i in range(len(before))},
        cost_estimate=cost(5),
        compiler_params=pltpu.CompilerParams(vmem_limit_bytes=ROOM * MIB),
        name="early_far" if before else "early_own",
    )(place, *parts, *before)


def late_kernel(far, place, ref, *refs):
    out, (grad_in, *small), sems = refs[-11:-6], refs[-6:-1], refs[-1]
    in_bias, up_bias, gains, shifts = small
    turn = 1 - place[0] if far else place[0]
    turned = []
    for pair in range(2):
        at = 4 * LANES * pair
        for c in range(3):
            grad_in[c, :, pair * LANES : (pair + 1) * LANES] = ref[
                :, at + c * LANES : at + (c + 1) * LANES
            ].astype(F32)
        turned.append(jnp.transpose(ref[:, at + 3 * LANES : at + 4 * LANES].astype(F32)))
    a, b = turned
    in_bias[...] = jnp.concatenate(
        [
            jnp.concatenate([a[2:3, :LANES], b[2:3, :LANES]], axis=1),
            jnp.concatenate([a[4:5, :LANES], b[4:5, :LANES]], axis=1),
        ],
        axis=0,
    )
    up_bias[...] = jnp.concatenate([a[12:13], a[13:14]], axis=1)
    gains[...] = jnp.concatenate([a[0:1] + b[0:1], a[8:9]], axis=0)
    shifts[...] = jnp.concatenate([a[1:2] + b[1:2], a[10:11], a[9:10], a[11:12]], axis=0)
    copies = [
        pltpu.make_async_copy(held, to.at[turn], sems.at[n])
        for n, (held, to) in enumerate(zip((grad_in, *small), out))
    ]
    for copy in copies:
        copy.start()
    for copy in copies:
        copy.wait()


def late_out(place, part, before, units):
    model = part.shape[0]
    shapes = (3, model, 2 * LANES), (2, 2 * LANES), (1, units), (2, model), (4, model)
    return pl.pallas_call(
        functools.partial(late_kernel, bool(before)),
        out_shape=tuple(shaped(2, *s, dtype=F32) for s in shapes),
        in_specs=[SMEM, VMEM] + [ANY] * len(before),
        out_specs=(ANY,) * 5,
        scratch_shapes=[
            *[pltpu.VMEM(s, F32) for s in shapes],
            pltpu.SemaphoreType.DMA((5,)),
        ],
        input_output_aliases={2 + i: i for i in range(len(before))},
        cost_estimate=cost(3),
        compiler_params=pltpu.CompilerParams(vmem_limit_bytes=ROOM * MIB),
        name="late_far" if before else "late_own",
    )(place, part, *before)


def gather_near(array):
    mine = [array] + [shift_by(array, "y", d) for d in range(1, lax.axis_size("y"))]
    return mine + [shift_by(a, "c", 1) for a in mine]


def return_near(parts):
    return [parts[0]] + [shift_by(p, "y", -j) for j, p in enumerate(parts) if j > 0]


def offsets(size):
    return [(step, flip) for step in range(size) for flip in range(2)]


def return_far(parts):
    return [parts[0]] + [shift_by(p, "z", step) for step, p in enumerate(parts) if step > 0]


PLANE = ("z", "y")


def core_sum(keep, give):
    return (keep.astype(F32) + shift_by(give, "c", 1).astype(F32)).astype(BF)


def crossed(array):
    n = lax.axis_size(("xl", "h"))
    return lax.ppermute(array, ("xl", "h"), [(i, n - 1 - i) for i in range(n)])


def across(low):
    done = low.astype(F32) + shift_by(low, "xl", 1).astype(F32)
    size = 4 * LANES
    ones = jnp.concatenate([low[:, i + 3 * LANES : i + size] for i in range(0, low.shape[1], size)], axis=1)
    more = shift_by(ones, "h", 1).astype(F32) + crossed(ones).astype(F32)
    more = jnp.where(jnp.arange(more.shape[1]) % LANES < 2, more, 0.0)
    nothing = jnp.zeros((low.shape[0], 3 * LANES), F32)
    laid = [[nothing, more[:, i : i + LANES]] for i in range(0, more.shape[1], LANES)]
    return (done + jnp.concatenate(sum(laid, []), axis=1)).astype(BF)


def tied(arrays, others):
    return lax.optimization_barrier((arrays, others))


def local(
    tokens,
    cotangents,
    segment_ids,
    in_weights,
    in_biases,
    out_weight,
    up_weight,
    up_biases,
    down_weight,
    gains,
    shifts,
):
    size, model = tokens.shape
    cols = in_weights.shape[2]
    heads = cols // HD
    rows = size - TILE
    units = up_weight.shape[1]
    c = lax.axis_index("c")

    told, copies, count = front(tokens, segment_ids, lax.axis_size(("z", "xl")))
    far = lax.all_to_all(copies, ("z", "xl"), 0, 0, tiled=True)
    near = gather_near(told)
    core = c.astype(jnp.int32).reshape(1)
    z, xl, z_size = lax.axis_index("z"), lax.axis_index("xl"), lax.axis_size("z")
    routes = [((z + step) % z_size) * 2 + (xl ^ flip) for step, flip in offsets(z_size)]
    place = jnp.stack([c, *routes, z, lax.axis_index("y")]).astype(jnp.int32)
    plane = lax.axis_size(PLANE)

    weights, biases, pairs, columns, bundle = prepare(
        core, in_weights, in_biases, gains, shifts, up_weight, down_weight, up_biases[None], heads
    )
    out_far = crossed(out_weight)
    far_one = crossed(bundle)
    far_two = shift_by(far_one, "c", 1)

    weights, (out_far, columns, place) = tied(weights, (out_far, columns, place))
    *parts, give, xq, xk, qx, kx, vx, counts = attend(
        near, far, weights, biases, gains, shifts, rows, heads
    )
    thumb_out, xhat, x = thumbs(tokens, weights, biases, gains, shifts, heads)
    parts = pair_merge(parts, shift_by(give, "c", 1), heads)
    low, full, lse = merge(count, return_near(parts), thumb_out, heads)
    low_far = shift_by(low, "h", 1)
    mixed, grad_mid, mid_low, packed, hidden, act, pre, small = feed_forward(
        tokens, cotangents, low, low_far, full, lse, out_weight, out_far, up_weight, up_biases[None],
        down_weight, far_one, far_two, gains, shifts, rows, heads,
    )
    grads = gather_near(packed)
    keep, give = weight_grads(core, act, cotangents, hidden, pre, low, mid_low, plane)
    mid_low, (keep, give) = tied(mid_low, (keep, give))
    thumb = thumbs_back(count, x, mid_low, out_weight, heads)
    early = core_sum(keep, give)

    grads, (early, thumb) = tied(grads, (early, thumb))
    early = lax.all_to_all(early, PLANE, 0, 0, tiled=True)
    *out, keep, give = reverse(
        counts, place, grads, (xq, xk, qx, kx, vx), xhat, thumb, pairs, columns, small, rows, heads
    )
    half = len(near) // 2
    out_q, give_q, out_kv = out[:half], out[half], out[half + 1 :]
    early = jnp.sum(early.astype(F32), axis=0).astype(BF)
    early = (early.astype(F32) + shift_by(early, "xl", 1).astype(F32)).astype(BF)
    early = jnp.broadcast_to(early[None], (z_size, *early.shape))
    late, early = tied(core_sum(keep, give), early)
    early = lax.all_to_all(early, "z", 0, 0, tiled=True)
    from_kv = return_far(out_kv)
    out_q = fold(out_q, shift_by(give_q, "c", 1))
    from_q = return_near(out_q)
    late, (early, from_kv[1], from_kv[-1], from_q) = tied(
        late, (early, from_kv[1], from_kv[-1], from_q)
    )
    late = late.reshape(plane, -1, late.shape[1])
    late = lax.all_to_all(late, PLANE, 0, 0, tiled=True)
    early = [early] + [shift_by(early, "y", d) for d in range(1, lax.axis_size("y"))]
    mine, other = grad_one(count, from_q, from_kv, thumb, pairs)
    late, (early[1], early[-1]) = tied(late, (early[1], early[-1]))
    late = across(jnp.sum(late.astype(F32), axis=0).astype(BF))
    arrived = [shift_by(mine, "h", 1), shift_by(other, "xl", 1), crossed(other)]
    late = jnp.broadcast_to(late[None], (plane, *late.shape))
    late = lax.all_to_all(late, PLANE, 0, 0, tiled=True).reshape(model, -1)

    early_far = [shift_by(e, "c", 1) for e in early]
    early, early_far = tied(early, early_far)
    early = early_out(place, early, (), units, cols)
    early = early_out(place, early_far, early, units, cols)
    late_far = shift_by(late, "c", 1)
    late = late_out(place, late, (), units)
    arrived, (early, late) = tied(arrived, (early, late))
    grad_tokens = close(count, tokens, grad_mid, mine, *arrived, gains)
    grad_down, grad_up, grad_out = early
    grad_in, in_bias, up_bias, grad_gains, grad_shifts = late_out(place, late_far, late, units)
    return (
        mixed,
        grad_tokens,
        grad_in,
        in_bias,
        grad_out,
        grad_up,
        up_bias.reshape(2, units),
        grad_down,
        grad_gains,
        grad_shifts,
    )


def solution(mesh):
    fine = Mesh(mesh.devices.reshape(4, 2, 4, 2, 2), ("z", "xl", "y", "c", "h"))
    blk = ("z", "xl", "y", "c")
    return jax.shard_map(
        local,
        mesh=fine,
        in_specs=(
            P(blk, None),
            P(None, blk, None),
            P(blk),
            P(None, None, "h"),
            P(None, "h"),
            P("h", None),
            P(None, "h"),
            P("h"),
            P("h", None),
            P(),
            P(),
        ),
        out_specs=(
            P(blk, None),
            P(None, blk, None),
            P(None, None, None, "h"),
            P(None, None, "h"),
            P(None, "h", None),
            P(None, None, "h"),
            P(None, "h"),
            P(None, "h", None),
            P(),
            P(),
        ),
        check_vma=False,
    )
```

```python
import functools

import jax
import jax.numpy as jnp
from jax import lax
from jax.experimental import pallas as pl
from jax.experimental.pallas import tpu as pltpu
from jax.sharding import Mesh
from jax.sharding import PartitionSpec as P

HD = 64
LANES = 128
TILE = 64
BLOCK = 256
EPS = 1e-06
SCALE = 0.125
FAR = -1e30
BF = jnp.bfloat16
F32 = jnp.float32
MIB = 1024 * 1024
ROOM = 56

NT = (((1,), (1,)), ((), ()))
TN = (((0,), (0,)), ((), ()))


def shift_by(array, axis, step):
    size = lax.axis_size(axis)
    return lax.ppermute(array, axis, [(i, (i + step) % size) for i in range(size)])


def dot(a, b):
    return jnp.dot(a, b, preferred_element_type=F32)


def dot_nt(a, b):
    return lax.dot_general(a, b, NT, preferred_element_type=F32)


def dot_tn(a, b):
    return lax.dot_general(a, b, TN, preferred_element_type=F32)


def standard(field):
    center = field - jnp.mean(field, axis=-1, keepdims=True)
    factor = lax.rsqrt(jnp.mean(center * center, axis=-1, keepdims=True) + EPS)
    return center * factor, factor


def norm_back(grad, gain, xhat, factor):
    h = grad * gain
    mean = jnp.mean(h, axis=-1, keepdims=True)
    return factor * (h - mean - xhat * jnp.mean(h * xhat, axis=-1, keepdims=True))


def pieces(value):
    high = value.astype(BF)
    rest = value - high.astype(F32)
    middle = rest.astype(BF)
    low = (rest - middle.astype(F32)).astype(BF)
    return high, middle, low


def zero_one(mask):
    return jnp.where(mask, 1.0, 0.0).astype(BF)


def iota(shape, dim):
    return lax.broadcasted_iota(jnp.int32, shape, dim)


VMEM = pl.BlockSpec(memory_space=pltpu.VMEM)
ANY = pl.BlockSpec(memory_space=pl.ANY)
SMEM = pl.BlockSpec(memory_space=pltpu.SMEM)


def local_call(body, name, out, ins, outs, args, scratch=(), cost=None, room=16):
    return pl.pallas_call(
        body,
        out_shape=out,
        in_specs=ins,
        out_specs=outs,
        scratch_shapes=scratch,
        cost_estimate=cost,
        compiler_params=pltpu.CompilerParams(vmem_limit_bytes=room * MIB),
        name=name,
    )(*args)


def shaped(*shape, dtype=BF):
    return jax.ShapeDtypeStruct(shape, dtype)


def cost(micros):
    return pl.CostEstimate(flops=int(micros * 1e9), bytes_accessed=0, transcendentals=0)


def front_kernel(tokens, ids, told, copies, number):
    rows = told.shape[0] - 16
    marks = jnp.where(ids[...] == 0, 1.0, 0.0)
    tiles = jnp.sum(marks).astype(jnp.int32) // TILE
    number[0] = tiles
    told[:rows, :] = tokens[:rows, :]
    told[rows:, :] = jnp.full((16, told.shape[1]), tiles.astype(F32), F32).astype(BF)
    for g in range(copies.shape[0]):
        copies[g] = told[...]


def front(tokens, ids, copies):
    size, model = tokens.shape
    told = size - TILE + 16
    return local_call(
        front_kernel,
        "front",
        (shaped(told, model), shaped(copies, told, model), shaped(1, dtype=jnp.int32)),
        [VMEM, VMEM],
        (VMEM, VMEM, SMEM),
        (tokens, ids.reshape(-1, LANES)),
        room=ROOM,
    )


def prepare_kernel(
    heads, place, in_weights, in_biases, gains, shifts, up, down, bias,
    weights, biases, pairs, columns, out,
):
    core = place[0]
    half = out.shape[1]
    at = pl.ds(pl.multiple_of(core * half, half), half)
    out[:half, :] = up[:, at]
    out[half : 2 * half, :] = down[at, :]
    mine = jnp.where(core == 0, bias[:, :half], bias[:, half:])
    row = iota((16, half), 0)
    rows = jnp.zeros((16, half), F32)
    for i, piece in enumerate(pieces(mine)):
        rows = jnp.where(row == i, piece.astype(F32), rows)
    out[2 * half :, :] = rows.astype(BF)

    model, cols = in_weights.shape[1:]
    width = heads * LANES
    row, col = (iota((cols, width), d) for d in (0, 1))
    spread = zero_one((row // HD == col // LANES) & (row % HD == col % LANES))
    lane = iota((1, width), 1) % LANES
    gap = jnp.zeros((1, HD), F32)

    def apart(line):
        return jnp.concatenate(
            sum([[line[:, h * HD : (h + 1) * HD], gap] for h in range(heads)], []), axis=1
        )

    extra = [
        apart(in_biases[0:1, :] * SCALE) + jnp.where(lane == HD, 1.0, 0.0),
        jnp.where((lane > HD) & (lane < HD + 4), 1.0, 0.0),
        apart(in_biases[1:2, :]) + jnp.where((lane >= HD) & (lane < HD + 3), 1.0, 0.0),
    ]
    for i in range(3):
        factor = SCALE if i == 0 else 1.0
        weights[:, i * width : (i + 1) * width] = (dot(in_weights[i], spread) * factor).astype(BF)
        biases[:, i * width : (i + 1) * width] = extra[i]
        for pair in range(heads // 2):
            pairs[pair, :, i * LANES : (i + 1) * LANES] = in_weights[
                i, :, pair * LANES : (pair + 1) * LANES
            ]
    tall = jnp.concatenate(
        [gains[0:1, :], shifts[0:1, :], jnp.zeros((LANES - 2, model), F32)], axis=0
    )
    columns[...] = jnp.transpose(tall)


def prepare(core, in_weights, in_biases, gains, shifts, up, down, bias, heads):
    model = up.shape[0]
    width = 3 * heads * LANES
    return local_call(
        functools.partial(prepare_kernel, heads),
        "prepare",
        (
            shaped(model, width),
            shaped(1, width, dtype=F32),
            shaped(heads // 2, model, 3 * LANES),
            shaped(model, LANES, dtype=F32),
            shaped(2 * model + 16, model),
        ),
        [SMEM] + [VMEM] * 7,
        (VMEM,) * 5,
        (core, in_weights, in_biases, gains, shifts, up, down, bias),
        cost=cost(4),
        room=ROOM,
    )


def count_of(ref, rows):
    return jnp.max(ref[rows : rows + 16, :LANES].astype(F32)).astype(jnp.int32)


def rows_at(start, rows, step=TILE):
    return pl.ds(pl.multiple_of(start, step), rows)


def attend_kernel(rows, groups, heads, *refs):
    near, far = refs[:groups], refs[groups]
    weights, biases, gains, shifts = refs[groups + 1 : groups + 5]
    at = groups + 5 + groups // 2
    out, give = refs[groups + 5 : at], refs[at]
    kept, counts, place = refs[at + 1 : at + 6], refs[at + 6], refs[at + 7]
    (xq, xk, qx, kx, vx), sems = refs[at + 8 : at + 13], refs[at + 13]
    model = xq.shape[1]
    q_counts = [count_of(r, rows) for r in near]
    k_counts = [count_of(far.at[g], rows) for g in range(groups)]
    for g in range(groups):
        counts[g] = q_counts[g]
        counts[groups + g] = k_counts[g]

    def compact(numbers, read, target):
        start = jnp.int32(0)
        for g, n in enumerate(numbers):
            target[rows_at(start, rows), :] = read(g)
            start = start + n * TILE
        target[rows_at(start, BLOCK), :] = jnp.zeros((BLOCK, model), BF)
        return start

    q_total = compact(q_counts, lambda g: near[g][:rows, :], xq)
    k_total = compact(k_counts, lambda g: far[g, :rows, :], xk)
    q_blocks = (q_total + BLOCK - 1) // BLOCK
    k_blocks = (k_total + BLOCK - 1) // BLOCK
    width = heads * LANES

    def hidden(ref, here):
        clean = standard(ref[here, :].astype(F32))[0].astype(BF)
        ref[here, :] = clean
        return (clean.astype(F32) * gains[0:1, :] + shifts[0:1, :]).astype(BF)

    @pl.loop(0, q_blocks)
    def _(b):
        here = rows_at(b * BLOCK, BLOCK, BLOCK)
        q = (dot(hidden(xq, here), weights[:, :width]) + biases[:, :width]).astype(BF)
        for h in range(heads):
            qx[h, here, :] = q[:, h * LANES : (h + 1) * LANES]

    @pl.loop(0, k_blocks)
    def _(b):
        here = rows_at(b * BLOCK, BLOCK, BLOCK)
        both = dot(hidden(xk, here), weights[:, width:]) + biases[:, width:]
        unseen = (iota((BLOCK, width), 0) + b * BLOCK >= k_total) & (
            iota((BLOCK, width), 1) % LANES == HD
        )
        k = jnp.where(unseen, FAR, both[:, :width]).astype(BF)
        v = both[:, width:].astype(BF)
        for h in range(heads):
            kx[h, here, :] = k[:, h * LANES : (h + 1) * LANES]
            vx[h, here, :] = v[:, h * LANES : (h + 1) * LANES]

    copies = [
        pltpu.make_async_copy(held, to, sems.at[i])
        for i, (held, to) in enumerate(zip((xq, xk, qx, kx, vx), kept))
    ]
    for copy in copies:
        copy.start()

    def attend_all(span):
        @pl.loop(0, q_blocks)
        def _(b):
            here = rows_at(b * BLOCK, BLOCK, BLOCK)
            lane = iota((BLOCK, LANES), 1)
            for h in range(heads):
                s = dot_nt(qx[h, here, :], kx[h, :span, :])
                top = jnp.max(s, axis=-1, keepdims=True)
                o = dot(jnp.exp(s - top).astype(BF), vx[h, :span, :])
                total = o[:, HD : HD + 1]
                o = o / total
                for i, piece in enumerate(pieces(top + jnp.log(total))):
                    o = jnp.where(lane == HD + i, piece.astype(F32), o)
                place[h, here, :] = o.astype(BF)

    for blocks in range(groups * TILE // BLOCK, groups * rows // BLOCK + 1):
        pl.when(k_blocks == blocks)(functools.partial(attend_all, blocks * BLOCK))

    gather = [
        (iota((LANES, LANES), 0) - HD + 3 * h == iota((LANES, LANES), 1))
        & (iota((LANES, LANES), 0) >= HD)
        & (iota((LANES, LANES), 0) < HD + 3)
        for h in range(heads)
    ]
    gather = [jnp.where(m, 1.0, 0.0).astype(BF) for m in gather]
    start = jnp.int32(0)
    for g in range(groups):
        mine = [place[h, rows_at(start, rows), :] for h in range(heads)]
        stats = sum(dot(m, s) for m, s in zip(mine, gather)).astype(BF)
        value = jnp.concatenate([m[:, :HD] for m in mine] + [stats], axis=1)
        if g < groups // 2:
            out[g][...] = value
        else:
            give[g - groups // 2] = value
        start = start + q_counts[g] * TILE
    for copy in copies:
        copy.wait()


def attend(near, far, weights, biases, gains, shifts, rows, heads):
    groups = len(near)
    model = near[0].shape[1]
    room = rows * groups + BLOCK
    parts = heads * HD + LANES
    kept = [(room, model)] * 2 + [(heads, room, LANES)] * 3
    return local_call(
        functools.partial(attend_kernel, rows, groups, heads),
        "attend",
        (
            *[shaped(rows, parts)] * (groups // 2),
            shaped(groups // 2, rows, parts),
            *[shaped(*k) for k in kept],
            shaped(2 * groups, dtype=jnp.int32),
        ),
        [VMEM] * (groups + 5),
        (*[VMEM] * (groups // 2 + 1), *[ANY] * 5, SMEM),
        (*near, far, weights, biases, gains, shifts),
        [
            pltpu.VMEM((heads, room, LANES), BF),
            *[pltpu.VMEM(k, BF) for k in kept],
            pltpu.SemaphoreType.DMA((5,)),
        ],
        cost(15),
        ROOM,
    )


def same_tile(rows):
    return iota((rows, rows), 0) // TILE == iota((rows, rows), 1) // TILE


def thumb_kernel(heads, tokens, weights, biases, gains, shifts, out, xhat, x):
    width = heads * LANES
    size = tokens.shape[0]
    clean = standard(tokens[...].astype(F32))[0].astype(BF)
    xhat[...] = clean
    hidden = (clean.astype(F32) * gains[0:1, :] + shifts[0:1, :]).astype(BF)
    x[...] = (dot(hidden, weights[...]) + biases[...]).astype(BF)
    visible = same_tile(size - TILE)
    out[:TILE, :] = jnp.zeros((TILE, heads * HD), F32)
    for h in range(heads):
        q = x[TILE:, h * LANES : (h + 1) * LANES]
        k = x[TILE:, width + h * LANES : width + (h + 1) * LANES]
        v = x[TILE:, 2 * width + h * LANES : 2 * width + (h + 1) * LANES]
        s = jnp.where(visible, dot_nt(q, k), FAR)
        e = jnp.exp(s - jnp.max(s, axis=-1, keepdims=True))
        o = dot(e.astype(BF), v)[:, :HD] / jnp.sum(e, axis=-1, keepdims=True)
        out[TILE:, h * HD : (h + 1) * HD] = o


def thumbs(tokens, weights, biases, gains, shifts, heads):
    size, model = tokens.shape
    return local_call(
        functools.partial(thumb_kernel, heads),
        "thumbs",
        (
            shaped(size, heads * HD, dtype=F32),
            shaped(size, model),
            shaped(size, 3 * heads * LANES),
        ),
        [VMEM] * 5,
        (VMEM,) * 3,
        (tokens, weights, biases, gains, shifts),
        cost=cost(5),
    )


def merged(parts, heads):
    cols = heads * HD
    row, col = (iota((LANES, cols), d) for d in (0, 1))
    spread = zero_one(row // 3 == col // HD)
    marks = [dot(p[:, cols:], spread) for p in parts]
    top = functools.reduce(jnp.maximum, marks)
    expos = [jnp.exp(m - top) for m in marks]
    total = sum(expos)
    mixed = sum(e * p[:, :cols].astype(F32) for p, e in zip(parts, expos)) / total
    row, col = (iota((cols, LANES), d) for d in (0, 1))
    packed = [
        dot(piece, zero_one((row % HD == 0) & (col == 3 * (row // HD) + i)))
        for i, piece in enumerate(pieces(top + jnp.log(total)))
    ]
    return mixed, sum(packed)


def pair_kernel(heads, *refs):
    count = (len(refs) - 1) // 2
    for j, (mine, out) in enumerate(zip(refs[:count], refs[count + 1 :])):
        mixed, marks = merged([mine[...], refs[count][j]], heads)
        out[...] = jnp.concatenate([mixed.astype(BF), marks.astype(BF)], axis=1)


def pair_merge(parts, other, heads):
    return local_call(
        functools.partial(pair_kernel, heads),
        "pair_merge",
        tuple(shaped(*p.shape) for p in parts),
        [VMEM] * (len(parts) + 1),
        (VMEM,) * len(parts),
        (*parts, other),
        cost=cost(3),
        room=ROOM,
    )


def merge_kernel(heads, counts, thumb, *refs):
    parts, (low, full, lse) = refs[:-3], refs[-3:]
    cols = heads * HD
    rows = lse.shape[0]
    mixed, marks = merged([p[...] for p in parts], heads)
    lse[...] = (-marks).astype(BF)
    image = iota((rows, cols), 0) < counts[0] * TILE
    full[:rows, :] = jnp.where(image, mixed, thumb[:rows, :])
    full[rows:, :] = thumb[rows:, :]
    low[...] = full[...].astype(BF)


def merge(count, parts, thumb, heads):
    size, cols = thumb.shape
    return local_call(
        functools.partial(merge_kernel, heads),
        "merge",
        (shaped(size, cols), shaped(size, cols, dtype=F32), shaped(parts[0].shape[0], LANES)),
        [SMEM] + [VMEM] * (1 + len(parts)),
        (VMEM,) * 3,
        (count, thumb, *parts),
        cost=cost(3),
    )


def fold_kernel(*refs):
    count = (len(refs) - 1) // 2
    for j, (mine, out) in enumerate(zip(refs[:count], refs[count + 1 :])):
        out[...] = (mine[...].astype(F32) + refs[count][j].astype(F32)).astype(BF)


def fold(parts, other):
    return local_call(
        fold_kernel,
        "fold",
        tuple(shaped(*p.shape) for p in parts),
        [VMEM] * (len(parts) + 1),
        (VMEM,) * len(parts),
        (*parts, other),
        cost=cost(2),
        room=ROOM,
    )


ROOT = 0.7978845608028654
CUBE = 0.044715


def ff_kernel(
    heads, tokens, outer, low, low_far, full, lse, out_weight, out_far, up, up_bias, down, far_one,
    far_two, gains, shifts, mixed, grad_mid, grad_low, packed, hidden_out, act_out, pre_out, small,
):
    size, model = tokens.shape
    passes = outer.shape[0]
    cols = heads * HD
    chunk = far_one.shape[1]
    units = up.shape[1]
    rows = packed.shape[0]
    branch = dot(low[...], out_weight[...]) + dot(low_far[...], out_far[...])
    middle = tokens[...].astype(F32) + (branch + shifts[1:2, :])
    xhat, factor = standard(middle)
    hidden = (xhat * gains[1:2, :] + shifts[2:3, :]).astype(BF)
    hidden_out[...] = hidden

    def one_chunk(up_part, bias, down_part, keep):
        v = dot(hidden, up_part) + bias
        t = jnp.tanh(ROOT * (v + CUBE * (v * v * v)))
        act = (0.5 * v * (1.0 + t)).astype(BF)
        slope = 0.5 * (1.0 + t) + 0.5 * v * (1.0 - t * t) * (ROOT * (1.0 + 3.0 * CUBE * (v * v)))
        two = []
        for p in range(passes):
            pre = (dot_nt(outer[p], down_part) * slope).astype(BF)
            if keep is not None:
                pre_out[p, :, keep] = pre
            two.append(dot_nt(pre, up_part))
        if keep is not None:
            act_out[:, keep] = act
        return dot(act, down_part), two

    def far_chunk(ref):
        told = ref[2 * chunk : 2 * chunk + 16, :].astype(F32)
        bias = told[0:1] + told[1:2] + told[2:3]
        return one_chunk(ref[:chunk, :], bias, ref[chunk : 2 * chunk, :], None)

    done = []
    for i in range(units // chunk):
        at = slice(i * chunk, (i + 1) * chunk)
        done.append(one_chunk(up[:, at], up_bias[:, at], down[at, :], at))
    done += [far_chunk(far_one), far_chunk(far_two)]

    def tree(parts):
        half = len(parts) // 2
        return sum(parts[:half]) + sum(parts[half:])

    output = tree([d[0] for d in done])
    mixed[...] = (middle + (output + shifts[3:4, :])).astype(BF)
    small[...] = jnp.zeros(small.shape, F32)
    lane = iota((rows, LANES), 1)
    stats = jnp.zeros((rows, LANES), F32)
    for p in range(passes):
        two = tree([d[1][p] for d in done])
        c = outer[p].astype(F32)
        mid = c + norm_back(two, gains[1:2, :], xhat, factor)
        mid_low = mid.astype(BF)
        grad_mid[p] = mid
        grad_low[p] = mid_low
        att = dot_nt(mid_low, out_weight[...]).astype(BF)
        packed[:, p * cols : (p + 1) * cols] = att[:rows, :]
        pre_out_p = pre_out[p].astype(F32)
        bias = jnp.sum(pre_out_p, axis=0, keepdims=True)
        small[p, 0:1, :] = jnp.sum(two * xhat, axis=0, keepdims=True)
        small[p, 1:2, :] = jnp.sum(two, axis=0, keepdims=True)
        small[p, 2:3, :] = jnp.sum(mid_low.astype(F32), axis=0, keepdims=True)
        small[p, 3:4, :] = jnp.sum(c, axis=0, keepdims=True)
        for i in range(units // model):
            small[p, 4 + i : 5 + i, :] = bias[:, i * model : (i + 1) * model]
        product = att[:rows, :].astype(F32) * full[:rows, :]
        for h in range(heads):
            delta = jnp.sum(product[:, h * HD : (h + 1) * HD], axis=-1, keepdims=True)
            for i, piece in enumerate(pieces(-delta)):
                stats = jnp.where(lane == 3 * heads * (p + 1) + 3 * h + i, piece.astype(F32), stats)
    packed[:, passes * cols :] = (stats + lse[...].astype(F32)).astype(BF)


def feed_forward(
    tokens, outer, low, low_far, full, lse, out_weight, out_far, up, up_bias, down, far_one, far_two,
    gains, shifts, rows, heads,
):
    size, model = tokens.shape
    passes = outer.shape[0]
    units = up.shape[1]
    return local_call(
        functools.partial(ff_kernel, heads),
        "feed_forward",
        (
            shaped(size, model),
            shaped(passes, size, model, dtype=F32),
            shaped(passes, size, model),
            shaped(rows, passes * heads * HD + LANES),
            shaped(size, model),
            shaped(size, units),
            shaped(passes, size, units),
            shaped(passes, 8, model, dtype=F32),
        ),
        [VMEM] * 15,
        (VMEM,) * 8,
        (
            tokens, outer, low, low_far, full, lse, out_weight, out_far, up, up_bias, down, far_one,
            far_two, gains, shifts,
        ),
        cost=cost(12),
        room=32,
    )


def thumb_back_kernel(heads, counts, x, mid_low, out_weight, out):
    width = heads * LANES
    size = x.shape[0]
    passes = mid_low.shape[0]
    visible = same_tile(size - TILE)
    outside = iota((size - TILE, HD), 0) + TILE >= counts[0] * TILE
    grads = [dot_nt(mid_low[p], out_weight[...]).astype(BF) for p in range(passes)]
    out[:, :, :TILE, :] = jnp.zeros((*out.shape[:2], TILE, out.shape[3]), BF)
    for h in range(heads):
        q = x[TILE:, h * LANES : (h + 1) * LANES]
        k = x[TILE:, width + h * LANES : width + (h + 1) * LANES]
        v = x[TILE:, 2 * width + h * LANES : 2 * width + h * LANES + HD]
        s = jnp.where(visible, dot_nt(q, k), FAR)
        e = jnp.exp(s - jnp.max(s, axis=-1, keepdims=True))
        w = e / jnp.sum(e, axis=-1, keepdims=True)
        w_low = w.astype(BF)
        for p in range(passes):
            g = grads[p][TILE:, h * HD : (h + 1) * HD]
            gw = dot_nt(g, v)
            ds = (w * (gw - jnp.sum(w * gw, axis=-1, keepdims=True))).astype(BF)
            dq = dot(ds, k[:, :HD]) * SCALE
            dk = dot_tn(ds, q)[:, :HD]
            dv = dot_tn(w_low, g)
            for c, piece in enumerate((dq, dk, dv)):
                at = c * LANES + (h % 2) * HD
                out[h // 2, p, TILE:, at : at + HD] = jnp.where(outside, piece, 0.0).astype(BF)


def thumbs_back(count, x, mid_low, out_weight, heads):
    passes, size, _ = mid_low.shape
    return local_call(
        functools.partial(thumb_back_kernel, heads),
        "thumbs_back",
        shaped(heads // 2, passes, size, 3 * LANES),
        [SMEM] + [VMEM] * 3,
        VMEM,
        (count, x, mid_low, out_weight),
        cost=cost(6),
    )


def early_at(units, model, low):
    ends = [model, 2 * model, 2 * model + units, 2 * model + units + low]
    return [slice(b - w, b) for b, w in zip(ends, (model, model, units, low))]


def early_cuts(parts, units, model, low):
    high, wide, turns = units // parts // 2, model // parts, model // low
    narrow = low * turns // parts
    for i in range(parts):
        yield (
            (slice(2 * i * high, (2 * i + 1) * high), slice(0, model)),
            (slice((2 * i + 1) * high, (2 * i + 2) * high), slice(0, model)),
            (slice(i * wide, (i + 1) * wide), slice(0, units)),
            (
                slice(i // turns * narrow, (i // turns + 1) * narrow),
                slice(i % turns * low, (i % turns + 1) * low),
            ),
        )


def weight_kernel(place, act, outer, hidden, pre, low, mid_low, keep, give):
    units, model, cols = act.shape[1], hidden.shape[1], low.shape[1]
    core = place[0]
    for turn, out in ((core, keep), (1 - core, give)):
        down = dot_tn(act[...], outer[turn]).astype(BF)
        up = dot_tn(hidden[...], pre[turn]).astype(BF)
        proj = dot_tn(low[...], mid_low[turn]).astype(BF)
        for i, cut in enumerate(early_cuts(keep.shape[0], units, model, cols)):
            for value, (rows, lanes), at in zip(
                (down, down, up, proj), cut, early_at(units, model, cols)
            ):
                out[i, :, at] = value[rows, lanes]


def weight_grads(core, act, outer, hidden, pre, low, mid_low, parts):
    units, model = act.shape[1], outer.shape[2]
    out = shaped(parts, model // parts, 2 * model + units + low.shape[1])
    return local_call(
        weight_kernel,
        "weight_grads",
        (out, out),
        [SMEM] + [VMEM] * 6,
        (VMEM,) * 2,
        (core, act, outer, hidden, pre, low, mid_low),
        cost=cost(8),
        room=24,
    )


def reverse_kernel(rows, groups, heads, passes, counts, place, *refs):
    grads, kept = refs[:groups], refs[groups : groups + 5]
    own, thumb, weights, columns, small = refs[groups + 5 : groups + 10]
    at = groups + 10
    out_q, give_q, at = refs[at : at + groups // 2], refs[at + groups // 2], at + groups // 2 + 1
    out_kv, at = refs[at : at + groups // 2], at + groups // 2
    keep, give = refs[at : at + 2]
    (
        stage, xq, xk, qx, kx, vx, packed, gx, kt, dq_t, dv, dk, low_q, low_kv, total, sums,
        starts, sems,
    ) = refs[at + 2 :]
    couples = heads // 2
    sources = [*grads, *kept[2:], *kept[:2]]
    targets = [*[stage.at[g] for g in range(groups)], qx, kx, vx, xq, xk]
    copies = [
        pltpu.make_async_copy(f, t, sems.at[i]) for i, (f, t) in enumerate(zip(sources, targets))
    ]
    for copy in copies:
        copy.start()
    cols = heads * HD
    wide = passes * LANES
    q_counts = [counts[g] for g in range(groups)]
    k_counts = [counts[groups + g] for g in range(groups)]
    start = jnp.int32(0)
    for g in range(groups):
        copies[g].wait()
        packed[rows_at(start, rows), :] = stage[g]
        start = start + q_counts[g] * TILE
    q_total, k_total = start, sum(k_counts) * TILE
    tail_lane = iota((BLOCK, packed.shape[1]), 1) - passes * cols
    empty = (tail_lane >= 0) & (tail_lane < 3 * heads) & (tail_lane % 3 == 0)
    packed[rows_at(q_total, BLOCK), :] = jnp.where(empty, FAR, 0.0).astype(BF)
    q_blocks = (q_total + BLOCK - 1) // BLOCK
    k_blocks = (k_total + BLOCK - 1) // BLOCK
    spans = range(groups * TILE // BLOCK, groups * rows // BLOCK + 1)

    row, col = (iota((LANES, heads * LANES), d) for d in (0, 1))
    head, lane = col // LANES, col % LANES
    to_marks = zero_one((lane > HD) & (lane < HD + 4) & (row == 3 * head + lane - HD - 1))
    row, col = (iota((LANES, heads * wide), d) for d in (0, 1))
    head, turn, lane = col // wide, col % wide // LANES, col % LANES
    to_deltas = zero_one(
        (lane >= HD) & (lane < HD + 3) & (row == 3 * heads * (turn + 1) + 3 * head + lane - HD)
    )
    for copy in copies[groups : groups + 3]:
        copy.wait()

    @pl.loop(0, q_blocks)
    def _(b):
        here = rows_at(b * BLOCK, BLOCK, BLOCK)
        stats = packed[here, passes * cols :]
        marks = dot(stats, to_marks)
        deltas = dot(stats, to_deltas).astype(BF)
        for h in range(heads):
            more = marks[:, h * LANES : (h + 1) * LANES]
            qx[h, here, :] = (qx[h, here, :].astype(F32) + more).astype(BF)
            for p in range(passes):
                at = p * cols + h * HD
                mine = (h * passes + p) * LANES
                gx[h, here, p * LANES : (p + 1) * LANES] = jnp.concatenate(
                    [packed[here, at : at + HD], deltas[:, mine + HD : mine + LANES]], axis=1
                )

    @pl.loop(0, k_blocks)
    def _(b):
        here = rows_at(b * BLOCK, BLOCK, BLOCK)
        for h in range(heads):
            kt[h, b] = jnp.transpose(kx[h, here, :].astype(F32))[:HD, :].astype(BF)

    def reverse_all(blocks):
        span = blocks * BLOCK

        @pl.loop(0, couples)
        def _(pair):
            dv[:, :span, :] = jnp.zeros((2, span, wide), F32)
            dk[:, :, :span, :] = jnp.zeros((passes, 2, span, LANES), F32)

            @pl.loop(0, q_blocks)
            def _(b):
                here = rows_at(b * BLOCK, BLOCK, BLOCK)
                for i in range(2):
                    h = 2 * pair + i
                    q, g = qx[h, here, :], gx[h, here, :]
                    k_t = jnp.concatenate([kt[h, j] for j in range(blocks)], axis=1)
                    w = jnp.exp(dot_nt(kx[h, :span, :], q))
                    dv[i, :span, :] += dot(w.astype(BF), g)
                    for p in range(passes):
                        ds = dot_nt(vx[h, :span, :], g[:, p * LANES : (p + 1) * LANES])
                        ds = (w * ds).astype(BF)
                        dk[p, i, :span, :] += dot(ds, q)
                        dq_t[p, i * HD : (i + 1) * HD, :] = dot(k_t, ds)
                for p in range(passes):
                    piece = jnp.transpose(dq_t[p]) * SCALE
                    low_q[pair, here, p * LANES : (p + 1) * LANES] = piece.astype(BF)

            for p in range(passes):
                for c, both in enumerate(
                    (
                        [dk[p, i, :span, :HD] for i in range(2)],
                        [dv[i, :span, p * LANES : p * LANES + HD] for i in range(2)],
                    )
                ):
                    lane = (2 * p + c) * LANES
                    low_kv[pair, :span, lane : lane + LANES] = jnp.concatenate(both, axis=1).astype(BF)

    for blocks in spans:
        pl.when(k_blocks == blocks)(functools.partial(reverse_all, blocks))

    start = jnp.int32(0)
    for g in range(groups):
        starts[g] = start
        start = start + k_counts[g] * TILE
    for g in range(groups):
        here = rows_at(starts[place[1 + g]], rows)
        out_kv[g // 2][g % 2] = jnp.concatenate([low_kv[i, here, :] for i in range(couples)], axis=1)
    start = jnp.int32(0)
    for g in range(groups):
        here = rows_at(start, rows)
        value = jnp.concatenate([low_q[i, here, :] for i in range(couples)], axis=1)
        if g < groups // 2:
            out_q[g][...] = value
        else:
            give_q[g - groups // 2] = value
        start = start + q_counts[g] * TILE

    copies[groups + 3].wait()
    copies[groups + 4].wait()

    def key_sums(blocks):
        span = blocks * BLOCK
        for i in range(couples):
            flat = low_kv[i, :span, :]
            total[i, :, wide:] = dot_tn(xk[:span, :], flat)
            sums[i, :, wide:] = dot(jnp.ones((8, span), BF), flat)

    for blocks in spans:
        pl.when(k_blocks == blocks)(functools.partial(key_sums, blocks))

    total[:, :, :wide] = jnp.zeros((couples, total.shape[1], wide), F32)
    sums[:, :, :wide] = jnp.zeros((couples, 8, wide), F32)

    @pl.loop(0, q_blocks)
    def _(b):
        here = rows_at(b * BLOCK, BLOCK, BLOCK)
        for i in range(couples):
            total[i, :, :wide] += dot_tn(xq[here, :], low_q[i, here, :])
            sums[i, :, :wide] += dot(jnp.ones((8, BLOCK), BF), low_q[i, here, :])

    model = total.shape[1]
    gain, shift = columns[:, 0:1], columns[:, 1:2]
    ones = jnp.ones((8, own.shape[0]), BF)
    for p in range(passes):
        whole = []
        for i in range(couples):
            mine = thumb[i, p]
            part = dot_tn(own[...], mine)
            part_sum = dot(ones, mine)[0:1, :]
            q_at = slice(p * LANES, (p + 1) * LANES)
            kv_at = slice((passes + 2 * p) * LANES, (passes + 2 * p + 2) * LANES)
            part += jnp.concatenate([total[i, :, q_at], total[i, :, kv_at]], axis=1)
            part_sum += jnp.concatenate([sums[i, 0:1, q_at], sums[i, 0:1, kv_at]], axis=1)
            w = weights[i].astype(F32)
            gain_one = jnp.sum(w * part, axis=1, keepdims=True)
            shift_one = jnp.sum(w * part_sum, axis=1, keepdims=True)
            lane = iota((model, LANES), 1)
            tall = jnp.where(lane == 0, gain_one, jnp.where(lane == 1, shift_one, 0.0))
            flat = jnp.concatenate(
                [jnp.zeros((2, LANES), F32)]
                + [part_sum[:, c * LANES : (c + 1) * LANES] for c in range(3)]
                + [jnp.zeros((LANES - 5, LANES), F32)],
                axis=0,
            )
            tall = jnp.concatenate([tall[:LANES] + jnp.transpose(flat), tall[LANES:]], axis=0)
            if i == 0:
                turned = jnp.concatenate(
                    [
                        jnp.zeros((8, model), F32),
                        small[p],
                        jnp.zeros((LANES - 16, model), F32),
                    ],
                    axis=0,
                )
                tall = tall + jnp.transpose(turned)
            whole += [part * gain + shift * part_sum, tall]
        whole = jnp.concatenate(whole, axis=1).astype(BF)

        @pl.when(place[0] == p)
        def _():
            keep[...] = whole

        @pl.when(place[0] != p)
        def _():
            give[...] = whole


def reverse(counts, place, grads, kept, own, thumb, weights, columns, small, rows, heads):
    groups = len(grads)
    couples, passes = thumb.shape[:2]
    model = own.shape[1]
    room = rows * groups + BLOCK
    cols = heads * HD
    wide = passes * LANES
    half = groups // 2
    late = shaped(model, couples * 4 * LANES)
    q, kv = shaped(rows, couples * wide), shaped(2, rows, couples * 2 * wide)
    out = (*[q] * half, shaped(half, rows, couples * wide), *[kv] * half, late, late)
    return local_call(
        functools.partial(reverse_kernel, rows, groups, heads, passes),
        "reverse",
        out,
        [SMEM, SMEM] + [ANY] * (groups + 5) + [VMEM] * 5,
        (VMEM,) * len(out),
        (counts, place, *grads, *kept, own, thumb, weights, columns, small),
        [
            pltpu.VMEM((groups, rows, passes * cols + LANES), BF),
            pltpu.VMEM((room, model), BF),
            pltpu.VMEM((room, model), BF),
            pltpu.VMEM((heads, room, LANES), BF),
            pltpu.VMEM((heads, room, LANES), BF),
            pltpu.VMEM((heads, room, LANES), BF),
            pltpu.VMEM((room, passes * cols + LANES), BF),
            pltpu.VMEM((heads, room, wide), BF),
            pltpu.VMEM((heads, room // BLOCK, HD, BLOCK), BF),
            pltpu.VMEM((passes, LANES, BLOCK), F32),
            pltpu.VMEM((2, room, wide), F32),
            pltpu.VMEM((passes, 2, room, LANES), F32),
            pltpu.VMEM((couples, room, wide), BF),
            pltpu.VMEM((couples, room, 2 * wide), BF),
            pltpu.VMEM((couples, model, 3 * wide), F32),
            pltpu.VMEM((couples, 8, 3 * wide), F32),
            pltpu.SMEM((groups,), jnp.int32),
            pltpu.SemaphoreType.DMA((groups + 5,)),
        ],
        cost(45),
        ROOM,
    )


def grad_one_kernel(near, counts, *refs):
    from_q, from_kv, (thumb, weights, mine, other) = refs[:near], refs[near:-4], refs[-4:]
    couples, passes, size, _ = thumb.shape
    rows = from_q[0].shape[0]
    sum_q = sum(r[...].astype(F32) for r in from_q)
    sum_kv = [sum(r[f].astype(F32) for r in from_kv) for f in range(2)]
    image = iota((rows, 3 * LANES), 0) < counts[0] * TILE
    for p in range(passes):
        parts = []
        for i in range(couples):
            at = (passes * i + p) * LANES
            there = slice(2 * at, 2 * at + 2 * LANES)
            far = jnp.concatenate([sum_q[:, at : at + LANES], sum_kv[0][:, there]], axis=1)
            flat = jnp.concatenate(
                [jnp.where(image, far.astype(BF), thumb[i, p, :rows]), thumb[i, p, rows:]], axis=0
            )
            parts.append(
                (
                    dot_nt(flat, weights[i]),
                    dot_nt(sum_kv[1][:, there].astype(BF), weights[i, :, LANES:]),
                )
            )
        mine[p] = sum(a for a, _ in parts).astype(BF)
        other[p] = sum(b for _, b in parts).astype(BF)


def grad_one(count, from_q, from_kv, thumb, weights):
    near = len(from_q)
    passes, size, _ = thumb.shape[1:]
    model = weights.shape[1]
    return local_call(
        functools.partial(grad_one_kernel, near),
        "grad_one",
        (shaped(passes, size, model), shaped(passes, from_q[0].shape[0], model)),
        [SMEM] + [VMEM] * (near + len(from_kv) + 2),
        (VMEM,) * 2,
        (count, *from_q, *from_kv, thumb, weights),
        cost=cost(5),
        room=ROOM,
    )


def close_kernel(counts, tokens, mid, mine, head, side, cross, gains, out):
    xhat, factor = standard(tokens[...].astype(F32))
    rows = side.shape[1]
    image = iota(side.shape[1:], 0) < counts[0] * TILE
    for p in range(mid.shape[0]):
        grad = mine[p].astype(F32) + head[p].astype(F32)
        more = jnp.where(image, side[p].astype(F32) + cross[p].astype(F32), 0.0)
        grad = jnp.concatenate([grad[:rows] + more, grad[rows:]], axis=0)
        out[p] = mid[p] + norm_back(grad, gains[0:1, :], xhat, factor)


def close(count, tokens, mid, mine, head, side, cross, gains):
    return local_call(
        close_kernel,
        "close",
        shaped(*mid.shape, dtype=F32),
        [SMEM] + [VMEM] * 7,
        VMEM,
        (count, tokens, mid, mine, head, side, cross, gains),
        cost=cost(4),
        room=ROOM,
    )


def early_kernel(lines, far, place, *refs):
    parts, refs = refs[:lines], refs[lines:]
    out, (down, up, proj, sems) = refs[-7:-4], refs[-4:]
    turn, y = place[0], place[10]
    turn = 1 - turn if far else turn
    (units, model), low = down.shape, proj.shape[0]
    steps, rows = parts[0].shape[:2]
    lane_down, lane_next, lane_up, lane_proj = early_at(units, model, low)
    turns = model // low
    for d, ref in enumerate(parts):
        for j in range(steps):
            i = j * lines + (y + lines - d) % lines
            at = pl.multiple_of(2 * rows * i, 2 * rows)
            down[pl.ds(at, rows), :] = ref[j, :, lane_down].astype(F32)
            down[pl.ds(at + rows, rows), :] = ref[j, :, lane_next].astype(F32)
            up[rows_at(rows * i, rows, rows), :] = ref[j, :, lane_up].astype(F32)
            here = rows_at(i // turns * rows, rows, rows)
            value = ref[j, :, lane_proj].astype(F32)
            for t in range(turns):

                @pl.when(i % turns == t)
                def _(value=value, here=here, t=t):
                    proj[here, t * low : (t + 1) * low] = value

    copies = [
        pltpu.make_async_copy(held, to.at[turn], sems.at[n])
        for n, (held, to) in enumerate(zip((down, up, proj), out))
    ]
    for copy in copies:
        copy.start()
    for copy in copies:
        copy.wait()


def early_out(place, parts, before, units, low):
    model = len(parts) * parts[0].shape[0] * parts[0].shape[1]
    shapes = (units, model), (model, units), (low, model)
    return pl.pallas_call(
        functools.partial(early_kernel, len(parts), bool(before)),
        out_shape=tuple(shaped(2, *s, dtype=F32) for s in shapes),
        in_specs=[SMEM] + [VMEM] * len(parts) + [ANY] * len(before),
        out_specs=(ANY,) * 3,
        scratch_shapes=[
            *[pltpu.VMEM(s, F32) for s in shapes],
            pltpu.SemaphoreType.DMA((3,)),
        ],
        input_output_aliases={1 + len(parts) + i: i for i in range(len(before))},
        cost_estimate=cost(5),
        compiler_params=pltpu.CompilerParams(vmem_limit_bytes=ROOM * MIB),
        name="early_far" if before else "early_own",
    )(place, *parts, *before)


def late_kernel(far, place, ref, *refs):
    out, (grad_in, *small), sems = refs[-11:-6], refs[-6:-1], refs[-1]
    in_bias, up_bias, gains, shifts = small
    turn = 1 - place[0] if far else place[0]
    turned = []
    for pair in range(2):
        at = 4 * LANES * pair
        for c in range(3):
            grad_in[c, :, pair * LANES : (pair + 1) * LANES] = ref[
                :, at + c * LANES : at + (c + 1) * LANES
            ].astype(F32)
        turned.append(jnp.transpose(ref[:, at + 3 * LANES : at + 4 * LANES].astype(F32)))
    a, b = turned
    in_bias[...] = jnp.concatenate(
        [
            jnp.concatenate([a[2:3, :LANES], b[2:3, :LANES]], axis=1),
            jnp.concatenate([a[4:5, :LANES], b[4:5, :LANES]], axis=1),
        ],
        axis=0,
    )
    up_bias[...] = jnp.concatenate([a[12:13], a[13:14]], axis=1)
    gains[...] = jnp.concatenate([a[0:1] + b[0:1], a[8:9]], axis=0)
    shifts[...] = jnp.concatenate([a[1:2] + b[1:2], a[10:11], a[9:10], a[11:12]], axis=0)
    copies = [
        pltpu.make_async_copy(held, to.at[turn], sems.at[n])
        for n, (held, to) in enumerate(zip((grad_in, *small), out))
    ]
    for copy in copies:
        copy.start()
    for copy in copies:
        copy.wait()


def late_out(place, part, before, units):
    model = part.shape[0]
    shapes = (3, model, 2 * LANES), (2, 2 * LANES), (1, units), (2, model), (4, model)
    return pl.pallas_call(
        functools.partial(late_kernel, bool(before)),
        out_shape=tuple(shaped(2, *s, dtype=F32) for s in shapes),
        in_specs=[SMEM, VMEM] + [ANY] * len(before),
        out_specs=(ANY,) * 5,
        scratch_shapes=[
            *[pltpu.VMEM(s, F32) for s in shapes],
            pltpu.SemaphoreType.DMA((5,)),
        ],
        input_output_aliases={2 + i: i for i in range(len(before))},
        cost_estimate=cost(3),
        compiler_params=pltpu.CompilerParams(vmem_limit_bytes=ROOM * MIB),
        name="late_far" if before else "late_own",
    )(place, part, *before)


def gather_near(array):
    mine = [array] + [shift_by(array, "y", d) for d in range(1, lax.axis_size("y"))]
    return mine + [shift_by(a, "c", 1) for a in mine]


def return_near(parts):
    return [parts[0]] + [shift_by(p, "y", -j) for j, p in enumerate(parts) if j > 0]


def offsets(size):
    return [(step, flip) for step in range(size) for flip in range(2)]


def return_far(parts):
    return [parts[0]] + [shift_by(p, "z", step) for step, p in enumerate(parts) if step > 0]


PLANE = ("z", "y")


def core_sum(keep, give):
    return (keep.astype(F32) + shift_by(give, "c", 1).astype(F32)).astype(BF)


def crossed(array):
    n = lax.axis_size(("xl", "h"))
    return lax.ppermute(array, ("xl", "h"), [(i, n - 1 - i) for i in range(n)])


def across(low):
    done = low.astype(F32) + shift_by(low, "xl", 1).astype(F32)
    size = 4 * LANES
    ones = jnp.concatenate([low[:, i + 3 * LANES : i + size] for i in range(0, low.shape[1], size)], axis=1)
    more = shift_by(ones, "h", 1).astype(F32) + crossed(ones).astype(F32)
    more = jnp.where(jnp.arange(more.shape[1]) % LANES < 2, more, 0.0)
    nothing = jnp.zeros((low.shape[0], 3 * LANES), F32)
    laid = [[nothing, more[:, i : i + LANES]] for i in range(0, more.shape[1], LANES)]
    return (done + jnp.concatenate(sum(laid, []), axis=1)).astype(BF)


def tied(arrays, others):
    return lax.optimization_barrier((arrays, others))


def local(
    tokens,
    cotangents,
    segment_ids,
    in_weights,
    in_biases,
    out_weight,
    up_weight,
    up_biases,
    down_weight,
    gains,
    shifts,
):
    size, model = tokens.shape
    cols = in_weights.shape[2]
    heads = cols // HD
    rows = size - TILE
    units = up_weight.shape[1]
    c = lax.axis_index("c")

    told, copies, count = front(tokens, segment_ids, lax.axis_size(("z", "xl")))
    far = lax.all_to_all(copies, ("z", "xl"), 0, 0, tiled=True)
    near = gather_near(told)
    core = c.astype(jnp.int32).reshape(1)
    z, xl, z_size = lax.axis_index("z"), lax.axis_index("xl"), lax.axis_size("z")
    routes = [((z + step) % z_size) * 2 + (xl ^ flip) for step, flip in offsets(z_size)]
    place = jnp.stack([c, *routes, z, lax.axis_index("y")]).astype(jnp.int32)
    plane = lax.axis_size(PLANE)

    weights, biases, pairs, columns, bundle = prepare(
        core, in_weights, in_biases, gains, shifts, up_weight, down_weight, up_biases[None], heads
    )
    out_far = crossed(out_weight)
    far_one = crossed(bundle)
    far_two = shift_by(far_one, "c", 1)

    weights, (out_far, columns, place) = tied(weights, (out_far, columns, place))
    *parts, give, xq, xk, qx, kx, vx, counts = attend(
        near, far, weights, biases, gains, shifts, rows, heads
    )
    thumb_out, xhat, x = thumbs(tokens, weights, biases, gains, shifts, heads)
    parts = pair_merge(parts, shift_by(give, "c", 1), heads)
    low, full, lse = merge(count, return_near(parts), thumb_out, heads)
    low_far = shift_by(low, "h", 1)
    mixed, grad_mid, mid_low, packed, hidden, act, pre, small = feed_forward(
        tokens, cotangents, low, low_far, full, lse, out_weight, out_far, up_weight, up_biases[None],
        down_weight, far_one, far_two, gains, shifts, rows, heads,
    )
    grads = gather_near(packed)
    keep, give = weight_grads(core, act, cotangents, hidden, pre, low, mid_low, plane)
    mid_low, (keep, give) = tied(mid_low, (keep, give))
    thumb = thumbs_back(count, x, mid_low, out_weight, heads)
    early = core_sum(keep, give)

    grads, (early, thumb) = tied(grads, (early, thumb))
    early = lax.all_to_all(early, PLANE, 0, 0, tiled=True)
    *out, keep, give = reverse(
        counts, place, grads, (xq, xk, qx, kx, vx), xhat, thumb, pairs, columns, small, rows, heads
    )
    half = len(near) // 2
    out_q, give_q, out_kv = out[:half], out[half], out[half + 1 :]
    early = jnp.sum(early.astype(F32), axis=0).astype(BF)
    early = (early.astype(F32) + shift_by(early, "xl", 1).astype(F32)).astype(BF)
    early = jnp.broadcast_to(early[None], (z_size, *early.shape))
    late, early = tied(core_sum(keep, give), early)
    early = lax.all_to_all(early, "z", 0, 0, tiled=True)
    from_kv = return_far(out_kv)
    out_q = fold(out_q, shift_by(give_q, "c", 1))
    from_q = return_near(out_q)
    late, (early, from_kv[1], from_kv[-1], from_q) = tied(
        late, (early, from_kv[1], from_kv[-1], from_q)
    )
    late = late.reshape(plane, -1, late.shape[1])
    late = lax.all_to_all(late, PLANE, 0, 0, tiled=True)
    early = [early] + [shift_by(early, "y", d) for d in range(1, lax.axis_size("y"))]
    mine, other = grad_one(count, from_q, from_kv, thumb, pairs)
    late, (early[1], early[-1]) = tied(late, (early[1], early[-1]))
    late = across(jnp.sum(late.astype(F32), axis=0).astype(BF))
    arrived = [shift_by(mine, "h", 1), shift_by(other, "xl", 1), crossed(other)]
    late = jnp.broadcast_to(late[None], (plane, *late.shape))
    late = lax.all_to_all(late, PLANE, 0, 0, tiled=True).reshape(model, -1)

    early_far = [shift_by(e, "c", 1) for e in early]
    late_far = shift_by(late, "c", 1)
    late = late_out(place, late, (), units)
    early, late = tied(early, late)
    early = early_out(place, early, (), units, cols)
    arrived, (early, late) = tied(arrived, (early, late))
    grad_tokens = close(count, tokens, grad_mid, mine, *arrived, gains)
    grad_down, grad_up, grad_out = early_out(place, early_far, early, units, cols)
    grad_in, in_bias, up_bias, grad_gains, grad_shifts = late_out(place, late_far, late, units)
    return (
        mixed,
        grad_tokens,
        grad_in,
        in_bias,
        grad_out,
        grad_up,
        up_bias.reshape(2, units),
        grad_down,
        grad_gains,
        grad_shifts,
    )


def solution(mesh):
    fine = Mesh(mesh.devices.reshape(4, 2, 4, 2, 2), ("z", "xl", "y", "c", "h"))
    blk = ("z", "xl", "y", "c")
    return jax.shard_map(
        local,
        mesh=fine,
        in_specs=(
            P(blk, None),
            P(None, blk, None),
            P(blk),
            P(None, None, "h"),
            P(None, "h"),
            P("h", None),
            P(None, "h"),
            P("h"),
            P("h", None),
            P(),
            P(),
        ),
        out_specs=(
            P(blk, None),
            P(None, blk, None),
            P(None, None, None, "h"),
            P(None, None, "h"),
            P(None, "h", None),
            P(None, None, "h"),
            P(None, "h"),
            P(None, "h", None),
            P(),
            P(),
        ),
        check_vma=False,
    )
```
